32 devices in a mesh: groups: 2 (over x), seq: 16 (over z, y, core).
Axes of the slice: x: 2, y: 2, z: 4, core: 2. Of those that a mesh axis runs over, the one named last changes fastest.
Arguments:
- queries: bfloat16 [256, 2560], P(('groups', 'seq')), parts along dimension 0, may hold values from -160 to 160
- new_keys: bfloat16 [256, 2560], P(('groups', 'seq')), parts along dimension 0, may hold values from -7 to 7
- new_values: bfloat16 [256, 2560], P(('groups', 'seq')), parts along dimension 0, may hold values from -6 to 6
- cache_keys: bfloat16 [16384, 2560], P(('groups', 'seq')), parts along dimension 0, may hold values from -6 to 6
- cache_values: bfloat16 [16384, 2560], P(('groups', 'seq')), parts along dimension 0, may hold values from -6 to 6
- victims: int32 [32], P('groups'), parts along dimension 0, may hold values from 0 to 63, as said below
Outputs:
- attended: bfloat16 [256, 2560], P(('groups', 'seq')), parts along dimension 0
The draws below stay inside these ranges and needn't reach their ends.
There are 2 independent parts, one for each index of `groups`. The reference program is written for one: setup_inputs(seed, part) draws one part's arguments, and reference() takes and returns one part's arrays. A program takes and returns all parts, laid end to end along the dimension named above; each array names one. Nothing has to cross between parts.
Inputs may be any that keep to these rules, and one draw needn't show every extreme that they name: `victims`: 16 distinct block ids of the cache; the first and the last block are always among them.
All inputs are finite; a program needn't handle non-finite values.
Results may differ from the reference program's by a relative error of at most 0.01.
Values may be sent and summed in bfloat16 or wider, within the bound.
No kernel may reach another device: no remote copies, remote signals or barrier semaphores. Data moves between devices by JAX's collectives and lax.ppermute only.
A program may use at most 128 MiB of HBM per device.

```python
import math
import jax
import jax.numpy as jnp
from jax import lax

H = 20
HD = 128
BLK = 128
TOK = 128
NBLK = 64
EVICT = 16


def drawn_pair(key):
    query_seed = jax.random.fold_in(key, 101)
    probe_seed = jax.random.fold_in(key, 202)
    columns = H * HD
    probe_rows = jax.random.truncated_normal(probe_seed, -6.0, 6.0, (TOK, columns), jnp.float32)
    query_rows = 3.0 * jax.random.truncated_normal(query_seed, -5.0, 5.0, (TOK, columns), jnp.float32)
    return (query_rows, probe_rows)


def draw_queries(key, part):
    return drawn_pair(key)[0].astype(jnp.bfloat16)


def draw_new_keys(key, part):
    return drawn_pair(key)[1].astype(jnp.bfloat16)


def draw_victims(key, part):
    middle = jax.random.permutation(jax.random.fold_in(key, 404), NBLK - 2).astype(jnp.int32) + 1
    ends = jnp.array([0, NBLK - 1]).astype(jnp.int32)
    chosen = jnp.concatenate([ends, middle[:EVICT - 2]])
    return jax.random.permutation(jax.random.fold_in(key, 505), chosen).astype(jnp.int32)


def block_levels(stream_key, extent, shards, smallest, top_value):
    def one(position, parts):
        steps = jax.random.uniform(jax.random.fold_in(jax.random.fold_in(stream_key, 6), position), (parts,), jnp.float32, smallest / len(shards), top_value / len(shards))
        return jnp.repeat(jnp.exp(steps), extent[position] // parts).reshape((-1,) + (1,) * (len(extent) - position - 1))

    factor_of = one(*shards[0])
    for cut in shards[1:]:
        factor_of = factor_of * one(*cut)
    return factor_of


def scatter_about(stream_key, dims, scale, reach, split=(), kind=jnp.bfloat16):
    values = jax.random.normal(stream_key, dims, jnp.float32) * scale
    if len(split) > 0:
        values = block_levels(stream_key, dims, split, -0.22, 0.18) * values
    return jnp.clip(values, min=-reach, max=reach).astype(kind)


def setup_inputs(seed: int = 0, part: int = 0) -> dict:
    streams_of = jax.random.split(jax.random.key(seed), 7)
    part_keys = jax.random.split(jax.random.fold_in(streams_of[6], part), 7)
    return {
        "queries": draw_queries(jax.random.fold_in(jax.random.fold_in(streams_of[6], part), 71), part),
        "new_keys": draw_new_keys(jax.random.fold_in(jax.random.fold_in(streams_of[6], part), 71), part),
        "new_values": scatter_about(part_keys[2], (TOK, H * HD), 1.0, 6.0, ((0, 16),)),
        "cache_keys": scatter_about(part_keys[3], (NBLK * BLK, H * HD), 1.0, 6.0, ((0, 16),)),
        "cache_values": scatter_about(part_keys[4], (NBLK * BLK, H * HD), 1.0, 6.0, ((0, 16),)),
        "victims": draw_victims(jax.random.fold_in(jax.random.fold_in(streams_of[6], part), 71), part),
    }


def similarity(query_cols, other):
    return lax.dot_general(query_cols, other, (((1,), (1,)), ((), ())), preferred_element_type=jnp.float32)

def reference(queries, new_keys, new_values, cache_keys, cache_values, victims):
    block_total = cache_keys.shape[0] // BLK
    evicted = jnp.zeros((block_total,), jnp.int32).at[victims].set(1)
    cache_live = jnp.repeat(evicted == 0, BLK)[None, :]
    scaling = 1.0 / math.sqrt(HD)

    def one_head(head):
        first_col = head * HD
        query_cols = lax.dynamic_slice_in_dim(queries, first_col, HD, 1)
        cached = similarity(query_cols, lax.dynamic_slice_in_dim(cache_keys, first_col, HD, 1)) * scaling
        cached = jnp.where(cache_live, cached, -1e+30)
        fresh_scores = similarity(query_cols, lax.dynamic_slice_in_dim(new_keys, first_col, HD, 1)) * scaling
        row_top = jnp.maximum(lax.optimization_barrier(jnp.max(cached, axis=1)), lax.optimization_barrier(jnp.max(fresh_scores, axis=1)))
        cached_exp = jnp.where(cache_live, jnp.exp(cached - row_top[:, None]), 0.0)
        fresh_exp = jnp.exp(fresh_scores - row_top[:, None])
        row_mass = lax.optimization_barrier(jnp.sum(cached_exp, axis=1)) + lax.optimization_barrier(jnp.sum(fresh_exp, axis=1))
        head_out = jnp.dot(cached_exp.astype(jnp.bfloat16), lax.dynamic_slice_in_dim(cache_values, first_col, HD, 1), preferred_element_type=jnp.float32)
        head_out = head_out + jnp.dot(fresh_exp.astype(jnp.bfloat16), lax.dynamic_slice_in_dim(new_values, first_col, HD, 1), preferred_element_type=jnp.float32)
        return head_out / row_mass[:, None]
    stacked = lax.map(one_head, jnp.arange(H, dtype=jnp.int32))
    return jnp.transpose(stacked, (1, 0, 2)).reshape(TOK, H * HD).astype(jnp.bfloat16)
```

```python
import functools
import math

import jax
import jax.numpy as jnp
from jax import lax
from jax.experimental import pallas as pl
from jax.experimental.pallas import tpu as pltpu
from jax.sharding import PartitionSpec as P

HD = 128
BLK = 128
STAT = 128
LANE = STAT // 3
NEG = -1e30
F32 = jnp.float32
BF16 = jnp.bfloat16


def factors(members):
    cores = 2 if members % 2 == 0 else 1
    chips = members // cores
    far = next(a for a in range(1, chips + 1) if chips % a == 0 and a * a >= chips)
    return far, chips // far, cores


def shift_perm(shape, axis, by):
    a_n, b_n, c_n = shape
    pairs = []
    for a in range(a_n):
        for b in range(b_n):
            for c in range(c_n):
                at = [a, b, c]
                src = list(at)
                src[axis] = (src[axis] + by) % shape[axis]
                flat = lambda p: (p[0] * b_n + p[1]) * c_n + p[2]
                pairs.append((flat(src), flat(at)))
    return pairs


def lanes(rows):
    return lax.broadcasted_iota(jnp.int32, (rows, STAT), 1)


def pack_stats(top, mass):
    high = mass.astype(BF16).astype(F32)
    return top + pltpu.roll(high, LANE, 1) + pltpu.roll(mass - high, 2 * LANE, 1)


def unpack_stats(packed, heads):
    used = lanes(packed.shape[0]) < heads
    mass = pltpu.roll(packed, STAT - LANE, 1) + pltpu.roll(packed, STAT - 2 * LANE, 1)
    return jnp.where(used, packed, 0.0), jnp.where(used, mass, 0.0)


def attend_kernel(group, scale, bias_ref, qs_refs, k_ref, v_ref, nk_ref, nv_ref, outs, top_acc, mass_acc):
    step = pl.program_id(1)
    rows = qs_refs[0].shape[0] * len(qs_refs)
    per = qs_refs[0].shape[0]
    lane = lanes(rows)

    @pl.when(step == 0)
    def _():
        top_acc[...] = jnp.zeros_like(top_acc)
        mass_acc[...] = jnp.zeros_like(mass_acc)

    contract_last = (((1,), (1,)), ((), ()))
    tops = top_acc[...]
    masses = mass_acc[...]
    bias = bias_ref[...]
    for i in range(group):
        cols = slice(i * HD, (i + 1) * HD)
        q = jnp.concatenate([r[:, cols] for r in qs_refs], axis=0)
        cached = lax.dot_general(q, k_ref[:, cols], contract_last, preferred_element_type=F32)
        fresh = lax.dot_general(q, nk_ref[:, cols], contract_last, preferred_element_type=F32)
        cached = cached * scale + bias
        fresh = fresh * scale
        top = jnp.maximum(
            jnp.max(cached, axis=1, keepdims=True), jnp.max(fresh, axis=1, keepdims=True)
        )
        top = top.astype(BF16).astype(F32)
        cached = jnp.exp2(cached - top)
        fresh = jnp.exp2(fresh - top)
        mass = jnp.sum(cached, axis=1, keepdims=True) + jnp.sum(fresh, axis=1, keepdims=True)
        out = jnp.dot(cached.astype(BF16), v_ref[:, cols], preferred_element_type=F32)
        out = out + jnp.dot(fresh.astype(BF16), nv_ref[:, cols], preferred_element_type=F32)
        head = step * group + i
        at = pl.multiple_of(head * HD, HD)
        for j, o_ref in enumerate(outs):
            o_ref[:, pl.ds(at, HD)] = out[j * per : (j + 1) * per].astype(o_ref.dtype)
        tops = jnp.where(lane == head, top, tops)
        masses = jnp.where(lane == head, mass, masses)
    top_acc[...] = tops
    mass_acc[...] = masses

    @pl.when(step == pl.num_programs(1) - 1)
    def _():
        packed = pack_stats(top_acc[...], mass_acc[...])
        for j, o_ref in enumerate(outs):
            width = o_ref.shape[1]
            o_ref[:, width - STAT :] = packed[j * per : (j + 1) * per].astype(o_ref.dtype)


def attend(parts, keys, values, new_keys, new_values, bias, first_head, heads):
    rows = parts[0].shape[0]
    group = next(g for g in (5, 4, 2, 1) if heads % g == 0 and first_head % g == 0)
    tile = min(rows, max(16, 128 // len(parts)))
    cache_rows = keys.shape[0]
    tok = new_keys.shape[0]
    width = heads * HD + STAT
    offset = first_head // group
    scale = math.log2(math.e) / math.sqrt(HD)
    n = len(parts)

    def body(*refs):
        attend_kernel(
            group, scale, refs[0], refs[1 : 1 + n], *refs[1 + n : 5 + n], refs[5 + n : 5 + 2 * n],
            *refs[5 + 2 * n :],
        )

    kv_spec = pl.BlockSpec((cache_rows, group * HD), lambda r, g: (0, g + offset))
    fresh_spec = pl.BlockSpec((tok, group * HD), lambda r, g: (0, g + offset))
    return pl.pallas_call(
        body,
        grid=(rows // tile, heads // group),
        in_specs=[pl.BlockSpec((1, cache_rows), lambda r, g: (0, 0))]
        + [pl.BlockSpec((tile, group * HD), lambda r, g: (r, g))] * n
        + [kv_spec, kv_spec, fresh_spec, fresh_spec],
        out_specs=[pl.BlockSpec((tile, width), lambda r, g: (r, 0))] * n,
        out_shape=[jax.ShapeDtypeStruct((rows, width), F32 if j == 0 else BF16) for j in range(n)],
        scratch_shapes=[pltpu.VMEM((tile * n, STAT), F32)] * 2,
        compiler_params=pltpu.CompilerParams(
            dimension_semantics=("arbitrary", "arbitrary"), vmem_limit_bytes=32 * 1024 * 1024
        ),
        cost_estimate=pl.CostEstimate(
            flops=4 * n * rows * cache_rows * heads * HD,
            bytes_accessed=4 * cache_rows * heads * HD,
            transcendentals=n * rows * cache_rows * heads,
        ),
        name="attend",
    )(bias, *parts, keys, values, new_keys, new_values)


def merge_kernel(heads, count, last, *refs):
    ins, outs = refs[:count], refs[count:]
    width = ins[0].shape[1]
    stats = [unpack_stats(r[:, width - STAT :].astype(F32), heads) for r in ins]
    top = functools.reduce(jnp.maximum, [t for t, _ in stats])
    weights = [jnp.exp2(t - top) for t, _ in stats]
    mass = functools.reduce(jnp.add, [w * m for w, (_, m) in zip(weights, stats)])
    if last:
        used = lanes(mass.shape[0]) < heads
        inverse = 1.0 / jnp.where(used, mass, 1.0)
        weights = [w * inverse for w in weights]
    per = outs[0].shape[0]
    for head in range(heads):
        cols = slice(head * HD, (head + 1) * HD)
        total = functools.reduce(
            jnp.add,
            [r[:, cols].astype(F32) * w[:, head : head + 1] for r, w in zip(ins, weights)],
        )
        for j, o_ref in enumerate(outs):
            o_ref[:, cols] = total[j * per : (j + 1) * per].astype(o_ref.dtype)
    if not last:
        packed = pack_stats(top, mass)
        for j, o_ref in enumerate(outs):
            o_ref[:, width - STAT :] = packed[j * per : (j + 1) * per].astype(o_ref.dtype)


def merge(partials, heads, pieces, last=False):
    rows, width = partials[0].shape
    per = rows // pieces
    if last:
        shapes = [jax.ShapeDtypeStruct((rows, heads * HD), BF16)]
    else:
        shapes = [
            jax.ShapeDtypeStruct((per, width), F32 if j == 0 else BF16) for j in range(pieces)
        ]
    return pl.pallas_call(
        functools.partial(merge_kernel, heads, len(partials), last),
        in_specs=[pl.BlockSpec(memory_space=pltpu.VMEM)] * len(partials),
        out_specs=[pl.BlockSpec(memory_space=pltpu.VMEM)] * len(shapes),
        out_shape=shapes,
        compiler_params=pltpu.CompilerParams(vmem_limit_bytes=48 * 1024 * 1024),
        cost_estimate=pl.CostEstimate(
            flops=4 * len(partials) * rows * width,
            bytes_accessed=4 * (len(partials) + 1) * rows * width,
            transcendentals=0,
        ),
        name="merge",
    )(*partials)


def per_device(queries, new_keys, new_values, cache_keys, cache_values, victims):
    members = lax.axis_size("seq")
    shape = factors(members)
    a_n, b_n, c_n = shape
    heads = queries.shape[1] // HD
    cache_rows = cache_keys.shape[0]
    block_count = cache_rows // BLK
    block_ids = lax.axis_index("seq") * block_count + jnp.arange(block_count, dtype=jnp.int32)
    evicted = jnp.any(victims[:, None] == block_ids[None, :], axis=0)
    bias = jnp.repeat(jnp.where(evicted, NEG, 0.0), BLK)[None, :]

    def fetch(x, axis, by):
        return lax.ppermute(x, "seq", shift_perm(shape, axis, by))

    def give(x, axis, by):
        return lax.ppermute(x, "seq", shift_perm(shape, axis, -by))

    plane = jnp.concatenate([queries] + [fetch(queries, 0, d) for d in range(1, a_n)], axis=0)
    plane = jnp.concatenate([plane] + [fetch(plane, 1, d) for d in range(1, b_n)], axis=0)
    parts = [plane] + [fetch(plane, 2, d) for d in range(1, c_n)]

    sums = attend(parts, cache_keys, cache_values, new_keys, new_values, bias, 0, heads)
    sums = [sums[0]] + [give(s, 2, d + 1) for d, s in enumerate(sums[1:])]
    sums = merge(sums, heads, b_n)
    sums = [sums[0]] + [give(s, 1, d + 1) for d, s in enumerate(sums[1:])]
    sums = merge(sums, heads, a_n)
    sums = [sums[0]] + [give(s, 0, d + 1) for d, s in enumerate(sums[1:])]
    return merge(sums, heads, 1, last=True)[0]


def solution(mesh):
    rows = P(("groups", "seq"), None)
    return jax.shard_map(
        per_device,
        mesh=mesh,
        in_specs=(rows, rows, rows, rows, rows, P("groups")),
        out_specs=rows,
        check_vma=False,
    )
```

```python
import functools
import math

import jax
import jax.numpy as jnp
from jax import lax
from jax.experimental import pallas as pl
from jax.experimental.pallas import tpu as pltpu
from jax.sharding import PartitionSpec as P

HD = 128
BLK = 128
STAT = 128
LANE = STAT // 3
NEG = -1e30
F32 = jnp.float32
BF16 = jnp.bfloat16


def factors(members):
    cores = 2 if members % 2 == 0 else 1
    chips = members // cores
    far = next(a for a in range(1, chips + 1) if chips % a == 0 and a * a >= chips)
    return far, chips // far, cores


def shift_perm(shape, axis, by):
    a_n, b_n, c_n = shape
    pairs = []
    for a in range(a_n):
        for b in range(b_n):
            for c in range(c_n):
                at = [a, b, c]
                src = list(at)
                src[axis] = (src[axis] + by) % shape[axis]
                flat = lambda p: (p[0] * b_n + p[1]) * c_n + p[2]
                pairs.append((flat(src), flat(at)))
    return pairs


def lanes(rows):
    return lax.broadcasted_iota(jnp.int32, (rows, STAT), 1)


def pack_stats(top, mass):
    high = mass.astype(BF16).astype(F32)
    return top + pltpu.roll(high, LANE, 1) + pltpu.roll(mass - high, 2 * LANE, 1)


def unpack_stats(packed, heads):
    used = lanes(packed.shape[0]) < heads
    mass = pltpu.roll(packed, STAT - LANE, 1) + pltpu.roll(packed, STAT - 2 * LANE, 1)
    return jnp.where(used, packed, 0.0), jnp.where(used, mass, 0.0)


def attend_kernel(sizes, scale, refs):
    parts, loads, group = sizes
    bias_ref, refs = refs[0], refs[1:]
    q_refs, refs = refs[:parts], refs[parts:]
    sources, refs = refs[:4], refs[4:]
    home_ref, away_refs, refs = refs[0], refs[1 : len(refs) - 7], refs[len(refs) - 7 :]
    buffers, sems, top_acc, mass_acc = refs[:4], refs[4], refs[5], refs[6]
    k_buf, v_buf, nk_buf, nv_buf = buffers
    outs = [(o, j) for o in (home_ref, *away_refs) for j in range(o.shape[0])]
    per = q_refs[0].shape[0]
    rows = per * parts
    wide = group * HD
    lane = lanes(rows)
    contract_last = (((1,), (1,)), ((), ()))

    def copies(load):
        cols = pl.ds(pl.multiple_of(load * wide, HD), wide)
        return [
            pltpu.make_async_copy(src.at[:, cols], dst.at[:, cols], sems.at[i, load])
            for i, (src, dst) in enumerate(zip(sources[:2], buffers[:2]))
        ]

    fresh_copies = [
        pltpu.make_async_copy(src, dst, sems.at[2 + i, 0])
        for i, (src, dst) in enumerate(zip(sources[2:], buffers[2:]))
    ]

    @pl.when(pl.program_id(0) == 0)
    def _():
        for copy in copies(0) + fresh_copies:
            copy.start()
        for load in range(1, loads):
            for copy in copies(load):
                copy.start()
        for copy in fresh_copies:
            copy.wait()

    top_acc[...] = jnp.zeros_like(top_acc)
    mass_acc[...] = jnp.zeros_like(mass_acc)
    bias = bias_ref[...]

    def heads_of(load, carry):
        @pl.when(pl.program_id(0) == 0)
        def _():
            for copy in copies(load):
                copy.wait()

        def columns(i):
            return pl.ds(pl.multiple_of((load * group + i) * HD, HD), HD)

        def scores(i):
            cols = columns(i)
            q = jnp.concatenate([r[:, cols] for r in q_refs], axis=0)
            cached = lax.dot_general(q, k_buf[:, cols], contract_last, preferred_element_type=F32)
            fresh = lax.dot_general(q, nk_buf[:, cols], contract_last, preferred_element_type=F32)
            return cached, fresh

        tops = top_acc[...]
        masses = mass_acc[...]
        ahead = scores(0)
        for i in range(group):
            cached, fresh = ahead
            if i + 1 < group:
                ahead = scores(i + 1)
            cached = cached * scale + bias
            fresh = fresh * scale
            top = jnp.maximum(
                jnp.max(cached, axis=1, keepdims=True), jnp.max(fresh, axis=1, keepdims=True)
            )
            top = top.astype(BF16).astype(F32)
            cached = jnp.exp2(cached - top)
            fresh = jnp.exp2(fresh - top)
            mass = jnp.sum(cached, axis=1, keepdims=True) + jnp.sum(fresh, axis=1, keepdims=True)
            cols = columns(i)
            out = jnp.dot(cached.astype(BF16), v_buf[:, cols], preferred_element_type=F32)
            out = out + jnp.dot(fresh.astype(BF16), nv_buf[:, cols], preferred_element_type=F32)
            for p, (o_ref, j) in enumerate(outs):
                o_ref[j, :, cols] = out[p * per : (p + 1) * per].astype(o_ref.dtype)
            head = load * group + i
            tops = jnp.where(lane == head, top, tops)
            masses = jnp.where(lane == head, mass, masses)
        top_acc[...] = tops
        mass_acc[...] = masses
        return carry

    lax.fori_loop(0, loads, heads_of, 0)
    packed = pack_stats(top_acc[...], mass_acc[...])
    for p, (o_ref, j) in enumerate(outs):
        width = o_ref.shape[2]
        o_ref[j, :, width - STAT :] = packed[p * per : (p + 1) * per].astype(o_ref.dtype)


def attend(parts, keys, values, new_keys, new_values, bias):
    flat = [p for core in parts for p in core]
    n = len(flat)
    rows, columns = flat[0].shape
    heads = columns // HD
    group = next(g for g in (5, 4, 2, 1) if heads % g == 0)
    loads = heads // group
    tile = min(rows, max(16, 128 // n))
    cache_rows = keys.shape[0]
    width = columns + STAT
    scale = math.log2(math.e) / math.sqrt(HD)
    stack = len(parts[0])

    def body(*refs):
        attend_kernel((n, loads, group), scale, refs)

    in_hbm = pl.BlockSpec(memory_space=pltpu.HBM)
    return pl.pallas_call(
        body,
        grid=(rows // tile,),
        in_specs=[pl.BlockSpec((1, cache_rows), lambda r: (0, 0))]
        + [pl.BlockSpec((tile, columns), lambda r: (r, 0))] * n
        + [in_hbm] * 4,
        out_specs=[pl.BlockSpec((stack, tile, width), lambda r: (0, r, 0))] * len(parts),
        out_shape=[
            jax.ShapeDtypeStruct((stack, rows, width), F32 if c == 0 else BF16)
            for c in range(len(parts))
        ],
        scratch_shapes=[pltpu.VMEM(x.shape, x.dtype) for x in (keys, values, new_keys, new_values)]
        + [pltpu.SemaphoreType.DMA((4, loads))]
        + [pltpu.VMEM((tile * n, STAT), F32)] * 2,
        compiler_params=pltpu.CompilerParams(
            dimension_semantics=("arbitrary",), vmem_limit_bytes=40 * 1024 * 1024
        ),
        cost_estimate=pl.CostEstimate(
            flops=4 * n * rows * cache_rows * columns,
            bytes_accessed=4 * cache_rows * columns,
            transcendentals=n * rows * cache_rows * heads,
        ),
        name="attend",
    )(bias, *flat, keys, values, new_keys, new_values)


def merged(arrays, heads, last):
    columns = heads * HD
    stats = [unpack_stats(get(slice(columns, columns + STAT)), heads) for get in arrays]
    top = functools.reduce(jnp.maximum, [t for t, _ in stats])
    weights = [jnp.exp2(t - top) for t, _ in stats]
    mass = functools.reduce(jnp.add, [w * m for w, (_, m) in zip(weights, stats)])
    if last:
        inverse = 1.0 / jnp.where(lanes(mass.shape[0]) < heads, mass, 1.0)
        weights = [w * inverse for w in weights]
    for head in range(heads):
        cols = slice(head * HD, (head + 1) * HD)
        yield cols, functools.reduce(
            jnp.add, [get(cols) * w[:, head : head + 1] for get, w in zip(arrays, weights)]
        )
    if not last:
        yield slice(columns, columns + STAT), pack_stats(top, mass)


def getter(ref, *index):
    return lambda cols: ref[(*index, slice(None), cols)].astype(F32)


def merge_stacks(ins, heads):
    layers, rows, width = ins[0].shape

    def body(*refs):
        for j in range(layers):
            out = refs[len(ins) + j]
            for cols, total in merged([getter(r, j) for r in refs[: len(ins)]], heads, False):
                out[:, cols] = total.astype(out.dtype)

    return call_merge(
        body, ins, [jax.ShapeDtypeStruct((rows, width), F32 if j == 0 else BF16) for j in range(layers)]
    )


def merge_rows(ins, heads, pieces):
    rows, width = ins[0].shape
    per = rows // pieces

    def body(*refs):
        out = refs[len(ins)]
        for cols, total in merged([getter(r) for r in refs[: len(ins)]], heads, False):
            for j in range(pieces):
                out[j, :, cols] = total[j * per : (j + 1) * per].astype(out.dtype)

    return call_merge(body, ins, [jax.ShapeDtypeStruct((pieces, per, width), BF16)])[0]


def finish(stack, heads):
    pieces, rows, width = stack.shape

    def body(ref, out):
        for cols, total in merged([getter(ref, j) for j in range(pieces)], heads, True):
            out[:, cols] = total.astype(out.dtype)

    return call_merge(body, [stack], [jax.ShapeDtypeStruct((rows, heads * HD), BF16)])[0]


def call_merge(body, ins, shapes):
    size = sum(math.prod(x.shape) for x in ins)
    return pl.pallas_call(
        body,
        in_specs=[pl.BlockSpec(memory_space=pltpu.VMEM)] * len(ins),
        out_specs=[pl.BlockSpec(memory_space=pltpu.VMEM)] * len(shapes),
        out_shape=shapes,
        compiler_params=pltpu.CompilerParams(vmem_limit_bytes=48 * 1024 * 1024),
        cost_estimate=pl.CostEstimate(flops=4 * size, bytes_accessed=4 * size, transcendentals=0),
        name="merge",
    )(*ins)


def per_device(queries, new_keys, new_values, cache_keys, cache_values, victims):
    members = lax.axis_size("seq")
    shape = factors(members)
    a_n, b_n, c_n = shape
    heads = queries.shape[1] // HD
    block_count = cache_keys.shape[0] // BLK
    block_ids = lax.axis_index("seq") * block_count + jnp.arange(block_count, dtype=jnp.int32)
    evicted = jnp.any(victims[:, None] == block_ids[None, :], axis=0)
    bias = jnp.repeat(jnp.where(evicted, NEG, 0.0), BLK)[None, :]

    def fetch(x, axis, by):
        return lax.ppermute(x, "seq", shift_perm(shape, axis, by))

    def give(x, axis, by):
        return lax.ppermute(x, "seq", shift_perm(shape, axis, -by))

    lines = [[(a * b_n * c_n) + rest for a in range(a_n)] for rest in range(b_n * c_n)]

    def exchange(stack):
        return lax.all_to_all(
            stack, "seq", split_axis=0, concat_axis=0, axis_index_groups=lines, tiled=True
        )

    tok = queries.shape[0]
    line = exchange(jnp.broadcast_to(queries[None], (a_n, *queries.shape)))
    line = line.reshape(a_n * tok, -1)
    plane = [line] + [fetch(line, 1, d) for d in range(1, b_n)]
    parts = [plane] + [[fetch(x, 2, d) for x in plane] for d in range(1, c_n)]

    sums = attend(parts, cache_keys, cache_values, new_keys, new_values, bias)
    sums = [sums[0]] + [give(s, 2, d + 1) for d, s in enumerate(sums[1:])]
    sums = merge_stacks(sums, heads)
    sums = [sums[0]] + [give(s, 1, d + 1) for d, s in enumerate(sums[1:])]
    return finish(exchange(merge_rows(sums, heads, a_n)), heads)


def solution(mesh):
    rows = P(("groups", "seq"), None)
    return jax.shard_map(
        per_device,
        mesh=mesh,
        in_specs=(rows, rows, rows, rows, rows, P("groups")),
        out_specs=rows,
        check_vma=False,
    )
```

```python
import functools
import math

import jax
import jax.numpy as jnp
from jax import lax
from jax.experimental import pallas as pl
from jax.experimental.pallas import tpu as pltpu
from jax.sharding import PartitionSpec as P

HD = 128
BLK = 128
STAT = 128
LANE = STAT // 3
NEG = -1e30
F32 = jnp.float32
BF16 = jnp.bfloat16


def factors(members):
    cores = 2 if members % 2 == 0 else 1
    chips = members // cores
    far = next(a for a in range(1, chips + 1) if chips % a == 0 and a * a >= chips)
    return far, chips // far, cores


def shift_perm(shape, axis, by):
    a_n, b_n, c_n = shape
    pairs = []
    for a in range(a_n):
        for b in range(b_n):
            for c in range(c_n):
                at = [a, b, c]
                src = list(at)
                src[axis] = (src[axis] + by) % shape[axis]
                flat = lambda p: (p[0] * b_n + p[1]) * c_n + p[2]
                pairs.append((flat(src), flat(at)))
    return pairs


def lanes(rows):
    return lax.broadcasted_iota(jnp.int32, (rows, STAT), 1)


def pack_stats(top, mass):
    high = mass.astype(BF16).astype(F32)
    return top + pltpu.roll(high, LANE, 1) + pltpu.roll(mass - high, 2 * LANE, 1)


def unpack_stats(packed, heads):
    used = lanes(packed.shape[0]) < heads
    mass = pltpu.roll(packed, STAT - LANE, 1) + pltpu.roll(packed, STAT - 2 * LANE, 1)
    return jnp.where(used, packed, 0.0), jnp.where(used, mass, 0.0)


def attend_kernel(sizes, scale, refs):
    parts, loads, group = sizes
    bias_ref, refs = refs[0], refs[1:]
    q_refs, refs = refs[:parts], refs[parts:]
    sources, refs = refs[:4], refs[4:]
    home_ref, away_refs, refs = refs[0], refs[1 : len(refs) - 7], refs[len(refs) - 7 :]
    buffers, sems, top_acc, mass_acc = refs[:4], refs[4], refs[5], refs[6]
    k_buf, v_buf, nk_buf, nv_buf = buffers
    outs = [(o, j) for o in (home_ref, *away_refs) for j in range(o.shape[0])]
    per = q_refs[0].shape[0]
    rows = per * parts
    wide = group * HD
    lane = lanes(rows)
    contract_last = (((1,), (1,)), ((), ()))

    def copies(load):
        cols = pl.ds(pl.multiple_of(load * wide, HD), wide)
        return [
            pltpu.make_async_copy(src.at[:, cols], dst.at[:, cols], sems.at[i, load])
            for i, (src, dst) in enumerate(zip(sources[:2], buffers[:2]))
        ]

    fresh_copies = [
        pltpu.make_async_copy(src, dst, sems.at[2 + i, 0])
        for i, (src, dst) in enumerate(zip(sources[2:], buffers[2:]))
    ]

    @pl.when(pl.program_id(0) == 0)
    def _():
        for copy in copies(0) + fresh_copies:
            copy.start()
        for load in range(1, loads):
            for copy in copies(load):
                copy.start()
        for copy in fresh_copies:
            copy.wait()

    top_acc[...] = jnp.zeros_like(top_acc)
    mass_acc[...] = jnp.zeros_like(mass_acc)
    bias = bias_ref[...]

    def heads_of(load, carry):
        @pl.when(pl.program_id(0) == 0)
        def _():
            for copy in copies(load):
                copy.wait()

        def columns(i):
            return pl.ds(pl.multiple_of((load * group + i) * HD, HD), HD)

        def scores(i):
            cols = columns(i)
            q = jnp.concatenate([r[:, cols] for r in q_refs], axis=0)
            cached = lax.dot_general(q, k_buf[:, cols], contract_last, preferred_element_type=F32)
            fresh = lax.dot_general(q, nk_buf[:, cols], contract_last, preferred_element_type=F32)
            return cached, fresh

        tops = top_acc[...]
        masses = mass_acc[...]
        ahead = scores(0)
        for i in range(group):
            cached, fresh = ahead
            if i + 1 < group:
                ahead = scores(i + 1)
            cached = cached * scale + bias
            fresh = fresh * scale
            top = jnp.maximum(
                jnp.max(cached, axis=1, keepdims=True), jnp.max(fresh, axis=1, keepdims=True)
            )
            top = top.astype(BF16).astype(F32)
            cached = jnp.exp2(cached - top)
            fresh = jnp.exp2(fresh - top)
            mass = jnp.sum(cached, axis=1, keepdims=True) + jnp.sum(fresh, axis=1, keepdims=True)
            cols = columns(i)
            out = jnp.dot(cached.astype(BF16), v_buf[:, cols], preferred_element_type=F32)
            out = out + jnp.dot(fresh.astype(BF16), nv_buf[:, cols], preferred_element_type=F32)
            for p, (o_ref, j) in enumerate(outs):
                o_ref[j, :, cols] = out[p * per : (p + 1) * per].astype(o_ref.dtype)
            head = load * group + i
            tops = jnp.where(lane == head, top, tops)
            masses = jnp.where(lane == head, mass, masses)
        top_acc[...] = tops
        mass_acc[...] = masses
        return carry

    lax.fori_loop(0, loads, heads_of, 0)
    packed = pack_stats(top_acc[...], mass_acc[...])
    for p, (o_ref, j) in enumerate(outs):
        width = o_ref.shape[2]
        o_ref[j, :, width - STAT :] = packed[p * per : (p + 1) * per].astype(o_ref.dtype)


def attend(parts, keys, values, new_keys, new_values, bias):
    flat = [p for core in parts for p in core]
    n = len(flat)
    rows, columns = flat[0].shape
    heads = columns // HD
    group = next(g for g in (5, 4, 2, 1) if heads % g == 0)
    loads = heads // group
    tile = min(rows, max(16, 128 // n))
    cache_rows = keys.shape[0]
    width = columns + STAT
    scale = math.log2(math.e) / math.sqrt(HD)
    stack = len(parts[0])

    def body(*refs):
        attend_kernel((n, loads, group), scale, refs)

    in_hbm = pl.BlockSpec(memory_space=pltpu.HBM)
    held = (keys, values, new_keys, new_values)
    return pl.pallas_call(
        body,
        grid=(rows // tile,),
        in_specs=[pl.BlockSpec((1, cache_rows), lambda r: (0, 0))]
        + [pl.BlockSpec((tile, columns), lambda r: (r, 0))] * n
        + [in_hbm] * 4,
        out_specs=[pl.BlockSpec((stack, tile, width), lambda r: (0, r, 0))] * len(parts),
        out_shape=[
            jax.ShapeDtypeStruct((stack, rows, width), F32 if c == 0 else BF16)
            for c in range(len(parts))
        ],
        scratch_shapes=[pltpu.VMEM(x.shape, x.dtype) for x in held]
        + [pltpu.SemaphoreType.DMA((4, loads))]
        + [pltpu.VMEM((tile * n, STAT), F32)] * 2,
        compiler_params=pltpu.CompilerParams(
            dimension_semantics=("arbitrary",), vmem_limit_bytes=40 * 1024 * 1024
        ),
        cost_estimate=pl.CostEstimate(
            flops=4 * n * rows * cache_rows * columns,
            bytes_accessed=4 * cache_rows * columns,
            transcendentals=n * rows * cache_rows * heads,
        ),
        name="attend",
    )(bias, *flat, *[pltpu.with_memory_space_constraint(x, pltpu.HBM) for x in held])


def merged(arrays, heads, last):
    columns = heads * HD
    stats = [unpack_stats(get(slice(columns, columns + STAT)), heads) for get in arrays]
    top = functools.reduce(jnp.maximum, [t for t, _ in stats])
    weights = [jnp.exp2(t - top) for t, _ in stats]
    mass = functools.reduce(jnp.add, [w * m for w, (_, m) in zip(weights, stats)])
    if last:
        inverse = 1.0 / jnp.where(lanes(mass.shape[0]) < heads, mass, 1.0)
        weights = [w * inverse for w in weights]
    for head in range(heads):
        cols = slice(head * HD, (head + 1) * HD)
        yield cols, functools.reduce(
            jnp.add, [get(cols) * w[:, head : head + 1] for get, w in zip(arrays, weights)]
        )
    if not last:
        yield slice(columns, columns + STAT), pack_stats(top, mass)


def getter(ref, *index):
    return lambda cols: ref[(*index, slice(None), cols)].astype(F32)


def merge_rows(ins, heads, pieces, kinds):
    rows, width = ins[0].shape
    per = rows // pieces

    def body(*refs):
        outs = refs[len(ins) :]
        for cols, total in merged([getter(r) for r in refs[: len(ins)]], heads, False):
            for j, out in enumerate(outs):
                out[:, cols] = total[j * per : (j + 1) * per].astype(out.dtype)

    return call_merge(body, ins, [jax.ShapeDtypeStruct((per, width), kind) for kind in kinds])


def finish(ins, heads):
    rows = ins[0].shape[0]

    def body(*refs):
        out = refs[len(ins)]
        for cols, total in merged([getter(r) for r in refs[: len(ins)]], heads, True):
            out[:, cols] = total.astype(out.dtype)

    return call_merge(body, ins, [jax.ShapeDtypeStruct((rows, heads * HD), BF16)])[0]


def join(pieces):
    rows = sum(p.shape[0] for p in pieces)

    def body(*refs):
        out = refs[-1]
        out[...] = jnp.concatenate([r[...].astype(F32) for r in refs[:-1]], axis=0).astype(out.dtype)

    shape = jax.ShapeDtypeStruct((rows, pieces[0].shape[1]), pieces[0].dtype)
    return call_merge(body, pieces, [shape])[0]


def call_merge(body, ins, shapes):
    size = sum(math.prod(x.shape) for x in ins)
    return pl.pallas_call(
        body,
        in_specs=[pl.BlockSpec(memory_space=pltpu.VMEM)] * len(ins),
        out_specs=[pl.BlockSpec(memory_space=pltpu.VMEM)] * len(shapes),
        out_shape=shapes,
        compiler_params=pltpu.CompilerParams(vmem_limit_bytes=48 * 1024 * 1024),
        cost_estimate=pl.CostEstimate(flops=4 * size, bytes_accessed=4 * size, transcendentals=0),
        name="merge",
    )(*ins)


def per_device(queries, new_keys, new_values, cache_keys, cache_values, victims):
    members = lax.axis_size("seq")
    shape = factors(members)
    a_n, b_n, c_n = shape
    heads = queries.shape[1] // HD
    block_count = cache_keys.shape[0] // BLK
    block_ids = lax.axis_index("seq") * block_count + jnp.arange(block_count, dtype=jnp.int32)
    evicted = jnp.any(victims[:, None] == block_ids[None, :], axis=0)
    bias = jnp.repeat(jnp.where(evicted, NEG, 0.0), BLK)[None, :]

    def fetch(x, axis, by):
        return lax.ppermute(x, "seq", shift_perm(shape, axis, by))

    def give(x, axis, by):
        return lax.ppermute(x, "seq", shift_perm(shape, axis, -by))

    far_first = sorted(range(1, a_n), key=lambda d: -min(d, a_n - d))
    line = [queries] + [None] * (a_n - 1)
    for d in far_first:
        line[d] = fetch(queries, 0, d)
    others = [[fetch(x, 1, d) for x in line] for d in range(1, b_n)]

    def both_cores(pieces):
        joined = join(pieces)
        return [joined] + [fetch(joined, 2, d) for d in range(1, c_n)]

    held = (cache_keys, cache_values, new_keys, new_values)

    def partials(blocks, kinds):
        cores = [both_cores(pieces) for pieces in blocks]
        stacks = attend([[c[d] for c in cores] for d in range(c_n)], *held, bias)
        back = [give(x, 2, d + 1) for d, x in enumerate(stacks[1:])]
        return [
            merge_rows([stacks[0][j]] + [x[j] for x in back], heads, a_n, kinds)
            for j in range(len(blocks))
        ]

    own = partials([line], [F32] * a_n)[0]
    got = [
        [give(x, 1, d + 1) for x in pieces]
        for d, pieces in enumerate(partials(others, [BF16] * a_n))
    ]
    sums = [[own[d]] + [pieces[d] for pieces in got] for d in range(a_n)]
    for d in far_first:
        sums[d] = [give(merge_rows(sums[d], heads, 1, [BF16])[0], 0, d)]
    return finish([x for pieces in sums for x in pieces], heads)


def solution(mesh):
    rows = P(("groups", "seq"), None)
    return jax.shard_map(
        per_device,
        mesh=mesh,
        in_specs=(rows, rows, rows, rows, rows, P("groups")),
        out_specs=rows,
        check_vma=False,
    )
```

```python
import functools
import itertools
import math

import jax
import jax.numpy as jnp
from jax import lax
from jax.experimental import pallas as pl
from jax.experimental.pallas import tpu as pltpu
from jax.sharding import PartitionSpec as P

HD = 128
BLK = 128
STAT = 128
LANE = STAT // 3
NEG = -1e30
F32 = jnp.float32
BF16 = jnp.bfloat16


def factors(members):
    cores = 2 if members % 2 == 0 else 1
    chips = members // cores
    far = next(a for a in range(1, chips + 1) if chips % a == 0 and a * a >= chips)
    return far, chips // far, cores


def shift_perm(shape, by):
    def flat(place):
        return functools.reduce(lambda at, kn: at * kn[1] + kn[0] % kn[1], zip(place, shape), 0)

    places = itertools.product(*map(range, shape))
    return [(flat([p + d for p, d in zip(at, by)]), flat(at)) for at in places]


def lanes(rows):
    return lax.broadcasted_iota(jnp.int32, (rows, STAT), 1)


def pack_stats(top, mass):
    high = mass.astype(BF16).astype(F32)
    return top + pltpu.roll(high, LANE, 1) + pltpu.roll(mass - high, 2 * LANE, 1)


def unpack_stats(packed, heads):
    used = lanes(packed.shape[0]) < heads
    mass = pltpu.roll(packed, STAT - LANE, 1) + pltpu.roll(packed, STAT - 2 * LANE, 1)
    return jnp.where(used, packed, 0.0), jnp.where(used, mass, 0.0)


def attend_kernel(sizes, scale, refs):
    parts, loads, group, pack = sizes
    bias_ref, refs = refs[0], refs[1:]
    q_refs, refs = refs[:parts], refs[parts:]
    sources, refs = refs[:4], refs[4:]
    outs, refs = refs[: len(refs) - 7], refs[len(refs) - 7 :]
    k_buf, v_buf, nk_buf, nv_buf, sems, top_acc, mass_acc = refs
    per = q_refs[0].shape[0]
    rows = per * parts
    wide = pack * HD
    cache_rows = sources[0].shape[0]
    lane = lanes(rows)
    contract_last = (((1,), (1,)), ((), ()))

    def copies(load):
        cols = pl.ds(pl.multiple_of(load * group * wide, HD), group * wide)
        return [
            pltpu.make_async_copy(
                src.at[:, cols], dst.at[pl.ds(0, cache_rows), cols], sems.at[i, load]
            )
            for i, (src, dst) in enumerate(zip(sources[:2], (k_buf, v_buf)))
        ]

    fresh_copies = [
        pltpu.make_async_copy(src, dst, sems.at[2 + i, 0])
        for i, (src, dst) in enumerate(zip(sources[2:], (nk_buf, nv_buf)))
    ]

    @pl.when(pl.program_id(0) == 0)
    def _():
        for copy in copies(0) + fresh_copies:
            copy.start()
        for load in range(1, loads):
            for copy in copies(load):
                copy.start()
        for copy, src, dst in zip(fresh_copies, (nk_buf, nv_buf), (k_buf, v_buf)):
            copy.wait()
            rest = dst.shape[0] - cache_rows - src.shape[0]
            tail = jnp.concatenate(
                [src[...].astype(F32), jnp.zeros((rest, src.shape[1]), F32)], axis=0
            )
            dst[cache_rows:, :] = tail.astype(BF16)

    top_acc[...] = jnp.zeros_like(top_acc)
    mass_acc[...] = jnp.zeros_like(mass_acc)
    bias = bias_ref[...]
    mine = [
        lax.broadcasted_iota(jnp.int32, (rows, wide), 1) // HD == k for k in range(pack)
    ]

    def heads_of(load, carry):
        @pl.when(pl.program_id(0) == 0)
        def _():
            for copy in copies(load):
                copy.wait()

        def columns(i):
            return pl.ds(pl.multiple_of((load * group + i) * wide, HD), wide)

        def scores(i):
            cols = columns(i)
            q = jnp.concatenate([r[:, cols] for r in q_refs], axis=0)
            if pack > 1:
                zero = jnp.zeros_like(q)
                q = jnp.concatenate([jnp.where(m, q, zero) for m in mine], axis=0)
            return lax.dot_general(q, k_buf[:, cols], contract_last, preferred_element_type=F32)

        tops = top_acc[...]
        masses = mass_acc[...]
        ahead = scores(0)
        for i in range(group):
            score = ahead
            if i + 1 < group:
                ahead = scores(i + 1)
            score = score * scale + bias
            top = jnp.max(score, axis=1, keepdims=True).astype(BF16).astype(F32)
            score = jnp.exp2(score - top)
            mass = jnp.sum(score, axis=1, keepdims=True)
            out = jnp.dot(score.astype(BF16), v_buf[:, columns(i)], preferred_element_type=F32)
            for k in range(pack):
                head = (load * group + i) * pack + k
                cols = pl.ds(pl.multiple_of(head * HD, HD), HD)
                one = out[k * rows : (k + 1) * rows, k * HD : (k + 1) * HD]
                for p in range(parts):
                    o_ref = outs[p]
                    o_ref[:, cols] = one[p * per : (p + 1) * per].astype(o_ref.dtype)
                tops = jnp.where(lane == head, top[k * rows : (k + 1) * rows], tops)
                masses = jnp.where(lane == head, mass[k * rows : (k + 1) * rows], masses)
        top_acc[...] = tops
        mass_acc[...] = masses
        return carry

    lax.fori_loop(0, loads, heads_of, 0)
    packed = pack_stats(top_acc[...], mass_acc[...])
    for p, o_ref in enumerate(outs):
        width = o_ref.shape[1]
        o_ref[:, width - STAT :] = packed[p * per : (p + 1) * per].astype(o_ref.dtype)


def attend(parts, keys, values, new_keys, new_values, bias):
    n = len(parts)
    rows, columns = parts[0].shape
    heads = columns // HD
    pack = 2 if heads % 2 == 0 else 1
    group = next(g for g in (2, 1) if heads % (g * pack) == 0)
    loads = heads // (group * pack)
    tile = next(t for t in (64, 32, 16, rows) if rows % t == 0)
    cache_rows = keys.shape[0]
    padded = cache_rows + -(-new_keys.shape[0] // BLK) * BLK
    width = columns + STAT
    scale = math.log2(math.e) / math.sqrt(HD)
    held = (keys, values, new_keys, new_values)

    def body(*refs):
        attend_kernel((n, loads, group, pack), scale, refs)

    return pl.pallas_call(
        body,
        grid=(rows // tile,),
        in_specs=[pl.BlockSpec((1, padded), lambda r: (0, 0))]
        + [pl.BlockSpec((tile, columns), lambda r: (r, 0))] * n
        + [pl.BlockSpec(memory_space=pltpu.HBM)] * 4,
        out_specs=[pl.BlockSpec((tile, width), lambda r: (r, 0))] * n,
        out_shape=[jax.ShapeDtypeStruct((rows, width), F32 if c == 0 else BF16) for c in range(n)],
        scratch_shapes=[pltpu.VMEM((padded, columns), BF16)] * 2
        + [pltpu.VMEM(new_keys.shape, BF16)] * 2
        + [pltpu.SemaphoreType.DMA((4, loads))]
        + [pltpu.VMEM((tile * n, STAT), F32)] * 2,
        compiler_params=pltpu.CompilerParams(
            dimension_semantics=("arbitrary",), vmem_limit_bytes=40 * 1024 * 1024
        ),
        cost_estimate=pl.CostEstimate(
            flops=4 * n * rows * cache_rows * columns,
            bytes_accessed=4 * cache_rows * columns,
            transcendentals=n * rows * cache_rows * heads,
        ),
        name="attend",
    )(bias, *parts, *[pltpu.with_memory_space_constraint(x, pltpu.HBM) for x in held])


def merged(arrays, heads, last):
    columns = heads * HD
    stats = [unpack_stats(get(slice(columns, columns + STAT)), heads) for get in arrays]
    top = functools.reduce(jnp.maximum, [t for t, _ in stats])
    weights = [jnp.exp2(t - top) for t, _ in stats]
    mass = functools.reduce(jnp.add, [w * m for w, (_, m) in zip(weights, stats)])
    if last:
        inverse = 1.0 / jnp.where(lanes(mass.shape[0]) < heads, mass, 1.0)
        weights = [w * inverse for w in weights]
    for head in range(heads):
        cols = slice(head * HD, (head + 1) * HD)
        yield cols, functools.reduce(
            jnp.add, [get(cols) * w[:, head : head + 1] for get, w in zip(arrays, weights)]
        )
    if not last:
        yield slice(columns, columns + STAT), pack_stats(top, mass)


def getter(ref, *index):
    return lambda cols: ref[(*index, slice(None), cols)].astype(F32)


def merge_rows(ins, heads, pieces, kinds):
    rows, width = ins[0].shape
    per = rows // pieces

    def body(*refs):
        outs = refs[len(ins) :]
        for cols, total in merged([getter(r) for r in refs[: len(ins)]], heads, False):
            for j, out in enumerate(outs):
                out[:, cols] = total[j * per : (j + 1) * per].astype(out.dtype)

    return call_merge(body, ins, [jax.ShapeDtypeStruct((per, width), kind) for kind in kinds])


def finish(ins, heads):
    rows = ins[0].shape[0]

    def body(*refs):
        out = refs[len(ins)]
        for cols, total in merged([getter(r) for r in refs[: len(ins)]], heads, True):
            out[:, cols] = total.astype(out.dtype)

    return call_merge(body, ins, [jax.ShapeDtypeStruct((rows, heads * HD), BF16)])[0]


def join(pieces):
    rows = sum(p.shape[0] for p in pieces)

    def body(*refs):
        out = refs[-1]
        out[...] = jnp.concatenate([r[...].astype(F32) for r in refs[:-1]], axis=0).astype(out.dtype)

    shape = jax.ShapeDtypeStruct((rows, pieces[0].shape[1]), pieces[0].dtype)
    return call_merge(body, pieces, [shape])[0]


def call_merge(body, ins, shapes):
    size = sum(math.prod(x.shape) for x in ins)
    return pl.pallas_call(
        body,
        in_specs=[pl.BlockSpec(memory_space=pltpu.VMEM)] * len(ins),
        out_specs=[pl.BlockSpec(memory_space=pltpu.VMEM)] * len(shapes),
        out_shape=shapes,
        compiler_params=pltpu.CompilerParams(vmem_limit_bytes=48 * 1024 * 1024),
        cost_estimate=pl.CostEstimate(flops=4 * size, bytes_accessed=4 * size, transcendentals=0),
        name="merge",
    )(*ins)


def per_device(queries, new_keys, new_values, cache_keys, cache_values, victims):
    members = lax.axis_size("seq")
    shape = factors(members)
    a_n, b_n, c_n = shape
    heads = queries.shape[1] // HD
    block_count = cache_keys.shape[0] // BLK
    block_ids = lax.axis_index("seq") * block_count + jnp.arange(block_count, dtype=jnp.int32)
    evicted = jnp.any(victims[:, None] == block_ids[None, :], axis=0)
    bias = jnp.repeat(jnp.where(evicted, NEG, 0.0), BLK)[None, :]
    tok = new_keys.shape[0]
    fresh_bias = jnp.where(jnp.arange(-(-tok // BLK) * BLK) < tok, 0.0, NEG)[None, :]
    bias = jnp.concatenate([bias, fresh_bias], axis=1)

    def fetch(x, by):
        return lax.ppermute(x, "seq", shift_perm(shape, by))

    def give(x, by):
        return lax.ppermute(x, "seq", shift_perm(shape, [-d for d in by]))

    chips = [(a, b, 0) for a in range(a_n) for b in range(b_n)]
    far_first = sorted(chips[1:], key=lambda at: (-min(at[0], a_n - at[0]), -at[1]))

    blocks = {at: fetch(queries, at) for at in far_first}
    blocks[chips[0]] = join([queries])
    plane = join([blocks[at] for at in chips])
    parts = [plane] + [fetch(plane, (0, 0, c)) for c in range(1, c_n)]
    parts = attend(parts, cache_keys, cache_values, new_keys, new_values, bias)
    parts = [parts[0]] + [give(x, (0, 0, c + 1)) for c, x in enumerate(parts[1:])]
    kinds = [F32] + [BF16] * (len(chips) - 1)
    pieces = dict(zip(chips, merge_rows(parts, heads, len(chips), kinds)))
    for at in far_first:
        pieces[at] = give(pieces[at], at)
    return finish([pieces[at] for at in chips], heads)


def solution(mesh):
    rows = P(("groups", "seq"), None)
    return jax.shard_map(
        per_device,
        mesh=mesh,
        in_specs=(rows, rows, rows, rows, rows, P("groups")),
        out_specs=rows,
        check_vma=False,
    )
```

```python
import functools
import itertools
import math

import jax
import jax.numpy as jnp
from jax import lax
from jax.experimental import pallas as pl
from jax.experimental.pallas import tpu as pltpu
from jax.sharding import PartitionSpec as P

HD = 128
BLK = 128
STAT = 128
LANE = STAT // 3
NEG = -1e30
F32 = jnp.float32
BF16 = jnp.bfloat16


def factors(members):
    cores = 2 if members % 2 == 0 else 1
    chips = members // cores
    far = next(a for a in range(1, chips + 1) if chips % a == 0 and a * a >= chips)
    return far, chips // far, cores


def shift_perm(shape, by):
    def flat(place):
        return functools.reduce(lambda at, kn: at * kn[1] + kn[0] % kn[1], zip(place, shape), 0)

    places = itertools.product(*map(range, shape))
    return [(flat([p + d for p, d in zip(at, by)]), flat(at)) for at in places]


def lanes(rows):
    return lax.broadcasted_iota(jnp.int32, (rows, STAT), 1)


def pack_stats(top, mass):
    high = mass.astype(BF16).astype(F32)
    return top + pltpu.roll(high, LANE, 1) + pltpu.roll(mass - high, 2 * LANE, 1)


def unpack_stats(packed, heads):
    used = lanes(packed.shape[0]) < heads
    mass = pltpu.roll(packed, STAT - LANE, 1) + pltpu.roll(packed, STAT - 2 * LANE, 1)
    return jnp.where(used, packed, 0.0), jnp.where(used, mass, 0.0)


def attend_kernel(sizes, scale, bias_ref, q_refs, k_ref, v_ref, outs, top_acc, mass_acc):
    tile, steps, group, pack = sizes
    parts = len(q_refs)
    rows = tile * parts
    wide = pack * HD
    lane = lanes(rows)
    contract_last = (((1,), (1,)), ((), ()))
    bias = bias_ref[...]
    mine = [lax.broadcasted_iota(jnp.int32, (rows, wide), 1) // HD == k for k in range(pack)]

    def row_tile(r, carry):
        at = pl.ds(pl.multiple_of(r * tile, tile), tile)
        top_acc[...] = jnp.zeros_like(top_acc)
        mass_acc[...] = jnp.zeros_like(mass_acc)

        def heads_of(step, carry):
            def columns(i):
                return pl.ds(pl.multiple_of((step * group + i) * wide, HD), wide)

            def scores(i):
                cols = columns(i)
                q = jnp.concatenate([ref[at, cols] for ref in q_refs], axis=0)
                if pack > 1:
                    zero = jnp.zeros_like(q)
                    q = jnp.concatenate([jnp.where(m, q, zero) for m in mine], axis=0)
                return lax.dot_general(q, k_ref[:, cols], contract_last, preferred_element_type=F32)

            tops = top_acc[...]
            masses = mass_acc[...]
            ahead = scores(0)
            for i in range(group):
                score = ahead
                if i + 1 < group:
                    ahead = scores(i + 1)
                score = score * scale + bias
                top = jnp.max(score, axis=1, keepdims=True).astype(BF16).astype(F32)
                score = jnp.exp2(score - top)
                mass = jnp.sum(score, axis=1, keepdims=True)
                out = jnp.dot(score.astype(BF16), v_ref[:, columns(i)], preferred_element_type=F32)
                for k in range(pack):
                    head = (step * group + i) * pack + k
                    cols = pl.ds(pl.multiple_of(head * HD, HD), HD)
                    one = out[k * rows : (k + 1) * rows, k * HD : (k + 1) * HD]
                    for p, o_ref in enumerate(outs):
                        o_ref[at, cols] = one[p * tile : (p + 1) * tile].astype(o_ref.dtype)
                    tops = jnp.where(lane == head, top[k * rows : (k + 1) * rows], tops)
                    masses = jnp.where(lane == head, mass[k * rows : (k + 1) * rows], masses)
            top_acc[...] = tops
            mass_acc[...] = masses
            return carry

        lax.fori_loop(0, steps, heads_of, 0)
        packed = pack_stats(top_acc[...], mass_acc[...])
        for p, o_ref in enumerate(outs):
            width = o_ref.shape[1]
            o_ref[at, width - STAT :] = packed[p * tile : (p + 1) * tile].astype(o_ref.dtype)
        return carry

    lax.fori_loop(0, q_refs[0].shape[0] // tile, row_tile, 0)


def attend(blocks, kinds, keys, values, bias):
    n = len(blocks)
    rows, columns = blocks[0].shape
    heads = columns // HD
    pack = 2 if heads % 2 == 0 else 1
    group = next(g for g in (2, 1) if heads % (g * pack) == 0)
    tile = next(t for t in (32, 16, rows) if rows % t == 0)
    width = columns + STAT
    scale = math.log2(math.e) / math.sqrt(HD)

    def body(*refs):
        attend_kernel(
            (tile, heads // (group * pack), group, pack), scale, refs[0], refs[1 : 1 + n],
            *refs[1 + n : 3 + n], refs[3 + n : 3 + 2 * n], *refs[3 + 2 * n :],
        )

    return pl.pallas_call(
        body,
        in_specs=[pl.BlockSpec(memory_space=pltpu.VMEM)] * (n + 3),
        out_specs=[pl.BlockSpec(memory_space=pltpu.VMEM)] * n,
        out_shape=[jax.ShapeDtypeStruct((rows, width), kind) for kind in kinds],
        scratch_shapes=[pltpu.VMEM((tile * n, STAT), F32)] * 2,
        compiler_params=pltpu.CompilerParams(vmem_limit_bytes=40 * 1024 * 1024),
        cost_estimate=pl.CostEstimate(
            flops=4 * n * rows * keys.shape[0] * columns,
            bytes_accessed=4 * keys.shape[0] * columns,
            transcendentals=n * rows * keys.shape[0] * heads,
        ),
        name="attend",
    )(bias, *blocks, keys, values)


def load(cached, fresh, after):
    cache_rows, columns = cached[0].shape
    tok = fresh[0].shape[0]
    padded = cache_rows + -(-tok // BLK) * BLK
    n = len(cached)

    def body(*refs):
        cached_refs, fresh_refs, outs = refs[:n], refs[n : 2 * n], refs[2 * n + 1 : 3 * n + 1]
        tails, sems = refs[3 * n + 1 : 4 * n + 1], refs[4 * n + 1]
        small = [
            pltpu.make_async_copy(src, dst, sems.at[1, i])
            for i, (src, dst) in enumerate(zip(fresh_refs, tails))
        ]
        large = [
            pltpu.make_async_copy(src, dst.at[pl.ds(0, cache_rows), :], sems.at[0, i])
            for i, (src, dst) in enumerate(zip(cached_refs, outs))
        ]
        for copy in small + large:
            copy.start()
        for copy, tail, out in zip(small, tails, outs):
            copy.wait()
            rest = jnp.zeros((padded - cache_rows - tok, columns), F32)
            rows = jnp.concatenate([tail[...].astype(F32), rest], axis=0)
            out[cache_rows:, :] = rows.astype(out.dtype)
        for copy in large:
            copy.wait()

    in_hbm = pl.BlockSpec(memory_space=pltpu.HBM)
    return pl.pallas_call(
        body,
        in_specs=[in_hbm] * (2 * n) + [pl.BlockSpec(memory_space=pl.ANY)],
        out_specs=[pl.BlockSpec(memory_space=pltpu.VMEM)] * n,
        out_shape=[jax.ShapeDtypeStruct((padded, columns), BF16)] * n,
        scratch_shapes=[pltpu.VMEM(x.shape, BF16) for x in fresh]
        + [pltpu.SemaphoreType.DMA((2, n))],
        compiler_params=pltpu.CompilerParams(vmem_limit_bytes=24 * 1024 * 1024),
        cost_estimate=pl.CostEstimate(
            flops=0, bytes_accessed=4 * n * cache_rows * columns, transcendentals=0
        ),
        name="load",
    )(*[pltpu.with_memory_space_constraint(x, pltpu.HBM) for x in (*cached, *fresh)], after)


def merged(arrays, heads, last):
    columns = heads * HD
    stats = [unpack_stats(get(slice(columns, columns + STAT)), heads) for get in arrays]
    top = functools.reduce(jnp.maximum, [t for t, _ in stats])
    weights = [jnp.exp2(t - top) for t, _ in stats]
    mass = functools.reduce(jnp.add, [w * m for w, (_, m) in zip(weights, stats)])
    if last:
        inverse = 1.0 / jnp.where(lanes(mass.shape[0]) < heads, mass, 1.0)
        weights = [w * inverse for w in weights]
    for head in range(heads):
        cols = slice(head * HD, (head + 1) * HD)
        yield cols, functools.reduce(
            jnp.add, [get(cols) * w[:, head : head + 1] for get, w in zip(arrays, weights)]
        )
    if not last:
        yield slice(columns, columns + STAT), pack_stats(top, mass)


def getter(ref, *index):
    return lambda cols: ref[(*index, slice(None), cols)].astype(F32)


def merge_rows(ins, heads, pieces, kinds):
    rows, width = ins[0].shape
    per = rows // pieces

    def body(*refs):
        outs = refs[len(ins) :]
        for cols, total in merged([getter(r) for r in refs[: len(ins)]], heads, False):
            for j, out in enumerate(outs):
                out[:, cols] = total[j * per : (j + 1) * per].astype(out.dtype)

    return call_merge(body, ins, [jax.ShapeDtypeStruct((per, width), kind) for kind in kinds])


def finish(ins, heads):
    rows = ins[0].shape[0]

    def body(*refs):
        out = refs[len(ins)]
        for cols, total in merged([getter(r) for r in refs[: len(ins)]], heads, True):
            out[:, cols] = total.astype(out.dtype)

    return call_merge(body, ins, [jax.ShapeDtypeStruct((rows, heads * HD), BF16)])[0]


def join(pieces, after=()):
    rows = sum(p.shape[0] for p in pieces)

    def body(*refs):
        out = refs[-1]
        ins = [r[...].astype(F32) for r in refs[: len(pieces)]]
        out[...] = jnp.concatenate(ins, axis=0).astype(out.dtype)

    shape = jax.ShapeDtypeStruct((rows, pieces[0].shape[1]), pieces[0].dtype)
    return call_merge(body, pieces, [shape], after)[0]


def call_merge(body, ins, shapes, after=()):
    size = sum(math.prod(x.shape) for x in ins)
    return pl.pallas_call(
        body,
        in_specs=[pl.BlockSpec(memory_space=pltpu.VMEM)] * len(ins)
        + [pl.BlockSpec(memory_space=pl.ANY)] * len(after),
        out_specs=[pl.BlockSpec(memory_space=pltpu.VMEM)] * len(shapes),
        out_shape=shapes,
        compiler_params=pltpu.CompilerParams(vmem_limit_bytes=48 * 1024 * 1024),
        cost_estimate=pl.CostEstimate(flops=4 * size, bytes_accessed=4 * size, transcendentals=0),
        name="merge",
    )(*ins, *after)


def per_device(queries, new_keys, new_values, cache_keys, cache_values, victims):
    members = lax.axis_size("seq")
    shape = factors(members)
    a_n, b_n, c_n = shape
    heads = queries.shape[1] // HD
    block_count = cache_keys.shape[0] // BLK
    block_ids = lax.axis_index("seq") * block_count + jnp.arange(block_count, dtype=jnp.int32)
    evicted = jnp.any(victims[:, None] == block_ids[None, :], axis=0)
    bias = jnp.repeat(jnp.where(evicted, NEG, 0.0), BLK)[None, :]
    tok = new_keys.shape[0]
    fresh_bias = jnp.where(jnp.arange(-(-tok // BLK) * BLK) < tok, 0.0, NEG)[None, :]
    bias = jnp.concatenate([bias, fresh_bias], axis=1)

    def fetch(x, by):
        return lax.ppermute(x, "seq", shift_perm(shape, by))

    def give(x, by):
        return lax.ppermute(x, "seq", shift_perm(shape, [-d for d in by]))

    far_first = sorted(range(1, a_n), key=lambda d: -min(d, a_n - d))
    line = [queries] + [None] * (a_n - 1)
    for d in far_first:
        line[d] = fetch(queries, (d, 0, 0))
    lines = [line] + [[fetch(x, (0, d, 0)) for x in line] for d in range(1, b_n)]
    last = line[far_first[-1]] if far_first else queries
    keys, values = load((cache_keys, cache_values), (new_keys, new_values), last)

    home = [join([join([queries])] + line[1:])] + [join(x, (keys,)) for x in lines[1:]]
    away = [[fetch(x, (0, 0, c)) for x in home] for c in range(1, c_n)]
    blocks = home + [x for core in away for x in core]
    kinds = [F32] * b_n + [BF16] * (b_n * (c_n - 1))
    blocks = attend(blocks, kinds, keys, values, bias)
    home, away = blocks[:b_n], blocks[b_n:]

    def over_cores(b, kind):
        got = [give(away[c * b_n + b], (0, 0, c + 1)) for c in range(c_n - 1)]
        return merge_rows([home[b]] + got, heads, a_n, [kind] * a_n)

    got = [[give(x, (0, d, 0)) for x in over_cores(d, BF16)] for d in range(1, b_n)]
    own = over_cores(0, F32)
    sums = [[own[d]] + [pieces[d] for pieces in got] for d in range(a_n)]
    for d in far_first:
        sums[d] = [give(merge_rows(sums[d], heads, 1, [BF16])[0], (d, 0, 0))]
    return finish([x for pieces in sums for x in pieces], heads)


def solution(mesh):
    rows = P(("groups", "seq"), None)
    return jax.shard_map(
        per_device,
        mesh=mesh,
        in_specs=(rows, rows, rows, rows, rows, P("groups")),
        out_specs=rows,
        check_vma=False,
    )
```

```python
import functools
import itertools
import math

import jax
import jax.numpy as jnp
from jax import lax
from jax.experimental import pallas as pl
from jax.experimental.pallas import tpu as pltpu
from jax.sharding import PartitionSpec as P

HD = 128
BLK = 128
STAT = 128
LANE = STAT // 3
NEG = -1e30
F32 = jnp.float32
BF16 = jnp.bfloat16


def factors(members):
    cores = 2 if members % 2 == 0 else 1
    chips = members // cores
    far = next(a for a in range(1, chips + 1) if chips % a == 0 and a * a >= chips)
    return far, chips // far, cores


def partner(at, by, size):
    return at ^ by if size & (size - 1) == 0 else (at + by) % size


def partner_perm(shape, by, back):
    def flat(place):
        return functools.reduce(lambda at, kn: at * kn[1] + kn[0], zip(place, shape), 0)

    places = itertools.product(*map(range, shape))
    pairs = [(flat([partner(*x) for x in zip(at, by, shape)]), flat(at)) for at in places]
    return [pair[::-1] for pair in pairs] if back else pairs


def lanes(rows):
    return lax.broadcasted_iota(jnp.int32, (rows, STAT), 1)


def pack_stats(top, mass):
    high = mass.astype(BF16).astype(F32)
    return top + pltpu.roll(high, LANE, 1) + pltpu.roll(mass - high, 2 * LANE, 1)


def unpack_stats(packed, heads):
    used = lanes(packed.shape[0]) < heads
    mass = pltpu.roll(packed, STAT - LANE, 1) + pltpu.roll(packed, STAT - 2 * LANE, 1)
    return jnp.where(used, packed, 0.0), jnp.where(used, mass, 0.0)


def attend_kernel(sizes, scale, bias_ref, q_refs, k_ref, v_ref, outs, top_acc, mass_acc):
    tile, steps, group, pack, lines = sizes
    rows = tile * len(outs)
    line_rows = outs[0].shape[0]
    wide = pack * HD
    lane = lanes(rows)
    contract_last = (((1,), (1,)), ((), ()))
    bias = bias_ref[...]
    mine = [lax.broadcasted_iota(jnp.int32, (rows, wide), 1) // HD == k for k in range(pack)]

    def row_tile(r, carry):
        at = pl.ds(pl.multiple_of(r * tile, tile), tile)
        in_plane = [pl.ds(pl.multiple_of(b * line_rows + r * tile, tile), tile) for b in range(lines)]
        top_acc[...] = jnp.zeros_like(top_acc)
        mass_acc[...] = jnp.zeros_like(mass_acc)

        def heads_of(step, carry):
            def columns(i):
                return pl.ds(pl.multiple_of((step * group + i) * wide, HD), wide)

            def scores(i):
                cols = columns(i)
                q = jnp.concatenate([ref[rs, cols] for ref in q_refs for rs in in_plane], axis=0)
                if pack > 1:
                    zero = jnp.zeros_like(q)
                    q = jnp.concatenate([jnp.where(m, q, zero) for m in mine], axis=0)
                return lax.dot_general(q, k_ref[:, cols], contract_last, preferred_element_type=F32)

            tops = top_acc[...]
            masses = mass_acc[...]
            ahead = scores(0)
            for i in range(group):
                score = ahead
                if i + 1 < group:
                    ahead = scores(i + 1)
                score = score * scale + bias
                top = jnp.max(score, axis=1, keepdims=True).astype(BF16).astype(F32)
                score = jnp.exp2(score - top)
                mass = jnp.sum(score, axis=1, keepdims=True)
                out = jnp.dot(score.astype(BF16), v_ref[:, columns(i)], preferred_element_type=F32)
                for k in range(pack):
                    head = (step * group + i) * pack + k
                    cols = pl.ds(pl.multiple_of(head * HD, HD), HD)
                    one = out[k * rows : (k + 1) * rows, k * HD : (k + 1) * HD]
                    for p, o_ref in enumerate(outs):
                        o_ref[at, cols] = one[p * tile : (p + 1) * tile].astype(o_ref.dtype)
                    tops = jnp.where(lane == head, top[k * rows : (k + 1) * rows], tops)
                    masses = jnp.where(lane == head, mass[k * rows : (k + 1) * rows], masses)
            top_acc[...] = tops
            mass_acc[...] = masses
            return carry

        lax.fori_loop(0, steps, heads_of, 0)
        packed = pack_stats(top_acc[...], mass_acc[...])
        for p, o_ref in enumerate(outs):
            width = o_ref.shape[1]
            o_ref[at, width - STAT :] = packed[p * tile : (p + 1) * tile].astype(o_ref.dtype)
        return carry

    lax.fori_loop(0, line_rows // tile, row_tile, 0)


def attend(planes, lines, kinds, keys, values, bias):
    n, m = len(planes), len(kinds)
    rows, columns = planes[0].shape[0] // lines, planes[0].shape[1]
    heads = columns // HD
    pack = 2 if heads % 2 == 0 else 1
    group = next(g for g in (2, 1) if heads % (g * pack) == 0)
    tile = next(t for t in (32, 16, rows) if rows % t == 0)
    width = columns + STAT
    scale = math.log2(math.e) / math.sqrt(HD)

    def body(*refs):
        attend_kernel(
            (tile, heads // (group * pack), group, pack, lines), scale, refs[0], refs[1 : 1 + n],
            *refs[1 + n : 3 + n], refs[3 + n : 3 + n + m], *refs[3 + n + m :],
        )

    return pl.pallas_call(
        body,
        in_specs=[pl.BlockSpec(memory_space=pltpu.VMEM)] * (n + 3),
        out_specs=[pl.BlockSpec(memory_space=pltpu.VMEM)] * m,
        out_shape=[jax.ShapeDtypeStruct((rows, width), kind) for kind in kinds],
        scratch_shapes=[pltpu.VMEM((tile * m, STAT), F32)] * 2,
        compiler_params=pltpu.CompilerParams(vmem_limit_bytes=40 * 1024 * 1024),
        cost_estimate=pl.CostEstimate(
            flops=4 * m * rows * keys.shape[0] * columns,
            bytes_accessed=4 * keys.shape[0] * columns,
            transcendentals=m * rows * keys.shape[0] * heads,
        ),
        name="attend",
    )(bias, *planes, keys, values)


def load(cached, fresh, victims, queries, after):
    cache_rows, columns = cached[0].shape
    tok = fresh[0].shape[0]
    padded = cache_rows + -(-tok // BLK) * BLK
    n = len(cached)

    def body(*refs):
        cached_refs, fresh_refs, victims_ref, queries_ref = refs[:n], refs[n : 2 * n], *refs[2 * n : 2 * n + 2]
        refs = refs[2 * n + 3 :]
        outs, bias_ref, q_ref, tails, ids_ref, sems = (
            refs[:n], refs[n], refs[n + 1], refs[n + 2 : 2 * n + 2], *refs[2 * n + 2 :]
        )
        ids = pltpu.make_async_copy(victims_ref, ids_ref, sems.at[1, n])
        rest = pltpu.make_async_copy(queries_ref, q_ref, sems.at[0, n])
        small = [
            pltpu.make_async_copy(src, dst, sems.at[1, i])
            for i, (src, dst) in enumerate(zip(fresh_refs, tails))
        ]
        large = [
            pltpu.make_async_copy(src, dst.at[pl.ds(0, cache_rows), :], sems.at[0, i])
            for i, (src, dst) in enumerate(zip(cached_refs, outs))
        ]
        for copy in [ids] + small + large + [rest]:
            copy.start()
        ids.wait()
        blocks = cache_rows // BLK
        first = lax.axis_index("seq") * blocks
        for block in range(blocks):
            hits = jnp.where(ids_ref[...] == first + block, 1.0, 0.0)
            hit = jnp.max(hits, axis=1, keepdims=True)
            gone = jnp.where(hit > 0.0, NEG, 0.0)
            bias_ref[:, block * BLK : (block + 1) * BLK] = jnp.broadcast_to(gone, (1, BLK))
        token = lax.broadcasted_iota(jnp.int32, (1, padded - cache_rows), 1)
        bias_ref[:, cache_rows:] = jnp.where(token < tok, 0.0, NEG)
        for copy, tail, out in zip(small, tails, outs):
            copy.wait()
            zeros = jnp.zeros((padded - cache_rows - tok, columns), F32)
            rows = jnp.concatenate([tail[...].astype(F32), zeros], axis=0)
            out[cache_rows:, :] = rows.astype(out.dtype)
        for copy in large + [rest]:
            copy.wait()

    in_hbm = pl.BlockSpec(memory_space=pltpu.HBM)
    held = (*cached, *fresh, victims, queries)
    return pl.pallas_call(
        body,
        in_specs=[in_hbm] * len(held) + [pl.BlockSpec(memory_space=pl.ANY)],
        out_specs=[pl.BlockSpec(memory_space=pltpu.VMEM)] * (n + 2),
        out_shape=[jax.ShapeDtypeStruct((padded, columns), BF16)] * n
        + [jax.ShapeDtypeStruct((1, padded), F32), jax.ShapeDtypeStruct(queries.shape, BF16)],
        scratch_shapes=[pltpu.VMEM(x.shape, BF16) for x in fresh]
        + [pltpu.VMEM(victims.shape, jnp.int32), pltpu.SemaphoreType.DMA((2, n + 1))],
        compiler_params=pltpu.CompilerParams(vmem_limit_bytes=24 * 1024 * 1024),
        cost_estimate=pl.CostEstimate(
            flops=0, bytes_accessed=4 * n * cache_rows * columns, transcendentals=0
        ),
        name="load",
    )(*[pltpu.with_memory_space_constraint(x, pltpu.HBM) for x in held], after)


def merged(arrays, heads, last):
    columns = heads * HD
    stats = [unpack_stats(get(slice(columns, columns + STAT)), heads) for get in arrays]
    top = functools.reduce(jnp.maximum, [t for t, _ in stats])
    weights = [jnp.exp2(t - top) for t, _ in stats]
    mass = functools.reduce(jnp.add, [w * m for w, (_, m) in zip(weights, stats)])
    if last:
        inverse = 1.0 / jnp.where(lanes(mass.shape[0]) < heads, mass, 1.0)
        weights = [w * inverse for w in weights]
    for head in range(heads):
        cols = slice(head * HD, (head + 1) * HD)
        yield cols, functools.reduce(
            jnp.add, [get(cols) * w[:, head : head + 1] for get, w in zip(arrays, weights)]
        )
    if not last:
        yield slice(columns, columns + STAT), pack_stats(top, mass)


def getter(ref, *index):
    return lambda cols: ref[(*index, slice(None), cols)].astype(F32)


def merge_rows(ins, heads, pieces, kinds):
    rows, width = ins[0].shape
    per = rows // pieces

    def body(*refs):
        outs = refs[len(ins) :]
        for cols, total in merged([getter(r) for r in refs[: len(ins)]], heads, False):
            for j, out in enumerate(outs):
                out[:, cols] = total[j * per : (j + 1) * per].astype(out.dtype)

    return call_merge(body, ins, [jax.ShapeDtypeStruct((per, width), kind) for kind in kinds])


def finish(ins, heads):
    rows = ins[0].shape[0]

    def body(*refs):
        out = refs[len(ins)]
        for cols, total in merged([getter(r) for r in refs[: len(ins)]], heads, True):
            out[:, cols] = total.astype(out.dtype)

    return call_merge(body, ins, [jax.ShapeDtypeStruct((rows, heads * HD), BF16)])[0]


def join(pieces, after=()):
    rows = sum(p.shape[0] for p in pieces)

    def body(*refs):
        out = refs[-1]
        ins = [r[...].astype(F32) for r in refs[: len(pieces)]]
        out[...] = jnp.concatenate(ins, axis=0).astype(out.dtype)

    shape = jax.ShapeDtypeStruct((rows, pieces[0].shape[1]), pieces[0].dtype)
    return call_merge(body, pieces, [shape], after)[0]


def call_merge(body, ins, shapes, after=()):
    size = sum(math.prod(x.shape) for x in ins)
    return pl.pallas_call(
        body,
        in_specs=[pl.BlockSpec(memory_space=pltpu.VMEM)] * len(ins)
        + [pl.BlockSpec(memory_space=pl.ANY)] * len(after),
        out_specs=[pl.BlockSpec(memory_space=pltpu.VMEM)] * len(shapes),
        out_shape=shapes,
        compiler_params=pltpu.CompilerParams(vmem_limit_bytes=48 * 1024 * 1024),
        cost_estimate=pl.CostEstimate(flops=4 * size, bytes_accessed=4 * size, transcendentals=0),
        name="merge",
    )(*ins, *after)


def per_device(queries, new_keys, new_values, cache_keys, cache_values, victims):
    members = lax.axis_size("seq")
    shape = factors(members)
    a_n, b_n, c_n = shape
    heads = queries.shape[1] // HD

    def fetch(x, *by):
        return lax.ppermute(x, "seq", partner_perm(shape, by, False))

    def give(x, *by):
        return lax.ppermute(x, "seq", partner_perm(shape, by, True))

    far_first = range(a_n - 1, 0, -1)
    line = [queries] + [None] * (a_n - 1)
    for a in far_first:
        line[a] = fetch(queries, a, 0, 0)
    lines = [line] + [[fetch(x, 0, b, 0) for x in line] for b in range(1, b_n)]
    keys, values, bias, line[0] = load(
        (cache_keys, cache_values), (new_keys, new_values), victims[None], queries, line[-1]
    )
    plane = join([x for pieces in lines for x in pieces])
    planes = [plane] + [fetch(plane, 0, 0, c) for c in range(1, c_n)]
    kinds = [F32] * b_n + [BF16] * (b_n * (c_n - 1))
    sums = attend(planes, b_n, kinds, keys, values, bias)

    def over_cores(b, kind):
        got = [give(sums[c * b_n + b], 0, 0, c) for c in range(1, c_n)]
        return merge_rows([sums[b]] + got, heads, a_n, [kind] * a_n)

    got = [[give(x, 0, b, 0) for x in over_cores(b, BF16)] for b in range(1, b_n)]
    own = over_cores(0, F32)
    total = [[own[a]] + [pieces[a] for pieces in got] for a in range(a_n)]
    last = [
        give(merge_rows(total[a], heads, 1, [BF16])[0], a, 0, 0) for a in far_first
    ]
    return finish([*merge_rows(total[0], heads, 1, [F32]), *last], heads)


def solution(mesh):
    rows = P(("groups", "seq"), None)
    return jax.shard_map(
        per_device,
        mesh=mesh,
        in_specs=(rows, rows, rows, rows, rows, P("groups")),
        out_specs=rows,
        check_vma=False,
    )
```

```python
import functools
import itertools
import math

import jax
import jax.numpy as jnp
from jax import lax
from jax.experimental import pallas as pl
from jax.experimental.pallas import tpu as pltpu
from jax.sharding import PartitionSpec as P

HD = 128
BLK = 128
STAT = 128
LANE = STAT // 3
NEG = -1e30
F32 = jnp.float32
BF16 = jnp.bfloat16


def factors(members):
    cores = 2 if members % 2 == 0 else 1
    chips = members // cores
    far = next(a for a in range(1, chips + 1) if chips % a == 0 and a * a >= chips)
    return far, chips // far, cores


def partner(at, by, size):
    return at ^ by if size & (size - 1) == 0 else (at + by) % size


def partner_perm(shape, by, back):
    def flat(place):
        return functools.reduce(lambda at, kn: at * kn[1] + kn[0], zip(place, shape), 0)

    places = itertools.product(*map(range, shape))
    pairs = [(flat([partner(*x) for x in zip(at, by, shape)]), flat(at)) for at in places]
    return [pair[::-1] for pair in pairs] if back else pairs


def lanes(rows):
    return lax.broadcasted_iota(jnp.int32, (rows, STAT), 1)


def pack_stats(top, mass):
    high = mass.astype(BF16).astype(F32)
    return top + pltpu.roll(high, LANE, 1) + pltpu.roll(mass - high, 2 * LANE, 1)


def unpack_stats(packed, heads):
    used = lanes(packed.shape[0]) < heads
    mass = pltpu.roll(packed, STAT - LANE, 1) + pltpu.roll(packed, STAT - 2 * LANE, 1)
    return jnp.where(used, packed, 0.0), jnp.where(used, mass, 0.0)


def attend_kernel(sizes, scale, bias_ref, q_refs, k_ref, v_ref, outs, top_acc, mass_acc):
    tile, steps, group, pack, lines = sizes
    rows = tile * len(outs)
    line_rows = outs[0].shape[0]
    wide = pack * HD
    lane = lanes(rows)
    contract_last = (((1,), (1,)), ((), ()))
    bias = bias_ref[...]
    mine = [lax.broadcasted_iota(jnp.int32, (rows, wide), 1) // HD == k for k in range(pack)]

    def row_tile(r, carry):
        at = pl.ds(pl.multiple_of(r * tile, tile), tile)
        in_plane = [pl.ds(pl.multiple_of(b * line_rows + r * tile, tile), tile) for b in range(lines)]
        top_acc[...] = jnp.zeros_like(top_acc)
        mass_acc[...] = jnp.zeros_like(mass_acc)

        def heads_of(step, carry):
            def columns(i):
                return pl.ds(pl.multiple_of((step * group + i) * wide, HD), wide)

            def scores(i):
                cols = columns(i)
                q = jnp.concatenate([ref[rs, cols] for ref in q_refs for rs in in_plane], axis=0)
                if pack > 1:
                    zero = jnp.zeros_like(q)
                    q = jnp.concatenate([jnp.where(m, q, zero) for m in mine], axis=0)
                return lax.dot_general(q, k_ref[:, cols], contract_last, preferred_element_type=F32)

            tops = top_acc[...]
            masses = mass_acc[...]
            ahead = scores(0)
            for i in range(group):
                score = ahead
                if i + 1 < group:
                    ahead = scores(i + 1)
                score = score * scale + bias
                top = jnp.max(score, axis=1, keepdims=True).astype(BF16).astype(F32)
                score = jnp.exp2(score - top)
                mass = jnp.sum(score, axis=1, keepdims=True)
                out = jnp.dot(score.astype(BF16), v_ref[:, columns(i)], preferred_element_type=F32)
                for k in range(pack):
                    head = (step * group + i) * pack + k
                    cols = pl.ds(pl.multiple_of(head * HD, HD), HD)
                    one = out[k * rows : (k + 1) * rows, k * HD : (k + 1) * HD]
                    for p, o_ref in enumerate(outs):
                        o_ref[at, cols] = one[p * tile : (p + 1) * tile].astype(o_ref.dtype)
                    tops = jnp.where(lane == head, top[k * rows : (k + 1) * rows], tops)
                    masses = jnp.where(lane == head, mass[k * rows : (k + 1) * rows], masses)
            top_acc[...] = tops
            mass_acc[...] = masses
            return carry

        lax.fori_loop(0, steps, heads_of, 0)
        packed = pack_stats(top_acc[...], mass_acc[...])
        for p, o_ref in enumerate(outs):
            width = o_ref.shape[1]
            o_ref[at, width - STAT :] = packed[p * tile : (p + 1) * tile].astype(o_ref.dtype)
        return carry

    lax.fori_loop(0, line_rows // tile, row_tile, 0)


def attend(planes, lines, kinds, keys, values, bias):
    n, m = len(planes), len(kinds)
    rows, columns = planes[0].shape[0] // lines, planes[0].shape[1]
    heads = columns // HD
    pack = 2 if heads % 2 == 0 else 1
    group = next(g for g in (2, 1) if heads % (g * pack) == 0)
    tile = next(t for t in (32, 16, rows) if rows % t == 0)
    width = columns + STAT
    scale = math.log2(math.e) / math.sqrt(HD)

    def body(*refs):
        attend_kernel(
            (tile, heads // (group * pack), group, pack, lines), scale, refs[0], refs[1 : 1 + n],
            *refs[1 + n : 3 + n], refs[3 + n : 3 + n + m], *refs[3 + n + m :],
        )

    return pl.pallas_call(
        body,
        in_specs=[pl.BlockSpec(memory_space=pltpu.VMEM)] * (n + 3),
        out_specs=[pl.BlockSpec(memory_space=pltpu.VMEM)] * m,
        out_shape=[jax.ShapeDtypeStruct((rows, width), kind) for kind in kinds],
        scratch_shapes=[pltpu.VMEM((tile * m, STAT), F32)] * 2,
        compiler_params=pltpu.CompilerParams(vmem_limit_bytes=40 * 1024 * 1024),
        cost_estimate=pl.CostEstimate(
            flops=4 * m * rows * keys.shape[0] * columns,
            bytes_accessed=4 * keys.shape[0] * columns,
            transcendentals=m * rows * keys.shape[0] * heads,
        ),
        name="attend",
    )(bias, *planes, keys, values)


def load(cached, fresh, victims, after):
    cache_rows, columns = cached[0].shape
    tok = fresh[0].shape[0]
    padded = cache_rows + -(-tok // BLK) * BLK
    blocks = cache_rows // BLK
    n = len(cached)

    def body(*refs):
        cached_refs, fresh_refs, victims_ref = refs[:n], refs[n : 2 * n], refs[2 * n]
        refs = refs[2 * n + 2 :]
        outs, bias_ref, tails, ids_ref, sems = refs[:n], refs[n], refs[n + 1 : 2 * n + 1], *refs[2 * n + 1 :]
        ids = pltpu.make_async_copy(victims_ref, ids_ref, sems.at[n, 0])
        small = [
            pltpu.make_async_copy(src, dst, sems.at[i, blocks])
            for i, (src, dst) in enumerate(zip(fresh_refs, tails))
        ]
        large = [
            pltpu.make_async_copy(
                src.at[pl.ds(j * BLK, BLK), :], dst.at[pl.ds(j * BLK, BLK), :], sems.at[i, j]
            )
            for i, (src, dst) in enumerate(zip(cached_refs, outs))
            for j in range(blocks)
        ]
        for copy in [ids] + small + large:
            copy.start()
        ids.wait()
        first = lax.axis_index("seq") * blocks
        for block in range(blocks):
            hits = jnp.where(ids_ref[...] == first + block, 1.0, 0.0)
            hit = jnp.max(hits, axis=1, keepdims=True)
            gone = jnp.where(hit > 0.0, NEG, 0.0)
            bias_ref[:, block * BLK : (block + 1) * BLK] = jnp.broadcast_to(gone, (1, BLK))
        token = lax.broadcasted_iota(jnp.int32, (1, padded - cache_rows), 1)
        bias_ref[:, cache_rows:] = jnp.where(token < tok, 0.0, NEG)
        for copy, tail, out in zip(small, tails, outs):
            copy.wait()
            zeros = jnp.zeros((padded - cache_rows - tok, columns), F32)
            rows = jnp.concatenate([tail[...].astype(F32), zeros], axis=0)
            out[cache_rows:, :] = rows.astype(out.dtype)
        for copy in large:
            copy.wait()

    in_hbm = pl.BlockSpec(memory_space=pltpu.HBM)
    held = (*cached, *fresh, victims)
    return pl.pallas_call(
        body,
        in_specs=[in_hbm] * len(held) + [pl.BlockSpec(memory_space=pl.ANY)],
        out_specs=[pl.BlockSpec(memory_space=pltpu.VMEM)] * (n + 1),
        out_shape=[jax.ShapeDtypeStruct((padded, columns), BF16)] * n
        + [jax.ShapeDtypeStruct((1, padded), F32)],
        scratch_shapes=[pltpu.VMEM(x.shape, BF16) for x in fresh]
        + [pltpu.VMEM(victims.shape, jnp.int32), pltpu.SemaphoreType.DMA((n + 1, blocks + 1))],
        compiler_params=pltpu.CompilerParams(vmem_limit_bytes=24 * 1024 * 1024),
        cost_estimate=pl.CostEstimate(
            flops=0, bytes_accessed=4 * n * cache_rows * columns, transcendentals=0
        ),
        name="load",
    )(*[pltpu.with_memory_space_constraint(x, pltpu.HBM) for x in held], after)


def merged(arrays, heads, last):
    columns = heads * HD
    stats = [unpack_stats(get(slice(columns, columns + STAT)), heads) for get in arrays]
    top = functools.reduce(jnp.maximum, [t for t, _ in stats])
    weights = [jnp.exp2(t - top) for t, _ in stats]
    mass = functools.reduce(jnp.add, [w * m for w, (_, m) in zip(weights, stats)])
    if last:
        inverse = 1.0 / jnp.where(lanes(mass.shape[0]) < heads, mass, 1.0)
        weights = [w * inverse for w in weights]
    for head in range(heads):
        cols = slice(head * HD, (head + 1) * HD)
        yield cols, functools.reduce(
            jnp.add, [get(cols) * w[:, head : head + 1] for get, w in zip(arrays, weights)]
        )
    if not last:
        yield slice(columns, columns + STAT), pack_stats(top, mass)


def getter(ref, *index):
    return lambda cols: ref[(*index, slice(None), cols)].astype(F32)


def merge_rows(ins, heads, pieces, kinds, after=()):
    rows, width = ins[0].shape
    per = rows // pieces

    def body(*refs):
        outs = refs[len(ins) + len(after) :]
        for cols, total in merged([getter(r) for r in refs[: len(ins)]], heads, False):
            for j, out in enumerate(outs):
                out[:, cols] = total[j * per : (j + 1) * per].astype(out.dtype)

    shapes = [jax.ShapeDtypeStruct((per, width), kind) for kind in kinds]
    return call_merge(body, ins, shapes, after)


def finish(ins, heads):
    rows = ins[0].shape[0]

    def body(*refs):
        out = refs[len(ins)]
        for cols, total in merged([getter(r) for r in refs[: len(ins)]], heads, True):
            out[:, cols] = total.astype(out.dtype)

    return call_merge(body, ins, [jax.ShapeDtypeStruct((rows, heads * HD), BF16)])[0]


def join(pieces, after=()):
    rows = sum(p.shape[0] for p in pieces)

    def body(*refs):
        out = refs[-1]
        ins = [r[...].astype(F32) for r in refs[: len(pieces)]]
        out[...] = jnp.concatenate(ins, axis=0).astype(out.dtype)

    shape = jax.ShapeDtypeStruct((rows, pieces[0].shape[1]), pieces[0].dtype)
    return call_merge(body, pieces, [shape], after)[0]


def call_merge(body, ins, shapes, after=()):
    size = sum(math.prod(x.shape) for x in ins)
    return pl.pallas_call(
        body,
        in_specs=[pl.BlockSpec(memory_space=pltpu.VMEM)] * len(ins)
        + [pl.BlockSpec(memory_space=pl.ANY)] * len(after),
        out_specs=[pl.BlockSpec(memory_space=pltpu.VMEM)] * len(shapes),
        out_shape=shapes,
        compiler_params=pltpu.CompilerParams(vmem_limit_bytes=48 * 1024 * 1024),
        cost_estimate=pl.CostEstimate(flops=4 * size, bytes_accessed=4 * size, transcendentals=0),
        name="merge",
    )(*ins, *after)


def per_device(queries, new_keys, new_values, cache_keys, cache_values, victims):
    members = lax.axis_size("seq")
    shape = factors(members)
    a_n, b_n, c_n = shape
    heads = queries.shape[1] // HD

    def fetch(x, *by):
        return lax.ppermute(x, "seq", partner_perm(shape, by, False))

    def give(x, *by):
        return lax.ppermute(x, "seq", partner_perm(shape, by, True))

    pieces = [join([queries])] + [fetch(queries, a, 0, 0) for a in range(1, a_n)]
    runs = [pieces[:2], pieces[2:-1], pieces[-1:]] if a_n > 3 else [pieces]
    runs = [x[0] if len(x) == 1 else join(x) for x in runs]
    lines = [runs] + [[fetch(x, 0, b, 0) for x in runs] for b in range(1, b_n)]
    keys, values, bias = load((cache_keys, cache_values), (new_keys, new_values), victims[None], runs[-1])
    plane = join([x for pieces in lines for x in pieces], (keys,))
    planes = [plane] + [fetch(plane, 0, 0, c) for c in range(1, c_n)]
    kinds = [F32] * b_n + [BF16] * (b_n * (c_n - 1))
    sums = attend(planes, b_n, kinds, keys, values, bias)

    halves = 2 if a_n % 2 == 0 else 1
    per = a_n // halves

    def over_cores(b, kind):
        got = [give(sums[c * b_n + b], 0, 0, c) for c in range(1, c_n)]
        return merge_rows([sums[b]] + got, heads, halves, [kind] * halves)

    got = [over_cores(b, BF16) for b in range(1, b_n)]
    got = [[give(x, 0, b, 0) for x in half[::-1]][::-1] for b, half in enumerate(got, 1)]
    own = over_cores(0, F32)
    pieces = []
    for h in range(halves)[::-1]:
        kinds = [BF16 if h + j else F32 for j in range(per)]
        parts = [own[h]] + [half[h] for half in got]
        pieces = [*merge_rows(parts, heads, per, kinds, pieces[:1]), *pieces]
    near, far = [
        [give(pieces[a], a, 0, 0) for a in part] for part in (range(1, per), range(max(per, 1), a_n))
    ]
    if far:
        pieces[:1] = merge_rows([pieces[0]] + far, heads, 1, [F32])
    return finish([pieces[0]] + near, heads)


def solution(mesh):
    rows = P(("groups", "seq"), None)
    return jax.shard_map(
        per_device,
        mesh=mesh,
        in_specs=(rows, rows, rows, rows, rows, P("groups")),
        out_specs=rows,
        check_vma=False,
    )
```

```python
import functools
import itertools
import math

import jax
import jax.numpy as jnp
from jax import lax
from jax.experimental import pallas as pl
from jax.experimental.pallas import tpu as pltpu
from jax.sharding import PartitionSpec as P

HD = 128
BLK = 128
STAT = 128
LANE = STAT // 3
NEG = -1e30
F32 = jnp.float32
BF16 = jnp.bfloat16


def factors(members):
    cores = 2 if members % 2 == 0 else 1
    chips = members // cores
    far = next(
        a for a in range(1, chips + 1) if chips % a == 0 and a * a >= chips and a % (chips // a) == 0
    )
    return far, chips // far, cores


def partner(at, by, size):
    return at ^ by if size & (size - 1) == 0 else (at + by) % size


def role_perm(shape, mine, others, back=False):
    def flat(place):
        return functools.reduce(lambda at, kn: at * kn[1] + kn[0], zip(place, shape), 0)

    pairs = []
    for at in itertools.product(*map(range, shape)):
        step = mine if is_first(at[2], shape[2]) else others
        to = list(at)
        if step is not None:
            axis, by = step
            to[axis] = partner(at[axis], by, shape[axis])
        pairs.append((flat(at), flat(to)) if back else (flat(to), flat(at)))
    return pairs


def is_first(core, cores):
    return core == cores - 1


def lanes(rows):
    return lax.broadcasted_iota(jnp.int32, (rows, STAT), 1)


def pack_stats(top, mass):
    high = mass.astype(BF16).astype(F32)
    return top + pltpu.roll(high, LANE, 1) + pltpu.roll(mass - high, 2 * LANE, 1)


def unpack_stats(packed, heads):
    used = lanes(packed.shape[0]) < heads
    mass = pltpu.roll(packed, STAT - LANE, 1) + pltpu.roll(packed, STAT - 2 * LANE, 1)
    return jnp.where(used, packed, 0.0), jnp.where(used, mass, 0.0)


def attend_kernel(sizes, scale, bias_ref, q_refs, k_ref, v_ref, outs, top_acc, mass_acc):
    tile, steps, group, pack, lines = sizes
    rows = tile * len(outs)
    line_rows = outs[0].shape[0]
    wide = pack * HD
    lane = lanes(rows)
    contract_last = (((1,), (1,)), ((), ()))
    bias = bias_ref[...]
    mine = [lax.broadcasted_iota(jnp.int32, (rows, wide), 1) // HD == k for k in range(pack)]

    def row_tile(r, carry):
        at = pl.ds(pl.multiple_of(r * tile, tile), tile)
        in_plane = [pl.ds(pl.multiple_of(b * line_rows + r * tile, tile), tile) for b in range(lines)]
        top_acc[...] = jnp.zeros_like(top_acc)
        mass_acc[...] = jnp.zeros_like(mass_acc)

        def heads_of(step, carry):
            def columns(i):
                return pl.ds(pl.multiple_of((step * group + i) * wide, HD), wide)

            def scores(i):
                cols = columns(i)
                q = jnp.concatenate([ref[rs, cols] for ref in q_refs for rs in in_plane], axis=0)
                if pack > 1:
                    zero = jnp.zeros_like(q)
                    q = jnp.concatenate([jnp.where(m, q, zero) for m in mine], axis=0)
                return lax.dot_general(q, k_ref[:, cols], contract_last, preferred_element_type=F32)

            tops = top_acc[...]
            masses = mass_acc[...]
            ahead = scores(0)
            for i in range(group):
                score = ahead
                if i + 1 < group:
                    ahead = scores(i + 1)
                score = score * scale + bias
                top = jnp.max(score, axis=1, keepdims=True).astype(BF16).astype(F32)
                score = jnp.exp2(score - top)
                mass = jnp.sum(score, axis=1, keepdims=True)
                out = jnp.dot(score.astype(BF16), v_ref[:, columns(i)], preferred_element_type=F32)
                for k in range(pack):
                    head = (step * group + i) * pack + k
                    cols = pl.ds(pl.multiple_of(head * HD, HD), HD)
                    one = out[k * rows : (k + 1) * rows, k * HD : (k + 1) * HD]
                    for p, o_ref in enumerate(outs):
                        o_ref[at, cols] = one[p * tile : (p + 1) * tile].astype(o_ref.dtype)
                    tops = jnp.where(lane == head, top[k * rows : (k + 1) * rows], tops)
                    masses = jnp.where(lane == head, mass[k * rows : (k + 1) * rows], masses)
            top_acc[...] = tops
            mass_acc[...] = masses
            return carry

        lax.fori_loop(0, steps, heads_of, 0)
        packed = pack_stats(top_acc[...], mass_acc[...])
        for p, o_ref in enumerate(outs):
            width = o_ref.shape[1]
            o_ref[at, width - STAT :] = packed[p * tile : (p + 1) * tile].astype(o_ref.dtype)
        return carry

    lax.fori_loop(0, line_rows // tile, row_tile, 0)


def attend(planes, lines, kinds, keys, values, bias):
    n, m = len(planes), len(kinds)
    rows, columns = planes[0].shape[0] // lines, planes[0].shape[1]
    heads = columns // HD
    pack = 2 if heads % 2 == 0 else 1
    group = next(g for g in (2, 1) if heads % (g * pack) == 0)
    tile = next(t for t in (32, 16, rows) if rows % t == 0)
    width = columns + STAT
    scale = math.log2(math.e) / math.sqrt(HD)

    def body(*refs):
        attend_kernel(
            (tile, heads // (group * pack), group, pack, lines), scale, refs[0], refs[1 : 1 + n],
            *refs[1 + n : 3 + n], refs[3 + n : 3 + n + m], *refs[3 + n + m :],
        )

    return pl.pallas_call(
        body,
        in_specs=[pl.BlockSpec(memory_space=pltpu.VMEM)] * (n + 3),
        out_specs=[pl.BlockSpec(memory_space=pltpu.VMEM)] * m,
        out_shape=[jax.ShapeDtypeStruct((rows, width), kind) for kind in kinds],
        scratch_shapes=[pltpu.VMEM((tile * m, STAT), F32)] * 2,
        compiler_params=pltpu.CompilerParams(vmem_limit_bytes=40 * 1024 * 1024),
        cost_estimate=pl.CostEstimate(
            flops=4 * m * rows * keys.shape[0] * columns,
            bytes_accessed=4 * keys.shape[0] * columns,
            transcendentals=m * rows * keys.shape[0] * heads,
        ),
        name="attend",
    )(bias, *planes, keys, values)


def load(cached, fresh, victims, after):
    cache_rows, columns = cached[0].shape
    tok = fresh[0].shape[0]
    padded = cache_rows + -(-tok // BLK) * BLK
    blocks = cache_rows // BLK
    n = len(cached)

    def body(*refs):
        cached_refs, fresh_refs, victims_ref = refs[:n], refs[n : 2 * n], refs[2 * n]
        refs = refs[2 * n + 2 :]
        outs, bias_ref, tails, ids_ref, sems = refs[:n], refs[n], refs[n + 1 : 2 * n + 1], *refs[2 * n + 1 :]
        ids = pltpu.make_async_copy(victims_ref, ids_ref, sems.at[n, 0])
        small = [
            pltpu.make_async_copy(src, dst, sems.at[i, blocks])
            for i, (src, dst) in enumerate(zip(fresh_refs, tails))
        ]
        large = [
            pltpu.make_async_copy(
                src.at[pl.ds(j * BLK, BLK), :], dst.at[pl.ds(j * BLK, BLK), :], sems.at[i, j]
            )
            for i, (src, dst) in enumerate(zip(cached_refs, outs))
            for j in range(blocks)
        ]
        for copy in [ids] + small + large:
            copy.start()
        ids.wait()
        first = lax.axis_index("seq") * blocks
        for block in range(blocks):
            hits = jnp.where(ids_ref[...] == first + block, 1.0, 0.0)
            hit = jnp.max(hits, axis=1, keepdims=True)
            gone = jnp.where(hit > 0.0, NEG, 0.0)
            bias_ref[:, block * BLK : (block + 1) * BLK] = jnp.broadcast_to(gone, (1, BLK))
        token = lax.broadcasted_iota(jnp.int32, (1, padded - cache_rows), 1)
        bias_ref[:, cache_rows:] = jnp.where(token < tok, 0.0, NEG)
        for copy, tail, out in zip(small, tails, outs):
            copy.wait()
            zeros = jnp.zeros((padded - cache_rows - tok, columns), F32)
            rows = jnp.concatenate([tail[...].astype(F32), zeros], axis=0)
            out[cache_rows:, :] = rows.astype(out.dtype)
        for copy in large:
            copy.wait()

    in_hbm = pl.BlockSpec(memory_space=pltpu.HBM)
    held = (*cached, *fresh, victims)
    return pl.pallas_call(
        body,
        in_specs=[in_hbm] * len(held) + [pl.BlockSpec(memory_space=pl.ANY)],
        out_specs=[pl.BlockSpec(memory_space=pltpu.VMEM)] * (n + 1),
        out_shape=[jax.ShapeDtypeStruct((padded, columns), BF16)] * n
        + [jax.ShapeDtypeStruct((1, padded), F32)],
        scratch_shapes=[pltpu.VMEM(x.shape, BF16) for x in fresh]
        + [pltpu.VMEM(victims.shape, jnp.int32), pltpu.SemaphoreType.DMA((n + 1, blocks + 1))],
        compiler_params=pltpu.CompilerParams(vmem_limit_bytes=24 * 1024 * 1024),
        cost_estimate=pl.CostEstimate(
            flops=0, bytes_accessed=4 * n * cache_rows * columns, transcendentals=0
        ),
        name="load",
    )(*[pltpu.with_memory_space_constraint(x, pltpu.HBM) for x in held], after)


def merged(arrays, heads, last):
    columns = heads * HD
    stats = [unpack_stats(get(slice(columns, columns + STAT)), heads) for get in arrays]
    top = functools.reduce(jnp.maximum, [t for t, _ in stats])
    weights = [jnp.exp2(t - top) for t, _ in stats]
    mass = functools.reduce(jnp.add, [w * m for w, (_, m) in zip(weights, stats)])
    if last:
        inverse = 1.0 / jnp.where(lanes(mass.shape[0]) < heads, mass, 1.0)
        weights = [w * inverse for w in weights]
    for head in range(heads):
        cols = slice(head * HD, (head + 1) * HD)
        yield cols, functools.reduce(
            jnp.add, [get(cols) * w[:, head : head + 1] for get, w in zip(arrays, weights)]
        )
    if not last:
        yield slice(columns, columns + STAT), pack_stats(top, mass)


def getter(ref, *index):
    return lambda cols: ref[(*index, slice(None), cols)].astype(F32)


def role_kernel(role, one, other):
    if one is other:
        return one()
    pl.when(role() == 1)(one)
    pl.when(role() != 1)(other)


def put(merged_rows, outs):
    for cols, total in merged_rows:
        per = total.shape[0] // len(outs)
        for j, out in enumerate(outs):
            if out is not None:
                out[:, cols] = total[j * per : (j + 1) * per].astype(out.dtype)


def merge_rows(ins, heads, kinds):
    rows, width = ins[0].shape
    n = len(ins)
    per = rows // len(kinds)
    flat = [kind for pair in kinds for kind in pair]

    def body(*refs):
        outs = iter(refs[n:])
        outs = [[next(outs) for _ in pair] for pair in kinds]
        for cols, total in merged([getter(r) for r in refs[:n]], heads, False):
            for j, pair in enumerate(outs):
                for out in pair:
                    out[:, cols] = total[j * per : (j + 1) * per].astype(out.dtype)

    return call_merge(body, ins, [jax.ShapeDtypeStruct((per, width), kind) for kind in flat])


def merge_unit(role, heads, slots, mine, others, own):
    ins = [*mine, *others] + ([own] if own is not None else [])
    rows, width = ins[0].shape
    per = rows // slots
    n = len(mine)

    def body(*refs):
        first, pieces = refs[len(ins)], refs[len(ins) + 1 :]

        def one():
            parts = [getter(r) for r in refs[:n]]
            if own is None:
                put(merged(parts, heads, False), [first, *pieces])
            else:
                put(merged(parts, heads, False), pieces)
                first[...] = refs[len(ins) - 1][...]

        def other():
            parts = [getter(r) for r in refs[n : n + len(others)]]
            skip = [] if own is None else [None]
            put(merged(parts, heads, False), [first, *pieces[len(skip) :]])

        if not others:
            pl.when(role() == 1)(one)
        elif others is mine:
            one()
        else:
            role_kernel(role, one, other)

    sent = slots if own is not None else slots - 1
    shapes = [jax.ShapeDtypeStruct((per, width), F32)]
    shapes += [jax.ShapeDtypeStruct((per, width), BF16)] * sent
    return call_merge(body, ins, shapes)


def finish(role, own, got, near, heads):
    rows = own.shape[0]
    ins = [own, *got]

    def body(*refs):
        out = refs[len(ins)]

        def add(parts):
            return lambda: put(merged([getter(r) for r in parts], heads, True), [out])

        role_kernel(role, add(refs[: len(ins)]), add([refs[0], *refs[len(ins) - near : len(ins)]]))

    return call_merge(body, ins, [jax.ShapeDtypeStruct((rows, heads * HD), BF16)])[0]


def join(pieces, after=()):
    rows = sum(p.shape[0] for p in pieces)

    def body(*refs):
        out = refs[-1]
        ins = [r[...].astype(F32) for r in refs[: len(pieces)]]
        out[...] = jnp.concatenate(ins, axis=0).astype(out.dtype)

    shape = jax.ShapeDtypeStruct((rows, pieces[0].shape[1]), pieces[0].dtype)
    return call_merge(body, pieces, [shape], after)[0]


def choose(role, mine, others, after=()):
    ins = [*mine, *others]
    rows = sum(p.shape[0] for p in mine)

    def body(*refs):
        out = refs[-1]

        def fill(parts):
            def store():
                rows = [r[...].astype(F32) for r in parts]
                out[...] = jnp.concatenate(rows, axis=0).astype(out.dtype)

            return store

        role_kernel(role, fill(refs[: len(mine)]), fill(refs[len(mine) : len(ins)]))

    shape = jax.ShapeDtypeStruct((rows, mine[0].shape[1]), mine[0].dtype)
    return call_merge(body, ins, [shape], after)[0]


def call_merge(body, ins, shapes, after=()):
    size = sum(math.prod(x.shape) for x in ins)
    return pl.pallas_call(
        body,
        in_specs=[pl.BlockSpec(memory_space=pltpu.VMEM)] * len(ins)
        + [pl.BlockSpec(memory_space=pl.ANY)] * len(after),
        out_specs=[pl.BlockSpec(memory_space=pltpu.VMEM)] * len(shapes),
        out_shape=shapes,
        compiler_params=pltpu.CompilerParams(vmem_limit_bytes=48 * 1024 * 1024),
        cost_estimate=pl.CostEstimate(flops=4 * size, bytes_accessed=4 * size, transcendentals=0),
        name="merge",
    )(*ins, *after)


def per_device(queries, new_keys, new_values, cache_keys, cache_values, victims):
    members = lax.axis_size("seq")
    shape = factors(members)
    a_n, b_n, c_n = shape
    heads = queries.shape[1] // HD

    def role():
        core = lax.rem(lax.axis_index("seq"), c_n)
        return jnp.where(core == c_n - 1, 1, 0)

    def swap(x, mine, others, back=False):
        return lax.ppermute(x, "seq", role_perm(shape, mine, others, back))

    far_a = [0, *range(a_n - 1, 0, -1)]
    far_b = [0, *range(b_n - 1, 0, -1)]
    ratio = a_n // b_n
    crossing = a_n - ratio

    slots = [join([queries])]
    for s in range(1, a_n):
        slots.append(swap(queries, (0, far_a[s]), (1, far_b[s]) if s < b_n else None))
    units = [join(slots[:b_n])]
    units += [
        choose(role, slots[i * b_n : (i + 1) * b_n], units[:1]) for i in range(1, ratio)
    ]

    def steps(j):
        return (1, far_b[j // ratio + 1]) if j < crossing else None, (0, far_a[j + 1])

    got = [
        swap(units[j % ratio] if j < crossing else units[0], *steps(j)) for j in range(a_n - 1)
    ]
    keys, values, bias = load(
        (cache_keys, cache_values), (new_keys, new_values), victims[None], slots[-1]
    )
    mine = [*units, *got[:crossing]]
    others = [units[0], *got[crossing:], *got[:crossing]]
    plane = choose(role, mine, others, (keys,))
    planes = [plane] + [swap(plane, (2, c), (2, c)) for c in range(1, c_n)]

    kinds = [F32] * b_n + [BF16] * (b_n * (c_n - 1))
    sums = attend(planes, b_n, kinds, keys, values, bias)

    def over_cores(b, pairs):
        back = [swap(sums[c * b_n + b], (2, c), (2, c), True) for c in range(1, c_n)]
        return merge_rows([sums[b]] + back, heads, pairs)

    sent = [x for b in range(1, b_n) for x in over_cores(b, [[BF16]] * ratio)]
    kept = over_cores(0, [[F32]] + [[F32, BF16]] * (ratio - 1))
    sent += kept[2::2]
    kept = [kept[0], *kept[1::2]]
    got = [swap(x, *steps(j), True) for j, x in enumerate(sent)]

    own, pieces = None, []
    for i in range(ratio):
        part = [kept[i], *got[i:crossing:ratio]]
        if i < ratio - 1:
            rest = []
        else:
            rest = part if ratio == 1 else [kept[0], *got]
        out = merge_unit(role, heads, b_n, part, rest, own)
        own, pieces = out[0], pieces + list(out[1:])
    got = []
    for s in range(1, a_n):
        near = s - (a_n - b_n)
        step = (1, far_b[near]) if near > 0 else None
        got.append(swap(pieces[s - 1], (0, far_a[s]), step, True))
    return finish(role, own, got, b_n - 1, heads)


def solution(mesh):
    rows = P(("groups", "seq"), None)
    return jax.shard_map(
        per_device,
        mesh=mesh,
        in_specs=(rows, rows, rows, rows, rows, P("groups")),
        out_specs=rows,
        check_vma=False,
    )
```

```python
import functools
import itertools
import math

import jax
import jax.numpy as jnp
from jax import lax
from jax.experimental import pallas as pl
from jax.experimental.pallas import tpu as pltpu
from jax.sharding import PartitionSpec as P

HD = 128
BLK = 128
STAT = 128
LANE = STAT // 3
NEG = -1e30
F32 = jnp.float32
BF16 = jnp.bfloat16


def factors(members):
    cores = 2 if members % 2 == 0 else 1
    chips = members // cores
    far = next(a for a in range(1, chips + 1) if chips % a == 0 and a * a >= chips)
    return far, chips // far, cores


def partner(at, by, size):
    return at ^ by if size & (size - 1) == 0 else (at + by) % size


def partner_perm(shape, by, back):
    def flat(place):
        return functools.reduce(lambda at, kn: at * kn[1] + kn[0], zip(place, shape), 0)

    places = itertools.product(*map(range, shape))
    pairs = [(flat([partner(*x) for x in zip(at, by, shape)]), flat(at)) for at in places]
    return [pair[::-1] for pair in pairs] if back else pairs


def lanes(rows):
    return lax.broadcasted_iota(jnp.int32, (rows, STAT), 1)


def pack_stats(top, mass):
    high = mass.astype(BF16).astype(F32)
    return top + pltpu.roll(high, LANE, 1) + pltpu.roll(mass - high, 2 * LANE, 1)


def unpack_stats(packed, heads):
    used = lanes(packed.shape[0]) < heads
    mass = pltpu.roll(packed, STAT - LANE, 1) + pltpu.roll(packed, STAT - 2 * LANE, 1)
    return jnp.where(used, packed, 0.0), jnp.where(used, mass, 0.0)


def attend_kernel(sizes, scale, bias_ref, q_refs, k_ref, v_ref, outs, top_acc, mass_acc):
    tile, steps, group, pack, lines = sizes
    rows = tile * len(outs)
    line_rows = outs[0].shape[0]
    wide = pack * HD
    contract_last = (((1,), (1,)), ((), ()))
    contract_first = (((0,), (0,)), ((), ()))
    mine = [lax.broadcasted_iota(jnp.int32, (rows, wide), 1) // HD == k for k in range(pack)]

    def row_tile(r, carry):
        at = pl.ds(pl.multiple_of(r * tile, tile), tile)
        in_plane = [pl.ds(pl.multiple_of(b * line_rows + r * tile, tile), tile) for b in range(lines)]
        top_acc[...] = jnp.zeros_like(top_acc)
        mass_acc[...] = jnp.zeros_like(mass_acc)

        def heads_of(step, carry):
            def columns(i):
                return pl.ds(pl.multiple_of((step * group + i) * wide, HD), wide)

            def scores(i):
                cols = columns(i)
                q = jnp.concatenate([ref[rs, cols] for ref in q_refs for rs in in_plane], axis=0)
                if pack > 1:
                    zero = jnp.zeros_like(q)
                    q = jnp.concatenate([jnp.where(m, q, zero) for m in mine], axis=0)
                return lax.dot_general(k_ref[:, cols], q, contract_last, preferred_element_type=F32)

            ahead = scores(0)
            for i in range(group):
                score = ahead
                if i + 1 < group:
                    ahead = scores(i + 1)
                bias = jnp.concatenate([bias_ref[...]] * (pack * rows // STAT), axis=1)
                score = score * scale + bias
                top = jnp.max(score, axis=0, keepdims=True).astype(BF16).astype(F32)
                score = jnp.exp2(score - top)
                mass = jnp.sum(score, axis=0, keepdims=True)
                score = score.astype(BF16)
                for k in range(pack):
                    head = (step * group + i) * pack + k
                    cols = pl.ds(pl.multiple_of(head * HD, HD), HD)
                    part = slice(k * rows, (k + 1) * rows)
                    one = lax.dot_general(
                        score[:, part], v_ref[:, cols], contract_first, preferred_element_type=F32
                    )
                    for p, o_ref in enumerate(outs):
                        o_ref[at, cols] = one[p * tile : (p + 1) * tile].astype(o_ref.dtype)
                    top_acc[pl.ds(head, 1), :] = top[:, part]
                    mass_acc[pl.ds(head, 1), :] = mass[:, part]
            return carry

        lax.fori_loop(0, steps, heads_of, 0)
        packed = pack_stats(top_acc[...].T, mass_acc[...].T)
        for p, o_ref in enumerate(outs):
            width = o_ref.shape[1]
            o_ref[at, width - STAT :] = packed[p * tile : (p + 1) * tile].astype(o_ref.dtype)
        return carry

    lax.fori_loop(0, line_rows // tile, row_tile, 0)


def attend(planes, lines, kinds, keys, values, bias):
    n, m = len(planes), len(kinds)
    rows, columns = planes[0].shape[0] // lines, planes[0].shape[1]
    heads = columns // HD
    pack = 2 if heads % 2 == 0 else 1
    group = next(g for g in (2, 1) if heads % (g * pack) == 0)
    tile = next(t for t in (32, 16, rows) if rows % t == 0)
    width = columns + STAT
    scale = math.log2(math.e) / math.sqrt(HD)

    def body(*refs):
        attend_kernel(
            (tile, heads // (group * pack), group, pack, lines), scale, refs[0], refs[1 : 1 + n],
            *refs[1 + n : 3 + n], refs[3 + n : 3 + n + m], *refs[3 + n + m :],
        )

    return pl.pallas_call(
        body,
        in_specs=[pl.BlockSpec(memory_space=pltpu.VMEM)] * (n + 3),
        out_specs=[pl.BlockSpec(memory_space=pltpu.VMEM)] * m,
        out_shape=[jax.ShapeDtypeStruct((rows, width), kind) for kind in kinds],
        scratch_shapes=[pltpu.VMEM((STAT, tile * m), F32)] * 2,
        compiler_params=pltpu.CompilerParams(vmem_limit_bytes=40 * 1024 * 1024),
        cost_estimate=pl.CostEstimate(
            flops=4 * m * rows * keys.shape[0] * columns,
            bytes_accessed=4 * keys.shape[0] * columns,
            transcendentals=m * rows * keys.shape[0] * heads,
        ),
        name="attend",
    )(bias, *planes, keys, values)


def load(cached, fresh, victims, queries, after):
    cache_rows, columns = cached[0].shape
    tok = fresh[0].shape[0]
    padded = cache_rows + -(-tok // 16) * 16
    n = len(cached)

    def body(*refs):
        cached_refs, fresh_refs, victims_ref, queries_ref = refs[:n], refs[n : 2 * n], *refs[2 * n : 2 * n + 2]
        refs = refs[2 * n + 3 :]
        outs, bias_ref, q_ref, tails, ids_ref, sems = (
            refs[:n], refs[n], refs[n + 1], refs[n + 2 : 2 * n + 2], *refs[2 * n + 2 :]
        )
        ids = pltpu.make_async_copy(victims_ref, ids_ref, sems.at[1, n])
        rest = pltpu.make_async_copy(queries_ref, q_ref, sems.at[0, n])
        small = [
            pltpu.make_async_copy(src, dst, sems.at[1, i])
            for i, (src, dst) in enumerate(zip(fresh_refs, tails))
        ]
        large = [
            pltpu.make_async_copy(src, dst.at[pl.ds(0, cache_rows), :], sems.at[0, i])
            for i, (src, dst) in enumerate(zip(cached_refs, outs))
        ]
        for copy in [ids] + small + large + [rest]:
            copy.start()
        ids.wait()
        blocks = cache_rows // BLK
        first = lax.axis_index("seq") * blocks
        for block in range(blocks):
            hits = jnp.where(ids_ref[...] == first + block, 1.0, 0.0)
            hit = jnp.max(hits, axis=1, keepdims=True)
            gone = jnp.where(hit > 0.0, NEG, 0.0)
            bias_ref[block * BLK : (block + 1) * BLK, :] = jnp.broadcast_to(gone, (BLK, STAT))
        token = lax.broadcasted_iota(jnp.int32, (padded - cache_rows, STAT), 0)
        bias_ref[cache_rows:, :] = jnp.where(token < tok, 0.0, NEG)
        for copy, tail, out in zip(small, tails, outs):
            copy.wait()
            zeros = jnp.zeros((padded - cache_rows - tok, columns), F32)
            rows = jnp.concatenate([tail[...].astype(F32), zeros], axis=0)
            out[cache_rows:, :] = rows.astype(out.dtype)
        for copy in large + [rest]:
            copy.wait()

    in_hbm = pl.BlockSpec(memory_space=pltpu.HBM)
    held = (*cached, *fresh, victims, queries)
    return pl.pallas_call(
        body,
        in_specs=[in_hbm] * len(held) + [pl.BlockSpec(memory_space=pl.ANY)],
        out_specs=[pl.BlockSpec(memory_space=pltpu.VMEM)] * (n + 2),
        out_shape=[jax.ShapeDtypeStruct((padded, columns), BF16)] * n
        + [jax.ShapeDtypeStruct((padded, STAT), F32), jax.ShapeDtypeStruct(queries.shape, BF16)],
        scratch_shapes=[pltpu.VMEM(x.shape, BF16) for x in fresh]
        + [pltpu.VMEM(victims.shape, jnp.int32), pltpu.SemaphoreType.DMA((2, n + 1))],
        compiler_params=pltpu.CompilerParams(vmem_limit_bytes=24 * 1024 * 1024),
        cost_estimate=pl.CostEstimate(
            flops=0, bytes_accessed=4 * n * cache_rows * columns, transcendentals=0
        ),
        name="load",
    )(*[pltpu.with_memory_space_constraint(x, pltpu.HBM) for x in held], after)


def merged(arrays, heads, last):
    columns = heads * HD
    stats = [unpack_stats(get(slice(columns, columns + STAT)), heads) for get in arrays]
    top = functools.reduce(jnp.maximum, [t for t, _ in stats])
    weights = [jnp.exp2(t - top) for t, _ in stats]
    mass = functools.reduce(jnp.add, [w * m for w, (_, m) in zip(weights, stats)])
    if last:
        inverse = 1.0 / jnp.where(lanes(mass.shape[0]) < heads, mass, 1.0)
        weights = [w * inverse for w in weights]
    for head in range(heads):
        cols = slice(head * HD, (head + 1) * HD)
        yield cols, functools.reduce(
            jnp.add, [get(cols) * w[:, head : head + 1] for get, w in zip(arrays, weights)]
        )
    if not last:
        yield slice(columns, columns + STAT), pack_stats(top, mass)


def getter(ref, *index):
    return lambda cols: ref[(*index, slice(None), cols)].astype(F32)


def merge_rows(ins, heads, cuts, rows, after=()):
    width = ins[0].shape[1]

    def body(*refs):
        outs = refs[len(ins) + len(after) :]
        for cols, total in merged([getter(r) for r in refs[: len(ins)]], heads, False):
            for (start, _), out in zip(cuts, outs):
                out[:, cols] = total[start : start + rows].astype(out.dtype)

    shapes = [jax.ShapeDtypeStruct((rows, width), kind) for _, kind in cuts]
    return call_merge(body, ins, shapes, after)


def finish(ins, heads):
    rows = ins[0].shape[0]

    def body(*refs):
        out = refs[len(ins)]
        for cols, total in merged([getter(r) for r in refs[: len(ins)]], heads, True):
            out[:, cols] = total.astype(out.dtype)

    return call_merge(body, ins, [jax.ShapeDtypeStruct((rows, heads * HD), BF16)])[0]


def join(pieces, after=()):
    rows = sum(p.shape[0] for p in pieces)

    def body(*refs):
        out = refs[-1]
        ins = [r[...].astype(F32) for r in refs[: len(pieces)]]
        out[...] = jnp.concatenate(ins, axis=0).astype(out.dtype)

    shape = jax.ShapeDtypeStruct((rows, pieces[0].shape[1]), pieces[0].dtype)
    return call_merge(body, pieces, [shape], after)[0]


def call_merge(body, ins, shapes, after=()):
    size = sum(math.prod(x.shape) for x in ins)
    return pl.pallas_call(
        body,
        in_specs=[pl.BlockSpec(memory_space=pltpu.VMEM)] * len(ins)
        + [pl.BlockSpec(memory_space=pl.ANY)] * len(after),
        out_specs=[pl.BlockSpec(memory_space=pltpu.VMEM)] * len(shapes),
        out_shape=shapes,
        compiler_params=pltpu.CompilerParams(vmem_limit_bytes=48 * 1024 * 1024),
        cost_estimate=pl.CostEstimate(flops=4 * size, bytes_accessed=4 * size, transcendentals=0),
        name="merge",
    )(*ins, *after)


def per_device(queries, new_keys, new_values, cache_keys, cache_values, victims):
    members = lax.axis_size("seq")
    shape = factors(members)
    a_n, b_n, c_n = shape
    heads = queries.shape[1] // HD
    tok = queries.shape[0]

    def fetch(x, *by):
        return lax.ppermute(x, "seq", partner_perm(shape, by, False))

    def give(x, *by):
        return lax.ppermute(x, "seq", partner_perm(shape, by, True))

    far_first = range(a_n - 1, 0, -1)
    line = [queries] + [None] * (a_n - 1)
    for a in far_first:
        line[a] = fetch(queries, a, 0, 0)
    lines = [line] + [[fetch(x, 0, b, 0) for x in line] for b in range(1, b_n)]
    keys, values, bias, line[0] = load(
        (cache_keys, cache_values), (new_keys, new_values), victims[None], queries, line[-1]
    )
    plane = join([x for pieces in lines for x in pieces])
    planes = [plane] + [fetch(plane, 0, 0, c) for c in range(1, c_n)]
    kinds = [F32] * b_n + [BF16] * (b_n * (c_n - 1))
    sums = attend(planes, b_n, kinds, keys, values, bias)

    def over_cores(b, first, kinds, after=()):
        cuts = [(first + j) * tok for j in range(len(kinds))]
        return merge_rows([sums[b]] + back[b], heads, list(zip(cuts, kinds)), tok, after)

    back = [[give(sums[c * b_n + b], 0, 0, c) for c in range(1, c_n)] for b in range(b_n)]
    far = [over_cores(b, 1, [BF16] * (a_n - 1)) for b in range(1, b_n)]
    far = [[give(x, 0, b, 0) for x in pieces[::-1]] for b, pieces in enumerate(far, 1)]
    own = over_cores(0, 0, [F32] * a_n)
    total, last = [], []
    for j, a in enumerate(range(a_n - 1, 0, -1)):
        total += merge_rows([own[a]] + [x[j] for x in far], heads, [(0, BF16)], tok)
        last.append(give(total[-1], a, 0, 0))
    near = [over_cores(b, 0, [BF16], total[:1])[0] for b in range(1, b_n)]
    near = [give(x, 0, b, 0) for b, x in enumerate(near, 1)]
    first = merge_rows([own[0]] + near, heads, [(0, F32)], tok)[0] if near else own[0]
    return finish([first] + last, heads)


def solution(mesh):
    rows = P(("groups", "seq"), None)
    return jax.shard_map(
        per_device,
        mesh=mesh,
        in_specs=(rows, rows, rows, rows, rows, P("groups")),
        out_specs=rows,
        check_vma=False,
    )
```

```python
import functools
import itertools
import math

import jax
import jax.numpy as jnp
from jax import lax
from jax.experimental import pallas as pl
from jax.experimental.pallas import tpu as pltpu
from jax.sharding import PartitionSpec as P

HD = 128
BLK = 128
STAT = 128
LANE = STAT // 3
NEG = -1e30
F32 = jnp.float32
BF16 = jnp.bfloat16


def factors(members):
    cores = 2 if members % 2 == 0 else 1
    chips = members // cores
    far = next(a for a in range(1, chips + 1) if chips % a == 0 and a * a >= chips)
    return far, chips // far, cores


def partner(at, by, size):
    return at ^ by if size & (size - 1) == 0 else (at + by) % size


def partner_perm(shape, by, back):
    def flat(place):
        return functools.reduce(lambda at, kn: at * kn[1] + kn[0], zip(place, shape), 0)

    places = itertools.product(*map(range, shape))
    pairs = [(flat([partner(*x) for x in zip(at, by, shape)]), flat(at)) for at in places]
    return [pair[::-1] for pair in pairs] if back else pairs


def lanes(rows):
    return lax.broadcasted_iota(jnp.int32, (rows, STAT), 1)


def pack_stats(top, mass):
    high = mass.astype(BF16).astype(F32)
    return top + pltpu.roll(high, LANE, 1) + pltpu.roll(mass - high, 2 * LANE, 1)


def unpack_stats(packed, heads):
    used = lanes(packed.shape[0]) < heads
    mass = pltpu.roll(packed, STAT - LANE, 1) + pltpu.roll(packed, STAT - 2 * LANE, 1)
    return jnp.where(used, packed, 0.0), jnp.where(used, mass, 0.0)


def attend_kernel(sizes, scale, bias_ref, q_refs, k_ref, v_ref, outs, top_acc, mass_acc):
    tile, steps, group, pack, lines = sizes
    rows = tile * len(outs)
    line_rows = outs[0].shape[0]
    wide = pack * HD
    contract_last = (((1,), (1,)), ((), ()))
    contract_first = (((0,), (0,)), ((), ()))
    mine = [lax.broadcasted_iota(jnp.int32, (rows, wide), 1) // HD == k for k in range(pack)]

    def row_tile(r, carry):
        at = pl.ds(pl.multiple_of(r * tile, tile), tile)
        in_plane = [pl.ds(pl.multiple_of(b * line_rows + r * tile, tile), tile) for b in range(lines)]
        top_acc[...] = jnp.zeros_like(top_acc)
        mass_acc[...] = jnp.zeros_like(mass_acc)

        def heads_of(step, carry):
            def columns(i):
                return pl.ds(pl.multiple_of((step * group + i) * wide, HD), wide)

            def scores(i):
                cols = columns(i)
                q = jnp.concatenate([ref[rs, cols] for ref in q_refs for rs in in_plane], axis=0)
                if pack > 1:
                    zero = jnp.zeros_like(q)
                    q = jnp.concatenate([jnp.where(m, q, zero) for m in mine], axis=0)
                return lax.dot_general(k_ref[:, cols], q, contract_last, preferred_element_type=F32)

            ahead = scores(0)
            for i in range(group):
                score = ahead
                if i + 1 < group:
                    ahead = scores(i + 1)
                bias = jnp.concatenate([bias_ref[...]] * (pack * rows // STAT), axis=1)
                score = score * scale + bias
                top = jnp.max(score, axis=0, keepdims=True).astype(BF16).astype(F32)
                score = jnp.exp2(score - top)
                mass = jnp.sum(score, axis=0, keepdims=True)
                score = score.astype(BF16)
                for k in range(pack):
                    head = (step * group + i) * pack + k
                    cols = pl.ds(pl.multiple_of(head * HD, HD), HD)
                    part = slice(k * rows, (k + 1) * rows)
                    one = lax.dot_general(
                        score[:, part], v_ref[:, cols], contract_first, preferred_element_type=F32
                    )
                    for p, o_ref in enumerate(outs):
                        o_ref[at, cols] = one[p * tile : (p + 1) * tile].astype(o_ref.dtype)
                    top_acc[pl.ds(head, 1), :] = top[:, part]
                    mass_acc[pl.ds(head, 1), :] = mass[:, part]
            return carry

        lax.fori_loop(0, steps, heads_of, 0)
        packed = pack_stats(top_acc[...].T, mass_acc[...].T)
        for p, o_ref in enumerate(outs):
            width = o_ref.shape[1]
            o_ref[at, width - STAT :] = packed[p * tile : (p + 1) * tile].astype(o_ref.dtype)
        return carry

    lax.fori_loop(0, line_rows // tile, row_tile, 0)


def attend(planes, lines, kinds, keys, values, bias):
    n, m = len(planes), len(kinds)
    rows, columns = planes[0].shape[0] // lines, planes[0].shape[1]
    heads = columns // HD
    pack = 2 if heads % 2 == 0 else 1
    group = next(g for g in (10, 5, 4, 3, 2, 1) if heads % (g * pack) == 0)
    tile = next(t for t in (32, 16, rows) if rows % t == 0)
    width = columns + STAT
    scale = math.log2(math.e) / math.sqrt(HD)

    def body(*refs):
        attend_kernel(
            (tile, heads // (group * pack), group, pack, lines), scale, refs[0], refs[1 : 1 + n],
            *refs[1 + n : 3 + n], refs[3 + n : 3 + n + m], *refs[3 + n + m :],
        )

    return pl.pallas_call(
        body,
        in_specs=[pl.BlockSpec(memory_space=pltpu.VMEM)] * (n + 3),
        out_specs=[pl.BlockSpec(memory_space=pltpu.VMEM)] * m,
        out_shape=[jax.ShapeDtypeStruct((rows, width), kind) for kind in kinds],
        scratch_shapes=[pltpu.VMEM((STAT, tile * m), F32)] * 2,
        compiler_params=pltpu.CompilerParams(vmem_limit_bytes=40 * 1024 * 1024),
        cost_estimate=pl.CostEstimate(
            flops=4 * m * rows * keys.shape[0] * columns,
            bytes_accessed=4 * keys.shape[0] * columns,
            transcendentals=m * rows * keys.shape[0] * heads,
        ),
        name="attend",
    )(bias, *planes, keys, values)


def load(cached, fresh, victims, queries, after):
    cache_rows, columns = cached[0].shape
    tok = fresh[0].shape[0]
    padded = cache_rows + -(-tok // 16) * 16
    n = len(cached)

    def body(*refs):
        cached_refs, fresh_refs, victims_ref, queries_ref = refs[:n], refs[n : 2 * n], *refs[2 * n : 2 * n + 2]
        refs = refs[2 * n + 3 :]
        outs, bias_ref, q_ref, tails, ids_ref, sems = (
            refs[:n], refs[n], refs[n + 1], refs[n + 2 : 2 * n + 2], *refs[2 * n + 2 :]
        )
        ids = pltpu.make_async_copy(victims_ref, ids_ref, sems.at[1, n])
        rest = pltpu.make_async_copy(queries_ref, q_ref, sems.at[0, n])
        small = [
            pltpu.make_async_copy(src, dst, sems.at[1, i])
            for i, (src, dst) in enumerate(zip(fresh_refs, tails))
        ]
        large = [
            pltpu.make_async_copy(src, dst.at[pl.ds(0, cache_rows), :], sems.at[0, i])
            for i, (src, dst) in enumerate(zip(cached_refs, outs))
        ]
        for copy in [ids] + small + large + [rest]:
            copy.start()
        ids.wait()
        blocks = cache_rows // BLK
        first = lax.axis_index("seq") * blocks
        for block in range(blocks):
            hits = jnp.where(ids_ref[...] == first + block, 1.0, 0.0)
            hit = jnp.max(hits, axis=1, keepdims=True)
            gone = jnp.where(hit > 0.0, NEG, 0.0)
            bias_ref[block * BLK : (block + 1) * BLK, :] = jnp.broadcast_to(gone, (BLK, STAT))
        token = lax.broadcasted_iota(jnp.int32, (padded - cache_rows, STAT), 0)
        bias_ref[cache_rows:, :] = jnp.where(token < tok, 0.0, NEG)
        for copy, tail, out in zip(small, tails, outs):
            copy.wait()
            zeros = jnp.zeros((padded - cache_rows - tok, columns), F32)
            rows = jnp.concatenate([tail[...].astype(F32), zeros], axis=0)
            out[cache_rows:, :] = rows.astype(out.dtype)
        for copy in large + [rest]:
            copy.wait()

    in_hbm = pl.BlockSpec(memory_space=pltpu.HBM)
    held = (*cached, *fresh, victims, queries)
    return pl.pallas_call(
        body,
        in_specs=[in_hbm] * len(held) + [pl.BlockSpec(memory_space=pl.ANY)],
        out_specs=[pl.BlockSpec(memory_space=pltpu.VMEM)] * (n + 2),
        out_shape=[jax.ShapeDtypeStruct((padded, columns), BF16)] * n
        + [jax.ShapeDtypeStruct((padded, STAT), F32), jax.ShapeDtypeStruct(queries.shape, BF16)],
        scratch_shapes=[pltpu.VMEM(x.shape, BF16) for x in fresh]
        + [pltpu.VMEM(victims.shape, jnp.int32), pltpu.SemaphoreType.DMA((2, n + 1))],
        compiler_params=pltpu.CompilerParams(vmem_limit_bytes=24 * 1024 * 1024),
        cost_estimate=pl.CostEstimate(
            flops=0, bytes_accessed=4 * n * cache_rows * columns, transcendentals=0
        ),
        name="load",
    )(*[pltpu.with_memory_space_constraint(x, pltpu.HBM) for x in held], after)


def merged(arrays, heads, last):
    columns = heads * HD
    stats = [unpack_stats(get(slice(columns, columns + STAT)), heads) for get in arrays]
    top = functools.reduce(jnp.maximum, [t for t, _ in stats])
    weights = [jnp.exp2(t - top) for t, _ in stats]
    mass = functools.reduce(jnp.add, [w * m for w, (_, m) in zip(weights, stats)])
    if last:
        inverse = 1.0 / jnp.where(lanes(mass.shape[0]) < heads, mass, 1.0)
        weights = [w * inverse for w in weights]
    for head in range(heads):
        cols = slice(head * HD, (head + 1) * HD)
        yield cols, functools.reduce(
            jnp.add, [get(cols) * w[:, head : head + 1] for get, w in zip(arrays, weights)]
        )
    if not last:
        yield slice(columns, columns + STAT), pack_stats(top, mass)


def getter(ref, *index):
    return lambda cols: ref[(*index, slice(None), cols)].astype(F32)


def merge_rows(ins, heads, pieces, kinds):
    rows, width = ins[0].shape
    per = rows // pieces

    def body(*refs):
        outs = refs[len(ins) :]
        for cols, total in merged([getter(r) for r in refs[: len(ins)]], heads, False):
            for j, out in enumerate(outs):
                out[:, cols] = total[j * per : (j + 1) * per].astype(out.dtype)

    return call_merge(body, ins, [jax.ShapeDtypeStruct((per, width), kind) for kind in kinds])


def finish(ins, heads):
    rows = ins[0].shape[0]

    def body(*refs):
        out = refs[len(ins)]
        for cols, total in merged([getter(r) for r in refs[: len(ins)]], heads, True):
            out[:, cols] = total.astype(out.dtype)

    return call_merge(body, ins, [jax.ShapeDtypeStruct((rows, heads * HD), BF16)])[0]


def join(pieces, after=()):
    rows = sum(p.shape[0] for p in pieces)

    def body(*refs):
        out = refs[-1]
        ins = [r[...].astype(F32) for r in refs[: len(pieces)]]
        out[...] = jnp.concatenate(ins, axis=0).astype(out.dtype)

    shape = jax.ShapeDtypeStruct((rows, pieces[0].shape[1]), pieces[0].dtype)
    return call_merge(body, pieces, [shape], after)[0]


def call_merge(body, ins, shapes, after=()):
    size = sum(math.prod(x.shape) for x in ins)
    return pl.pallas_call(
        body,
        in_specs=[pl.BlockSpec(memory_space=pltpu.VMEM)] * len(ins)
        + [pl.BlockSpec(memory_space=pl.ANY)] * len(after),
        out_specs=[pl.BlockSpec(memory_space=pltpu.VMEM)] * len(shapes),
        out_shape=shapes,
        compiler_params=pltpu.CompilerParams(vmem_limit_bytes=48 * 1024 * 1024),
        cost_estimate=pl.CostEstimate(flops=4 * size, bytes_accessed=4 * size, transcendentals=0),
        name="merge",
    )(*ins, *after)


def per_device(queries, new_keys, new_values, cache_keys, cache_values, victims):
    members = lax.axis_size("seq")
    shape = factors(members)
    a_n, b_n, c_n = shape
    heads = queries.shape[1] // HD
    tok = queries.shape[0]

    def fetch(x, *by):
        return lax.ppermute(x, "seq", partner_perm(shape, by, False))

    def give(x, *by):
        return lax.ppermute(x, "seq", partner_perm(shape, by, True))

    far_first = range(a_n - 1, 0, -1)
    line = [queries] + [None] * (a_n - 1)
    for a in far_first:
        line[a] = fetch(queries, a, 0, 0)
    lines = [line] + [[fetch(x, 0, b, 0) for x in line] for b in range(1, b_n)]
    keys, values, bias, line[0] = load(
        (cache_keys, cache_values), (new_keys, new_values), victims[None], queries, line[-1]
    )
    plane = join([x for pieces in lines for x in pieces])
    planes = [plane] + [fetch(plane, 0, 0, c) for c in range(1, c_n)]
    kinds = [F32] * b_n + [BF16] * (b_n * (c_n - 1))
    sums = attend(planes, b_n, kinds, keys, values, bias)

    def over_cores(b, kind):
        got = [give(sums[c * b_n + b], 0, 0, c) for c in range(1, c_n)]
        return merge_rows([sums[b]] + got, heads, a_n, [kind] * a_n)

    got = [[give(x, 0, b, 0) for x in over_cores(b, BF16)] for b in range(1, b_n)]
    own = over_cores(0, F32)
    total = [[own[a]] + [pieces[a] for pieces in got] for a in range(a_n)]
    last = [
        give(merge_rows(total[a], heads, 1, [BF16])[0], a, 0, 0) for a in far_first
    ]
    return finish([*merge_rows(total[0], heads, 1, [F32]), *last], heads)


def solution(mesh):
    rows = P(("groups", "seq"), None)
    return jax.shard_map(
        per_device,
        mesh=mesh,
        in_specs=(rows, rows, rows, rows, rows, P("groups")),
        out_specs=rows,
        check_vma=False,
    )
```

```python
import functools
import itertools
import math

import jax
import jax.numpy as jnp
from jax import lax
from jax.experimental import pallas as pl
from jax.experimental.pallas import tpu as pltpu
from jax.sharding import PartitionSpec as P

HD = 128
BLK = 128
STAT = 128
LANE = STAT // 3
NEG = -1e30
F32 = jnp.float32
BF16 = jnp.bfloat16


def factors(members):
    cores = 2 if members % 2 == 0 else 1
    chips = members // cores
    far = next(a for a in range(1, chips + 1) if chips % a == 0 and a * a >= chips)
    return far, chips // far, cores


def partner(at, by, size):
    return at ^ by if size & (size - 1) == 0 else (at + by) % size


def partner_perm(shape, by, back):
    def flat(place):
        return functools.reduce(lambda at, kn: at * kn[1] + kn[0], zip(place, shape), 0)

    places = itertools.product(*map(range, shape))
    pairs = [(flat([partner(*x) for x in zip(at, by, shape)]), flat(at)) for at in places]
    return [pair[::-1] for pair in pairs] if back else pairs


def lanes(rows):
    return lax.broadcasted_iota(jnp.int32, (rows, STAT), 1)


def pack_stats(top, mass):
    high = mass.astype(BF16).astype(F32)
    return top + pltpu.roll(high, LANE, 1) + pltpu.roll(mass - high, 2 * LANE, 1)


def unpack_stats(packed, heads):
    used = lanes(packed.shape[0]) < heads
    mass = pltpu.roll(packed, STAT - LANE, 1) + pltpu.roll(packed, STAT - 2 * LANE, 1)
    return jnp.where(used, packed, 0.0), jnp.where(used, mass, 0.0)


def attend_kernel(sizes, scale, bias_ref, q_refs, k_ref, v_ref, outs, top_acc, mass_acc):
    tile, steps, group, pack, lines = sizes
    rows = tile * len(outs)
    line_rows = outs[0].shape[0]
    wide = pack * HD
    contract_last = (((1,), (1,)), ((), ()))
    contract_first = (((0,), (0,)), ((), ()))
    mine = [lax.broadcasted_iota(jnp.int32, (rows, wide), 1) // HD == k for k in range(pack)]

    def row_tile(r, carry):
        at = pl.ds(pl.multiple_of(r * tile, tile), tile)
        in_plane = [pl.ds(pl.multiple_of(b * line_rows + r * tile, tile), tile) for b in range(lines)]
        top_acc[...] = jnp.zeros_like(top_acc)
        mass_acc[...] = jnp.zeros_like(mass_acc)

        def heads_of(step, carry):
            def columns(i):
                return pl.ds(pl.multiple_of((step * group + i) * wide, HD), wide)

            def scores(i):
                cols = columns(i)
                q = jnp.concatenate([ref[rs, cols] for ref in q_refs for rs in in_plane], axis=0)
                if pack > 1:
                    zero = jnp.zeros_like(q)
                    q = jnp.concatenate([jnp.where(m, q, zero) for m in mine], axis=0)
                return lax.dot_general(k_ref[:, cols], q, contract_last, preferred_element_type=F32)

            def weigh(i, score):
                bias = jnp.concatenate([bias_ref[...]] * (pack * rows // STAT), axis=1)
                score = score * scale + bias
                top = jnp.max(score, axis=0, keepdims=True).astype(BF16).astype(F32)
                score = jnp.exp2(score - top)
                mass = jnp.sum(score, axis=0, keepdims=True)
                for k in range(pack):
                    head = (step * group + i) * pack + k
                    part = slice(k * rows, (k + 1) * rows)
                    top_acc[pl.ds(head, 1), :] = top[:, part]
                    mass_acc[pl.ds(head, 1), :] = mass[:, part]
                return score.astype(BF16)

            def gather_values(i, weights):
                for k in range(pack):
                    head = (step * group + i) * pack + k
                    cols = pl.ds(pl.multiple_of(head * HD, HD), HD)
                    one = lax.dot_general(
                        weights[:, k * rows : (k + 1) * rows],
                        v_ref[:, cols],
                        contract_first,
                        preferred_element_type=F32,
                    )
                    for p, o_ref in enumerate(outs):
                        o_ref[at, cols] = one[p * tile : (p + 1) * tile].astype(o_ref.dtype)

            ahead = [scores(i) for i in range(min(2, group))]
            weights = None
            for i in range(group):
                if i + 2 < group:
                    ahead.append(scores(i + 2))
                done, weights = weights, weigh(i, ahead[i])
                if i > 0:
                    gather_values(i - 1, done)
            gather_values(group - 1, weights)
            return carry

        lax.fori_loop(0, steps, heads_of, 0)
        packed = pack_stats(top_acc[...].T, mass_acc[...].T)
        for p, o_ref in enumerate(outs):
            width = o_ref.shape[1]
            o_ref[at, width - STAT :] = packed[p * tile : (p + 1) * tile].astype(o_ref.dtype)
        return carry

    lax.fori_loop(0, line_rows // tile, row_tile, 0)


def attend(planes, lines, kinds, keys, values, bias):
    n, m = len(planes), len(kinds)
    rows, columns = planes[0].shape[0] // lines, planes[0].shape[1]
    heads = columns // HD
    pack = 2 if heads % 2 == 0 else 1
    group = next(g for g in (10, 5, 4, 3, 2, 1) if heads % (g * pack) == 0)
    tile = next(t for t in (32, 16, rows) if rows % t == 0)
    width = columns + STAT
    scale = math.log2(math.e) / math.sqrt(HD)

    def body(*refs):
        attend_kernel(
            (tile, heads // (group * pack), group, pack, lines), scale, refs[0], refs[1 : 1 + n],
            *refs[1 + n : 3 + n], refs[3 + n : 3 + n + m], *refs[3 + n + m :],
        )

    return pl.pallas_call(
        body,
        in_specs=[pl.BlockSpec(memory_space=pltpu.VMEM)] * (n + 3),
        out_specs=[pl.BlockSpec(memory_space=pltpu.VMEM)] * m,
        out_shape=[jax.ShapeDtypeStruct((rows, width), kind) for kind in kinds],
        scratch_shapes=[pltpu.VMEM((STAT, tile * m), F32)] * 2,
        compiler_params=pltpu.CompilerParams(vmem_limit_bytes=40 * 1024 * 1024),
        cost_estimate=pl.CostEstimate(
            flops=4 * m * rows * keys.shape[0] * columns,
            bytes_accessed=4 * keys.shape[0] * columns,
            transcendentals=m * rows * keys.shape[0] * heads,
        ),
        name="attend",
    )(bias, *planes, keys, values)


def load(cached, fresh, victims, queries, after):
    cache_rows, columns = cached[0].shape
    tok = fresh[0].shape[0]
    padded = cache_rows + -(-tok // 16) * 16
    n = len(cached)

    def body(*refs):
        cached_refs, fresh_refs, victims_ref, queries_ref = refs[:n], refs[n : 2 * n], *refs[2 * n : 2 * n + 2]
        refs = refs[2 * n + 3 :]
        outs, bias_ref, q_ref, tails, ids_ref, sems = (
            refs[:n], refs[n], refs[n + 1], refs[n + 2 : 2 * n + 2], *refs[2 * n + 2 :]
        )
        ids = pltpu.make_async_copy(victims_ref, ids_ref, sems.at[1, n])
        rest = pltpu.make_async_copy(queries_ref, q_ref, sems.at[0, n])
        small = [
            pltpu.make_async_copy(src, dst, sems.at[1, i])
            for i, (src, dst) in enumerate(zip(fresh_refs, tails))
        ]
        large = [
            pltpu.make_async_copy(src, dst.at[pl.ds(0, cache_rows), :], sems.at[0, i])
            for i, (src, dst) in enumerate(zip(cached_refs, outs))
        ]
        for copy in [ids] + small + large + [rest]:
            copy.start()
        ids.wait()
        blocks = cache_rows // BLK
        first = lax.axis_index("seq") * blocks
        for block in range(blocks):
            hits = jnp.where(ids_ref[...] == first + block, 1.0, 0.0)
            hit = jnp.max(hits, axis=1, keepdims=True)
            gone = jnp.where(hit > 0.0, NEG, 0.0)
            bias_ref[block * BLK : (block + 1) * BLK, :] = jnp.broadcast_to(gone, (BLK, STAT))
        token = lax.broadcasted_iota(jnp.int32, (padded - cache_rows, STAT), 0)
        bias_ref[cache_rows:, :] = jnp.where(token < tok, 0.0, NEG)
        for copy, tail, out in zip(small, tails, outs):
            copy.wait()
            zeros = jnp.zeros((padded - cache_rows - tok, columns), F32)
            rows = jnp.concatenate([tail[...].astype(F32), zeros], axis=0)
            out[cache_rows:, :] = rows.astype(out.dtype)
        for copy in large + [rest]:
            copy.wait()

    in_hbm = pl.BlockSpec(memory_space=pltpu.HBM)
    held = (*cached, *fresh, victims, queries)
    return pl.pallas_call(
        body,
        in_specs=[in_hbm] * len(held) + [pl.BlockSpec(memory_space=pl.ANY)],
        out_specs=[pl.BlockSpec(memory_space=pltpu.VMEM)] * (n + 2),
        out_shape=[jax.ShapeDtypeStruct((padded, columns), BF16)] * n
        + [jax.ShapeDtypeStruct((padded, STAT), F32), jax.ShapeDtypeStruct(queries.shape, BF16)],
        scratch_shapes=[pltpu.VMEM(x.shape, BF16) for x in fresh]
        + [pltpu.VMEM(victims.shape, jnp.int32), pltpu.SemaphoreType.DMA((2, n + 1))],
        compiler_params=pltpu.CompilerParams(vmem_limit_bytes=24 * 1024 * 1024),
        cost_estimate=pl.CostEstimate(
            flops=0, bytes_accessed=4 * n * cache_rows * columns, transcendentals=0
        ),
        name="load",
    )(*[pltpu.with_memory_space_constraint(x, pltpu.HBM) for x in held], after)


def merged(arrays, heads, last):
    columns = heads * HD
    stats = [unpack_stats(get(slice(columns, columns + STAT)), heads) for get in arrays]
    top = functools.reduce(jnp.maximum, [t for t, _ in stats])
    weights = [jnp.exp2(t - top) for t, _ in stats]
    mass = functools.reduce(jnp.add, [w * m for w, (_, m) in zip(weights, stats)])
    if last:
        inverse = 1.0 / jnp.where(lanes(mass.shape[0]) < heads, mass, 1.0)
        weights = [w * inverse for w in weights]
    for head in range(heads):
        cols = slice(head * HD, (head + 1) * HD)
        yield cols, functools.reduce(
            jnp.add, [get(cols) * w[:, head : head + 1] for get, w in zip(arrays, weights)]
        )
    if not last:
        yield slice(columns, columns + STAT), pack_stats(top, mass)


def getter(ref, *index):
    return lambda cols: ref[(*index, slice(None), cols)].astype(F32)


def merge_rows(ins, heads, pieces, kinds):
    rows, width = ins[0].shape
    per = rows // pieces

    def body(*refs):
        outs = refs[len(ins) :]
        for cols, total in merged([getter(r) for r in refs[: len(ins)]], heads, False):
            for j, out in enumerate(outs):
                out[:, cols] = total[j * per : (j + 1) * per].astype(out.dtype)

    return call_merge(body, ins, [jax.ShapeDtypeStruct((per, width), kind) for kind in kinds])


def finish(ins, heads):
    rows = ins[0].shape[0]

    def body(*refs):
        out = refs[len(ins)]
        for cols, total in merged([getter(r) for r in refs[: len(ins)]], heads, True):
            out[:, cols] = total.astype(out.dtype)

    return call_merge(body, ins, [jax.ShapeDtypeStruct((rows, heads * HD), BF16)])[0]


def join(pieces, after=()):
    rows = sum(p.shape[0] for p in pieces)

    def body(*refs):
        out = refs[-1]
        ins = [r[...].astype(F32) for r in refs[: len(pieces)]]
        out[...] = jnp.concatenate(ins, axis=0).astype(out.dtype)

    shape = jax.ShapeDtypeStruct((rows, pieces[0].shape[1]), pieces[0].dtype)
    return call_merge(body, pieces, [shape], after)[0]


def call_merge(body, ins, shapes, after=()):
    size = sum(math.prod(x.shape) for x in ins)
    return pl.pallas_call(
        body,
        in_specs=[pl.BlockSpec(memory_space=pltpu.VMEM)] * len(ins)
        + [pl.BlockSpec(memory_space=pl.ANY)] * len(after),
        out_specs=[pl.BlockSpec(memory_space=pltpu.VMEM)] * len(shapes),
        out_shape=shapes,
        compiler_params=pltpu.CompilerParams(vmem_limit_bytes=48 * 1024 * 1024),
        cost_estimate=pl.CostEstimate(flops=4 * size, bytes_accessed=4 * size, transcendentals=0),
        name="merge",
    )(*ins, *after)


def per_device(queries, new_keys, new_values, cache_keys, cache_values, victims):
    members = lax.axis_size("seq")
    shape = factors(members)
    a_n, b_n, c_n = shape
    heads = queries.shape[1] // HD
    tok = queries.shape[0]

    def fetch(x, *by):
        return lax.ppermute(x, "seq", partner_perm(shape, by, False))

    def give(x, *by):
        return lax.ppermute(x, "seq", partner_perm(shape, by, True))

    far_first = [0, *range(a_n - 1, 0, -1)]
    line = [queries] + [fetch(queries, a, 0, 0) for a in far_first[1:]]
    lines = [line] + [[fetch(x, 0, b, 0) for x in line] for b in range(1, b_n)]
    keys, values, bias, line[0] = load(
        (cache_keys, cache_values), (new_keys, new_values), victims[None], queries, line[min(2, a_n - 1)]
    )
    plane = join([x for pieces in lines for x in pieces])
    planes = [plane] + [fetch(plane, 0, 0, c) for c in range(1, c_n)]
    kinds = [F32] * b_n + [BF16] * (b_n * (c_n - 1))
    sums = attend(planes, b_n, kinds, keys, values, bias)

    def over_cores(b, kind):
        got = [give(sums[c * b_n + b], 0, 0, c) for c in range(1, c_n)]
        return merge_rows([sums[b]] + got, heads, a_n, [kind] * a_n)

    got = [[give(x, 0, b, 0) for x in over_cores(b, BF16)] for b in range(1, b_n)]
    own = over_cores(0, F32)
    total = [[own[s]] + [pieces[s] for pieces in got] for s in range(a_n)]
    last = [
        give(merge_rows(total[s], heads, 1, [BF16])[0], far_first[s], 0, 0) for s in range(1, a_n)
    ]
    return finish([*merge_rows(total[0], heads, 1, [F32]), *last], heads)


def solution(mesh):
    rows = P(("groups", "seq"), None)
    return jax.shard_map(
        per_device,
        mesh=mesh,
        in_specs=(rows, rows, rows, rows, rows, P("groups")),
        out_specs=rows,
        check_vma=False,
    )
```

```python
import functools
import itertools
import math

import jax
import jax.numpy as jnp
from jax import lax
from jax.experimental import pallas as pl
from jax.experimental.pallas import tpu as pltpu
from jax.sharding import PartitionSpec as P

HD = 128
BLK = 128
STAT = 128
LANE = STAT // 3
NEG = -1e30
F32 = jnp.float32
BF16 = jnp.bfloat16


def factors(members):
    cores = 2 if members % 2 == 0 else 1
    chips = members // cores
    far = next(a for a in range(1, chips + 1) if chips % a == 0 and a * a >= chips)
    return far, chips // far, cores


def partner(at, by, size):
    return at ^ by if size & (size - 1) == 0 else (at + by) % size


def partner_perm(shape, by, back):
    def flat(place):
        return functools.reduce(lambda at, kn: at * kn[1] + kn[0], zip(place, shape), 0)

    places = itertools.product(*map(range, shape))
    pairs = [(flat([partner(*x) for x in zip(at, by, shape)]), flat(at)) for at in places]
    return [pair[::-1] for pair in pairs] if back else pairs


def lanes(rows):
    return lax.broadcasted_iota(jnp.int32, (rows, STAT), 1)


def pack_stats(top, mass):
    high = mass.astype(BF16).astype(F32)
    return top + pltpu.roll(high, LANE, 1) + pltpu.roll(mass - high, 2 * LANE, 1)


def unpack_stats(packed, heads):
    used = lanes(packed.shape[0]) < heads
    mass = pltpu.roll(packed, STAT - LANE, 1) + pltpu.roll(packed, STAT - 2 * LANE, 1)
    return jnp.where(used, packed, 0.0), jnp.where(used, mass, 0.0)


def attend_kernel(sizes, scale, bias_ref, q_refs, k_ref, v_ref, outs, top_acc, mass_acc):
    tile, steps, group, pack, lines = sizes
    rows = tile * len(outs)
    line_rows = outs[0].shape[0]
    wide = pack * HD
    contract_last = (((1,), (1,)), ((), ()))
    contract_first = (((0,), (0,)), ((), ()))
    mine = [lax.broadcasted_iota(jnp.int32, (rows, wide), 1) // HD == k for k in range(pack)]

    def row_tile(r, carry):
        at = pl.ds(pl.multiple_of(r * tile, tile), tile)
        in_plane = [pl.ds(pl.multiple_of(b * line_rows + r * tile, tile), tile) for b in range(lines)]
        top_acc[...] = jnp.zeros_like(top_acc)
        mass_acc[...] = jnp.zeros_like(mass_acc)

        def heads_of(step, carry):
            def columns(i):
                return pl.ds(pl.multiple_of((step * group + i) * wide, HD), wide)

            def scores(i):
                cols = columns(i)
                q = jnp.concatenate([ref[rs, cols] for ref in q_refs for rs in in_plane], axis=0)
                if pack > 1:
                    zero = jnp.zeros_like(q)
                    q = jnp.concatenate([jnp.where(m, q, zero) for m in mine], axis=0)
                return lax.dot_general(k_ref[:, cols], q, contract_last, preferred_element_type=F32)

            def weigh(i, score):
                bias = jnp.concatenate([bias_ref[...]] * (pack * rows // STAT), axis=1)
                score = score * scale + bias
                top = jnp.max(score, axis=0, keepdims=True).astype(BF16).astype(F32)
                score = jnp.exp2(score - top)
                mass = jnp.sum(score, axis=0, keepdims=True)
                for k in range(pack):
                    head = (step * group + i) * pack + k
                    part = slice(k * rows, (k + 1) * rows)
                    top_acc[pl.ds(head, 1), :] = top[:, part]
                    mass_acc[pl.ds(head, 1), :] = mass[:, part]
                return score.astype(BF16)

            def gather_values(i, weights):
                for k in range(pack):
                    head = (step * group + i) * pack + k
                    cols = pl.ds(pl.multiple_of(head * HD, HD), HD)
                    one = lax.dot_general(
                        weights[:, k * rows : (k + 1) * rows],
                        v_ref[:, cols],
                        contract_first,
                        preferred_element_type=F32,
                    )
                    for p, o_ref in enumerate(outs):
                        o_ref[at, cols] = one[p * tile : (p + 1) * tile].astype(o_ref.dtype)

            ahead = [scores(i) for i in range(min(2, group))]
            weights = None
            for i in range(group):
                if i + 2 < group:
                    ahead.append(scores(i + 2))
                done, weights = weights, weigh(i, ahead[i])
                if i > 0:
                    gather_values(i - 1, done)
            gather_values(group - 1, weights)
            return carry

        lax.fori_loop(0, steps, heads_of, 0)
        packed = pack_stats(top_acc[...].T, mass_acc[...].T)
        for p, o_ref in enumerate(outs):
            width = o_ref.shape[1]
            o_ref[at, width - STAT :] = packed[p * tile : (p + 1) * tile].astype(o_ref.dtype)
        return carry

    lax.fori_loop(0, line_rows // tile, row_tile, 0)


def attend(planes, lines, kinds, keys, values, bias):
    n, m = len(planes), len(kinds)
    rows, columns = planes[0].shape[0] // lines, planes[0].shape[1]
    heads = columns // HD
    pack = 2 if heads % 2 == 0 else 1
    group = next(g for g in (10, 5, 4, 3, 2, 1) if heads % (g * pack) == 0)
    tile = next(t for t in (32, 16, rows) if rows % t == 0)
    width = columns + STAT
    scale = math.log2(math.e) / math.sqrt(HD)

    def body(*refs):
        attend_kernel(
            (tile, heads // (group * pack), group, pack, lines), scale, refs[0], refs[1 : 1 + n],
            *refs[1 + n : 3 + n], refs[3 + n : 3 + n + m], *refs[3 + n + m :],
        )

    return pl.pallas_call(
        body,
        in_specs=[pl.BlockSpec(memory_space=pltpu.VMEM)] * (n + 3),
        out_specs=[pl.BlockSpec(memory_space=pltpu.VMEM)] * m,
        out_shape=[jax.ShapeDtypeStruct((rows, width), kind) for kind in kinds],
        scratch_shapes=[pltpu.VMEM((STAT, tile * m), F32)] * 2,
        compiler_params=pltpu.CompilerParams(vmem_limit_bytes=40 * 1024 * 1024),
        cost_estimate=pl.CostEstimate(
            flops=4 * m * rows * keys.shape[0] * columns,
            bytes_accessed=4 * keys.shape[0] * columns,
            transcendentals=m * rows * keys.shape[0] * heads,
        ),
        name="attend",
    )(bias, *planes, keys, values)


def load(cached, fresh, after, victims=None, queries=None):
    cache_rows, columns = cached.shape
    tok = fresh.shape[0]
    padded = cache_rows + -(-tok // 16) * 16
    blocks = cache_rows // BLK
    extra = victims is not None

    def body(*refs):
        refs = iter(refs)
        take = lambda n: [next(refs) for _ in range(n)]
        cached_ref, fresh_ref = take(2)
        sides = take(2) if extra else []
        take(1)
        out, = take(1)
        bias_ref, q_ref = take(2) if extra else (None, None)
        tail, sems = take(2)
        large = pltpu.make_async_copy(cached_ref, out.at[pl.ds(0, cache_rows), :], sems.at[0])
        small = pltpu.make_async_copy(fresh_ref, tail, sems.at[1])
        small.start()
        if extra:
            ids_ref, = take(1)
            ids = pltpu.make_async_copy(sides[0], ids_ref, sems.at[2])
            rest = pltpu.make_async_copy(sides[1], q_ref, sems.at[3])
            ids.start()
        large.start()
        if extra:
            rest.start()
            ids.wait()
            first = lax.axis_index("seq") * blocks
            for block in range(blocks):
                hits = jnp.where(ids_ref[...] == first + block, 1.0, 0.0)
                hit = jnp.max(hits, axis=1, keepdims=True)
                gone = jnp.where(hit > 0.0, NEG, 0.0)
                bias_ref[block * BLK : (block + 1) * BLK, :] = jnp.broadcast_to(gone, (BLK, STAT))
            token = lax.broadcasted_iota(jnp.int32, (padded - cache_rows, STAT), 0)
            bias_ref[cache_rows:, :] = jnp.where(token < tok, 0.0, NEG)
        small.wait()
        zeros = jnp.zeros((padded - cache_rows - tok, columns), F32)
        rows = [tail[...].astype(F32)] + ([zeros] if zeros.shape[0] else [])
        out[cache_rows:, :] = jnp.concatenate(rows, axis=0).astype(out.dtype)
        if extra:
            rest.wait()
        large.wait()

    in_hbm = pl.BlockSpec(memory_space=pltpu.HBM)
    held = (cached, fresh) + ((victims, queries) if extra else ())
    shapes = [jax.ShapeDtypeStruct((padded, columns), BF16)]
    scratch = [pltpu.VMEM(fresh.shape, BF16), pltpu.SemaphoreType.DMA((4,))]
    if extra:
        shapes += [jax.ShapeDtypeStruct((padded, STAT), F32), jax.ShapeDtypeStruct(queries.shape, BF16)]
        scratch += [pltpu.VMEM(victims.shape, jnp.int32)]
    return pl.pallas_call(
        body,
        in_specs=[in_hbm] * len(held) + [pl.BlockSpec(memory_space=pl.ANY)],
        out_specs=[pl.BlockSpec(memory_space=pltpu.VMEM)] * len(shapes),
        out_shape=shapes,
        scratch_shapes=scratch,
        compiler_params=pltpu.CompilerParams(vmem_limit_bytes=24 * 1024 * 1024),
        cost_estimate=pl.CostEstimate(
            flops=0, bytes_accessed=4 * cache_rows * columns, transcendentals=0
        ),
        name="load",
    )(*[pltpu.with_memory_space_constraint(x, pltpu.HBM) for x in held], after)


def merged(arrays, heads, last):
    columns = heads * HD
    stats = [unpack_stats(get(slice(columns, columns + STAT)), heads) for get in arrays]
    top = functools.reduce(jnp.maximum, [t for t, _ in stats])
    weights = [jnp.exp2(t - top) for t, _ in stats]
    mass = functools.reduce(jnp.add, [w * m for w, (_, m) in zip(weights, stats)])
    if last:
        inverse = 1.0 / jnp.where(lanes(mass.shape[0]) < heads, mass, 1.0)
        weights = [w * inverse for w in weights]
    for head in range(heads):
        cols = slice(head * HD, (head + 1) * HD)
        yield cols, functools.reduce(
            jnp.add, [get(cols) * w[:, head : head + 1] for get, w in zip(arrays, weights)]
        )
    if not last:
        yield slice(columns, columns + STAT), pack_stats(top, mass)


def getter(ref, *index):
    return lambda cols: ref[(*index, slice(None), cols)].astype(F32)


def merge_rows(ins, heads, pieces, kinds):
    rows, width = ins[0].shape
    per = rows // pieces

    def body(*refs):
        outs = refs[len(ins) :]
        for cols, total in merged([getter(r) for r in refs[: len(ins)]], heads, False):
            for j, out in enumerate(outs):
                out[:, cols] = total[j * per : (j + 1) * per].astype(out.dtype)

    return call_merge(body, ins, [jax.ShapeDtypeStruct((per, width), kind) for kind in kinds])


def finish(ins, heads):
    rows = ins[0].shape[0]

    def body(*refs):
        out = refs[len(ins)]
        for cols, total in merged([getter(r) for r in refs[: len(ins)]], heads, True):
            out[:, cols] = total.astype(out.dtype)

    return call_merge(body, ins, [jax.ShapeDtypeStruct((rows, heads * HD), BF16)])[0]


def join(pieces, after=()):
    rows = sum(p.shape[0] for p in pieces)

    def body(*refs):
        out = refs[-1]
        ins = [r[...].astype(F32) for r in refs[: len(pieces)]]
        out[...] = jnp.concatenate(ins, axis=0).astype(out.dtype)

    shape = jax.ShapeDtypeStruct((rows, pieces[0].shape[1]), pieces[0].dtype)
    return call_merge(body, pieces, [shape], after)[0]


def call_merge(body, ins, shapes, after=()):
    size = sum(math.prod(x.shape) for x in ins)
    return pl.pallas_call(
        body,
        in_specs=[pl.BlockSpec(memory_space=pltpu.VMEM)] * len(ins)
        + [pl.BlockSpec(memory_space=pl.ANY)] * len(after),
        out_specs=[pl.BlockSpec(memory_space=pltpu.VMEM)] * len(shapes),
        out_shape=shapes,
        compiler_params=pltpu.CompilerParams(vmem_limit_bytes=48 * 1024 * 1024),
        cost_estimate=pl.CostEstimate(flops=4 * size, bytes_accessed=4 * size, transcendentals=0),
        name="merge",
    )(*ins, *after)


def per_device(queries, new_keys, new_values, cache_keys, cache_values, victims):
    members = lax.axis_size("seq")
    shape = factors(members)
    a_n, b_n, c_n = shape
    heads = queries.shape[1] // HD
    tok = queries.shape[0]

    def fetch(x, *by):
        return lax.ppermute(x, "seq", partner_perm(shape, by, False))

    def give(x, *by):
        return lax.ppermute(x, "seq", partner_perm(shape, by, True))

    far_first = [0, *range(a_n - 1, 0, -1)]
    staged = max(a_n - 1, 1)
    line = [queries] + [fetch(queries, a, 0, 0) for a in far_first[1:]]
    lines = [line]
    for b in range(1, b_n):
        direct = [fetch(queries, a, b, 0) for a in far_first[staged:]]
        lines.append([fetch(x, 0, b, 0) for x in line[:staged]] + direct)
    keys, bias, line[0] = load(
        cache_keys, new_keys, line[min(2, a_n - 1)], victims[None], queries
    )
    plane = join([x for pieces in lines for x in pieces], (keys,))
    planes = [plane] + [fetch(plane, 0, 0, c) for c in range(1, c_n)]
    values = load(cache_values, new_values, plane)[0]
    kinds = [F32] * b_n + [BF16] * (b_n * (c_n - 1))
    sums = attend(planes, b_n, kinds, keys, values, bias)

    def over_cores(b, kinds):
        got = [give(sums[c * b_n + b], 0, 0, c) for c in range(1, c_n)]
        return merge_rows([sums[b]] + got, heads, a_n, kinds)

    got = [over_cores(b, [BF16] * a_n) for b in range(1, b_n)]
    own = over_cores(0, [F32] * staged + [BF16] * (a_n - staged))
    near = [
        give(pieces[s], far_first[s], b, 0)
        for s in range(staged, a_n)
        for b, pieces in enumerate([own, *got])
    ]
    got = [[give(x, 0, b, 0) for x in pieces[:staged]] for b, pieces in enumerate(got, 1)]
    total = [[own[s]] + [pieces[s] for pieces in got] for s in range(staged)]
    last = [
        give(merge_rows(total[s], heads, 1, [BF16])[0], far_first[s], 0, 0)
        for s in range(1, staged)
    ]
    return finish([*merge_rows(total[0] + near, heads, 1, [F32]), *last], heads)


def solution(mesh):
    rows = P(("groups", "seq"), None)
    return jax.shard_map(
        per_device,
        mesh=mesh,
        in_specs=(rows, rows, rows, rows, rows, P("groups")),
        out_specs=rows,
        check_vma=False,
    )
```

```python
import functools
import itertools
import math

import jax
import jax.numpy as jnp
from jax import lax
from jax.experimental import pallas as pl
from jax.experimental.pallas import tpu as pltpu
from jax.sharding import PartitionSpec as P

HD = 128
BLK = 128
STAT = 128
LANE = STAT // 3
NEG = -1e30
F32 = jnp.float32
BF16 = jnp.bfloat16


def factors(members):
    cores = 2 if members % 2 == 0 else 1
    chips = members // cores
    far = next(a for a in range(1, chips + 1) if chips % a == 0 and a * a >= chips)
    return far, chips // far, cores


def partner(at, by, size):
    return at ^ by if size & (size - 1) == 0 else (at + by) % size


def partner_perm(shape, by, back):
    def flat(place):
        return functools.reduce(lambda at, kn: at * kn[1] + kn[0], zip(place, shape), 0)

    places = itertools.product(*map(range, shape))
    pairs = [(flat([partner(*x) for x in zip(at, by, shape)]), flat(at)) for at in places]
    return [pair[::-1] for pair in pairs] if back else pairs


def lanes(rows):
    return lax.broadcasted_iota(jnp.int32, (rows, STAT), 1)


def pack_stats(top, mass):
    high = mass.astype(BF16).astype(F32)
    return top + pltpu.roll(high, LANE, 1) + pltpu.roll(mass - high, 2 * LANE, 1)


def unpack_stats(packed, heads):
    used = lanes(packed.shape[0]) < heads
    mass = pltpu.roll(packed, STAT - LANE, 1) + pltpu.roll(packed, STAT - 2 * LANE, 1)
    return jnp.where(used, packed, 0.0), jnp.where(used, mass, 0.0)


def attend_kernel(sizes, scale, bias_ref, q_refs, k_ref, v_refs, outs, top_acc, mass_acc):
    tile, steps, group, pack, lines = sizes
    rows = tile * len(outs)
    line_rows = outs[0].shape[0]
    wide = pack * HD
    contract_last = (((1,), (1,)), ((), ()))
    contract_first = (((0,), (0,)), ((), ()))
    mine = [lax.broadcasted_iota(jnp.int32, (rows, wide), 1) // HD == k for k in range(pack)]

    def row_tile(r, carry):
        at = pl.ds(pl.multiple_of(r * tile, tile), tile)
        in_plane = [pl.ds(pl.multiple_of(b * line_rows + r * tile, tile), tile) for b in range(lines)]
        top_acc[...] = jnp.zeros_like(top_acc)
        mass_acc[...] = jnp.zeros_like(mass_acc)

        def heads_of(step, carry):
            def columns(i):
                return pl.ds(pl.multiple_of((step * group + i) * wide, HD), wide)

            def scores(i):
                cols = columns(i)
                q = jnp.concatenate([ref[rs, cols] for ref in q_refs for rs in in_plane], axis=0)
                if pack > 1:
                    zero = jnp.zeros_like(q)
                    q = jnp.concatenate([jnp.where(m, q, zero) for m in mine], axis=0)
                return lax.dot_general(k_ref[:, cols], q, contract_last, preferred_element_type=F32)

            def weigh(i, score):
                bias = jnp.concatenate([bias_ref[...]] * (pack * rows // STAT), axis=1)
                score = score * scale + bias
                top = jnp.max(score, axis=0, keepdims=True).astype(BF16).astype(F32)
                score = jnp.exp2(score - top)
                mass = jnp.sum(score, axis=0, keepdims=True)
                for k in range(pack):
                    head = (step * group + i) * pack + k
                    part = slice(k * rows, (k + 1) * rows)
                    top_acc[pl.ds(head, 1), :] = top[:, part]
                    mass_acc[pl.ds(head, 1), :] = mass[:, part]
                return score.astype(BF16)

            def gather_values(i, weights):
                for k in range(pack):
                    head = (step * group + i) * pack + k
                    cols = pl.ds(pl.multiple_of(head * HD, HD), HD)
                    one, start = 0.0, 0
                    for v_ref in v_refs:
                        part = weights[start : start + v_ref.shape[0], k * rows : (k + 1) * rows]
                        start += v_ref.shape[0]
                        one += lax.dot_general(
                            part, v_ref[:, cols], contract_first, preferred_element_type=F32
                        )
                    for p, o_ref in enumerate(outs):
                        o_ref[at, cols] = one[p * tile : (p + 1) * tile].astype(o_ref.dtype)

            ahead = [scores(i) for i in range(min(2, group))]
            weights = None
            for i in range(group):
                if i + 2 < group:
                    ahead.append(scores(i + 2))
                done, weights = weights, weigh(i, ahead[i])
                if i > 0:
                    gather_values(i - 1, done)
            gather_values(group - 1, weights)
            return carry

        lax.fori_loop(0, steps, heads_of, 0)
        packed = pack_stats(top_acc[...].T, mass_acc[...].T)
        for p, o_ref in enumerate(outs):
            width = o_ref.shape[1]
            o_ref[at, width - STAT :] = packed[p * tile : (p + 1) * tile].astype(o_ref.dtype)
        return carry

    lax.fori_loop(0, line_rows // tile, row_tile, 0)


def attend(planes, lines, kinds, keys, values, bias):
    n, m, v = len(planes), len(kinds), len(values)
    rows, columns = planes[0].shape[0] // lines, planes[0].shape[1]
    heads = columns // HD
    pack = 2 if heads % 2 == 0 else 1
    group = next(g for g in (10, 5, 4, 3, 2, 1) if heads % (g * pack) == 0)
    tile = next(t for t in (32, 16, rows) if rows % t == 0)
    width = columns + STAT
    scale = math.log2(math.e) / math.sqrt(HD)

    def body(*refs):
        attend_kernel(
            (tile, heads // (group * pack), group, pack, lines), scale, refs[0], refs[1 : 1 + n],
            refs[1 + n], refs[2 + n : 2 + n + v], refs[2 + n + v : 2 + n + v + m],
            *refs[2 + n + v + m :],
        )

    return pl.pallas_call(
        body,
        in_specs=[pl.BlockSpec(memory_space=pltpu.VMEM)] * (n + v + 2),
        out_specs=[pl.BlockSpec(memory_space=pltpu.VMEM)] * m,
        out_shape=[jax.ShapeDtypeStruct((rows, width), kind) for kind in kinds],
        scratch_shapes=[pltpu.VMEM((STAT, tile * m), F32)] * 2,
        compiler_params=pltpu.CompilerParams(vmem_limit_bytes=40 * 1024 * 1024),
        cost_estimate=pl.CostEstimate(
            flops=4 * m * rows * keys.shape[0] * columns,
            bytes_accessed=4 * keys.shape[0] * columns,
            transcendentals=m * rows * keys.shape[0] * heads,
        ),
        name="attend",
    )(bias, *planes, keys, *values)


def load(parts, after, victims=None, queries=None):
    shapes, scratch, held, plans = [], [], [], []
    for cached, start, rows, fresh in parts:
        tok = 0 if fresh is None else fresh.shape[0]
        padded = rows + -(-tok // 16) * 16
        columns = cached.shape[1]
        shapes.append(jax.ShapeDtypeStruct((padded, columns), BF16))
        plans.append((start, rows, tok, padded, columns))
        held += [cached] if fresh is None else [cached, fresh]
        scratch += [] if fresh is None else [pltpu.VMEM(fresh.shape, BF16)]
    extra = victims is not None
    if extra:
        held += [victims, queries]
        all_rows = parts[0][0].shape[0]
        tok = queries.shape[0]
        mask_rows = all_rows + -(-tok // 16) * 16
        shapes += [jax.ShapeDtypeStruct((mask_rows, STAT), F32), jax.ShapeDtypeStruct(queries.shape, BF16)]
        scratch += [pltpu.VMEM(victims.shape, jnp.int32)]

    def fill_mask(ids_ref, bias_ref):
        blocks = all_rows // BLK
        first = lax.axis_index("seq") * blocks
        for block in range(blocks):
            hits = jnp.where(ids_ref[...] == first + block, 1.0, 0.0)
            hit = jnp.max(hits, axis=1, keepdims=True)
            gone = jnp.where(hit > 0.0, NEG, 0.0)
            bias_ref[block * BLK : (block + 1) * BLK, :] = jnp.broadcast_to(gone, (BLK, STAT))
        token = lax.broadcasted_iota(jnp.int32, (mask_rows - all_rows, STAT), 0)
        bias_ref[all_rows:, :] = jnp.where(token < tok, 0.0, NEG)

    def body(*refs):
        ins, outs = refs[: len(held)], refs[len(held) + 1 : len(held) + 1 + len(shapes)]
        work, sems = refs[len(held) + 1 + len(shapes) : -1], refs[-1]
        ins, work = iter(ins), iter(work)
        large, small, tails = [], [], []
        for i, ((start, rows, tok_i, _, _), out) in enumerate(zip(plans, outs)):
            src = next(ins).at[pl.ds(start, rows), :]
            large.append(pltpu.make_async_copy(src, out.at[pl.ds(0, rows), :], sems.at[0, i]))
            if tok_i:
                tail = next(work)
                small.append(pltpu.make_async_copy(next(ins), tail, sems.at[1, i]))
                tails.append((tail, out, plans[i]))
        if extra:
            ids_ref = next(work)
            ids = pltpu.make_async_copy(next(ins), ids_ref, sems.at[0, len(plans)])
            rest = pltpu.make_async_copy(next(ins), outs[-1], sems.at[1, len(plans)])
            ids.start()
        for copy in small + large:
            copy.start()
        if extra:
            rest.start()
            ids.wait()
            fill_mask(ids_ref, outs[-2])
        for copy, (tail, out, (_, rows, tok_i, padded, columns)) in zip(small, tails):
            copy.wait()
            filled = tail[...].astype(F32)
            if padded > rows + tok_i:
                zeros = jnp.zeros((padded - rows - tok_i, columns), F32)
                filled = jnp.concatenate([filled, zeros], axis=0)
            out[rows:, :] = filled.astype(out.dtype)
        for copy in large + ([rest] if extra else []):
            copy.wait()

    in_hbm = pl.BlockSpec(memory_space=pltpu.HBM)
    return pl.pallas_call(
        body,
        in_specs=[in_hbm] * len(held) + [pl.BlockSpec(memory_space=pl.ANY)],
        out_specs=[pl.BlockSpec(memory_space=pltpu.VMEM)] * len(shapes),
        out_shape=shapes,
        scratch_shapes=scratch + [pltpu.SemaphoreType.DMA((2, len(plans) + 1))],
        compiler_params=pltpu.CompilerParams(vmem_limit_bytes=24 * 1024 * 1024),
        cost_estimate=pl.CostEstimate(
            flops=0,
            bytes_accessed=4 * sum(math.prod(x.shape) for x in shapes),
            transcendentals=0,
        ),
        name="load",
    )(*[pltpu.with_memory_space_constraint(x, pltpu.HBM) for x in held], after)


def merged(arrays, heads, last):
    columns = heads * HD
    stats = [unpack_stats(get(slice(columns, columns + STAT)), heads) for get in arrays]
    top = functools.reduce(jnp.maximum, [t for t, _ in stats])
    weights = [jnp.exp2(t - top) for t, _ in stats]
    mass = functools.reduce(jnp.add, [w * m for w, (_, m) in zip(weights, stats)])
    if last:
        inverse = 1.0 / jnp.where(lanes(mass.shape[0]) < heads, mass, 1.0)
        weights = [w * inverse for w in weights]
    for head in range(heads):
        cols = slice(head * HD, (head + 1) * HD)
        yield cols, functools.reduce(
            jnp.add, [get(cols) * w[:, head : head + 1] for get, w in zip(arrays, weights)]
        )
    if not last:
        yield slice(columns, columns + STAT), pack_stats(top, mass)


def getter(ref, *index):
    return lambda cols: ref[(*index, slice(None), cols)].astype(F32)


def merge_rows(ins, heads, pieces, kinds):
    rows, width = ins[0].shape
    per = rows // pieces

    def body(*refs):
        outs = refs[len(ins) :]
        for cols, total in merged([getter(r) for r in refs[: len(ins)]], heads, False):
            for j, out in enumerate(outs):
                out[:, cols] = total[j * per : (j + 1) * per].astype(out.dtype)

    return call_merge(body, ins, [jax.ShapeDtypeStruct((per, width), kind) for kind in kinds])


def finish(ins, heads):
    rows = ins[0].shape[0]

    def body(*refs):
        out = refs[len(ins)]
        for cols, total in merged([getter(r) for r in refs[: len(ins)]], heads, True):
            out[:, cols] = total.astype(out.dtype)

    return call_merge(body, ins, [jax.ShapeDtypeStruct((rows, heads * HD), BF16)])[0]


def join(pieces, after=()):
    rows = sum(p.shape[0] for p in pieces)

    def body(*refs):
        out = refs[-1]
        ins = [r[...].astype(F32) for r in refs[: len(pieces)]]
        out[...] = jnp.concatenate(ins, axis=0).astype(out.dtype)

    shape = jax.ShapeDtypeStruct((rows, pieces[0].shape[1]), pieces[0].dtype)
    return call_merge(body, pieces, [shape], after)[0]


def call_merge(body, ins, shapes, after=()):
    size = sum(math.prod(x.shape) for x in ins)
    return pl.pallas_call(
        body,
        in_specs=[pl.BlockSpec(memory_space=pltpu.VMEM)] * len(ins)
        + [pl.BlockSpec(memory_space=pl.ANY)] * len(after),
        out_specs=[pl.BlockSpec(memory_space=pltpu.VMEM)] * len(shapes),
        out_shape=shapes,
        compiler_params=pltpu.CompilerParams(vmem_limit_bytes=48 * 1024 * 1024),
        cost_estimate=pl.CostEstimate(flops=4 * size, bytes_accessed=4 * size, transcendentals=0),
        name="merge",
    )(*ins, *after)


def per_device(queries, new_keys, new_values, cache_keys, cache_values, victims):
    members = lax.axis_size("seq")
    shape = factors(members)
    a_n, b_n, c_n = shape
    heads = queries.shape[1] // HD
    tok = queries.shape[0]

    def fetch(x, *by):
        return lax.ppermute(x, "seq", partner_perm(shape, by, False))

    def give(x, *by):
        return lax.ppermute(x, "seq", partner_perm(shape, by, True))

    line = [queries] + [None] * (a_n - 1)
    for a in range(a_n - 1, 0, -1):
        line[a] = fetch(queries, a, 0, 0)
    lines = [line] + [[fetch(x, 0, b, 0) for x in line] for b in range(1, b_n)]
    cache_rows = cache_keys.shape[0]
    half = cache_rows // 2 if cache_rows % 32 == 0 else cache_rows
    keys, first_values, bias, line[0] = load(
        [(cache_keys, 0, cache_rows, new_keys), (cache_values, 0, half, None)],
        line[-1], victims[None], queries,
    )
    plane = join([x for pieces in lines for x in pieces], (keys,))
    planes = [plane] + [fetch(plane, 0, 0, c) for c in range(1, c_n)]
    last_values = load([(cache_values, half, cache_rows - half, new_values)], plane)[0]
    kinds = [F32] * b_n + [BF16] * (b_n * (c_n - 1))
    sums = attend(planes, b_n, kinds, keys, [first_values, last_values], bias)

    def over_cores(b, kind):
        got = [give(sums[c * b_n + b], 0, 0, c) for c in range(1, c_n)]
        return merge_rows([sums[b]] + got, heads, a_n, [kind] * a_n)

    def total(a, kind, more=()):
        parts = [own[a]] + [pieces[a] for pieces in got] + list(more)
        return merge_rows(parts, heads, 1, [kind])[0]

    got = [over_cores(b, BF16) for b in range(1, b_n)]
    got = [[give(x, 0, b, 0) for x in pieces[::-1]][::-1] for b, pieces in enumerate(got, 1)]
    own = over_cores(0, F32)
    pair = 2 if a_n & (a_n - 1) == 0 and a_n > 2 else 1
    near = {
        f: [give(total(f + n, BF16), n, 0, 0) for n in range(1, pair)]
        for f in range(a_n - pair, -1, -pair)
    }
    far = [give(total(f, BF16, near[f]), f, 0, 0) for f in range(a_n - pair, 0, -pair)]
    return finish([total(0, F32, near[0])] + far, heads)


def solution(mesh):
    rows = P(("groups", "seq"), None)
    return jax.shard_map(
        per_device,
        mesh=mesh,
        in_specs=(rows, rows, rows, rows, rows, P("groups")),
        out_specs=rows,
        check_vma=False,
    )
```

```python
import functools
import itertools
import math

import jax
import jax.numpy as jnp
from jax import lax
from jax.experimental import pallas as pl
from jax.experimental.pallas import tpu as pltpu
from jax.sharding import PartitionSpec as P

HD = 128
BLK = 128
STAT = 128
LANE = STAT // 3
PACK = 2
NEG = -1e30
F32 = jnp.float32
BF16 = jnp.bfloat16


def factors(members):
    cores = 2 if members % 2 == 0 else 1
    chips = members // cores
    far = next(a for a in range(1, chips + 1) if chips % a == 0 and a * a >= chips)
    return far, chips // far, cores


def partner(at, by, size):
    return at ^ by if size & (size - 1) == 0 else (at + by) % size


def partner_perm(shape, by, back):
    def flat(place):
        return functools.reduce(lambda at, kn: at * kn[1] + kn[0], zip(place, shape), 0)

    places = itertools.product(*map(range, shape))
    pairs = [(flat([partner(*x) for x in zip(at, by, shape)]), flat(at)) for at in places]
    return [pair[::-1] for pair in pairs] if back else pairs


def lanes(rows):
    return lax.broadcasted_iota(jnp.int32, (rows, STAT), 1)


def pack_stats(top, mass):
    high = mass.astype(BF16).astype(F32)
    return top + pltpu.roll(high, LANE, 1) + pltpu.roll(mass - high, 2 * LANE, 1)


def unpack_stats(packed):
    used = lanes(packed.shape[0]) < LANE
    mass = pltpu.roll(packed, STAT - LANE, 1) + pltpu.roll(packed, STAT - 2 * LANE, 1)
    return jnp.where(used, packed, 0.0), jnp.where(used, mass, 0.0)


def lane_of(head):
    return head % PACK * (LANE // PACK) + head // PACK


def attend_kernel(sizes, scale, bias_ref, q_ref, k_ref, v_ref, outs, top_acc, mass_acc):
    tile, steps, group = sizes
    lines = len(outs)
    rows = tile * lines
    line_rows = outs[0].shape[0]
    wide = PACK * HD
    contract_last = (((1,), (1,)), ((), ()))
    contract_first = (((0,), (0,)), ((), ()))
    mine = [lax.broadcasted_iota(jnp.int32, (rows, wide), 1) // HD == k for k in range(PACK)]

    def row_tile(r, carry):
        at = pl.ds(pl.multiple_of(r * tile, tile), tile)
        in_plane = [pl.ds(pl.multiple_of(b * line_rows + r * tile, tile), tile) for b in range(lines)]
        top_acc[...] = jnp.zeros_like(top_acc)
        mass_acc[...] = jnp.zeros_like(mass_acc)

        def heads_of(step, carry):
            def columns(i):
                return pl.ds(pl.multiple_of((step * group + i) * wide, HD), wide)

            def scores(i):
                cols = columns(i)
                q = jnp.concatenate([q_ref[rs, cols] for rs in in_plane], axis=0)
                q = jnp.concatenate([jnp.where(m, q, jnp.zeros_like(q)) for m in mine], axis=0)
                return lax.dot_general(k_ref[:, cols], q, contract_last, preferred_element_type=F32)

            def weigh(i, score):
                bias = jnp.concatenate([bias_ref[...]] * (PACK * rows // STAT), axis=1)
                score = score * scale + bias
                top = jnp.max(score, axis=0, keepdims=True).astype(BF16).astype(F32)
                score = jnp.exp2(score - top)
                top_acc[pl.ds(step * group + i, 1), :] = top
                mass_acc[pl.ds(step * group + i, 1), :] = jnp.sum(score, axis=0, keepdims=True)
                return score.astype(BF16)

            def gather_values(i, weights):
                both = lax.dot_general(
                    weights, v_ref[:, columns(i)], contract_first, preferred_element_type=F32
                )
                for k in range(PACK):
                    at_head = ((step * group + i) * PACK + k) * HD
                    cols = pl.ds(pl.multiple_of(at_head, HD), HD)
                    for b, o_ref in enumerate(outs):
                        start = k * rows + b * tile
                        one = both[start : start + tile, k * HD : (k + 1) * HD]
                        o_ref[at, cols] = one.astype(o_ref.dtype)

            ahead = [scores(i) for i in range(min(2, group))]
            weights = None
            for i in range(group):
                if i + 2 < group:
                    ahead.append(scores(i + 2))
                done, weights = weights, weigh(i, ahead[i])
                if i > 0:
                    gather_values(i - 1, done)
            gather_values(group - 1, weights)
            return carry

        lax.fori_loop(0, steps, heads_of, 0)
        tops, masses = top_acc[...].T, mass_acc[...].T
        packed = 0.0
        for k in range(PACK):
            part = slice(k * rows, (k + 1) * rows)
            stats = pack_stats(tops[part], masses[part])
            packed += pltpu.roll(stats, k * (LANE // PACK), 1) if k else stats
        for b, o_ref in enumerate(outs):
            width = o_ref.shape[1]
            o_ref[at, width - STAT :] = packed[b * tile : (b + 1) * tile].astype(o_ref.dtype)
        return carry

    lax.fori_loop(0, line_rows // tile, row_tile, 0)


def attend(plane, lines, kind, keys, values, bias, after=()):
    rows, columns = plane.shape[0] // lines, plane.shape[1]
    heads = columns // HD
    pairs = heads // PACK
    group = next(g for g in (10, 5, 4, 3, 2, 1) if pairs % g == 0)
    tile = next(t for t in (32, 16, rows) if rows % t == 0)
    width = columns + STAT
    scale = math.log2(math.e) / math.sqrt(HD)

    def body(*refs):
        work = refs[4 + len(after) :]
        attend_kernel(
            (tile, pairs // group, group), scale, *refs[:4], work[:lines], *work[lines:]
        )

    return pl.pallas_call(
        body,
        in_specs=[pl.BlockSpec(memory_space=pltpu.VMEM)] * 4
        + [pl.BlockSpec(memory_space=pl.ANY)] * len(after),
        out_specs=[pl.BlockSpec(memory_space=pltpu.VMEM)] * lines,
        out_shape=[jax.ShapeDtypeStruct((rows, width), kind)] * lines,
        scratch_shapes=[pltpu.VMEM((STAT, PACK * tile * lines), F32)] * 2,
        compiler_params=pltpu.CompilerParams(vmem_limit_bytes=40 * 1024 * 1024),
        cost_estimate=pl.CostEstimate(
            flops=4 * lines * rows * keys.shape[0] * columns,
            bytes_accessed=4 * keys.shape[0] * columns,
            transcendentals=lines * rows * keys.shape[0] * heads,
        ),
        name="attend",
    )(bias, plane, keys, values, *after)


def load(cached, fresh, victims, queries, after):
    cache_rows, columns = cached[0].shape
    tok = fresh[0].shape[0]
    padded = cache_rows + -(-tok // 16) * 16
    n = len(cached)

    def body(*refs):
        cached_refs, fresh_refs, victims_ref, queries_ref = refs[:n], refs[n : 2 * n], *refs[2 * n : 2 * n + 2]
        refs = refs[2 * n + 3 :]
        outs, bias_ref, q_ref, tails, ids_ref, sems = (
            refs[:n], refs[n], refs[n + 1], refs[n + 2 : 2 * n + 2], *refs[2 * n + 2 :]
        )
        ids = pltpu.make_async_copy(victims_ref, ids_ref, sems.at[1, n])
        rest = pltpu.make_async_copy(queries_ref, q_ref, sems.at[0, n])
        small = [
            pltpu.make_async_copy(src, dst, sems.at[1, i])
            for i, (src, dst) in enumerate(zip(fresh_refs, tails))
        ]
        large = [
            pltpu.make_async_copy(src, dst.at[pl.ds(0, cache_rows), :], sems.at[0, i])
            for i, (src, dst) in enumerate(zip(cached_refs, outs))
        ]
        for copy in [ids] + small + large + [rest]:
            copy.start()
        ids.wait()
        blocks = cache_rows // BLK
        first = lax.axis_index("seq") * blocks
        for block in range(blocks):
            hits = jnp.where(ids_ref[...] == first + block, 1.0, 0.0)
            hit = jnp.max(hits, axis=1, keepdims=True)
            gone = jnp.where(hit > 0.0, NEG, 0.0)
            bias_ref[block * BLK : (block + 1) * BLK, :] = jnp.broadcast_to(gone, (BLK, STAT))
        token = lax.broadcasted_iota(jnp.int32, (padded - cache_rows, STAT), 0)
        bias_ref[cache_rows:, :] = jnp.where(token < tok, 0.0, NEG)
        for copy, tail, out in zip(small, tails, outs):
            copy.wait()
            zeros = jnp.zeros((padded - cache_rows - tok, columns), F32)
            rows = jnp.concatenate([tail[...].astype(F32), zeros], axis=0)
            out[cache_rows:, :] = rows.astype(out.dtype)
        for copy in large + [rest]:
            copy.wait()

    in_hbm = pl.BlockSpec(memory_space=pltpu.HBM)
    held = (*cached, *fresh, victims, queries)
    return pl.pallas_call(
        body,
        in_specs=[in_hbm] * len(held) + [pl.BlockSpec(memory_space=pl.ANY)],
        out_specs=[pl.BlockSpec(memory_space=pltpu.VMEM)] * (n + 2),
        out_shape=[jax.ShapeDtypeStruct((padded, columns), BF16)] * n
        + [jax.ShapeDtypeStruct((padded, STAT), F32), jax.ShapeDtypeStruct(queries.shape, BF16)],
        scratch_shapes=[pltpu.VMEM(x.shape, BF16) for x in fresh]
        + [pltpu.VMEM(victims.shape, jnp.int32), pltpu.SemaphoreType.DMA((2, n + 1))],
        compiler_params=pltpu.CompilerParams(vmem_limit_bytes=24 * 1024 * 1024),
        cost_estimate=pl.CostEstimate(
            flops=0, bytes_accessed=4 * n * cache_rows * columns, transcendentals=0
        ),
        name="load",
    )(*[pltpu.with_memory_space_constraint(x, pltpu.HBM) for x in held], after)


def merged(arrays, heads, last):
    columns = heads * HD
    stats = [unpack_stats(get(slice(columns, columns + STAT))) for get in arrays]
    top = functools.reduce(jnp.maximum, [t for t, _ in stats])
    weights = [jnp.exp2(t - top) for t, _ in stats]
    mass = functools.reduce(jnp.add, [w * m for w, (_, m) in zip(weights, stats)])
    if last:
        inverse = 1.0 / jnp.where(mass > 0.0, mass, 1.0)
        weights = [w * inverse for w in weights]
    for head in range(heads):
        cols = slice(head * HD, (head + 1) * HD)
        yield cols, functools.reduce(
            jnp.add, [get(cols) * w[:, lane_of(head) : lane_of(head) + 1] for get, w in zip(arrays, weights)]
        )
    if not last:
        yield slice(columns, columns + STAT), pack_stats(top, mass)


def getter(ref, *index):
    return lambda cols: ref[(*index, slice(None), cols)].astype(F32)


def merge_rows(ins, heads, pieces, kinds):
    rows, width = ins[0].shape
    per = rows // pieces

    def body(*refs):
        outs = refs[len(ins) :]
        for cols, total in merged([getter(r) for r in refs[: len(ins)]], heads, False):
            for j, out in enumerate(outs):
                out[:, cols] = total[j * per : (j + 1) * per].astype(out.dtype)

    return call_merge(body, ins, [jax.ShapeDtypeStruct((per, width), kind) for kind in kinds])


def finish(ins, heads):
    rows = ins[0].shape[0]

    def body(*refs):
        out = refs[len(ins)]
        for cols, total in merged([getter(r) for r in refs[: len(ins)]], heads, True):
            out[:, cols] = total.astype(out.dtype)

    return call_merge(body, ins, [jax.ShapeDtypeStruct((rows, heads * HD), BF16)])[0]


def join(pieces, after=()):
    rows = sum(p.shape[0] for p in pieces)

    def body(*refs):
        out = refs[-1]
        ins = [r[...].astype(F32) for r in refs[: len(pieces)]]
        out[...] = jnp.concatenate(ins, axis=0).astype(out.dtype)

    shape = jax.ShapeDtypeStruct((rows, pieces[0].shape[1]), pieces[0].dtype)
    return call_merge(body, pieces, [shape], after)[0]


def call_merge(body, ins, shapes, after=()):
    size = sum(math.prod(x.shape) for x in ins)
    return pl.pallas_call(
        body,
        in_specs=[pl.BlockSpec(memory_space=pltpu.VMEM)] * len(ins)
        + [pl.BlockSpec(memory_space=pl.ANY)] * len(after),
        out_specs=[pl.BlockSpec(memory_space=pltpu.VMEM)] * len(shapes),
        out_shape=shapes,
        compiler_params=pltpu.CompilerParams(vmem_limit_bytes=48 * 1024 * 1024),
        cost_estimate=pl.CostEstimate(flops=4 * size, bytes_accessed=4 * size, transcendentals=0),
        name="merge",
    )(*ins, *after)


def per_device(queries, new_keys, new_values, cache_keys, cache_values, victims):
    members = lax.axis_size("seq")
    shape = factors(members)
    a_n, b_n, c_n = shape
    heads = queries.shape[1] // HD
    tok = queries.shape[0]

    def fetch(x, *by):
        return lax.ppermute(x, "seq", partner_perm(shape, by, False))

    def give(x, *by):
        return lax.ppermute(x, "seq", partner_perm(shape, by, True))

    line = [queries] + [None] * (a_n - 1)
    for a in range(a_n - 1, 0, -1):
        line[a] = fetch(queries, a, 0, 0)
    lines = [line] + [[fetch(x, 0, b, 0) for x in line] for b in range(1, b_n)]
    keys, values, bias, line[0] = load(
        (cache_keys, cache_values), (new_keys, new_values), victims[None], queries, line[-1]
    )
    plane = join([x for pieces in lines for x in pieces])
    planes = [plane] + [fetch(plane, 0, 0, c) for c in range(1, c_n)]
    sums = []
    for c, rows in enumerate(planes):
        sums += attend(rows, b_n, BF16 if c else F32, keys, values, bias, sums[:1])

    def over_cores(b, kind):
        got = [give(sums[c * b_n + b], 0, 0, c) for c in range(1, c_n)]
        return merge_rows([sums[b]] + got, heads, a_n, [kind] * a_n)

    got = [[give(x, 0, b, 0) for x in over_cores(b, BF16)] for b in range(1, b_n)]
    own = over_cores(0, F32)
    total = [[own[a]] + [pieces[a] for pieces in got] for a in range(a_n)]
    last = [
        give(merge_rows(total[a], heads, 1, [BF16])[0], a, 0, 0) for a in range(a_n - 1, 0, -1)
    ]
    return finish([*merge_rows(total[0], heads, 1, [F32]), *last], heads)


def solution(mesh):
    rows = P(("groups", "seq"), None)
    return jax.shard_map(
        per_device,
        mesh=mesh,
        in_specs=(rows, rows, rows, rows, rows, P("groups")),
        out_specs=rows,
        check_vma=False,
    )
```

```python
import functools
import itertools
import math

import jax
import jax.numpy as jnp
from jax import lax
from jax.experimental import pallas as pl
from jax.experimental.pallas import tpu as pltpu
from jax.sharding import PartitionSpec as P

HD = 128
BLK = 128
STAT = 128
LANE = STAT // 3
PACK = 2
NEG = -1e30
F32 = jnp.float32
BF16 = jnp.bfloat16


def factors(members):
    cores = 2 if members % 2 == 0 else 1
    chips = members // cores
    far = next(a for a in range(1, chips + 1) if chips % a == 0 and a * a >= chips)
    return far, chips // far, cores


def partner(at, by, size):
    return at ^ by if size & (size - 1) == 0 else (at + by) % size


def partner_perm(shape, by, back):
    def flat(place):
        return functools.reduce(lambda at, kn: at * kn[1] + kn[0], zip(place, shape), 0)

    places = itertools.product(*map(range, shape))
    pairs = [(flat([partner(*x) for x in zip(at, by, shape)]), flat(at)) for at in places]
    return [pair[::-1] for pair in pairs] if back else pairs


def lanes(rows):
    return lax.broadcasted_iota(jnp.int32, (rows, STAT), 1)


def pack_stats(top, mass):
    high = mass.astype(BF16).astype(F32)
    return top + pltpu.roll(high, LANE, 1) + pltpu.roll(mass - high, 2 * LANE, 1)


def unpack_stats(packed):
    used = lanes(packed.shape[0]) < LANE
    mass = pltpu.roll(packed, STAT - LANE, 1) + pltpu.roll(packed, STAT - 2 * LANE, 1)
    return jnp.where(used, packed, 0.0), jnp.where(used, mass, 0.0)


def lane_of(head):
    return head % PACK * (LANE // PACK) + head // PACK


def attend_kernel(sizes, scale, bias_ref, q_ref, k_ref, v_ref, outs, top_acc, mass_acc):
    tile, steps, group = sizes
    lines = len(outs)
    rows = tile * lines
    line_rows = outs[0].shape[0]
    wide = PACK * HD
    contract_last = (((1,), (1,)), ((), ()))
    contract_first = (((0,), (0,)), ((), ()))
    mine = [lax.broadcasted_iota(jnp.int32, (rows, wide), 1) // HD == k for k in range(PACK)]

    def row_tile(r, carry):
        at = pl.ds(pl.multiple_of(r * tile, tile), tile)
        in_plane = [pl.ds(pl.multiple_of(b * line_rows + r * tile, tile), tile) for b in range(lines)]
        top_acc[...] = jnp.zeros_like(top_acc)
        mass_acc[...] = jnp.zeros_like(mass_acc)

        def heads_of(step, carry):
            def columns(i):
                return pl.ds(pl.multiple_of((step * group + i) * wide, HD), wide)

            def scores(i):
                cols = columns(i)
                q = jnp.concatenate([q_ref[rs, cols] for rs in in_plane], axis=0)
                q = jnp.concatenate([jnp.where(m, q, jnp.zeros_like(q)) for m in mine], axis=0)
                return lax.dot_general(k_ref[:, cols], q, contract_last, preferred_element_type=F32)

            def weigh(i, score):
                bias = jnp.concatenate([bias_ref[...]] * (PACK * rows // STAT), axis=1)
                score = score * scale + bias
                top = jnp.max(score, axis=0, keepdims=True).astype(BF16).astype(F32)
                score = jnp.exp2(score - top)
                top_acc[pl.ds(step * group + i, 1), :] = top
                mass_acc[pl.ds(step * group + i, 1), :] = jnp.sum(score, axis=0, keepdims=True)
                return score.astype(BF16)

            def gather_values(i, weights):
                both = lax.dot_general(
                    weights, v_ref[:, columns(i)], contract_first, preferred_element_type=F32
                )
                for k in range(PACK):
                    at_head = ((step * group + i) * PACK + k) * HD
                    cols = pl.ds(pl.multiple_of(at_head, HD), HD)
                    for b, o_ref in enumerate(outs):
                        start = k * rows + b * tile
                        one = both[start : start + tile, k * HD : (k + 1) * HD]
                        o_ref[at, cols] = one.astype(o_ref.dtype)

            ahead = [scores(i) for i in range(min(2, group))]
            weights = None
            for i in range(group):
                if i + 2 < group:
                    ahead.append(scores(i + 2))
                done, weights = weights, weigh(i, ahead[i])
                if i > 0:
                    gather_values(i - 1, done)
            gather_values(group - 1, weights)
            return carry

        lax.fori_loop(0, steps, heads_of, 0)
        tops, masses = top_acc[...].T, mass_acc[...].T
        packed = 0.0
        for k in range(PACK):
            part = slice(k * rows, (k + 1) * rows)
            stats = pack_stats(tops[part], masses[part])
            packed += pltpu.roll(stats, k * (LANE // PACK), 1) if k else stats
        for b, o_ref in enumerate(outs):
            width = o_ref.shape[1]
            o_ref[at, width - STAT :] = packed[b * tile : (b + 1) * tile].astype(o_ref.dtype)
        return carry

    lax.fori_loop(0, line_rows // tile, row_tile, 0)


def attend(plane, lines, kind, keys, values, bias, after=()):
    rows, columns = plane.shape[0] // lines, plane.shape[1]
    heads = columns // HD
    pairs = heads // PACK
    group = next(g for g in (10, 5, 4, 3, 2, 1) if pairs % g == 0)
    tile = next(t for t in (32, 16, rows) if rows % t == 0)
    width = columns + STAT
    scale = math.log2(math.e) / math.sqrt(HD)

    def body(*refs):
        work = refs[4 + len(after) :]
        attend_kernel(
            (tile, pairs // group, group), scale, *refs[:4], work[:lines], *work[lines:]
        )

    return pl.pallas_call(
        body,
        in_specs=[pl.BlockSpec(memory_space=pltpu.VMEM)] * 4
        + [pl.BlockSpec(memory_space=pl.ANY)] * len(after),
        out_specs=[pl.BlockSpec(memory_space=pltpu.VMEM)] * lines,
        out_shape=[jax.ShapeDtypeStruct((rows, width), kind)] * lines,
        scratch_shapes=[pltpu.VMEM((STAT, PACK * tile * lines), F32)] * 2,
        compiler_params=pltpu.CompilerParams(vmem_limit_bytes=40 * 1024 * 1024),
        cost_estimate=pl.CostEstimate(
            flops=4 * lines * rows * keys.shape[0] * columns,
            bytes_accessed=4 * keys.shape[0] * columns,
            transcendentals=lines * rows * keys.shape[0] * heads,
        ),
        name="attend",
    )(bias, plane, keys, values, *after)


def load(cached, fresh, victims, queries, after):
    cache_rows, columns = cached[0].shape
    tok = fresh[0].shape[0]
    padded = cache_rows + -(-tok // 16) * 16
    n = len(cached)

    def body(*refs):
        cached_refs, fresh_refs, victims_ref, queries_ref = refs[:n], refs[n : 2 * n], *refs[2 * n : 2 * n + 2]
        refs = refs[2 * n + 3 :]
        outs, bias_ref, q_ref, tails, ids_ref, sems = (
            refs[:n], refs[n], refs[n + 1], refs[n + 2 : 2 * n + 2], *refs[2 * n + 2 :]
        )
        ids = pltpu.make_async_copy(victims_ref, ids_ref, sems.at[1, n])
        rest = pltpu.make_async_copy(queries_ref, q_ref, sems.at[0, n])
        small = [
            pltpu.make_async_copy(src, dst, sems.at[1, i])
            for i, (src, dst) in enumerate(zip(fresh_refs, tails))
        ]
        large = [
            pltpu.make_async_copy(src, dst.at[pl.ds(0, cache_rows), :], sems.at[0, i])
            for i, (src, dst) in enumerate(zip(cached_refs, outs))
        ]
        for copy in [ids] + small + large + [rest]:
            copy.start()
        ids.wait()
        blocks = cache_rows // BLK
        first = lax.axis_index("seq") * blocks
        for block in range(blocks):
            hits = jnp.where(ids_ref[...] == first + block, 1.0, 0.0)
            hit = jnp.max(hits, axis=1, keepdims=True)
            gone = jnp.where(hit > 0.0, NEG, 0.0)
            bias_ref[block * BLK : (block + 1) * BLK, :] = jnp.broadcast_to(gone, (BLK, STAT))
        token = lax.broadcasted_iota(jnp.int32, (padded - cache_rows, STAT), 0)
        bias_ref[cache_rows:, :] = jnp.where(token < tok, 0.0, NEG)
        for copy, tail, out in zip(small, tails, outs):
            copy.wait()
            zeros = jnp.zeros((padded - cache_rows - tok, columns), F32)
            rows = jnp.concatenate([tail[...].astype(F32), zeros], axis=0)
            out[cache_rows:, :] = rows.astype(out.dtype)
        for copy in large + [rest]:
            copy.wait()

    in_hbm = pl.BlockSpec(memory_space=pltpu.HBM)
    held = (*cached, *fresh, victims, queries)
    return pl.pallas_call(
        body,
        in_specs=[in_hbm] * len(held) + [pl.BlockSpec(memory_space=pl.ANY)],
        out_specs=[pl.BlockSpec(memory_space=pltpu.VMEM)] * (n + 2),
        out_shape=[jax.ShapeDtypeStruct((padded, columns), BF16)] * n
        + [jax.ShapeDtypeStruct((padded, STAT), F32), jax.ShapeDtypeStruct(queries.shape, BF16)],
        scratch_shapes=[pltpu.VMEM(x.shape, BF16) for x in fresh]
        + [pltpu.VMEM(victims.shape, jnp.int32), pltpu.SemaphoreType.DMA((2, n + 1))],
        compiler_params=pltpu.CompilerParams(vmem_limit_bytes=24 * 1024 * 1024),
        cost_estimate=pl.CostEstimate(
            flops=0, bytes_accessed=4 * n * cache_rows * columns, transcendentals=0
        ),
        name="load",
    )(*[pltpu.with_memory_space_constraint(x, pltpu.HBM) for x in held], after)


def merged(arrays, heads, last):
    columns = heads * HD
    stats = [unpack_stats(get(slice(columns, columns + STAT))) for get in arrays]
    top = functools.reduce(jnp.maximum, [t for t, _ in stats])
    weights = [jnp.exp2(t - top) for t, _ in stats]
    mass = functools.reduce(jnp.add, [w * m for w, (_, m) in zip(weights, stats)])
    if last:
        inverse = 1.0 / jnp.where(mass > 0.0, mass, 1.0)
        weights = [w * inverse for w in weights]
    for head in range(heads):
        cols = slice(head * HD, (head + 1) * HD)
        yield cols, functools.reduce(
            jnp.add, [get(cols) * w[:, lane_of(head) : lane_of(head) + 1] for get, w in zip(arrays, weights)]
        )
    if not last:
        yield slice(columns, columns + STAT), pack_stats(top, mass)


def getter(ref, *index):
    return lambda cols: ref[(*index, slice(None), cols)].astype(F32)


def merge_rows(ins, heads, pieces, kinds):
    rows, width = ins[0].shape
    per = rows // pieces

    def body(*refs):
        outs = refs[len(ins) :]
        for cols, total in merged([getter(r) for r in refs[: len(ins)]], heads, False):
            for j, out in enumerate(outs):
                out[:, cols] = total[j * per : (j + 1) * per].astype(out.dtype)

    return call_merge(body, ins, [jax.ShapeDtypeStruct((per, width), kind) for kind in kinds])


def finish(ins, heads):
    rows = ins[0].shape[0]

    def body(*refs):
        out = refs[len(ins)]
        for cols, total in merged([getter(r) for r in refs[: len(ins)]], heads, True):
            out[:, cols] = total.astype(out.dtype)

    return call_merge(body, ins, [jax.ShapeDtypeStruct((rows, heads * HD), BF16)])[0]


def join(pieces, after=()):
    rows = sum(p.shape[0] for p in pieces)

    def body(*refs):
        out = refs[-1]
        ins = [r[...].astype(F32) for r in refs[: len(pieces)]]
        out[...] = jnp.concatenate(ins, axis=0).astype(out.dtype)

    shape = jax.ShapeDtypeStruct((rows, pieces[0].shape[1]), pieces[0].dtype)
    return call_merge(body, pieces, [shape], after)[0]


def call_merge(body, ins, shapes, after=()):
    size = sum(math.prod(x.shape) for x in ins)
    return pl.pallas_call(
        body,
        in_specs=[pl.BlockSpec(memory_space=pltpu.VMEM)] * len(ins)
        + [pl.BlockSpec(memory_space=pl.ANY)] * len(after),
        out_specs=[pl.BlockSpec(memory_space=pltpu.VMEM)] * len(shapes),
        out_shape=shapes,
        compiler_params=pltpu.CompilerParams(vmem_limit_bytes=48 * 1024 * 1024),
        cost_estimate=pl.CostEstimate(flops=4 * size, bytes_accessed=4 * size, transcendentals=0),
        name="merge",
    )(*ins, *after)


def per_device(queries, new_keys, new_values, cache_keys, cache_values, victims):
    members = lax.axis_size("seq")
    shape = factors(members)
    a_n, b_n, c_n = shape
    heads = queries.shape[1] // HD
    tok = queries.shape[0]

    def fetch(x, *by):
        return lax.ppermute(x, "seq", partner_perm(shape, by, False))

    def give(x, *by):
        return lax.ppermute(x, "seq", partner_perm(shape, by, True))

    far_first = [0, *range(a_n - 1, 0, -1)]
    line = [queries] + [fetch(queries, a, 0, 0) for a in far_first[1:]]
    lines = [line] + [[fetch(x, 0, b, 0) for x in line] for b in range(1, b_n)]
    keys, values, bias, line[0] = load(
        (cache_keys, cache_values), (new_keys, new_values), victims[None], queries, line[-1]
    )
    plane = join([x for pieces in lines for x in pieces])
    planes = [plane] + [fetch(plane, 0, 0, c) for c in range(1, c_n)]
    sums = []
    for c, rows in enumerate(planes):
        sums += attend(rows, b_n, BF16 if c else F32, keys, values, bias, sums[:1])

    def over_cores(b, kind):
        got = [give(sums[c * b_n + b], 0, 0, c) for c in range(1, c_n)]
        return merge_rows([sums[b]] + got, heads, a_n, [kind] * a_n)

    got = [[give(x, 0, b, 0) for x in over_cores(b, BF16)] for b in range(1, b_n)]
    own = over_cores(0, F32)
    total = [[own[s]] + [pieces[s] for pieces in got] for s in range(a_n)]
    last = [
        give(merge_rows(total[s], heads, 1, [BF16])[0], far_first[s], 0, 0) for s in range(1, a_n)
    ]
    return finish([*merge_rows(total[0], heads, 1, [F32]), *last], heads)


def solution(mesh):
    rows = P(("groups", "seq"), None)
    return jax.shard_map(
        per_device,
        mesh=mesh,
        in_specs=(rows, rows, rows, rows, rows, P("groups")),
        out_specs=rows,
        check_vma=False,
    )
```

```python
import functools
import itertools
import math

import jax
import jax.numpy as jnp
from jax import lax
from jax.experimental import pallas as pl
from jax.experimental.pallas import tpu as pltpu
from jax.sharding import PartitionSpec as P

HD = 128
BLK = 128
STAT = 128
LANE = STAT // 3
PACK = 2
NEG = -1e30
F32 = jnp.float32
BF16 = jnp.bfloat16


def factors(members):
    cores = 2 if members % 2 == 0 else 1
    chips = members // cores
    far = next(a for a in range(1, chips + 1) if chips % a == 0 and a * a >= chips)
    return far, chips // far, cores


def partner(at, by, size):
    return at ^ by if size & (size - 1) == 0 else (at + by) % size


def partner_perm(shape, by, back):
    def flat(place):
        return functools.reduce(lambda at, kn: at * kn[1] + kn[0], zip(place, shape), 0)

    places = itertools.product(*map(range, shape))
    pairs = [(flat([partner(*x) for x in zip(at, by, shape)]), flat(at)) for at in places]
    return [pair[::-1] for pair in pairs] if back else pairs


def lanes(rows):
    return lax.broadcasted_iota(jnp.int32, (rows, STAT), 1)


def pack_stats(top, mass):
    high = mass.astype(BF16).astype(F32)
    return top + pltpu.roll(high, LANE, 1) + pltpu.roll(mass - high, 2 * LANE, 1)


def unpack_stats(packed):
    used = lanes(packed.shape[0]) < LANE
    mass = pltpu.roll(packed, STAT - LANE, 1) + pltpu.roll(packed, STAT - 2 * LANE, 1)
    return jnp.where(used, packed, 0.0), jnp.where(used, mass, 0.0)


def lane_of(head):
    return head % PACK * (LANE // PACK) + head // PACK


def attend_kernel(sizes, scale, bias_ref, q_ref, k_ref, v_ref, outs, top_acc, mass_acc):
    tile, steps, group = sizes
    lines = len(outs)
    rows = tile * lines
    line_rows = outs[0].shape[0]
    wide = PACK * HD
    contract_last = (((1,), (1,)), ((), ()))
    contract_first = (((0,), (0,)), ((), ()))
    mine = [lax.broadcasted_iota(jnp.int32, (rows, wide), 1) // HD == k for k in range(PACK)]

    def row_tile(r, carry):
        at = pl.ds(pl.multiple_of(r * tile, tile), tile)
        in_plane = [pl.ds(pl.multiple_of(b * line_rows + r * tile, tile), tile) for b in range(lines)]
        top_acc[...] = jnp.zeros_like(top_acc)
        mass_acc[...] = jnp.zeros_like(mass_acc)

        def heads_of(step, carry):
            def columns(i):
                return pl.ds(pl.multiple_of((step * group + i) * wide, HD), wide)

            def scores(i):
                cols = columns(i)
                q = jnp.concatenate([q_ref[rs, cols] for rs in in_plane], axis=0)
                q = jnp.concatenate([jnp.where(m, q, jnp.zeros_like(q)) for m in mine], axis=0)
                return lax.dot_general(k_ref[:, cols], q, contract_last, preferred_element_type=F32)

            def weigh(i, score):
                bias = jnp.concatenate([bias_ref[...]] * (PACK * rows // STAT), axis=1)
                score = score * scale + bias
                top = jnp.max(score, axis=0, keepdims=True).astype(BF16).astype(F32)
                score = jnp.exp2(score - top)
                top_acc[pl.ds(step * group + i, 1), :] = top
                mass_acc[pl.ds(step * group + i, 1), :] = jnp.sum(score, axis=0, keepdims=True)
                return score.astype(BF16)

            def gather_values(i, weights):
                both = lax.dot_general(
                    weights, v_ref[:, columns(i)], contract_first, preferred_element_type=F32
                )
                for k in range(PACK):
                    at_head = ((step * group + i) * PACK + k) * HD
                    cols = pl.ds(pl.multiple_of(at_head, HD), HD)
                    for b, o_ref in enumerate(outs):
                        start = k * rows + b * tile
                        one = both[start : start + tile, k * HD : (k + 1) * HD]
                        o_ref[at, cols] = one.astype(o_ref.dtype)

            ahead = [scores(i) for i in range(min(2, group))]
            weights = None
            for i in range(group):
                if i + 2 < group:
                    ahead.append(scores(i + 2))
                done, weights = weights, weigh(i, ahead[i])
                if i > 0:
                    gather_values(i - 1, done)
            gather_values(group - 1, weights)
            return carry

        lax.fori_loop(0, steps, heads_of, 0)
        tops, masses = top_acc[...].T, mass_acc[...].T
        packed = 0.0
        for k in range(PACK):
            part = slice(k * rows, (k + 1) * rows)
            stats = pack_stats(tops[part], masses[part])
            packed += pltpu.roll(stats, k * (LANE // PACK), 1) if k else stats
        for b, o_ref in enumerate(outs):
            width = o_ref.shape[1]
            o_ref[at, width - STAT :] = packed[b * tile : (b + 1) * tile].astype(o_ref.dtype)
        return carry

    lax.fori_loop(0, line_rows // tile, row_tile, 0)


def attend(plane, lines, kind, keys, values, bias, after=()):
    rows, columns = plane.shape[0] // lines, plane.shape[1]
    heads = columns // HD
    pairs = heads // PACK
    group = next(g for g in (10, 5, 4, 3, 2, 1) if pairs % g == 0)
    tile = next(t for t in (32, 16, rows) if rows % t == 0)
    width = columns + STAT
    scale = math.log2(math.e) / math.sqrt(HD)

    def body(*refs):
        work = refs[4 + len(after) :]
        attend_kernel(
            (tile, pairs // group, group), scale, *refs[:4], work[:lines], *work[lines:]
        )

    return pl.pallas_call(
        body,
        in_specs=[pl.BlockSpec(memory_space=pltpu.VMEM)] * 4
        + [pl.BlockSpec(memory_space=pl.ANY)] * len(after),
        out_specs=[pl.BlockSpec(memory_space=pltpu.VMEM)] * lines,
        out_shape=[jax.ShapeDtypeStruct((rows, width), kind)] * lines,
        scratch_shapes=[pltpu.VMEM((STAT, PACK * tile * lines), F32)] * 2,
        compiler_params=pltpu.CompilerParams(vmem_limit_bytes=40 * 1024 * 1024),
        cost_estimate=pl.CostEstimate(
            flops=4 * lines * rows * keys.shape[0] * columns,
            bytes_accessed=4 * keys.shape[0] * columns,
            transcendentals=lines * rows * keys.shape[0] * heads,
        ),
        name="attend",
    )(bias, plane, keys, values, *after)


def load(cached, fresh, victims, queries, after):
    cache_rows, columns = cached[0].shape
    tok = fresh[0].shape[0]
    padded = cache_rows + -(-tok // 16) * 16
    n = len(cached)

    def body(*refs):
        cached_refs, fresh_refs, victims_ref, queries_ref = refs[:n], refs[n : 2 * n], *refs[2 * n : 2 * n + 2]
        refs = refs[2 * n + 3 :]
        outs, bias_ref, q_ref, tails, ids_ref, sems = (
            refs[:n], refs[n], refs[n + 1], refs[n + 2 : 2 * n + 2], *refs[2 * n + 2 :]
        )
        ids = pltpu.make_async_copy(victims_ref, ids_ref, sems.at[1, n])
        rest = pltpu.make_async_copy(queries_ref, q_ref, sems.at[0, n])
        small = [
            pltpu.make_async_copy(src, dst, sems.at[1, i])
            for i, (src, dst) in enumerate(zip(fresh_refs, tails))
        ]
        large = [
            pltpu.make_async_copy(src, dst.at[pl.ds(0, cache_rows), :], sems.at[0, i])
            for i, (src, dst) in enumerate(zip(cached_refs, outs))
        ]
        for copy in [ids] + small + large + [rest]:
            copy.start()
        ids.wait()
        blocks = cache_rows // BLK
        first = lax.axis_index("seq") * blocks
        for block in range(blocks):
            hits = jnp.where(ids_ref[...] == first + block, 1.0, 0.0)
            hit = jnp.max(hits, axis=1, keepdims=True)
            gone = jnp.where(hit > 0.0, NEG, 0.0)
            bias_ref[block * BLK : (block + 1) * BLK, :] = jnp.broadcast_to(gone, (BLK, STAT))
        token = lax.broadcasted_iota(jnp.int32, (padded - cache_rows, STAT), 0)
        bias_ref[cache_rows:, :] = jnp.where(token < tok, 0.0, NEG)
        for copy, tail, out in zip(small, tails, outs):
            copy.wait()
            zeros = jnp.zeros((padded - cache_rows - tok, columns), F32)
            rows = jnp.concatenate([tail[...].astype(F32), zeros], axis=0)
            out[cache_rows:, :] = rows.astype(out.dtype)
        for copy in large + [rest]:
            copy.wait()

    in_hbm = pl.BlockSpec(memory_space=pltpu.HBM)
    held = (*cached, *fresh, victims, queries)
    return pl.pallas_call(
        body,
        in_specs=[in_hbm] * len(held) + [pl.BlockSpec(memory_space=pl.ANY)],
        out_specs=[pl.BlockSpec(memory_space=pltpu.VMEM)] * (n + 2),
        out_shape=[jax.ShapeDtypeStruct((padded, columns), BF16)] * n
        + [jax.ShapeDtypeStruct((padded, STAT), F32), jax.ShapeDtypeStruct(queries.shape, BF16)],
        scratch_shapes=[pltpu.VMEM(x.shape, BF16) for x in fresh]
        + [pltpu.VMEM(victims.shape, jnp.int32), pltpu.SemaphoreType.DMA((2, n + 1))],
        compiler_params=pltpu.CompilerParams(vmem_limit_bytes=24 * 1024 * 1024),
        cost_estimate=pl.CostEstimate(
            flops=0, bytes_accessed=4 * n * cache_rows * columns, transcendentals=0
        ),
        name="load",
    )(*[pltpu.with_memory_space_constraint(x, pltpu.HBM) for x in held], after)


def merged(arrays, heads, last):
    columns = heads * HD
    stats = [unpack_stats(get(slice(columns, columns + STAT))) for get in arrays]
    top = functools.reduce(jnp.maximum, [t for t, _ in stats])
    weights = [jnp.exp2(t - top) for t, _ in stats]
    mass = functools.reduce(jnp.add, [w * m for w, (_, m) in zip(weights, stats)])
    if last:
        inverse = 1.0 / jnp.where(mass > 0.0, mass, 1.0)
        weights = [w * inverse for w in weights]
    for head in range(heads):
        cols = slice(head * HD, (head + 1) * HD)
        yield cols, functools.reduce(
            jnp.add, [get(cols) * w[:, lane_of(head) : lane_of(head) + 1] for get, w in zip(arrays, weights)]
        )
    if not last:
        yield slice(columns, columns + STAT), pack_stats(top, mass)


def getter(ref, *index):
    return lambda cols: ref[(*index, slice(None), cols)].astype(F32)


def merge_rows(ins, heads, cuts, after=()):
    width = ins[0].shape[1]
    starts = [sum(n for n, _ in cuts[:j]) for j in range(len(cuts))]

    def body(*refs):
        for cols, total in merged([getter(r) for r in refs[: len(ins)]], heads, False):
            for (n, _), start, out in zip(cuts, starts, refs[len(ins) + len(after) :]):
                out[:, cols] = total[start : start + n].astype(out.dtype)

    shapes = [jax.ShapeDtypeStruct((n, width), kind) for n, kind in cuts]
    return call_merge(body, ins, shapes, after)


def finish(ins, heads):
    rows = ins[0].shape[0]

    def body(*refs):
        out = refs[len(ins)]
        for cols, total in merged([getter(r) for r in refs[: len(ins)]], heads, True):
            out[:, cols] = total.astype(out.dtype)

    return call_merge(body, ins, [jax.ShapeDtypeStruct((rows, heads * HD), BF16)])[0]


def join(pieces, after=()):
    rows = sum(p.shape[0] for p in pieces)

    def body(*refs):
        out = refs[-1]
        ins = [r[...].astype(F32) for r in refs[: len(pieces)]]
        out[...] = jnp.concatenate(ins, axis=0).astype(out.dtype)

    shape = jax.ShapeDtypeStruct((rows, pieces[0].shape[1]), pieces[0].dtype)
    return call_merge(body, pieces, [shape], after)[0]


def call_merge(body, ins, shapes, after=()):
    size = sum(math.prod(x.shape) for x in ins)
    return pl.pallas_call(
        body,
        in_specs=[pl.BlockSpec(memory_space=pltpu.VMEM)] * len(ins)
        + [pl.BlockSpec(memory_space=pl.ANY)] * len(after),
        out_specs=[pl.BlockSpec(memory_space=pltpu.VMEM)] * len(shapes),
        out_shape=shapes,
        compiler_params=pltpu.CompilerParams(vmem_limit_bytes=48 * 1024 * 1024),
        cost_estimate=pl.CostEstimate(flops=4 * size, bytes_accessed=4 * size, transcendentals=0),
        name="merge",
    )(*ins, *after)


def per_device(queries, new_keys, new_values, cache_keys, cache_values, victims):
    members = lax.axis_size("seq")
    shape = factors(members)
    a_n, b_n, c_n = shape
    heads = queries.shape[1] // HD
    tok = queries.shape[0]
    tok = queries.shape[0]

    def fetch(x, *by):
        return lax.ppermute(x, "seq", partner_perm(shape, by, False))

    def give(x, *by):
        return lax.ppermute(x, "seq", partner_perm(shape, by, True))

    order = [*range(a_n - 1, -1, -1)]
    line = [fetch(queries, a, 0, 0) for a in order[:-1]] + [queries]
    lines = [line] + [[fetch(x, 0, b, 0) for x in line] for b in range(1, b_n)]
    keys, values, bias, line[-1] = load(
        (cache_keys, cache_values), (new_keys, new_values), victims[None], queries, line[min(2, a_n - 1)]
    )
    plane = join([x for pieces in lines for x in pieces])
    planes = [plane] + [fetch(plane, 0, 0, c) for c in range(1, c_n)]
    sums = []
    for c, rows in enumerate(planes):
        sums += attend(rows, b_n, BF16 if c else F32, keys, values, bias, sums[:1])

    def over_cores(b, cuts, kind):
        got = [give(sums[c * b_n + b], 0, 0, c) for c in range(1, c_n)]
        return merge_rows([sums[b]] + got, heads, [(n * tok, kind) for n in cuts])

    cuts = [2] * ((a_n - 2) // 2) + [1] * (a_n - max(a_n - 2, 0) // 2 * 2)
    got = [over_cores(b, cuts, BF16) for b in range(1, b_n)]
    got = [[give(x, 0, b, 0) for x in runs] for b, runs in enumerate(got, 1)]
    own = over_cores(0, cuts, F32)
    sent, first = [], ()
    for i, size in enumerate(cuts):
        slots = order[sum(cuts[:i]) :][:size]
        kinds = [(tok, BF16 if a else F32) for a in slots]
        pieces = merge_rows([own[i]] + [runs[i] for runs in got], heads, kinds, first)
        first = pieces[:1] if not first else first
        sent += [give(x, a, 0, 0) for x, a in zip(pieces, slots) if a]
    far, near = sent[:-1], sent[-1:]
    return finish([*merge_rows([pieces[-1], *far], heads, [(tok, F32)]), *near], heads)


def solution(mesh):
    rows = P(("groups", "seq"), None)
    return jax.shard_map(
        per_device,
        mesh=mesh,
        in_specs=(rows, rows, rows, rows, rows, P("groups")),
        out_specs=rows,
        check_vma=False,
    )
```

```python
import functools
import itertools
import math

import jax
import jax.numpy as jnp
from jax import lax
from jax.experimental import pallas as pl
from jax.experimental.pallas import tpu as pltpu
from jax.sharding import PartitionSpec as P

HD = 128
BLK = 128
STAT = 128
LANE = STAT // 3
PACK = 2
NEG = -1e30
F32 = jnp.float32
BF16 = jnp.bfloat16


def factors(members):
    cores = 2 if members % 2 == 0 else 1
    chips = members // cores
    far = next(a for a in range(1, chips + 1) if chips % a == 0 and a * a >= chips)
    return far, chips // far, cores


def partner(at, by, size):
    return at ^ by if size & (size - 1) == 0 else (at + by) % size


def partner_perm(shape, by, back):
    def flat(place):
        return functools.reduce(lambda at, kn: at * kn[1] + kn[0], zip(place, shape), 0)

    places = itertools.product(*map(range, shape))
    pairs = [(flat([partner(*x) for x in zip(at, by, shape)]), flat(at)) for at in places]
    return [pair[::-1] for pair in pairs] if back else pairs


def lanes(rows):
    return lax.broadcasted_iota(jnp.int32, (rows, STAT), 1)


def pack_stats(top, mass):
    high = mass.astype(BF16).astype(F32)
    return top + pltpu.roll(high, LANE, 1) + pltpu.roll(mass - high, 2 * LANE, 1)


def unpack_stats(packed):
    used = lanes(packed.shape[0]) < LANE
    mass = pltpu.roll(packed, STAT - LANE, 1) + pltpu.roll(packed, STAT - 2 * LANE, 1)
    return jnp.where(used, packed, 0.0), jnp.where(used, mass, 0.0)


def lane_of(head):
    return head % PACK * (LANE // PACK) + head // PACK


def attend_kernel(scale, bias_ref, q_refs, k_refs, v_refs, outs, top_acc, mass_acc):
    tok = q_refs[0].shape[0]
    rows = tok * len(q_refs)
    wide = PACK * HD
    pairs = q_refs[0].shape[1] // wide
    contract_last = (((1,), (1,)), ((), ()))
    contract_first = (((0,), (0,)), ((), ()))
    mine = [lax.broadcasted_iota(jnp.int32, (rows, wide), 1) // HD == k for k in range(PACK)]
    starts = [sum(r.shape[0] for r in k_refs[:j]) for j in range(len(k_refs))]
    top_acc[...] = jnp.zeros_like(top_acc)
    mass_acc[...] = jnp.zeros_like(mass_acc)

    def scores(i):
        cols = slice(i * wide, (i + 1) * wide)
        q = jnp.concatenate([ref[:, cols].astype(F32) for ref in q_refs], axis=0)
        q = jnp.concatenate([jnp.where(m, q, 0.0) for m in mine], axis=0).astype(BF16)
        return [
            lax.dot_general(k[:, cols], q, contract_last, preferred_element_type=F32) for k in k_refs
        ]

    def weigh(i, parts):
        masked = []
        for start, score in zip(starts, parts):
            bias = bias_ref[start : start + score.shape[0], :]
            bias = jnp.concatenate([bias] * (PACK * rows // STAT), axis=1)
            masked.append(score * scale + bias)
        tops = [jnp.max(score, axis=0, keepdims=True) for score in masked]
        top = functools.reduce(jnp.maximum, tops).astype(BF16).astype(F32)
        parts = [jnp.exp2(score - top) for score in masked]
        masses = [jnp.sum(part, axis=0, keepdims=True) for part in parts]
        top_acc[i : i + 1, :] = top
        mass_acc[i : i + 1, :] = functools.reduce(jnp.add, masses)
        return [part.astype(BF16) for part in parts]

    def gather_values(i, weights):
        cols = slice(i * wide, (i + 1) * wide)
        both = functools.reduce(
            jnp.add,
            [
                lax.dot_general(w, v[:, cols], contract_first, preferred_element_type=F32)
                for w, v in zip(weights, v_refs)
            ],
        )
        for k in range(PACK):
            one = both[k * rows : (k + 1) * rows, k * HD : (k + 1) * HD]
            at_head = (i * PACK + k) * HD
            for p, o_ref in enumerate(outs):
                o_ref[:, at_head : at_head + HD] = one[p * tok : (p + 1) * tok].astype(o_ref.dtype)

    ahead = [scores(i) for i in range(min(2, pairs))]
    weights = None
    for i in range(pairs):
        if i + 2 < pairs:
            ahead.append(scores(i + 2))
        done, weights = weights, weigh(i, ahead[i])
        if i > 0:
            gather_values(i - 1, done)
    gather_values(pairs - 1, weights)

    tops, masses = top_acc[...].T, mass_acc[...].T
    packed = 0.0
    for k in range(PACK):
        part = slice(k * rows, (k + 1) * rows)
        stats = pack_stats(tops[part], masses[part])
        packed += pltpu.roll(stats, k * (LANE // PACK), 1) if k else stats
    for p, o_ref in enumerate(outs):
        width = o_ref.shape[1]
        o_ref[:, width - STAT :] = packed[p * tok : (p + 1) * tok].astype(o_ref.dtype)


def attend(blocks, kinds, keys, values, bias):
    n, m = len(blocks), len(keys)
    tok, columns = blocks[0].shape
    total = sum(k.shape[0] for k in keys)

    def body(*refs):
        bias_ref, refs = refs[0], refs[1:]
        attend_kernel(
            math.log2(math.e) / math.sqrt(HD), bias_ref, refs[:n], refs[n : n + m],
            refs[n + m : n + 2 * m], refs[n + 2 * m : 2 * n + 2 * m], *refs[2 * n + 2 * m :],
        )

    return pl.pallas_call(
        body,
        in_specs=[pl.BlockSpec(memory_space=pltpu.VMEM)] * (1 + n + 2 * m),
        out_specs=[pl.BlockSpec(memory_space=pltpu.VMEM)] * n,
        out_shape=[jax.ShapeDtypeStruct((tok, columns + STAT), kind) for kind in kinds],
        scratch_shapes=[pltpu.VMEM((STAT, PACK * tok * n), F32)] * 2,
        compiler_params=pltpu.CompilerParams(vmem_limit_bytes=32 * 1024 * 1024),
        cost_estimate=pl.CostEstimate(
            flops=4 * n * tok * total * columns,
            bytes_accessed=4 * total * columns,
            transcendentals=n * tok * total * columns // HD,
        ),
        name="attend",
    )(bias, *blocks, *keys, *values)


def load(cached, fresh, victims, queries, cores, after):
    cache_rows, columns = cached[0].shape
    tok = queries.shape[0]
    fresh_rows = tok * len(fresh[0])
    padded = cache_rows + -(-fresh_rows // 16) * 16
    mask_rows = padded + (cores - 1) * cache_rows
    blocks = cache_rows // BLK
    n, m = len(cached), len(fresh[0])
    flat = [x for parts in fresh for x in parts]

    def body(*refs):
        cached_refs, fresh_refs = refs[:n], refs[n : n + n * m]
        victims_ref, queries_ref = refs[n + n * m : n + n * m + 2]
        refs = refs[n + n * m + 3 :]
        outs, bias_ref, q_ref, refs = refs[:n], refs[n], refs[n + 1], refs[n + 2 :]
        tails, ids_ref, sems = refs[: n * m], refs[n * m], refs[n * m + 1]
        ids = pltpu.make_async_copy(victims_ref, ids_ref, sems.at[n * m + n])
        rest = pltpu.make_async_copy(queries_ref, q_ref, sems.at[n * m + n + 1])
        small = [
            pltpu.make_async_copy(src, dst, sems.at[i])
            for i, (src, dst) in enumerate(zip(fresh_refs, tails))
        ]
        large = [
            pltpu.make_async_copy(src, dst.at[pl.ds(0, cache_rows), :], sems.at[n * m + i])
            for i, (src, dst) in enumerate(zip(cached_refs, outs))
        ]
        for copy in [ids] + small + large + [rest]:
            copy.start()
        ids.wait()
        me = lax.axis_index("seq")
        core = lax.rem(me, cores)

        def mask(first, start):
            for block in range(blocks):
                hits = jnp.where(ids_ref[...] == first + block, 1.0, 0.0)
                hit = jnp.max(hits, axis=1, keepdims=True)
                gone = jnp.where(hit > 0.0, NEG, 0.0)
                at = start + block * BLK
                bias_ref[at : at + BLK, :] = jnp.broadcast_to(gone, (BLK, STAT))

        mask(me * blocks, 0)
        token = lax.broadcasted_iota(jnp.int32, (padded - cache_rows, STAT), 0)
        bias_ref[cache_rows:padded, :] = jnp.where(token < fresh_rows, 0.0, NEG)
        for c in range(1, cores):
            other = me - core + lax.rem(core + c, cores)
            mask(other * blocks, padded + (c - 1) * cache_rows)
        for copy in small:
            copy.wait()
        for i, out in enumerate(outs):
            rows = [t[...].astype(F32) for t in tails[i * m : (i + 1) * m]]
            if padded - cache_rows > fresh_rows:
                rows.append(jnp.zeros((padded - cache_rows - fresh_rows, columns), F32))
            out[cache_rows:, :] = jnp.concatenate(rows, axis=0).astype(out.dtype)
        for copy in large + [rest]:
            copy.wait()

    hbm = lambda x: pltpu.with_memory_space_constraint(x, pltpu.HBM)
    in_hbm = pl.BlockSpec(memory_space=pltpu.HBM)
    anywhere = pl.BlockSpec(memory_space=pl.ANY)
    return pl.pallas_call(
        body,
        in_specs=[in_hbm] * n
        + [in_hbm if i % m == 0 else anywhere for i in range(n * m)]
        + [in_hbm] * 2
        + [anywhere],
        out_specs=[pl.BlockSpec(memory_space=pltpu.VMEM)] * (n + 2),
        out_shape=[jax.ShapeDtypeStruct((padded, columns), BF16)] * n
        + [jax.ShapeDtypeStruct((mask_rows, STAT), F32), jax.ShapeDtypeStruct(queries.shape, BF16)],
        scratch_shapes=[pltpu.VMEM(queries.shape, BF16)] * (n * m)
        + [pltpu.VMEM(victims.shape, jnp.int32), pltpu.SemaphoreType.DMA((n * m + n + 2,))],
        compiler_params=pltpu.CompilerParams(vmem_limit_bytes=16 * 1024 * 1024),
        cost_estimate=pl.CostEstimate(
            flops=0, bytes_accessed=4 * n * cache_rows * columns, transcendentals=0
        ),
        name="load",
    )(
        *[hbm(x) for x in cached],
        *[hbm(x) if i % m == 0 else x for i, x in enumerate(flat)],
        hbm(victims), hbm(queries), after,
    )


def merged(arrays, heads, last):
    columns = heads * HD
    stats = [unpack_stats(get(slice(columns, columns + STAT))) for get in arrays]
    top = functools.reduce(jnp.maximum, [t for t, _ in stats])
    weights = [jnp.exp2(t - top) for t, _ in stats]
    mass = functools.reduce(jnp.add, [w * m for w, (_, m) in zip(weights, stats)])
    if last:
        inverse = 1.0 / jnp.where(mass > 0.0, mass, 1.0)
        weights = [w * inverse for w in weights]
    for head in range(heads):
        cols = slice(head * HD, (head + 1) * HD)
        yield cols, functools.reduce(
            jnp.add, [get(cols) * w[:, lane_of(head) : lane_of(head) + 1] for get, w in zip(arrays, weights)]
        )
    if not last:
        yield slice(columns, columns + STAT), pack_stats(top, mass)


def getter(ref, *index):
    return lambda cols: ref[(*index, slice(None), cols)].astype(F32)


def merge_rows(ins, heads, pieces, kinds):
    rows, width = ins[0].shape
    per = rows // pieces

    def body(*refs):
        outs = refs[len(ins) :]
        for cols, total in merged([getter(r) for r in refs[: len(ins)]], heads, False):
            for j, out in enumerate(outs):
                out[:, cols] = total[j * per : (j + 1) * per].astype(out.dtype)

    return call_merge(body, ins, [jax.ShapeDtypeStruct((per, width), kind) for kind in kinds])


def finish(ins, heads):
    rows = ins[0].shape[0]

    def body(*refs):
        out = refs[len(ins)]
        for cols, total in merged([getter(r) for r in refs[: len(ins)]], heads, True):
            out[:, cols] = total.astype(out.dtype)

    return call_merge(body, ins, [jax.ShapeDtypeStruct((rows, heads * HD), BF16)])[0]


def join(pieces, after=()):
    rows = sum(p.shape[0] for p in pieces)

    def body(*refs):
        out = refs[-1]
        ins = [r[...].astype(F32) for r in refs[: len(pieces)]]
        out[...] = jnp.concatenate(ins, axis=0).astype(out.dtype)

    shape = jax.ShapeDtypeStruct((rows, pieces[0].shape[1]), pieces[0].dtype)
    return call_merge(body, pieces, [shape], after)[0]


def call_merge(body, ins, shapes, after=()):
    size = sum(math.prod(x.shape) for x in ins)
    return pl.pallas_call(
        body,
        in_specs=[pl.BlockSpec(memory_space=pltpu.VMEM)] * len(ins)
        + [pl.BlockSpec(memory_space=pl.ANY)] * len(after),
        out_specs=[pl.BlockSpec(memory_space=pltpu.VMEM)] * len(shapes),
        out_shape=shapes,
        compiler_params=pltpu.CompilerParams(vmem_limit_bytes=48 * 1024 * 1024),
        cost_estimate=pl.CostEstimate(flops=4 * size, bytes_accessed=4 * size, transcendentals=0),
        name="merge",
    )(*ins, *after)


def per_device(queries, new_keys, new_values, cache_keys, cache_values, victims):
    members = lax.axis_size("seq")
    shape = factors(members)
    a_n, b_n, c_n = shape
    heads = queries.shape[1] // HD
    tok = queries.shape[0]
    tok = queries.shape[0]

    def fetch(x, *by):
        return lax.ppermute(x, "seq", partner_perm(shape, by, False))

    def give(x, *by):
        return lax.ppermute(x, "seq", partner_perm(shape, by, True))

    others = [[fetch(x, 0, 0, c) for c in range(1, c_n)] for x in (cache_keys, cache_values)]
    fresh = [[x] + [fetch(x, 0, 0, c) for c in range(1, c_n)] for x in (new_keys, new_values)]

    far_first = [0, *range(a_n - 1, 0, -1)]
    line = [queries] + [fetch(queries, a, 0, 0) for a in far_first[1:]]
    lines = [line] + [[fetch(x, 0, b, 0) for x in line] for b in range(1, b_n)]
    keys, values, bias, line[0] = load(
        (cache_keys, cache_values), fresh, victims[None], queries, c_n, line[min(2, a_n - 1)]
    )
    keys, values = [keys, *others[0]], [values, *others[1]]
    at_once = next(n for n in range(b_n, 0, -1) if b_n % n == 0 and n * a_n * tok <= max(64, a_n * tok))
    sums = []
    for start in range(0, b_n, at_once):
        blocks = [x for pieces in lines[start : start + at_once] for x in pieces]
        kinds = [F32 if start * a_n + i < a_n else BF16 for i in range(len(blocks))]
        sums += attend(blocks, kinds, keys, values, bias)

    own = sums[:a_n]
    got = [[give(x, 0, b, 0) for x in sums[b * a_n : (b + 1) * a_n]] for b in range(1, b_n)]
    total = [[own[s]] + [pieces[s] for pieces in got] for s in range(a_n)]
    last = [
        give(merge_rows(total[s], heads, 1, [BF16])[0], far_first[s], 0, 0) for s in range(1, a_n)
    ]
    return finish([*merge_rows(total[0], heads, 1, [F32]), *last], heads)


def solution(mesh):
    rows = P(("groups", "seq"), None)
    return jax.shard_map(
        per_device,
        mesh=mesh,
        in_specs=(rows, rows, rows, rows, rows, P("groups")),
        out_specs=rows,
        check_vma=False,
    )
```

```python
import functools
import itertools
import math

import jax
import jax.numpy as jnp
from jax import lax
from jax.experimental import pallas as pl
from jax.experimental.pallas import tpu as pltpu
from jax.sharding import PartitionSpec as P

HD = 128
BLK = 128
STAT = 128
LANE = STAT // 3
PACK = 2
NEG = -1e30
F32 = jnp.float32
BF16 = jnp.bfloat16


def factors(members):
    cores = 2 if members % 2 == 0 else 1
    chips = members // cores
    far = next(a for a in range(1, chips + 1) if chips % a == 0 and a * a >= chips)
    return far, chips // far, cores


def partner(at, by, size):
    return at ^ by if size & (size - 1) == 0 else (at + by) % size


def partner_perm(shape, by, back):
    def flat(place):
        return functools.reduce(lambda at, kn: at * kn[1] + kn[0], zip(place, shape), 0)

    places = itertools.product(*map(range, shape))
    pairs = [(flat([partner(*x) for x in zip(at, by, shape)]), flat(at)) for at in places]
    return [pair[::-1] for pair in pairs] if back else pairs


def lanes(rows):
    return lax.broadcasted_iota(jnp.int32, (rows, STAT), 1)


def pack_stats(top, mass):
    high = mass.astype(BF16).astype(F32)
    return top + pltpu.roll(high, LANE, 1) + pltpu.roll(mass - high, 2 * LANE, 1)


def unpack_stats(packed):
    used = lanes(packed.shape[0]) < LANE
    mass = pltpu.roll(packed, STAT - LANE, 1) + pltpu.roll(packed, STAT - 2 * LANE, 1)
    return jnp.where(used, packed, 0.0), jnp.where(used, mass, 0.0)


def lane_of(head):
    return head % PACK * (LANE // PACK) + head // PACK


def attend_kernel(scale, bias_ref, q_refs, k_refs, v_refs, outs, top_acc, mass_acc):
    tok = q_refs[0].shape[0]
    rows = tok * len(q_refs)
    wide = PACK * HD
    pairs = q_refs[0].shape[1] // wide
    contract_last = (((1,), (1,)), ((), ()))
    contract_first = (((0,), (0,)), ((), ()))
    mine = [lax.broadcasted_iota(jnp.int32, (rows, wide), 1) // HD == k for k in range(PACK)]
    starts = [sum(r.shape[0] for r in k_refs[:j]) for j in range(len(k_refs))]
    top_acc[...] = jnp.zeros_like(top_acc)
    mass_acc[...] = jnp.zeros_like(mass_acc)

    def scores(i):
        cols = slice(i * wide, (i + 1) * wide)
        q = jnp.concatenate([ref[:, cols].astype(F32) for ref in q_refs], axis=0)
        q = jnp.concatenate([jnp.where(m, q, 0.0) for m in mine], axis=0).astype(BF16)
        return [
            lax.dot_general(k[:, cols], q, contract_last, preferred_element_type=F32) for k in k_refs
        ]

    def weigh(i, parts):
        masked = []
        for start, score in zip(starts, parts):
            bias = bias_ref[start : start + score.shape[0], :]
            bias = jnp.concatenate([bias] * (PACK * rows // STAT), axis=1)
            masked.append(score * scale + bias)
        tops = [jnp.max(score, axis=0, keepdims=True) for score in masked]
        top = functools.reduce(jnp.maximum, tops).astype(BF16).astype(F32)
        parts = [jnp.exp2(score - top) for score in masked]
        masses = [jnp.sum(part, axis=0, keepdims=True) for part in parts]
        top_acc[i : i + 1, :] = top
        mass_acc[i : i + 1, :] = functools.reduce(jnp.add, masses)
        return [part.astype(BF16) for part in parts]

    def gather_values(i, weights):
        cols = slice(i * wide, (i + 1) * wide)
        both = functools.reduce(
            jnp.add,
            [
                lax.dot_general(w, v[:, cols], contract_first, preferred_element_type=F32)
                for w, v in zip(weights, v_refs)
            ],
        )
        for k in range(PACK):
            one = both[k * rows : (k + 1) * rows, k * HD : (k + 1) * HD]
            at_head = (i * PACK + k) * HD
            for p, o_ref in enumerate(outs):
                o_ref[:, at_head : at_head + HD] = one[p * tok : (p + 1) * tok].astype(o_ref.dtype)

    ahead = [scores(i) for i in range(min(2, pairs))]
    weights = None
    for i in range(pairs):
        if i + 2 < pairs:
            ahead.append(scores(i + 2))
        done, weights = weights, weigh(i, ahead[i])
        if i > 0:
            gather_values(i - 1, done)
    gather_values(pairs - 1, weights)

    tops, masses = top_acc[...].T, mass_acc[...].T
    packed = 0.0
    for k in range(PACK):
        part = slice(k * rows, (k + 1) * rows)
        stats = pack_stats(tops[part], masses[part])
        packed += pltpu.roll(stats, k * (LANE // PACK), 1) if k else stats
    for p, o_ref in enumerate(outs):
        width = o_ref.shape[1]
        o_ref[:, width - STAT :] = packed[p * tok : (p + 1) * tok].astype(o_ref.dtype)


def attend(blocks, kinds, keys, values, bias):
    n, m = len(blocks), len(keys)
    tok, columns = blocks[0].shape
    total = sum(k.shape[0] for k in keys)

    def body(*refs):
        bias_ref, refs = refs[0], refs[1:]
        attend_kernel(
            math.log2(math.e) / math.sqrt(HD), bias_ref, refs[:n], refs[n : n + m],
            refs[n + m : n + 2 * m], refs[n + 2 * m : 2 * n + 2 * m], *refs[2 * n + 2 * m :],
        )

    return pl.pallas_call(
        body,
        in_specs=[pl.BlockSpec(memory_space=pltpu.VMEM)] * (1 + n + 2 * m),
        out_specs=[pl.BlockSpec(memory_space=pltpu.VMEM)] * n,
        out_shape=[jax.ShapeDtypeStruct((tok, columns + STAT), kind) for kind in kinds],
        scratch_shapes=[pltpu.VMEM((STAT, PACK * tok * n), F32)] * 2,
        compiler_params=pltpu.CompilerParams(vmem_limit_bytes=32 * 1024 * 1024),
        cost_estimate=pl.CostEstimate(
            flops=4 * n * tok * total * columns,
            bytes_accessed=4 * total * columns,
            transcendentals=n * tok * total * columns // HD,
        ),
        name="attend",
    )(bias, *blocks, *keys, *values)


def load(cached, fresh, victims, queries, cores, after):
    cache_rows, columns = cached[0].shape
    tok = queries.shape[0]
    fresh_rows = tok * len(fresh[0])
    padded = cache_rows + -(-fresh_rows // 16) * 16
    mask_rows = padded + (cores - 1) * cache_rows
    blocks = cache_rows // BLK
    n, m = len(cached), len(fresh[0])
    flat = [x for parts in fresh for x in parts]

    def body(*refs):
        cached_refs, fresh_refs = refs[:n], refs[n : n + n * m]
        victims_ref, queries_ref = refs[n + n * m : n + n * m + 2]
        refs = refs[n + n * m + 3 :]
        outs, bias_ref, q_ref, refs = refs[:n], refs[n], refs[n + 1], refs[n + 2 :]
        tails, ids_ref, sems = refs[: n * m], refs[n * m], refs[n * m + 1]
        ids = pltpu.make_async_copy(victims_ref, ids_ref, sems.at[n * m + n])
        rest = pltpu.make_async_copy(queries_ref, q_ref, sems.at[n * m + n + 1])
        small = [
            pltpu.make_async_copy(src, dst, sems.at[i])
            for i, (src, dst) in enumerate(zip(fresh_refs, tails))
        ]
        large = [
            pltpu.make_async_copy(src, dst.at[pl.ds(0, cache_rows), :], sems.at[n * m + i])
            for i, (src, dst) in enumerate(zip(cached_refs, outs))
        ]
        for copy in [ids] + small + large + [rest]:
            copy.start()
        ids.wait()
        me = lax.axis_index("seq")
        core = lax.rem(me, cores)

        def mask(first, start):
            for block in range(blocks):
                hits = jnp.where(ids_ref[...] == first + block, 1.0, 0.0)
                hit = jnp.max(hits, axis=1, keepdims=True)
                gone = jnp.where(hit > 0.0, NEG, 0.0)
                at = start + block * BLK
                bias_ref[at : at + BLK, :] = jnp.broadcast_to(gone, (BLK, STAT))

        mask(me * blocks, 0)
        token = lax.broadcasted_iota(jnp.int32, (padded - cache_rows, STAT), 0)
        bias_ref[cache_rows:padded, :] = jnp.where(token < fresh_rows, 0.0, NEG)
        for c in range(1, cores):
            other = me - core + lax.rem(core + c, cores)
            mask(other * blocks, padded + (c - 1) * cache_rows)
        for copy in small:
            copy.wait()
        for i, out in enumerate(outs):
            rows = [t[...].astype(F32) for t in tails[i * m : (i + 1) * m]]
            if padded - cache_rows > fresh_rows:
                rows.append(jnp.zeros((padded - cache_rows - fresh_rows, columns), F32))
            out[cache_rows:, :] = jnp.concatenate(rows, axis=0).astype(out.dtype)
        for copy in large + [rest]:
            copy.wait()

    hbm = lambda x: pltpu.with_memory_space_constraint(x, pltpu.HBM)
    in_hbm = pl.BlockSpec(memory_space=pltpu.HBM)
    anywhere = pl.BlockSpec(memory_space=pl.ANY)
    return pl.pallas_call(
        body,
        in_specs=[in_hbm] * n
        + [in_hbm if i % m == 0 else anywhere for i in range(n * m)]
        + [in_hbm] * 2
        + [anywhere],
        out_specs=[pl.BlockSpec(memory_space=pltpu.VMEM)] * (n + 2),
        out_shape=[jax.ShapeDtypeStruct((padded, columns), BF16)] * n
        + [jax.ShapeDtypeStruct((mask_rows, STAT), F32), jax.ShapeDtypeStruct(queries.shape, BF16)],
        scratch_shapes=[pltpu.VMEM(queries.shape, BF16)] * (n * m)
        + [pltpu.VMEM(victims.shape, jnp.int32), pltpu.SemaphoreType.DMA((n * m + n + 2,))],
        compiler_params=pltpu.CompilerParams(vmem_limit_bytes=16 * 1024 * 1024),
        cost_estimate=pl.CostEstimate(
            flops=0, bytes_accessed=4 * n * cache_rows * columns, transcendentals=0
        ),
        name="load",
    )(
        *[hbm(x) for x in cached],
        *[hbm(x) if i % m == 0 else x for i, x in enumerate(flat)],
        hbm(victims), hbm(queries), after,
    )


def merged(arrays, heads, last):
    columns = heads * HD
    stats = [unpack_stats(get(slice(columns, columns + STAT))) for get in arrays]
    top = functools.reduce(jnp.maximum, [t for t, _ in stats])
    weights = [jnp.exp2(t - top) for t, _ in stats]
    mass = functools.reduce(jnp.add, [w * m for w, (_, m) in zip(weights, stats)])
    if last:
        inverse = 1.0 / jnp.where(mass > 0.0, mass, 1.0)
        weights = [w * inverse for w in weights]
    for head in range(heads):
        cols = slice(head * HD, (head + 1) * HD)
        yield cols, functools.reduce(
            jnp.add, [get(cols) * w[:, lane_of(head) : lane_of(head) + 1] for get, w in zip(arrays, weights)]
        )
    if not last:
        yield slice(columns, columns + STAT), pack_stats(top, mass)


def getter(ref, *index):
    return lambda cols: ref[(*index, slice(None), cols)].astype(F32)


def merge_rows(ins, heads, pieces, kinds):
    rows, width = ins[0].shape
    per = rows // pieces

    def body(*refs):
        outs = refs[len(ins) :]
        for cols, total in merged([getter(r) for r in refs[: len(ins)]], heads, False):
            for j, out in enumerate(outs):
                out[:, cols] = total[j * per : (j + 1) * per].astype(out.dtype)

    return call_merge(body, ins, [jax.ShapeDtypeStruct((per, width), kind) for kind in kinds])


def finish(ins, heads):
    rows = ins[0].shape[0]

    def body(*refs):
        out = refs[len(ins)]
        for cols, total in merged([getter(r) for r in refs[: len(ins)]], heads, True):
            out[:, cols] = total.astype(out.dtype)

    return call_merge(body, ins, [jax.ShapeDtypeStruct((rows, heads * HD), BF16)])[0]


def join(pieces, after=()):
    rows = sum(p.shape[0] for p in pieces)

    def body(*refs):
        out = refs[-1]
        ins = [r[...].astype(F32) for r in refs[: len(pieces)]]
        out[...] = jnp.concatenate(ins, axis=0).astype(out.dtype)

    shape = jax.ShapeDtypeStruct((rows, pieces[0].shape[1]), pieces[0].dtype)
    return call_merge(body, pieces, [shape], after)[0]


def call_merge(body, ins, shapes, after=()):
    size = sum(math.prod(x.shape) for x in ins)
    return pl.pallas_call(
        body,
        in_specs=[pl.BlockSpec(memory_space=pltpu.VMEM)] * len(ins)
        + [pl.BlockSpec(memory_space=pl.ANY)] * len(after),
        out_specs=[pl.BlockSpec(memory_space=pltpu.VMEM)] * len(shapes),
        out_shape=shapes,
        compiler_params=pltpu.CompilerParams(vmem_limit_bytes=48 * 1024 * 1024),
        cost_estimate=pl.CostEstimate(flops=4 * size, bytes_accessed=4 * size, transcendentals=0),
        name="merge",
    )(*ins, *after)


def per_device(queries, new_keys, new_values, cache_keys, cache_values, victims):
    members = lax.axis_size("seq")
    shape = factors(members)
    a_n, b_n, c_n = shape
    heads = queries.shape[1] // HD
    tok = queries.shape[0]
    tok = queries.shape[0]

    def fetch(x, *by):
        return lax.ppermute(x, "seq", partner_perm(shape, by, False))

    def give(x, *by):
        return lax.ppermute(x, "seq", partner_perm(shape, by, True))

    fresh = [[x] + [fetch(x, 0, 0, c) for c in range(1, c_n)] for x in (new_keys, new_values)]
    bulk, fresh = lax.optimization_barrier(((cache_keys, cache_values), fresh))
    others = [[fetch(x, 0, 0, c) for c in range(1, c_n)] for x in bulk]

    far_first = [0, *range(a_n - 1, 0, -1)]
    line = [queries] + [fetch(queries, a, 0, 0) for a in far_first[1:]]
    lines = [line] + [[fetch(x, 0, b, 0) for x in line] for b in range(1, b_n)]
    keys, values, bias, line[0] = load(
        (cache_keys, cache_values), fresh, victims[None], queries, c_n, line[min(2, a_n - 1)]
    )
    keys, values = [keys, *others[0]], [values, *others[1]]
    at_once = next(n for n in range(b_n, 0, -1) if b_n % n == 0 and n * a_n * tok <= max(64, a_n * tok))
    sums = []
    for start in range(0, b_n, at_once):
        blocks = [x for pieces in lines[start : start + at_once] for x in pieces]
        kinds = [F32 if start * a_n + i < a_n else BF16 for i in range(len(blocks))]
        sums += attend(blocks, kinds, keys, values, bias)

    own = sums[:a_n]
    got = [[give(x, 0, b, 0) for x in sums[b * a_n : (b + 1) * a_n]] for b in range(1, b_n)]
    total = [[own[s]] + [pieces[s] for pieces in got] for s in range(a_n)]
    last = [
        give(merge_rows(total[s], heads, 1, [BF16])[0], far_first[s], 0, 0) for s in range(1, a_n)
    ]
    return finish([*merge_rows(total[0], heads, 1, [F32]), *last], heads)


def solution(mesh):
    rows = P(("groups", "seq"), None)
    return jax.shard_map(
        per_device,
        mesh=mesh,
        in_specs=(rows, rows, rows, rows, rows, P("groups")),
        out_specs=rows,
        check_vma=False,
    )
```

```python
import functools
import itertools
import math

import jax
import jax.numpy as jnp
from jax import lax
from jax.experimental import pallas as pl
from jax.experimental.pallas import tpu as pltpu
from jax.sharding import PartitionSpec as P

HD = 128
BLK = 128
STAT = 128
LANE = STAT // 3
PACK = 2
NEG = -1e30
F32 = jnp.float32
BF16 = jnp.bfloat16


def factors(members):
    cores = 2 if members % 2 == 0 else 1
    chips = members // cores
    far = next(a for a in range(1, chips + 1) if chips % a == 0 and a * a >= chips)
    return far, chips // far, cores


def partner(at, by, size):
    return at ^ by if size & (size - 1) == 0 else (at + by) % size


def partner_perm(shape, by, back):
    def flat(place):
        return functools.reduce(lambda at, kn: at * kn[1] + kn[0], zip(place, shape), 0)

    places = itertools.product(*map(range, shape))
    pairs = [(flat([partner(*x) for x in zip(at, by, shape)]), flat(at)) for at in places]
    return [pair[::-1] for pair in pairs] if back else pairs


def lanes(rows):
    return lax.broadcasted_iota(jnp.int32, (rows, STAT), 1)


def pack_stats(top, mass):
    high = mass.astype(BF16).astype(F32)
    return top + pltpu.roll(high, LANE, 1) + pltpu.roll(mass - high, 2 * LANE, 1)


def unpack_stats(packed):
    used = lanes(packed.shape[0]) < LANE
    mass = pltpu.roll(packed, STAT - LANE, 1) + pltpu.roll(packed, STAT - 2 * LANE, 1)
    return jnp.where(used, packed, 0.0), jnp.where(used, mass, 0.0)


def lane_of(head):
    return head % PACK * (LANE // PACK) + head // PACK


def whole_tiles(rows):
    return -(-rows // 16) * 16


def filled(ref, cols):
    rows, missing = ref.shape[0], whole_tiles(ref.shape[0]) - ref.shape[0]
    if not missing:
        return ref[:, cols]
    block = ref[:, cols].astype(F32)
    return jnp.concatenate([block, jnp.zeros((missing, block.shape[1]), F32)], axis=0).astype(BF16)


def attend_kernel(scale, bias_ref, q_refs, k_refs, v_refs, outs, top_acc, mass_acc):
    tok = q_refs[0].shape[0]
    rows = tok * len(q_refs)
    wide = PACK * HD
    pairs = q_refs[0].shape[1] // wide
    contract_last = (((1,), (1,)), ((), ()))
    contract_first = (((0,), (0,)), ((), ()))
    mine = [lax.broadcasted_iota(jnp.int32, (rows, wide), 1) // HD == k for k in range(PACK)]
    starts = [sum(whole_tiles(r.shape[0]) for r in k_refs[:j]) for j in range(len(k_refs))]
    top_acc[...] = jnp.zeros_like(top_acc)
    mass_acc[...] = jnp.zeros_like(mass_acc)

    def scores(i):
        cols = slice(i * wide, (i + 1) * wide)
        q = jnp.concatenate([ref[:, cols].astype(F32) for ref in q_refs], axis=0)
        q = jnp.concatenate([jnp.where(m, q, 0.0) for m in mine], axis=0).astype(BF16)
        return [
            lax.dot_general(filled(k, cols), q, contract_last, preferred_element_type=F32)
            for k in k_refs
        ]

    def weigh(i, parts):
        masked = []
        for start, score in zip(starts, parts):
            bias = bias_ref[start : start + score.shape[0], :]
            bias = jnp.concatenate([bias] * (PACK * rows // STAT), axis=1)
            masked.append(score * scale + bias)
        tops = [jnp.max(score, axis=0, keepdims=True) for score in masked]
        top = functools.reduce(jnp.maximum, tops).astype(BF16).astype(F32)
        parts = [jnp.exp2(score - top) for score in masked]
        masses = [jnp.sum(part, axis=0, keepdims=True) for part in parts]
        top_acc[i : i + 1, :] = top
        mass_acc[i : i + 1, :] = functools.reduce(jnp.add, masses)
        return [part.astype(BF16) for part in parts]

    def gather_values(i, weights):
        cols = slice(i * wide, (i + 1) * wide)
        both = functools.reduce(
            jnp.add,
            [
                lax.dot_general(w, filled(v, cols), contract_first, preferred_element_type=F32)
                for w, v in zip(weights, v_refs)
            ],
        )
        for k in range(PACK):
            one = both[k * rows : (k + 1) * rows, k * HD : (k + 1) * HD]
            at_head = (i * PACK + k) * HD
            for p, o_ref in enumerate(outs):
                o_ref[:, at_head : at_head + HD] = one[p * tok : (p + 1) * tok].astype(o_ref.dtype)

    ahead = [scores(i) for i in range(min(2, pairs))]
    weights = None
    for i in range(pairs):
        if i + 2 < pairs:
            ahead.append(scores(i + 2))
        done, weights = weights, weigh(i, ahead[i])
        if i > 0:
            gather_values(i - 1, done)
    gather_values(pairs - 1, weights)

    tops, masses = top_acc[...].T, mass_acc[...].T
    packed = 0.0
    for k in range(PACK):
        part = slice(k * rows, (k + 1) * rows)
        stats = pack_stats(tops[part], masses[part])
        packed += pltpu.roll(stats, k * (LANE // PACK), 1) if k else stats
    for p, o_ref in enumerate(outs):
        width = o_ref.shape[1]
        o_ref[:, width - STAT :] = packed[p * tok : (p + 1) * tok].astype(o_ref.dtype)


def attend(blocks, kinds, keys, values, bias):
    n, m = len(blocks), len(keys)
    tok, columns = blocks[0].shape
    total = sum(k.shape[0] for k in keys)

    def body(*refs):
        bias_ref, refs = refs[0], refs[1:]
        attend_kernel(
            math.log2(math.e) / math.sqrt(HD), bias_ref, refs[:n], refs[n : n + m],
            refs[n + m : n + 2 * m], refs[n + 2 * m : 2 * n + 2 * m], *refs[2 * n + 2 * m :],
        )

    return pl.pallas_call(
        body,
        in_specs=[pl.BlockSpec(memory_space=pltpu.VMEM)] * (1 + n + 2 * m),
        out_specs=[pl.BlockSpec(memory_space=pltpu.VMEM)] * n,
        out_shape=[jax.ShapeDtypeStruct((tok, columns + STAT), kind) for kind in kinds],
        scratch_shapes=[pltpu.VMEM((STAT, PACK * tok * n), F32)] * 2,
        compiler_params=pltpu.CompilerParams(vmem_limit_bytes=32 * 1024 * 1024),
        cost_estimate=pl.CostEstimate(
            flops=4 * n * tok * total * columns,
            bytes_accessed=4 * total * columns,
            transcendentals=n * tok * total * columns // HD,
        ),
        name="attend",
    )(bias, *blocks, *keys, *values)


def load(cached, fresh, victims, queries, cores, after):
    cache_rows, columns = cached[0].shape
    tok = queries.shape[0]
    padded = cache_rows + whole_tiles(tok)
    mask_rows = padded * cores
    blocks = cache_rows // BLK
    n = len(cached)

    def body(*refs):
        cached_refs, fresh_refs, (victims_ref, queries_ref) = refs[:n], refs[n : 2 * n], refs[2 * n : 2 * n + 2]
        refs = refs[2 * n + 3 :]
        outs, bias_ref, q_ref, refs = refs[:n], refs[n], refs[n + 1], refs[n + 2 :]
        tails, ids_ref, sems = refs[:n], refs[n], refs[n + 1]
        ids = pltpu.make_async_copy(victims_ref, ids_ref, sems.at[2 * n])
        rest = pltpu.make_async_copy(queries_ref, q_ref, sems.at[2 * n + 1])
        small = [
            pltpu.make_async_copy(src, dst, sems.at[i])
            for i, (src, dst) in enumerate(zip(fresh_refs, tails))
        ]
        large = [
            pltpu.make_async_copy(src, dst.at[pl.ds(0, cache_rows), :], sems.at[n + i])
            for i, (src, dst) in enumerate(zip(cached_refs, outs))
        ]
        for copy in [ids] + small + large + [rest]:
            copy.start()
        ids.wait()
        me = lax.axis_index("seq")
        core = lax.rem(me, cores)
        token = lax.broadcasted_iota(jnp.int32, (padded - cache_rows, STAT), 0)
        unused = jnp.where(token < tok, 0.0, NEG)
        bias_ref[cache_rows:padded, :] = unused
        for c in range(cores):
            start = padded + (c - 1) * cache_rows if c else 0
            first = (me - core + lax.rem(core + c, cores)) * blocks
            for block in range(blocks):
                hits = jnp.where(ids_ref[...] == first + block, 1.0, 0.0)
                hit = jnp.max(hits, axis=1, keepdims=True)
                gone = jnp.where(hit > 0.0, NEG, 0.0)
                at = start + block * BLK
                bias_ref[at : at + BLK, :] = jnp.broadcast_to(gone, (BLK, STAT))
            if c:
                at = padded + (cores - 1) * cache_rows + (c - 1) * (padded - cache_rows)
                bias_ref[at : at + padded - cache_rows, :] = unused
        for copy in small:
            copy.wait()
        for tail, out in zip(tails, outs):
            out[cache_rows:, :] = filled(tail, slice(0, columns))
        for copy in large + [rest]:
            copy.wait()

    held = (*cached, *fresh, victims, queries)
    return pl.pallas_call(
        body,
        in_specs=[pl.BlockSpec(memory_space=pltpu.HBM)] * len(held)
        + [pl.BlockSpec(memory_space=pl.ANY)],
        out_specs=[pl.BlockSpec(memory_space=pltpu.VMEM)] * (n + 2),
        out_shape=[jax.ShapeDtypeStruct((padded, columns), BF16)] * n
        + [jax.ShapeDtypeStruct((mask_rows, STAT), F32), jax.ShapeDtypeStruct(queries.shape, BF16)],
        scratch_shapes=[pltpu.VMEM(queries.shape, BF16)] * n
        + [pltpu.VMEM(victims.shape, jnp.int32), pltpu.SemaphoreType.DMA((2 * n + 2,))],
        compiler_params=pltpu.CompilerParams(vmem_limit_bytes=16 * 1024 * 1024),
        cost_estimate=pl.CostEstimate(
            flops=0, bytes_accessed=4 * n * cache_rows * columns, transcendentals=0
        ),
        name="load",
    )(*[pltpu.with_memory_space_constraint(x, pltpu.HBM) for x in held], after)


def merged(arrays, heads, last):
    columns = heads * HD
    stats = [unpack_stats(get(slice(columns, columns + STAT))) for get in arrays]
    top = functools.reduce(jnp.maximum, [t for t, _ in stats])
    weights = [jnp.exp2(t - top) for t, _ in stats]
    mass = functools.reduce(jnp.add, [w * m for w, (_, m) in zip(weights, stats)])
    if last:
        inverse = 1.0 / jnp.where(mass > 0.0, mass, 1.0)
        weights = [w * inverse for w in weights]
    for head in range(heads):
        cols = slice(head * HD, (head + 1) * HD)
        yield cols, functools.reduce(
            jnp.add, [get(cols) * w[:, lane_of(head) : lane_of(head) + 1] for get, w in zip(arrays, weights)]
        )
    if not last:
        yield slice(columns, columns + STAT), pack_stats(top, mass)


def getter(ref, *index):
    return lambda cols: ref[(*index, slice(None), cols)].astype(F32)


def merge_rows(ins, heads, pieces, kinds):
    rows, width = ins[0].shape
    per = rows // pieces

    def body(*refs):
        outs = refs[len(ins) :]
        for cols, total in merged([getter(r) for r in refs[: len(ins)]], heads, False):
            for j, out in enumerate(outs):
                out[:, cols] = total[j * per : (j + 1) * per].astype(out.dtype)

    return call_merge(body, ins, [jax.ShapeDtypeStruct((per, width), kind) for kind in kinds])


def finish(ins, heads):
    rows = ins[0].shape[0]

    def body(*refs):
        out = refs[len(ins)]
        for cols, total in merged([getter(r) for r in refs[: len(ins)]], heads, True):
            out[:, cols] = total.astype(out.dtype)

    return call_merge(body, ins, [jax.ShapeDtypeStruct((rows, heads * HD), BF16)])[0]


def join(pieces, after=()):
    rows = sum(p.shape[0] for p in pieces)

    def body(*refs):
        out = refs[-1]
        ins = [r[...].astype(F32) for r in refs[: len(pieces)]]
        out[...] = jnp.concatenate(ins, axis=0).astype(out.dtype)

    shape = jax.ShapeDtypeStruct((rows, pieces[0].shape[1]), pieces[0].dtype)
    return call_merge(body, pieces, [shape], after)[0]


def call_merge(body, ins, shapes, after=()):
    size = sum(math.prod(x.shape) for x in ins)
    return pl.pallas_call(
        body,
        in_specs=[pl.BlockSpec(memory_space=pltpu.VMEM)] * len(ins)
        + [pl.BlockSpec(memory_space=pl.ANY)] * len(after),
        out_specs=[pl.BlockSpec(memory_space=pltpu.VMEM)] * len(shapes),
        out_shape=shapes,
        compiler_params=pltpu.CompilerParams(vmem_limit_bytes=48 * 1024 * 1024),
        cost_estimate=pl.CostEstimate(flops=4 * size, bytes_accessed=4 * size, transcendentals=0),
        name="merge",
    )(*ins, *after)


def per_device(queries, new_keys, new_values, cache_keys, cache_values, victims):
    members = lax.axis_size("seq")
    shape = factors(members)
    a_n, b_n, c_n = shape
    heads = queries.shape[1] // HD
    tok = queries.shape[0]
    tok = queries.shape[0]

    def fetch(x, *by):
        return lax.ppermute(x, "seq", partner_perm(shape, by, False))

    def give(x, *by):
        return lax.ppermute(x, "seq", partner_perm(shape, by, True))

    def other_cores(x):
        return [fetch(x, 0, 0, c) for c in range(1, c_n)]

    def other_cores(x):
        return [fetch(x, 0, 0, c) for c in range(1, c_n)]

    far_first = [0, *range(a_n - 1, 0, -1)]
    other_keys, other_values = other_cores(cache_keys), other_cores(cache_values)
    line = [queries] + [fetch(queries, a, 0, 0) for a in far_first[1:]]
    own = queries
    if a_n > 2:
        own, line[1] = lax.optimization_barrier((own, line[1]))
    lines = [line] + [[fetch(x, 0, b, 0) for x in [own] + line[1:]] for b in range(1, b_n)]
    keys, values, bias, line[0] = load(
        (cache_keys, cache_values), (new_keys, new_values), victims[None], queries, c_n, lines[-1][0]
    )
    held, bias = lax.optimization_barrier(((new_keys, new_values), bias))
    other_fresh = [other_cores(x) for x in held]
    keys = [keys, *other_keys, *other_fresh[0]]
    values = [values, *other_values, *other_fresh[1]]
    at_once = next(n for n in range(b_n, 0, -1) if b_n % n == 0 and n * a_n * tok <= max(64, a_n * tok))
    sums = []
    for start in range(0, b_n, at_once):
        blocks = [x for pieces in lines[start : start + at_once] for x in pieces]
        kinds = [F32 if start * a_n + i < a_n else BF16 for i in range(len(blocks))]
        sums += attend(blocks, kinds, keys, values, bias)

    own = sums[:a_n]
    got = [[give(x, 0, b, 0) for x in sums[b * a_n : (b + 1) * a_n]] for b in range(1, b_n)]
    total = [[own[s]] + [pieces[s] for pieces in got] for s in range(a_n)]
    last = [
        give(merge_rows(total[s], heads, 1, [BF16])[0], far_first[s], 0, 0) for s in range(1, a_n)
    ]
    return finish([*merge_rows(total[0], heads, 1, [F32]), *last], heads)


def solution(mesh):
    rows = P(("groups", "seq"), None)
    return jax.shard_map(
        per_device,
        mesh=mesh,
        in_specs=(rows, rows, rows, rows, rows, P("groups")),
        out_specs=rows,
        check_vma=False,
    )
```

```python
import functools
import itertools
import math

import jax
import jax.numpy as jnp
from jax import lax
from jax.experimental import pallas as pl
from jax.experimental.pallas import tpu as pltpu
from jax.sharding import PartitionSpec as P

HD = 128
BLK = 128
STAT = 128
LANE = STAT // 3
PACK = 2
NEG = -1e30
F32 = jnp.float32
BF16 = jnp.bfloat16


def factors(members):
    cores = 2 if members % 2 == 0 else 1
    chips = members // cores
    far = next(a for a in range(1, chips + 1) if chips % a == 0 and a * a >= chips)
    return far, chips // far, cores


def partner(at, by, size):
    return at ^ by if size & (size - 1) == 0 else (at + by) % size


def partner_perm(shape, by, back):
    def flat(place):
        return functools.reduce(lambda at, kn: at * kn[1] + kn[0], zip(place, shape), 0)

    places = itertools.product(*map(range, shape))
    pairs = [(flat([partner(*x) for x in zip(at, by, shape)]), flat(at)) for at in places]
    return [pair[::-1] for pair in pairs] if back else pairs


def lanes(rows):
    return lax.broadcasted_iota(jnp.int32, (rows, STAT), 1)


def pack_stats(top, mass):
    high = mass.astype(BF16).astype(F32)
    return top + pltpu.roll(high, LANE, 1) + pltpu.roll(mass - high, 2 * LANE, 1)


def unpack_stats(packed):
    used = lanes(packed.shape[0]) < LANE
    mass = pltpu.roll(packed, STAT - LANE, 1) + pltpu.roll(packed, STAT - 2 * LANE, 1)
    return jnp.where(used, packed, 0.0), jnp.where(used, mass, 0.0)


def lane_of(head):
    return head % PACK * (LANE // PACK) + head // PACK


def attend_kernel(sizes, scale, bias_ref, q_ref, k_ref, v_ref, outs, top_acc, mass_acc):
    tile, steps, group, line_rows = sizes
    lines = len(outs)
    rows = tile * lines
    wide = PACK * HD
    contract_last = (((1,), (1,)), ((), ()))
    contract_first = (((0,), (0,)), ((), ()))
    mine = [lax.broadcasted_iota(jnp.int32, (rows, wide), 1) // HD == k for k in range(PACK)]

    def row_tile(r, carry):
        at = pl.ds(pl.multiple_of(r * tile, tile), tile)
        in_plane = [pl.ds(pl.multiple_of(b * line_rows + r * tile, tile), tile) for b in range(lines)]
        top_acc[...] = jnp.zeros_like(top_acc)
        mass_acc[...] = jnp.zeros_like(mass_acc)

        def heads_of(step, carry):
            def columns(i):
                return pl.ds(pl.multiple_of((step * group + i) * wide, HD), wide)

            def scores(i):
                cols = columns(i)
                q = jnp.concatenate([q_ref[rs, cols] for rs in in_plane], axis=0)
                q = jnp.concatenate([jnp.where(m, q, jnp.zeros_like(q)) for m in mine], axis=0)
                return lax.dot_general(k_ref[:, cols], q, contract_last, preferred_element_type=F32)

            def weigh(i, score):
                bias = jnp.concatenate([bias_ref[...]] * (PACK * rows // STAT), axis=1)
                score = score * scale + bias
                top = jnp.max(score, axis=0, keepdims=True).astype(BF16).astype(F32)
                score = jnp.exp2(score - top)
                top_acc[pl.ds(step * group + i, 1), :] = top
                mass_acc[pl.ds(step * group + i, 1), :] = jnp.sum(score, axis=0, keepdims=True)
                return score.astype(BF16)

            def gather_values(i, weights):
                both = lax.dot_general(
                    weights, v_ref[:, columns(i)], contract_first, preferred_element_type=F32
                )
                for k in range(PACK):
                    at_head = ((step * group + i) * PACK + k) * HD
                    cols = pl.ds(pl.multiple_of(at_head, HD), HD)
                    for b, o_ref in enumerate(outs):
                        start = k * rows + b * tile
                        one = both[start : start + tile, k * HD : (k + 1) * HD]
                        o_ref[at, cols] = one.astype(o_ref.dtype)

            ahead = [scores(i) for i in range(min(2, group))]
            weights = None
            for i in range(group):
                if i + 2 < group:
                    ahead.append(scores(i + 2))
                done, weights = weights, weigh(i, ahead[i])
                if i > 0:
                    gather_values(i - 1, done)
            gather_values(group - 1, weights)
            return carry

        lax.fori_loop(0, steps, heads_of, 0)
        tops, masses = top_acc[...].T, mass_acc[...].T
        packed = 0.0
        for k in range(PACK):
            part = slice(k * rows, (k + 1) * rows)
            stats = pack_stats(tops[part], masses[part])
            packed += pltpu.roll(stats, k * (LANE // PACK), 1) if k else stats
        for b, o_ref in enumerate(outs):
            width = o_ref.shape[1]
            o_ref[at, width - STAT :] = packed[b * tile : (b + 1) * tile].astype(o_ref.dtype)
        return carry

    lax.fori_loop(0, line_rows // tile, row_tile, 0)


def attend(plane, lines, kind, keys, values, bias, after=(), extra=0):
    rows, columns = plane.shape[0] // lines, plane.shape[1]
    heads = columns // HD
    pairs = heads // PACK
    group = next(g for g in (10, 5, 4, 3, 2, 1) if pairs % g == 0)
    tile = next(t for t in (32, 16, rows) if rows % t == 0)
    width = columns + STAT
    more = -(-extra // 16) * 16
    scale = math.log2(math.e) / math.sqrt(HD)

    def body(*refs):
        work = refs[4 + len(after) :]
        attend_kernel(
            (tile, pairs // group, group, rows), scale, *refs[:4], work[:lines], *work[lines:]
        )
        if extra:
            for home, out in list(zip(refs[4:], work[:lines]))[1:]:
                block = home[:extra, :].astype(F32)
                block = jnp.concatenate([block, jnp.zeros((more - extra, width), F32)], axis=0)
                out[rows:, :] = block.astype(out.dtype)

    return pl.pallas_call(
        body,
        in_specs=[pl.BlockSpec(memory_space=pltpu.VMEM)] * 4
        + [pl.BlockSpec(memory_space=pltpu.VMEM if extra else pl.ANY)] * len(after),
        out_specs=[pl.BlockSpec(memory_space=pltpu.VMEM)] * lines,
        out_shape=[
            jax.ShapeDtypeStruct((rows + (more if b else 0), width), kind) for b in range(lines)
        ],
        scratch_shapes=[pltpu.VMEM((STAT, PACK * tile * lines), F32)] * 2,
        compiler_params=pltpu.CompilerParams(vmem_limit_bytes=40 * 1024 * 1024),
        cost_estimate=pl.CostEstimate(
            flops=4 * lines * rows * keys.shape[0] * columns,
            bytes_accessed=4 * keys.shape[0] * columns,
            transcendentals=lines * rows * keys.shape[0] * heads,
        ),
        name="attend",
    )(bias, plane, keys, values, *after)


def load(cached, fresh, victims, queries, after):
    cache_rows, columns = cached[0].shape
    tok = fresh[0].shape[0]
    padded = cache_rows + -(-tok // 16) * 16
    n = len(cached)

    def body(*refs):
        cached_refs, fresh_refs, victims_ref, queries_ref = refs[:n], refs[n : 2 * n], *refs[2 * n : 2 * n + 2]
        refs = refs[2 * n + 3 :]
        outs, bias_ref, q_ref, tails, ids_ref, sems = (
            refs[:n], refs[n], refs[n + 1], refs[n + 2 : 2 * n + 2], *refs[2 * n + 2 :]
        )
        ids = pltpu.make_async_copy(victims_ref, ids_ref, sems.at[1, n])
        rest = pltpu.make_async_copy(queries_ref, q_ref, sems.at[0, n])
        small = [
            pltpu.make_async_copy(src, dst, sems.at[1, i])
            for i, (src, dst) in enumerate(zip(fresh_refs, tails))
        ]
        large = [
            pltpu.make_async_copy(src, dst.at[pl.ds(0, cache_rows), :], sems.at[0, i])
            for i, (src, dst) in enumerate(zip(cached_refs, outs))
        ]
        for copy in [ids] + small + large + [rest]:
            copy.start()
        ids.wait()
        blocks = cache_rows // BLK
        first = lax.axis_index("seq") * blocks
        for block in range(blocks):
            hits = jnp.where(ids_ref[...] == first + block, 1.0, 0.0)
            hit = jnp.max(hits, axis=1, keepdims=True)
            gone = jnp.where(hit > 0.0, NEG, 0.0)
            bias_ref[block * BLK : (block + 1) * BLK, :] = jnp.broadcast_to(gone, (BLK, STAT))
        token = lax.broadcasted_iota(jnp.int32, (padded - cache_rows, STAT), 0)
        bias_ref[cache_rows:, :] = jnp.where(token < tok, 0.0, NEG)
        for copy, tail, out in zip(small, tails, outs):
            copy.wait()
            zeros = jnp.zeros((padded - cache_rows - tok, columns), F32)
            rows = jnp.concatenate([tail[...].astype(F32), zeros], axis=0)
            out[cache_rows:, :] = rows.astype(out.dtype)
        for copy in large + [rest]:
            copy.wait()

    in_hbm = pl.BlockSpec(memory_space=pltpu.HBM)
    held = (*cached, *fresh, victims, queries)
    return pl.pallas_call(
        body,
        in_specs=[in_hbm] * len(held) + [pl.BlockSpec(memory_space=pl.ANY)],
        out_specs=[pl.BlockSpec(memory_space=pltpu.VMEM)] * (n + 2),
        out_shape=[jax.ShapeDtypeStruct((padded, columns), BF16)] * n
        + [jax.ShapeDtypeStruct((padded, STAT), F32), jax.ShapeDtypeStruct(queries.shape, BF16)],
        scratch_shapes=[pltpu.VMEM(x.shape, BF16) for x in fresh]
        + [pltpu.VMEM(victims.shape, jnp.int32), pltpu.SemaphoreType.DMA((2, n + 1))],
        compiler_params=pltpu.CompilerParams(vmem_limit_bytes=24 * 1024 * 1024),
        cost_estimate=pl.CostEstimate(
            flops=0, bytes_accessed=4 * n * cache_rows * columns, transcendentals=0
        ),
        name="load",
    )(*[pltpu.with_memory_space_constraint(x, pltpu.HBM) for x in held], after)


def merged(arrays, heads, last):
    columns = heads * HD
    stats = [unpack_stats(get(slice(columns, columns + STAT))) for get in arrays]
    top = functools.reduce(jnp.maximum, [t for t, _ in stats])
    weights = [jnp.exp2(t - top) for t, _ in stats]
    mass = functools.reduce(jnp.add, [w * m for w, (_, m) in zip(weights, stats)])
    if last:
        inverse = 1.0 / jnp.where(mass > 0.0, mass, 1.0)
        weights = [w * inverse for w in weights]
    for head in range(heads):
        cols = slice(head * HD, (head + 1) * HD)
        yield cols, functools.reduce(
            jnp.add, [get(cols) * w[:, lane_of(head) : lane_of(head) + 1] for get, w in zip(arrays, weights)]
        )
    if not last:
        yield slice(columns, columns + STAT), pack_stats(top, mass)


def getter(ref, *index):
    return lambda cols: ref[(*index, slice(None), cols)].astype(F32)


def merge_rows(ins, heads, pieces, kinds):
    rows, width = ins[0].shape
    per = rows // pieces

    def body(*refs):
        outs = refs[len(ins) :]
        for cols, total in merged([getter(r) for r in refs[: len(ins)]], heads, False):
            for j, out in enumerate(outs):
                out[:, cols] = total[j * per : (j + 1) * per].astype(out.dtype)

    return call_merge(body, ins, [jax.ShapeDtypeStruct((per, width), kind) for kind in kinds])


def merge_line(home, got, away, heads, tok):
    rows, width = home.shape
    per = -(-tok // 16) * 16

    def body(home_ref, got_ref, away_ref, *outs):
        get = lambda ref, start, n: lambda cols: ref[start : start + n, cols].astype(F32)
        for cols, total in merged([get(home_ref, 0, rows), get(got_ref, 0, rows)], heads, False):
            for j, out in enumerate(outs[:-1]):
                out[:, cols] = total[j * tok : (j + 1) * tok].astype(out.dtype)
        for cols, total in merged([get(away_ref, 0, per), get(got_ref, rows, per)], heads, False):
            outs[-1][:, cols] = total[:tok].astype(outs[-1].dtype)

    shapes = [jax.ShapeDtypeStruct((tok, width), BF16)] * (rows // tok + 1)
    return call_merge(body, [home, got, away], shapes)


def merge_own(own, last, first, cores, heads):
    n = len(last)

    def body(*refs):
        out = refs[-1]
        on_last = lax.rem(lax.axis_index("seq"), cores) == cores - 1

        def either(one, other):
            return lambda cols: jnp.where(on_last, one[:, cols], other[:, cols]).astype(F32)

        parts = [getter(refs[0])] + [either(refs[1 + i], refs[1 + n + i]) for i in range(n)]
        for cols, total in merged(parts, heads, False):
            out[:, cols] = total.astype(out.dtype)

    return call_merge(body, [own, *last, *first], [jax.ShapeDtypeStruct(own.shape, F32)])[0]


def finish(ins, heads):
    rows = ins[0].shape[0]

    def body(*refs):
        out = refs[len(ins)]
        for cols, total in merged([getter(r) for r in refs[: len(ins)]], heads, True):
            out[:, cols] = total.astype(out.dtype)

    return call_merge(body, ins, [jax.ShapeDtypeStruct((rows, heads * HD), BF16)])[0]


def join(pieces, after=()):
    rows = sum(p.shape[0] for p in pieces)

    def body(*refs):
        out = refs[-1]
        ins = [r[...].astype(F32) for r in refs[: len(pieces)]]
        out[...] = jnp.concatenate(ins, axis=0).astype(out.dtype)

    shape = jax.ShapeDtypeStruct((rows, pieces[0].shape[1]), pieces[0].dtype)
    return call_merge(body, pieces, [shape], after)[0]


def call_merge(body, ins, shapes, after=()):
    size = sum(math.prod(x.shape) for x in ins)
    return pl.pallas_call(
        body,
        in_specs=[pl.BlockSpec(memory_space=pltpu.VMEM)] * len(ins)
        + [pl.BlockSpec(memory_space=pl.ANY)] * len(after),
        out_specs=[pl.BlockSpec(memory_space=pltpu.VMEM)] * len(shapes),
        out_shape=shapes,
        compiler_params=pltpu.CompilerParams(vmem_limit_bytes=48 * 1024 * 1024),
        cost_estimate=pl.CostEstimate(flops=4 * size, bytes_accessed=4 * size, transcendentals=0),
        name="merge",
    )(*ins, *after)


def per_device(queries, new_keys, new_values, cache_keys, cache_values, victims):
    members = lax.axis_size("seq")
    shape = factors(members)
    a_n, b_n, c_n = shape
    heads = queries.shape[1] // HD
    tok = queries.shape[0]
    tok = queries.shape[0]

    def fetch(x, *by):
        return lax.ppermute(x, "seq", partner_perm(shape, by, False))

    def give(x, *by):
        return lax.ppermute(x, "seq", partner_perm(shape, by, True))

    far_first = [0, *range(a_n - 1, 0, -1)]
    line = [queries] + [fetch(queries, a, 0, 0) for a in far_first[1:]]
    lines = [line] + [[fetch(x, 0, b, 0) for x in line] for b in range(1, b_n)]
    keys, values, bias, line[0] = load(
        (cache_keys, cache_values), (new_keys, new_values), victims[None], queries, line[-1]
    )
    plane = join([x for pieces in lines for x in pieces])
    planes = [plane] + [fetch(plane, 0, 0, c) for c in range(1, c_n)]
    shared = c_n == 2 and b_n > 1
    sums = []
    for c, rows in enumerate(planes):
        extra = tok if c and shared else 0
        sums += attend(rows, b_n, BF16 if c else F32, keys, values, bias, sums[:b_n], extra)

    def over_cores(b, kind):
        got = [give(sums[c * b_n + b], 0, 0, c) for c in range(1, c_n)]
        if b and shared:
            return merge_line(sums[b], got[0], sums[b_n + b], heads, tok)
        return merge_rows([sums[b]] + got, heads, a_n, [kind] * a_n)

    def give_from_last(x, by, core):
        pairs = partner_perm(shape, (0, by, 0), True)
        pairs = [(i, j - j % c_n + core) for i, j in pairs if i % c_n == c_n - 1]
        return lax.ppermute(x, "seq", pairs)

    got, first = [], [[], []]
    for b in range(1, b_n):
        pieces = over_cores(b, BF16)
        start = 1 if shared else 0
        got.append([None] * start + [give(x, 0, b, 0) for x in pieces[start:a_n]])
        if shared:
            first[0].append(give_from_last(pieces[0], b, c_n - 1))
            first[1].append(give_from_last(pieces[a_n], b, 0))
    own = over_cores(0, F32)
    last = []
    for s in range(1, a_n):
        total = [own[s]] + [pieces[s] for pieces in got]
        last.append(give(merge_rows(total, heads, 1, [BF16])[0], far_first[s], 0, 0))
    if shared:
        mine = merge_own(own[0], *first, c_n, heads)
    else:
        mine = merge_rows([own[0]] + [pieces[0] for pieces in got], heads, 1, [F32])[0]
    return finish([mine, *last], heads)


def solution(mesh):
    rows = P(("groups", "seq"), None)
    return jax.shard_map(
        per_device,
        mesh=mesh,
        in_specs=(rows, rows, rows, rows, rows, P("groups")),
        out_specs=rows,
        check_vma=False,
    )
```

```python
import functools
import itertools
import math

import jax
import jax.numpy as jnp
from jax import lax
from jax.experimental import pallas as pl
from jax.experimental.pallas import tpu as pltpu
from jax.sharding import PartitionSpec as P

HD = 128
BLK = 128
STAT = 128
LANE = STAT // 3
PACK = 2
NEG = -1e30
F32 = jnp.float32
BF16 = jnp.bfloat16


def factors(members):
    cores = 2 if members % 2 == 0 else 1
    chips = members // cores
    far = next(a for a in range(1, chips + 1) if chips % a == 0 and a * a >= chips)
    return far, chips // far, cores


def partner(at, by, size):
    return at ^ by if size & (size - 1) == 0 else (at + by) % size


def partner_perm(shape, by, back):
    def flat(place):
        return functools.reduce(lambda at, kn: at * kn[1] + kn[0], zip(place, shape), 0)

    places = itertools.product(*map(range, shape))
    pairs = [(flat([partner(*x) for x in zip(at, by, shape)]), flat(at)) for at in places]
    return [pair[::-1] for pair in pairs] if back else pairs


def lanes(rows):
    return lax.broadcasted_iota(jnp.int32, (rows, STAT), 1)


def pack_stats(top, mass):
    high = mass.astype(BF16).astype(F32)
    return top + pltpu.roll(high, LANE, 1) + pltpu.roll(mass - high, 2 * LANE, 1)


def unpack_stats(packed):
    used = lanes(packed.shape[0]) < LANE
    mass = pltpu.roll(packed, STAT - LANE, 1) + pltpu.roll(packed, STAT - 2 * LANE, 1)
    return jnp.where(used, packed, 0.0), jnp.where(used, mass, 0.0)


def lane_of(head):
    return head % PACK * (LANE // PACK) + head // PACK


def loop(steps, body):
    if steps == 1:
        body(0, 0)
    else:
        lax.fori_loop(0, steps, body, 0)


def span(start, size, unit):
    return pl.ds(start if isinstance(start, int) else pl.multiple_of(start, unit), size)


def attend_kernel(sizes, scale, bias_ref, q_ref, k_ref, v_ref, outs, top_acc, mass_acc):
    tile, steps, group = sizes
    lines = len(outs)
    rows = tile * lines
    line_rows = outs[0].shape[0]
    wide = PACK * HD
    contract_last = (((1,), (1,)), ((), ()))
    contract_first = (((0,), (0,)), ((), ()))
    mine = [lax.broadcasted_iota(jnp.int32, (rows, wide), 1) // HD == k for k in range(PACK)]

    def row_tile(r, carry):
        at = span(r * tile, tile, tile)
        in_plane = [span(b * line_rows + r * tile, tile, tile) for b in range(lines)]
        top_acc[...] = jnp.zeros_like(top_acc)
        mass_acc[...] = jnp.zeros_like(mass_acc)

        def heads_of(step, carry):
            def columns(i):
                return span((step * group + i) * wide, wide, HD)

            def scores(i):
                cols = columns(i)
                q = jnp.concatenate([q_ref[rs, cols] for rs in in_plane], axis=0)
                q = jnp.concatenate([jnp.where(m, q, jnp.zeros_like(q)) for m in mine], axis=0)
                return lax.dot_general(k_ref[:, cols], q, contract_last, preferred_element_type=F32)

            def weigh(i, score):
                bias = jnp.concatenate([bias_ref[...]] * (PACK * rows // STAT), axis=1)
                score = score * scale + bias
                top = jnp.max(score, axis=0, keepdims=True).astype(BF16).astype(F32)
                score = jnp.exp2(score - top)
                top_acc[pl.ds(step * group + i, 1), :] = top
                mass_acc[pl.ds(step * group + i, 1), :] = jnp.sum(score, axis=0, keepdims=True)
                return score.astype(BF16)

            def gather_values(i, weights):
                both = lax.dot_general(
                    weights, v_ref[:, columns(i)], contract_first, preferred_element_type=F32
                )
                for k in range(PACK):
                    cols = span(((step * group + i) * PACK + k) * HD, HD, HD)
                    for b, o_ref in enumerate(outs):
                        start = k * rows + b * tile
                        one = both[start : start + tile, k * HD : (k + 1) * HD]
                        o_ref[at, cols] = one.astype(o_ref.dtype)

            ahead = [scores(i) for i in range(min(2, group))]
            weights = None
            for i in range(group):
                if i + 2 < group:
                    ahead.append(scores(i + 2))
                done, weights = weights, weigh(i, ahead[i])
                if i > 0:
                    gather_values(i - 1, done)
            gather_values(group - 1, weights)
            return carry

        loop(steps, heads_of)
        tops, masses = top_acc[...].T, mass_acc[...].T
        packed = 0.0
        for k in range(PACK):
            part = slice(k * rows, (k + 1) * rows)
            stats = pack_stats(tops[part], masses[part])
            packed += pltpu.roll(stats, k * (LANE // PACK), 1) if k else stats
        for b, o_ref in enumerate(outs):
            width = o_ref.shape[1]
            o_ref[at, width - STAT :] = packed[b * tile : (b + 1) * tile].astype(o_ref.dtype)
        return carry

    loop(line_rows // tile, row_tile)


def attend(plane, lines, kind, keys, values, bias, after=()):
    rows, columns = plane.shape[0] // lines, plane.shape[1]
    heads = columns // HD
    pairs = heads // PACK
    group = next(g for g in (10, 5, 4, 3, 2, 1) if pairs % g == 0)
    tile = next(t for t in (32, 16, rows) if rows % t == 0)
    width = columns + STAT
    scale = math.log2(math.e) / math.sqrt(HD)

    def body(*refs):
        work = refs[4 + len(after) :]
        attend_kernel(
            (tile, pairs // group, group), scale, *refs[:4], work[:lines], *work[lines:]
        )

    return pl.pallas_call(
        body,
        in_specs=[pl.BlockSpec(memory_space=pltpu.VMEM)] * 4
        + [pl.BlockSpec(memory_space=pl.ANY)] * len(after),
        out_specs=[pl.BlockSpec(memory_space=pltpu.VMEM)] * lines,
        out_shape=[jax.ShapeDtypeStruct((rows, width), kind)] * lines,
        scratch_shapes=[pltpu.VMEM((STAT, PACK * tile * lines), F32)] * 2,
        compiler_params=pltpu.CompilerParams(vmem_limit_bytes=40 * 1024 * 1024),
        cost_estimate=pl.CostEstimate(
            flops=4 * lines * rows * keys.shape[0] * columns,
            bytes_accessed=4 * keys.shape[0] * columns,
            transcendentals=lines * rows * keys.shape[0] * heads,
        ),
        name="attend",
    )(bias, plane, keys, values, *after)


def load(cached, fresh, victims, queries, after):
    cache_rows, columns = cached[0].shape
    tok = fresh[0].shape[0]
    padded = cache_rows + -(-tok // 16) * 16
    n = len(cached)

    def body(*refs):
        cached_refs, fresh_refs, victims_ref, queries_ref = refs[:n], refs[n : 2 * n], *refs[2 * n : 2 * n + 2]
        refs = refs[2 * n + 3 :]
        outs, bias_ref, q_ref, tails, ids_ref, sems = (
            refs[:n], refs[n], refs[n + 1], refs[n + 2 : 2 * n + 2], *refs[2 * n + 2 :]
        )
        ids = pltpu.make_async_copy(victims_ref, ids_ref, sems.at[1, n])
        rest = pltpu.make_async_copy(queries_ref, q_ref, sems.at[0, n])
        small = [
            pltpu.make_async_copy(src, dst, sems.at[1, i])
            for i, (src, dst) in enumerate(zip(fresh_refs, tails))
        ]
        large = [
            pltpu.make_async_copy(src, dst.at[pl.ds(0, cache_rows), :], sems.at[0, i])
            for i, (src, dst) in enumerate(zip(cached_refs, outs))
        ]
        for copy in [ids] + small + large + [rest]:
            copy.start()
        ids.wait()
        blocks = cache_rows // BLK
        first = lax.axis_index("seq") * blocks
        for block in range(blocks):
            hits = jnp.where(ids_ref[...] == first + block, 1.0, 0.0)
            hit = jnp.max(hits, axis=1, keepdims=True)
            gone = jnp.where(hit > 0.0, NEG, 0.0)
            bias_ref[block * BLK : (block + 1) * BLK, :] = jnp.broadcast_to(gone, (BLK, STAT))
        token = lax.broadcasted_iota(jnp.int32, (padded - cache_rows, STAT), 0)
        bias_ref[cache_rows:, :] = jnp.where(token < tok, 0.0, NEG)
        for copy, tail, out in zip(small, tails, outs):
            copy.wait()
            zeros = jnp.zeros((padded - cache_rows - tok, columns), F32)
            rows = jnp.concatenate([tail[...].astype(F32), zeros], axis=0)
            out[cache_rows:, :] = rows.astype(out.dtype)
        for copy in large + [rest]:
            copy.wait()

    in_hbm = pl.BlockSpec(memory_space=pltpu.HBM)
    held = (*cached, *fresh, victims, queries)
    return pl.pallas_call(
        body,
        in_specs=[in_hbm] * len(held) + [pl.BlockSpec(memory_space=pl.ANY)],
        out_specs=[pl.BlockSpec(memory_space=pltpu.VMEM)] * (n + 2),
        out_shape=[jax.ShapeDtypeStruct((padded, columns), BF16)] * n
        + [jax.ShapeDtypeStruct((padded, STAT), F32), jax.ShapeDtypeStruct(queries.shape, BF16)],
        scratch_shapes=[pltpu.VMEM(x.shape, BF16) for x in fresh]
        + [pltpu.VMEM(victims.shape, jnp.int32), pltpu.SemaphoreType.DMA((2, n + 1))],
        compiler_params=pltpu.CompilerParams(vmem_limit_bytes=24 * 1024 * 1024),
        cost_estimate=pl.CostEstimate(
            flops=0, bytes_accessed=4 * n * cache_rows * columns, transcendentals=0
        ),
        name="load",
    )(*[pltpu.with_memory_space_constraint(x, pltpu.HBM) for x in held], after)


def merged(arrays, heads, last):
    columns = heads * HD
    stats = [unpack_stats(get(slice(columns, columns + STAT))) for get in arrays]
    top = functools.reduce(jnp.maximum, [t for t, _ in stats])
    weights = [jnp.exp2(t - top) for t, _ in stats]
    mass = functools.reduce(jnp.add, [w * m for w, (_, m) in zip(weights, stats)])
    if last:
        inverse = 1.0 / jnp.where(mass > 0.0, mass, 1.0)
        weights = [w * inverse for w in weights]
    for head in range(heads):
        cols = slice(head * HD, (head + 1) * HD)
        yield cols, functools.reduce(
            jnp.add, [get(cols) * w[:, lane_of(head) : lane_of(head) + 1] for get, w in zip(arrays, weights)]
        )
    if not last:
        yield slice(columns, columns + STAT), pack_stats(top, mass)


def getter(ref, *index):
    return lambda cols: ref[(*index, slice(None), cols)].astype(F32)


def merge_rows(ins, heads, pieces, kinds):
    rows, width = ins[0].shape
    per = rows // pieces

    def body(*refs):
        outs = refs[len(ins) :]
        for cols, total in merged([getter(r) for r in refs[: len(ins)]], heads, False):
            for j, out in enumerate(outs):
                out[:, cols] = total[j * per : (j + 1) * per].astype(out.dtype)

    return call_merge(body, ins, [jax.ShapeDtypeStruct((per, width), kind) for kind in kinds])


def merge_piece(lines, s, pieces, heads, tok, kind):
    rows, width = tok, lines[0].shape[1]

    def rows_of(ref):
        start = s * rows
        if ref.dtype == F32:
            return lambda cols: ref[start : start + rows, cols]
        first = start // 16 * 16
        last = min(-(-(start + rows) // 16) * 16, ref.shape[0])
        return lambda cols: ref[first:last, cols].astype(F32)[start - first :][:rows]

    def body(*refs):
        out = refs[-1]
        parts = [rows_of(r) for r in refs[: len(lines)]] + [getter(r) for r in refs[len(lines) : -1]]
        for cols, total in merged(parts, heads, False):
            out[:, cols] = total.astype(out.dtype)

    return call_merge(body, [*lines, *pieces], [jax.ShapeDtypeStruct((rows, width), kind)])[0]


def finish(ins, heads):
    rows = ins[0].shape[0]

    def body(*refs):
        out = refs[len(ins)]
        for cols, total in merged([getter(r) for r in refs[: len(ins)]], heads, True):
            out[:, cols] = total.astype(out.dtype)

    return call_merge(body, ins, [jax.ShapeDtypeStruct((rows, heads * HD), BF16)])[0]


def join(pieces, after=()):
    rows = sum(p.shape[0] for p in pieces)

    def body(*refs):
        out = refs[-1]
        ins = [r[...].astype(F32) for r in refs[: len(pieces)]]
        out[...] = jnp.concatenate(ins, axis=0).astype(out.dtype)

    shape = jax.ShapeDtypeStruct((rows, pieces[0].shape[1]), pieces[0].dtype)
    return call_merge(body, pieces, [shape], after)[0]


def call_merge(body, ins, shapes, after=()):
    size = sum(math.prod(x.shape) for x in ins)
    return pl.pallas_call(
        body,
        in_specs=[pl.BlockSpec(memory_space=pltpu.VMEM)] * len(ins)
        + [pl.BlockSpec(memory_space=pl.ANY)] * len(after),
        out_specs=[pl.BlockSpec(memory_space=pltpu.VMEM)] * len(shapes),
        out_shape=shapes,
        compiler_params=pltpu.CompilerParams(vmem_limit_bytes=48 * 1024 * 1024),
        cost_estimate=pl.CostEstimate(flops=4 * size, bytes_accessed=4 * size, transcendentals=0),
        name="merge",
    )(*ins, *after)


def per_device(queries, new_keys, new_values, cache_keys, cache_values, victims):
    members = lax.axis_size("seq")
    shape = factors(members)
    a_n, b_n, c_n = shape
    heads = queries.shape[1] // HD
    tok = queries.shape[0]

    def fetch(x, *by):
        return lax.ppermute(x, "seq", partner_perm(shape, by, False))

    def give(x, *by):
        return lax.ppermute(x, "seq", partner_perm(shape, by, True))

    far_first = [0, *range(a_n - 1, 0, -1)]
    line = [queries] + [fetch(queries, a, 0, 0) for a in far_first[1:]]
    lines = [line] + [[fetch(x, 0, b, 0) for x in line] for b in range(1, b_n)]
    keys, values, bias, line[0] = load(
        (cache_keys, cache_values), (new_keys, new_values), victims[None], queries, line[-1]
    )
    plane = join([x for pieces in lines for x in pieces])
    planes = [plane] + [fetch(plane, 0, 0, c) for c in range(1, c_n)]
    sums = []
    for c, rows in enumerate(planes):
        sums += attend(rows, b_n, BF16 if c else F32, keys, values, bias, sums[:1])

    def over_cores(b, kind):
        got = [give(sums[c * b_n + b], 0, 0, c) for c in range(1, c_n)]
        return merge_rows([sums[b]] + got, heads, a_n, [kind] * a_n)

    got = [[give(x, 0, b, 0) for x in over_cores(b, BF16)] for b in range(1, b_n)]
    own = [sums[0]] + [give(sums[c * b_n], 0, 0, c) for c in range(1, c_n)]

    def total(s, kind):
        return merge_piece(own, s, [pieces[s] for pieces in got], heads, tok, kind)

    last = [give(total(s, BF16), far_first[s], 0, 0) for s in range(1, a_n)]
    return finish([total(0, F32), *last], heads)


def solution(mesh):
    rows = P(("groups", "seq"), None)
    return jax.shard_map(
        per_device,
        mesh=mesh,
        in_specs=(rows, rows, rows, rows, rows, P("groups")),
        out_specs=rows,
        check_vma=False,
    )
```

```python
import functools
import itertools
import math

import jax
import jax.numpy as jnp
from jax import lax
from jax.experimental import pallas as pl
from jax.experimental.pallas import tpu as pltpu
from jax.sharding import PartitionSpec as P

HD = 128
BLK = 128
STAT = 128
LANE = STAT // 3
PACK = 2
NEG = -1e30
F32 = jnp.float32
BF16 = jnp.bfloat16


def factors(members):
    cores = 2 if members % 2 == 0 else 1
    chips = members // cores
    far = next(a for a in range(1, chips + 1) if chips % a == 0 and a * a >= chips)
    return far, chips // far, cores


def partner(at, by, size):
    return at ^ by if size & (size - 1) == 0 else (at + by) % size


def partner_perm(shape, by, back):
    def flat(place):
        return functools.reduce(lambda at, kn: at * kn[1] + kn[0], zip(place, shape), 0)

    places = itertools.product(*map(range, shape))
    pairs = [(flat([partner(*x) for x in zip(at, by, shape)]), flat(at)) for at in places]
    return [pair[::-1] for pair in pairs] if back else pairs


def lanes(rows):
    return lax.broadcasted_iota(jnp.int32, (rows, STAT), 1)


def pack_stats(top, mass):
    high = mass.astype(BF16).astype(F32)
    return top + pltpu.roll(high, LANE, 1) + pltpu.roll(mass - high, 2 * LANE, 1)


def unpack_stats(packed):
    used = lanes(packed.shape[0]) < LANE
    mass = pltpu.roll(packed, STAT - LANE, 1) + pltpu.roll(packed, STAT - 2 * LANE, 1)
    return jnp.where(used, packed, 0.0), jnp.where(used, mass, 0.0)


def lane_of(head):
    return head % PACK * (LANE // PACK) + head // PACK


def attend_kernel(sizes, scale, bias_ref, q_ref, k_ref, v_ref, outs, top_acc, mass_acc):
    tile, steps, group = sizes
    lines = len(outs)
    rows = tile * lines
    line_rows = outs[0].shape[0]
    wide = PACK * HD
    contract_last = (((1,), (1,)), ((), ()))
    contract_first = (((0,), (0,)), ((), ()))
    mine = [lax.broadcasted_iota(jnp.int32, (rows, wide), 1) // HD == k for k in range(PACK)]

    def row_tile(r, carry):
        at = pl.ds(pl.multiple_of(r * tile, tile), tile)
        in_plane = [pl.ds(pl.multiple_of(b * line_rows + r * tile, tile), tile) for b in range(lines)]
        top_acc[...] = jnp.zeros_like(top_acc)
        mass_acc[...] = jnp.zeros_like(mass_acc)

        def heads_of(step, carry):
            def columns(i):
                return pl.ds(pl.multiple_of((step * group + i) * wide, HD), wide)

            def scores(i):
                cols = columns(i)
                q = jnp.concatenate([q_ref[rs, cols] for rs in in_plane], axis=0)
                q = jnp.concatenate([jnp.where(m, q, jnp.zeros_like(q)) for m in mine], axis=0)
                return lax.dot_general(k_ref[:, cols], q, contract_last, preferred_element_type=F32)

            def masked(score):
                bias = jnp.concatenate([bias_ref[...]] * (PACK * rows // STAT), axis=1)
                score = score * scale + bias
                top = jnp.max(score, axis=0, keepdims=True).astype(BF16).astype(F32)
                return score, top

            def weigh(i, score, top):
                score = jnp.exp2(score - top)
                top_acc[pl.ds(step * group + i, 1), :] = top
                mass_acc[pl.ds(step * group + i, 1), :] = jnp.sum(score, axis=0, keepdims=True)
                return score.astype(BF16)

            def gather_values(i, weights):
                both = lax.dot_general(
                    weights, v_ref[:, columns(i)], contract_first, preferred_element_type=F32
                )
                for k in range(PACK):
                    at_head = ((step * group + i) * PACK + k) * HD
                    cols = pl.ds(pl.multiple_of(at_head, HD), HD)
                    for b, o_ref in enumerate(outs):
                        start = k * rows + b * tile
                        one = both[start : start + tile, k * HD : (k + 1) * HD]
                        o_ref[at, cols] = one.astype(o_ref.dtype)

            score, top, weights = {}, {}, {}
            for t in range(-3, group + 1):
                if 0 <= t + 3 < group:
                    score[t + 3] = scores(t + 3)
                if 0 <= t + 1 < group:
                    score[t + 1], top[t + 1] = masked(score[t + 1])
                if 0 <= t < group:
                    weights[t] = weigh(t, score.pop(t), top.pop(t))
                if 0 <= t - 1:
                    gather_values(t - 1, weights.pop(t - 1))
            return carry

        lax.fori_loop(0, steps, heads_of, 0)
        tops, masses = top_acc[...].T, mass_acc[...].T
        packed = 0.0
        for k in range(PACK):
            part = slice(k * rows, (k + 1) * rows)
            stats = pack_stats(tops[part], masses[part])
            packed += pltpu.roll(stats, k * (LANE // PACK), 1) if k else stats
        for b, o_ref in enumerate(outs):
            width = o_ref.shape[1]
            o_ref[at, width - STAT :] = packed[b * tile : (b + 1) * tile].astype(o_ref.dtype)
        return carry

    lax.fori_loop(0, line_rows // tile, row_tile, 0)


def attend(plane, lines, kind, keys, values, bias, after=()):
    rows, columns = plane.shape[0] // lines, plane.shape[1]
    heads = columns // HD
    pairs = heads // PACK
    group = next(g for g in (10, 5, 4, 3, 2, 1) if pairs % g == 0)
    tile = next(t for t in (32, 16, rows) if rows % t == 0)
    width = columns + STAT
    scale = math.log2(math.e) / math.sqrt(HD)

    def body(*refs):
        work = refs[4 + len(after) :]
        attend_kernel(
            (tile, pairs // group, group), scale, *refs[:4], work[:lines], *work[lines:]
        )

    return pl.pallas_call(
        body,
        in_specs=[pl.BlockSpec(memory_space=pltpu.VMEM)] * 4
        + [pl.BlockSpec(memory_space=pl.ANY)] * len(after),
        out_specs=[pl.BlockSpec(memory_space=pltpu.VMEM)] * lines,
        out_shape=[jax.ShapeDtypeStruct((rows, width), kind)] * lines,
        scratch_shapes=[pltpu.VMEM((STAT, PACK * tile * lines), F32)] * 2,
        compiler_params=pltpu.CompilerParams(vmem_limit_bytes=40 * 1024 * 1024),
        cost_estimate=pl.CostEstimate(
            flops=4 * lines * rows * keys.shape[0] * columns,
            bytes_accessed=4 * keys.shape[0] * columns,
            transcendentals=lines * rows * keys.shape[0] * heads,
        ),
        name="attend",
    )(bias, plane, keys, values, *after)


def load(cached, fresh, victims, queries, after):
    cache_rows, columns = cached[0].shape
    tok = fresh[0].shape[0]
    padded = cache_rows + -(-tok // 16) * 16
    n = len(cached)

    def body(*refs):
        cached_refs, fresh_refs, victims_ref, queries_ref = refs[:n], refs[n : 2 * n], *refs[2 * n : 2 * n + 2]
        refs = refs[2 * n + 3 :]
        outs, bias_ref, q_ref, tails, ids_ref, sems = (
            refs[:n], refs[n], refs[n + 1], refs[n + 2 : 2 * n + 2], *refs[2 * n + 2 :]
        )
        ids = pltpu.make_async_copy(victims_ref, ids_ref, sems.at[1, n])
        rest = pltpu.make_async_copy(queries_ref, q_ref, sems.at[0, n])
        small = [
            pltpu.make_async_copy(src, dst, sems.at[1, i])
            for i, (src, dst) in enumerate(zip(fresh_refs, tails))
        ]
        large = [
            pltpu.make_async_copy(src, dst.at[pl.ds(0, cache_rows), :], sems.at[0, i])
            for i, (src, dst) in enumerate(zip(cached_refs, outs))
        ]
        for copy in [ids] + small + large + [rest]:
            copy.start()
        ids.wait()
        blocks = cache_rows // BLK
        first = lax.axis_index("seq") * blocks
        for block in range(blocks):
            hits = jnp.where(ids_ref[...] == first + block, 1.0, 0.0)
            hit = jnp.max(hits, axis=1, keepdims=True)
            gone = jnp.where(hit > 0.0, NEG, 0.0)
            bias_ref[block * BLK : (block + 1) * BLK, :] = jnp.broadcast_to(gone, (BLK, STAT))
        token = lax.broadcasted_iota(jnp.int32, (padded - cache_rows, STAT), 0)
        bias_ref[cache_rows:, :] = jnp.where(token < tok, 0.0, NEG)
        for copy, tail, out in zip(small, tails, outs):
            copy.wait()
            zeros = jnp.zeros((padded - cache_rows - tok, columns), F32)
            rows = jnp.concatenate([tail[...].astype(F32), zeros], axis=0)
            out[cache_rows:, :] = rows.astype(out.dtype)
        for copy in large + [rest]:
            copy.wait()

    in_hbm = pl.BlockSpec(memory_space=pltpu.HBM)
    held = (*cached, *fresh, victims, queries)
    return pl.pallas_call(
        body,
        in_specs=[in_hbm] * len(held) + [pl.BlockSpec(memory_space=pl.ANY)],
        out_specs=[pl.BlockSpec(memory_space=pltpu.VMEM)] * (n + 2),
        out_shape=[jax.ShapeDtypeStruct((padded, columns), BF16)] * n
        + [jax.ShapeDtypeStruct((padded, STAT), F32), jax.ShapeDtypeStruct(queries.shape, BF16)],
        scratch_shapes=[pltpu.VMEM(x.shape, BF16) for x in fresh]
        + [pltpu.VMEM(victims.shape, jnp.int32), pltpu.SemaphoreType.DMA((2, n + 1))],
        compiler_params=pltpu.CompilerParams(vmem_limit_bytes=24 * 1024 * 1024),
        cost_estimate=pl.CostEstimate(
            flops=0, bytes_accessed=4 * n * cache_rows * columns, transcendentals=0
        ),
        name="load",
    )(*[pltpu.with_memory_space_constraint(x, pltpu.HBM) for x in held], after)


def merged(arrays, heads, last):
    columns = heads * HD
    stats = [unpack_stats(get(slice(columns, columns + STAT))) for get in arrays]
    top = functools.reduce(jnp.maximum, [t for t, _ in stats])
    weights = [jnp.exp2(t - top) for t, _ in stats]
    mass = functools.reduce(jnp.add, [w * m for w, (_, m) in zip(weights, stats)])
    if last:
        inverse = 1.0 / jnp.where(mass > 0.0, mass, 1.0)
        weights = [w * inverse for w in weights]
    for head in range(heads):
        cols = slice(head * HD, (head + 1) * HD)
        yield cols, functools.reduce(
            jnp.add, [get(cols) * w[:, lane_of(head) : lane_of(head) + 1] for get, w in zip(arrays, weights)]
        )
    if not last:
        yield slice(columns, columns + STAT), pack_stats(top, mass)


def getter(ref, *index):
    return lambda cols: ref[(*index, slice(None), cols)].astype(F32)


def merge_rows(ins, heads, pieces, kinds):
    rows, width = ins[0].shape
    per = rows // pieces

    def body(*refs):
        outs = refs[len(ins) :]
        for cols, total in merged([getter(r) for r in refs[: len(ins)]], heads, False):
            for j, out in enumerate(outs):
                out[:, cols] = total[j * per : (j + 1) * per].astype(out.dtype)

    return call_merge(body, ins, [jax.ShapeDtypeStruct((per, width), kind) for kind in kinds])


def finish(ins, heads):
    rows = ins[0].shape[0]

    def body(*refs):
        out = refs[len(ins)]
        for cols, total in merged([getter(r) for r in refs[: len(ins)]], heads, True):
            out[:, cols] = total.astype(out.dtype)

    return call_merge(body, ins, [jax.ShapeDtypeStruct((rows, heads * HD), BF16)])[0]


def join(pieces, after=()):
    rows = sum(p.shape[0] for p in pieces)

    def body(*refs):
        out = refs[-1]
        ins = [r[...].astype(F32) for r in refs[: len(pieces)]]
        out[...] = jnp.concatenate(ins, axis=0).astype(out.dtype)

    shape = jax.ShapeDtypeStruct((rows, pieces[0].shape[1]), pieces[0].dtype)
    return call_merge(body, pieces, [shape], after)[0]


def call_merge(body, ins, shapes, after=()):
    size = sum(math.prod(x.shape) for x in ins)
    return pl.pallas_call(
        body,
        in_specs=[pl.BlockSpec(memory_space=pltpu.VMEM)] * len(ins)
        + [pl.BlockSpec(memory_space=pl.ANY)] * len(after),
        out_specs=[pl.BlockSpec(memory_space=pltpu.VMEM)] * len(shapes),
        out_shape=shapes,
        compiler_params=pltpu.CompilerParams(vmem_limit_bytes=48 * 1024 * 1024),
        cost_estimate=pl.CostEstimate(flops=4 * size, bytes_accessed=4 * size, transcendentals=0),
        name="merge",
    )(*ins, *after)


def per_device(queries, new_keys, new_values, cache_keys, cache_values, victims):
    members = lax.axis_size("seq")
    shape = factors(members)
    a_n, b_n, c_n = shape
    heads = queries.shape[1] // HD
    tok = queries.shape[0]

    def fetch(x, *by):
        return lax.ppermute(x, "seq", partner_perm(shape, by, False))

    def give(x, *by):
        return lax.ppermute(x, "seq", partner_perm(shape, by, True))

    far_first = [0, *range(a_n - 1, 0, -1)]
    line = [queries] + [fetch(queries, a, 0, 0) for a in far_first[1:]]
    lines = [line] + [[fetch(x, 0, b, 0) for x in line] for b in range(1, b_n)]
    keys, values, bias, line[0] = load(
        (cache_keys, cache_values), (new_keys, new_values), victims[None], queries, line[-1]
    )
    plane = join([x for pieces in lines for x in pieces])
    planes = [plane] + [fetch(plane, 0, 0, c) for c in range(1, c_n)]
    sums = []
    for c, rows in enumerate(planes):
        sums += attend(rows, b_n, BF16 if c else F32, keys, values, bias, sums[:1])

    def over_cores(b, kind):
        got = [give(sums[c * b_n + b], 0, 0, c) for c in range(1, c_n)]
        return merge_rows([sums[b]] + got, heads, a_n, [kind] * a_n)

    got = [[give(x, 0, b, 0) for x in over_cores(b, BF16)] for b in range(1, b_n)]
    own = over_cores(0, F32)
    total = [[own[s]] + [pieces[s] for pieces in got] for s in range(a_n)]
    last = [
        give(merge_rows(total[s], heads, 1, [BF16])[0], far_first[s], 0, 0) for s in range(1, a_n)
    ]
    return finish([*merge_rows(total[0], heads, 1, [F32]), *last], heads)


def solution(mesh):
    rows = P(("groups", "seq"), None)
    return jax.shard_map(
        per_device,
        mesh=mesh,
        in_specs=(rows, rows, rows, rows, rows, P("groups")),
        out_specs=rows,
        check_vma=False,
    )
```

```python
import functools
import itertools
import math

import jax
import jax.numpy as jnp
from jax import lax
from jax.experimental import pallas as pl
from jax.experimental.pallas import tpu as pltpu
from jax.sharding import PartitionSpec as P

HD = 128
BLK = 128
STAT = 128
LANE = STAT // 3
PACK = 2
NEG = -1e30
F32 = jnp.float32
BF16 = jnp.bfloat16


def factors(members):
    cores = 2 if members % 2 == 0 else 1
    chips = members // cores
    far = next(a for a in range(1, chips + 1) if chips % a == 0 and a * a >= chips)
    return far, chips // far, cores


def partner(at, by, size):
    return at ^ by if size & (size - 1) == 0 else (at + by) % size


def partner_perm(shape, by, back):
    def flat(place):
        return functools.reduce(lambda at, kn: at * kn[1] + kn[0], zip(place, shape), 0)

    places = itertools.product(*map(range, shape))
    pairs = [(flat([partner(*x) for x in zip(at, by, shape)]), flat(at)) for at in places]
    return [pair[::-1] for pair in pairs] if back else pairs


def lanes(rows):
    return lax.broadcasted_iota(jnp.int32, (rows, STAT), 1)


def pack_stats(top, mass):
    high = mass.astype(BF16).astype(F32)
    return top + pltpu.roll(high, LANE, 1) + pltpu.roll(mass - high, 2 * LANE, 1)


def unpack_stats(packed):
    used = lanes(packed.shape[0]) < LANE
    mass = pltpu.roll(packed, STAT - LANE, 1) + pltpu.roll(packed, STAT - 2 * LANE, 1)
    return jnp.where(used, packed, 0.0), jnp.where(used, mass, 0.0)


def lane_of(head):
    return head % PACK * (LANE // PACK) + head // PACK


def attend_kernel(sizes, scale, bias_ref, q_ref, k_ref, v_ref, outs, top_acc, mass_acc):
    tile, steps, group = sizes
    lines = len(outs)
    rows = tile * lines
    line_rows = outs[0].shape[0]
    wide = PACK * HD
    contract_last = (((1,), (1,)), ((), ()))
    contract_first = (((0,), (0,)), ((), ()))
    mine = [lax.broadcasted_iota(jnp.int32, (rows, wide), 1) // HD == k for k in range(PACK)]

    def row_tile(r, carry):
        at = pl.ds(pl.multiple_of(r * tile, tile), tile)
        in_plane = [pl.ds(pl.multiple_of(b * line_rows + r * tile, tile), tile) for b in range(lines)]
        top_acc[...] = jnp.zeros_like(top_acc)
        mass_acc[...] = jnp.zeros_like(mass_acc)

        def heads_of(step, carry):
            def columns(i):
                return pl.ds(pl.multiple_of((step * group + i) * wide, HD), wide)

            def scores(i):
                cols = columns(i)
                q = jnp.concatenate([q_ref[rs, cols] for rs in in_plane], axis=0)
                q = jnp.concatenate([jnp.where(m, q, jnp.zeros_like(q)) for m in mine], axis=0)
                return lax.dot_general(k_ref[:, cols], q, contract_last, preferred_element_type=F32)

            def masked(score):
                bias = jnp.concatenate([bias_ref[...]] * (PACK * rows // STAT), axis=1)
                score = score * scale + bias
                top = jnp.max(score, axis=0, keepdims=True).astype(BF16).astype(F32)
                return score, top

            def weigh(i, score, top):
                score = jnp.exp2(score - top)
                top_acc[pl.ds(step * group + i, 1), :] = top
                mass_acc[pl.ds(step * group + i, 1), :] = jnp.sum(score, axis=0, keepdims=True)
                return score.astype(BF16)

            def gather_values(i, weights):
                both = lax.dot_general(
                    weights, v_ref[:, columns(i)], contract_first, preferred_element_type=F32
                )
                for k in range(PACK):
                    at_head = ((step * group + i) * PACK + k) * HD
                    cols = pl.ds(pl.multiple_of(at_head, HD), HD)
                    for b, o_ref in enumerate(outs):
                        start = k * rows + b * tile
                        one = both[start : start + tile, k * HD : (k + 1) * HD]
                        o_ref[at, cols] = one.astype(o_ref.dtype)

            score, top, weights = {}, {}, {}
            for t in range(-3, group + 1):
                if 0 <= t + 3 < group:
                    score[t + 3] = scores(t + 3)
                if 0 <= t + 1 < group:
                    score[t + 1], top[t + 1] = masked(score[t + 1])
                if 0 <= t < group:
                    weights[t] = weigh(t, score.pop(t), top.pop(t))
                if 0 <= t - 1:
                    gather_values(t - 1, weights.pop(t - 1))
            return carry

        lax.fori_loop(0, steps, heads_of, 0)
        tops, masses = top_acc[...].T, mass_acc[...].T
        packed = 0.0
        for k in range(PACK):
            part = slice(k * rows, (k + 1) * rows)
            stats = pack_stats(tops[part], masses[part])
            packed += pltpu.roll(stats, k * (LANE // PACK), 1) if k else stats
        for b, o_ref in enumerate(outs):
            width = o_ref.shape[1]
            o_ref[at, width - STAT :] = packed[b * tile : (b + 1) * tile].astype(o_ref.dtype)
        return carry

    lax.fori_loop(0, line_rows // tile, row_tile, 0)


def attend(plane, lines, kind, keys, values, bias, after=()):
    rows, columns = plane.shape[0] // lines, plane.shape[1]
    heads = columns // HD
    pairs = heads // PACK
    group = next(g for g in (10, 5, 4, 3, 2, 1) if pairs % g == 0)
    tile = next(t for t in (32, 16, rows) if rows % t == 0)
    width = columns + STAT
    scale = math.log2(math.e) / math.sqrt(HD)

    def body(*refs):
        work = refs[4 + len(after) :]
        attend_kernel(
            (tile, pairs // group, group), scale, *refs[:4], work[:lines], *work[lines:]
        )

    return pl.pallas_call(
        body,
        in_specs=[pl.BlockSpec(memory_space=pltpu.VMEM)] * 4
        + [pl.BlockSpec(memory_space=pl.ANY)] * len(after),
        out_specs=[pl.BlockSpec(memory_space=pltpu.VMEM)] * lines,
        out_shape=[jax.ShapeDtypeStruct((rows, width), kind)] * lines,
        scratch_shapes=[pltpu.VMEM((STAT, PACK * tile * lines), F32)] * 2,
        compiler_params=pltpu.CompilerParams(vmem_limit_bytes=40 * 1024 * 1024),
        cost_estimate=pl.CostEstimate(
            flops=4 * lines * rows * keys.shape[0] * columns,
            bytes_accessed=4 * keys.shape[0] * columns,
            transcendentals=lines * rows * keys.shape[0] * heads,
        ),
        name="attend",
    )(bias, plane, keys, values, *after)


def load(cached, fresh, victims, queries, after):
    cache_rows, columns = cached[0].shape
    tok = fresh[0].shape[0]
    padded = cache_rows + -(-tok // 16) * 16
    n = len(cached)

    def body(*refs):
        cached_refs, fresh_refs, victims_ref, queries_ref = refs[:n], refs[n : 2 * n], *refs[2 * n : 2 * n + 2]
        refs = refs[2 * n + 3 :]
        outs, bias_ref, q_ref, tails, ids_ref, sems = (
            refs[:n], refs[n], refs[n + 1], refs[n + 2 : 2 * n + 2], *refs[2 * n + 2 :]
        )
        ids = pltpu.make_async_copy(victims_ref, ids_ref, sems.at[1, n])
        rest = pltpu.make_async_copy(queries_ref, q_ref, sems.at[0, n])
        small = [
            pltpu.make_async_copy(src, dst, sems.at[1, i])
            for i, (src, dst) in enumerate(zip(fresh_refs, tails))
        ]
        large = [
            pltpu.make_async_copy(src, dst.at[pl.ds(0, cache_rows), :], sems.at[0, i])
            for i, (src, dst) in enumerate(zip(cached_refs, outs))
        ]
        for copy in [ids] + small + large + [rest]:
            copy.start()
        ids.wait()
        blocks = cache_rows // BLK
        first = lax.axis_index("seq") * blocks
        for block in range(blocks):
            hits = jnp.where(ids_ref[...] == first + block, 1.0, 0.0)
            hit = jnp.max(hits, axis=1, keepdims=True)
            gone = jnp.where(hit > 0.0, NEG, 0.0)
            bias_ref[block * BLK : (block + 1) * BLK, :] = jnp.broadcast_to(gone, (BLK, STAT))
        token = lax.broadcasted_iota(jnp.int32, (padded - cache_rows, STAT), 0)
        bias_ref[cache_rows:, :] = jnp.where(token < tok, 0.0, NEG)
        for copy, tail, out in zip(small, tails, outs):
            copy.wait()
            zeros = jnp.zeros((padded - cache_rows - tok, columns), F32)
            rows = jnp.concatenate([tail[...].astype(F32), zeros], axis=0)
            out[cache_rows:, :] = rows.astype(out.dtype)
        for copy in large + [rest]:
            copy.wait()

    in_hbm = pl.BlockSpec(memory_space=pltpu.HBM)
    held = (*cached, *fresh, victims, queries)
    return pl.pallas_call(
        body,
        in_specs=[in_hbm] * len(held) + [pl.BlockSpec(memory_space=pl.ANY)],
        out_specs=[pl.BlockSpec(memory_space=pltpu.VMEM)] * (n + 2),
        out_shape=[jax.ShapeDtypeStruct((padded, columns), BF16)] * n
        + [jax.ShapeDtypeStruct((padded, STAT), F32), jax.ShapeDtypeStruct(queries.shape, BF16)],
        scratch_shapes=[pltpu.VMEM(x.shape, BF16) for x in fresh]
        + [pltpu.VMEM(victims.shape, jnp.int32), pltpu.SemaphoreType.DMA((2, n + 1))],
        compiler_params=pltpu.CompilerParams(vmem_limit_bytes=24 * 1024 * 1024),
        cost_estimate=pl.CostEstimate(
            flops=0, bytes_accessed=4 * n * cache_rows * columns, transcendentals=0
        ),
        name="load",
    )(*[pltpu.with_memory_space_constraint(x, pltpu.HBM) for x in held], after)


def merged(arrays, heads, last):
    columns = heads * HD
    stats = [unpack_stats(get(slice(columns, columns + STAT))) for get in arrays]
    top = functools.reduce(jnp.maximum, [t for t, _ in stats])
    weights = [jnp.exp2(t - top) for t, _ in stats]
    mass = functools.reduce(jnp.add, [w * m for w, (_, m) in zip(weights, stats)])
    if last:
        inverse = 1.0 / jnp.where(mass > 0.0, mass, 1.0)
        weights = [w * inverse for w in weights]
    for head in range(heads):
        cols = slice(head * HD, (head + 1) * HD)
        yield cols, functools.reduce(
            jnp.add, [get(cols) * w[:, lane_of(head) : lane_of(head) + 1] for get, w in zip(arrays, weights)]
        )
    if not last:
        yield slice(columns, columns + STAT), pack_stats(top, mass)


def getter(ref, *index):
    return lambda cols: ref[(*index, slice(None), cols)].astype(F32)


def merge_rows(ins, heads, pieces, kinds):
    rows, width = ins[0].shape
    per = rows // pieces

    def body(*refs):
        outs = refs[len(ins) :]
        for cols, total in merged([getter(r) for r in refs[: len(ins)]], heads, False):
            for j, out in enumerate(outs):
                out[:, cols] = total[j * per : (j + 1) * per].astype(out.dtype)

    return call_merge(body, ins, [jax.ShapeDtypeStruct((per, width), kind) for kind in kinds])


def merge_cuts(ins, heads, cuts, rows, after=()):
    width = ins[0].shape[1]

    def body(*refs):
        outs = refs[len(ins) + len(after) :]
        for cols, total in merged([getter(r) for r in refs[: len(ins)]], heads, False):
            for start, out in zip(cuts, outs):
                out[:, cols] = total[start : start + rows].astype(out.dtype)

    return call_merge(body, ins, [jax.ShapeDtypeStruct((rows, width), BF16)] * len(cuts), after)


def finish(ins, heads):
    rows = ins[0].shape[0]

    def body(*refs):
        out = refs[len(ins)]
        for cols, total in merged([getter(r) for r in refs[: len(ins)]], heads, True):
            out[:, cols] = total.astype(out.dtype)

    return call_merge(body, ins, [jax.ShapeDtypeStruct((rows, heads * HD), BF16)])[0]


def join(pieces, after=()):
    rows = sum(p.shape[0] for p in pieces)

    def body(*refs):
        out = refs[-1]
        ins = [r[...].astype(F32) for r in refs[: len(pieces)]]
        out[...] = jnp.concatenate(ins, axis=0).astype(out.dtype)

    shape = jax.ShapeDtypeStruct((rows, pieces[0].shape[1]), pieces[0].dtype)
    return call_merge(body, pieces, [shape], after)[0]


def call_merge(body, ins, shapes, after=()):
    size = sum(math.prod(x.shape) for x in ins)
    return pl.pallas_call(
        body,
        in_specs=[pl.BlockSpec(memory_space=pltpu.VMEM)] * len(ins)
        + [pl.BlockSpec(memory_space=pl.ANY)] * len(after),
        out_specs=[pl.BlockSpec(memory_space=pltpu.VMEM)] * len(shapes),
        out_shape=shapes,
        compiler_params=pltpu.CompilerParams(vmem_limit_bytes=48 * 1024 * 1024),
        cost_estimate=pl.CostEstimate(flops=4 * size, bytes_accessed=4 * size, transcendentals=0),
        name="merge",
    )(*ins, *after)


def per_device(queries, new_keys, new_values, cache_keys, cache_values, victims):
    members = lax.axis_size("seq")
    shape = factors(members)
    a_n, b_n, c_n = shape
    heads = queries.shape[1] // HD
    tok = queries.shape[0]

    def fetch(x, *by):
        return lax.ppermute(x, "seq", partner_perm(shape, by, False))

    def give(x, *by):
        return lax.ppermute(x, "seq", partner_perm(shape, by, True))

    far_first = [0, *range(a_n - 1, 0, -1)]
    line = [queries] + [fetch(queries, a, 0, 0) for a in far_first[1:]]
    lines = [line] + [[fetch(x, 0, b, 0) for x in line] for b in range(1, b_n)]
    keys, values, bias, line[0] = load(
        (cache_keys, cache_values), (new_keys, new_values), victims[None], queries, line[-1]
    )
    plane = join([x for pieces in lines for x in pieces])
    planes = [plane] + [fetch(plane, 0, 0, c) for c in range(1, c_n)]
    sums = []
    for c, rows in enumerate(planes):
        sums += attend(rows, b_n, BF16 if c else F32, keys, values, bias, sums[:1])

    back = [[give(sums[c * b_n + b], 0, 0, c) for c in range(1, c_n)] for b in range(b_n)]
    cuts = [s * tok for s in range(a_n)]
    got = []
    for b in range(1, b_n):
        pieces = merge_cuts([sums[b]] + back[b], heads, cuts[1:], tok)
        got.append([give(x, 0, b, 0) for x in pieces])
    own = merge_rows([sums[0]] + back[0], heads, a_n, [F32] * a_n)
    sent = [
        merge_rows([own[s]] + [pieces[s - 1] for pieces in got], heads, 1, [BF16])[0]
        for s in range(1, a_n)
    ]
    last = [give(x, a, 0, 0) for x, a in zip(sent, far_first[1:])]
    near = [
        give(merge_cuts([sums[b]] + back[b], heads, cuts[:1], tok, sent[-1:])[0], 0, b, 0)
        for b in range(1, b_n)
    ]
    return finish([*merge_rows([own[0], *last], heads, 1, [F32]), *near], heads)


def solution(mesh):
    rows = P(("groups", "seq"), None)
    return jax.shard_map(
        per_device,
        mesh=mesh,
        in_specs=(rows, rows, rows, rows, rows, P("groups")),
        out_specs=rows,
        check_vma=False,
    )
```

```python
import functools
import itertools
import math

import jax
import jax.numpy as jnp
from jax import lax
from jax.experimental import pallas as pl
from jax.experimental.pallas import tpu as pltpu
from jax.sharding import PartitionSpec as P

HD = 128
BLK = 128
STAT = 128
LANE = STAT // 3
PACK = 2
NEG = -1e30
F32 = jnp.float32
BF16 = jnp.bfloat16


def factors(members):
    cores = 2 if members % 2 == 0 else 1
    chips = members // cores
    far = next(a for a in range(1, chips + 1) if chips % a == 0 and a * a >= chips)
    return far, chips // far, cores


def partner(at, by, size):
    return at ^ by if size & (size - 1) == 0 else (at + by) % size


def partner_perm(shape, by, back):
    def flat(place):
        return functools.reduce(lambda at, kn: at * kn[1] + kn[0], zip(place, shape), 0)

    places = itertools.product(*map(range, shape))
    pairs = [(flat([partner(*x) for x in zip(at, by, shape)]), flat(at)) for at in places]
    return [pair[::-1] for pair in pairs] if back else pairs


def lanes(rows):
    return lax.broadcasted_iota(jnp.int32, (rows, STAT), 1)


def pack_stats(top, mass):
    high = mass.astype(BF16).astype(F32)
    return top + pltpu.roll(high, LANE, 1) + pltpu.roll(mass - high, 2 * LANE, 1)


def unpack_stats(packed):
    used = lanes(packed.shape[0]) < LANE
    mass = pltpu.roll(packed, STAT - LANE, 1) + pltpu.roll(packed, STAT - 2 * LANE, 1)
    return jnp.where(used, packed, 0.0), jnp.where(used, mass, 0.0)


def lane_of(head):
    return head % PACK * (LANE // PACK) + head // PACK


def attend_kernel(sizes, scale, bias_ref, q_ref, k_ref, v_ref, outs, top_acc, mass_acc):
    tile, steps, group = sizes
    lines = len(outs)
    rows = tile * lines
    line_rows = outs[0].shape[0]
    wide = PACK * HD
    contract_last = (((1,), (1,)), ((), ()))
    contract_first = (((0,), (0,)), ((), ()))
    mine = [lax.broadcasted_iota(jnp.int32, (rows, wide), 1) // HD == k for k in range(PACK)]

    def row_tile(r, carry):
        at = pl.ds(pl.multiple_of(r * tile, tile), tile)
        in_plane = [pl.ds(pl.multiple_of(b * line_rows + r * tile, tile), tile) for b in range(lines)]
        top_acc[...] = jnp.zeros_like(top_acc)
        mass_acc[...] = jnp.zeros_like(mass_acc)

        def heads_of(step, carry):
            def columns(i):
                return pl.ds(pl.multiple_of((step * group + i) * wide, HD), wide)

            def scores(i):
                cols = columns(i)
                q = jnp.concatenate([q_ref[rs, cols] for rs in in_plane], axis=0)
                q = jnp.concatenate([jnp.where(m, q, jnp.zeros_like(q)) for m in mine], axis=0)
                return lax.dot_general(k_ref[:, cols], q, contract_last, preferred_element_type=F32)

            def masked(score):
                bias = jnp.concatenate([bias_ref[...]] * (PACK * rows // STAT), axis=1)
                score = score * scale + bias
                top = jnp.max(score, axis=0, keepdims=True).astype(BF16).astype(F32)
                return score, top

            def weigh(i, score, top):
                score = jnp.exp2(score - top)
                top_acc[pl.ds(step * group + i, 1), :] = top
                mass_acc[pl.ds(step * group + i, 1), :] = jnp.sum(score, axis=0, keepdims=True)
                return score.astype(BF16)

            def gather_values(i, weights):
                both = lax.dot_general(
                    weights, v_ref[:, columns(i)], contract_first, preferred_element_type=F32
                )
                for k in range(PACK):
                    at_head = ((step * group + i) * PACK + k) * HD
                    cols = pl.ds(pl.multiple_of(at_head, HD), HD)
                    for b, o_ref in enumerate(outs):
                        start = k * rows + b * tile
                        one = both[start : start + tile, k * HD : (k + 1) * HD]
                        o_ref[at, cols] = one.astype(o_ref.dtype)

            score, top, weights = {}, {}, {}
            for t in range(-4, group + 2):
                if 0 <= t + 4 < group:
                    score[t + 4] = scores(t + 4)
                if 0 <= t + 1 < group:
                    score[t + 1], top[t + 1] = masked(score[t + 1])
                if 0 <= t < group:
                    weights[t] = weigh(t, score.pop(t), top.pop(t))
                if 0 <= t - 2:
                    gather_values(t - 2, weights.pop(t - 2))
            return carry

        lax.fori_loop(0, steps, heads_of, 0)
        tops, masses = top_acc[...].T, mass_acc[...].T
        packed = 0.0
        for k in range(PACK):
            part = slice(k * rows, (k + 1) * rows)
            stats = pack_stats(tops[part], masses[part])
            packed += pltpu.roll(stats, k * (LANE // PACK), 1) if k else stats
        for b, o_ref in enumerate(outs):
            width = o_ref.shape[1]
            o_ref[at, width - STAT :] = packed[b * tile : (b + 1) * tile].astype(o_ref.dtype)
        return carry

    lax.fori_loop(0, line_rows // tile, row_tile, 0)


def attend(plane, lines, kind, keys, values, bias, after=()):
    rows, columns = plane.shape[0] // lines, plane.shape[1]
    heads = columns // HD
    pairs = heads // PACK
    group = next(g for g in (10, 5, 4, 3, 2, 1) if pairs % g == 0)
    tile = next(t for t in (32, 16, rows) if rows % t == 0)
    width = columns + STAT
    scale = math.log2(math.e) / math.sqrt(HD)

    def body(*refs):
        work = refs[4 + len(after) :]
        attend_kernel(
            (tile, pairs // group, group), scale, *refs[:4], work[:lines], *work[lines:]
        )

    return pl.pallas_call(
        body,
        in_specs=[pl.BlockSpec(memory_space=pltpu.VMEM)] * 4
        + [pl.BlockSpec(memory_space=pl.ANY)] * len(after),
        out_specs=[pl.BlockSpec(memory_space=pltpu.VMEM)] * lines,
        out_shape=[jax.ShapeDtypeStruct((rows, width), kind)] * lines,
        scratch_shapes=[pltpu.VMEM((STAT, PACK * tile * lines), F32)] * 2,
        compiler_params=pltpu.CompilerParams(vmem_limit_bytes=40 * 1024 * 1024),
        cost_estimate=pl.CostEstimate(
            flops=4 * lines * rows * keys.shape[0] * columns,
            bytes_accessed=4 * keys.shape[0] * columns,
            transcendentals=lines * rows * keys.shape[0] * heads,
        ),
        name="attend",
    )(bias, plane, keys, values, *after)


def load(cached, fresh, victims, queries, after):
    cache_rows, columns = cached[0].shape
    tok = fresh[0].shape[0]
    padded = cache_rows + -(-tok // 16) * 16
    n = len(cached)

    def body(*refs):
        cached_refs, fresh_refs, victims_ref, queries_ref = refs[:n], refs[n : 2 * n], *refs[2 * n : 2 * n + 2]
        refs = refs[2 * n + 3 :]
        outs, bias_ref, q_ref, tails, ids_ref, sems = (
            refs[:n], refs[n], refs[n + 1], refs[n + 2 : 2 * n + 2], *refs[2 * n + 2 :]
        )
        ids = pltpu.make_async_copy(victims_ref, ids_ref, sems.at[1, n])
        rest = pltpu.make_async_copy(queries_ref, q_ref, sems.at[0, n])
        small = [
            pltpu.make_async_copy(src, dst, sems.at[1, i])
            for i, (src, dst) in enumerate(zip(fresh_refs, tails))
        ]
        large = [
            pltpu.make_async_copy(src, dst.at[pl.ds(0, cache_rows), :], sems.at[0, i])
            for i, (src, dst) in enumerate(zip(cached_refs, outs))
        ]
        for copy in [ids] + small + large + [rest]:
            copy.start()
        ids.wait()
        blocks = cache_rows // BLK
        first = lax.axis_index("seq") * blocks
        for block in range(blocks):
            hits = jnp.where(ids_ref[...] == first + block, 1.0, 0.0)
            hit = jnp.max(hits, axis=1, keepdims=True)
            gone = jnp.where(hit > 0.0, NEG, 0.0)
            bias_ref[block * BLK : (block + 1) * BLK, :] = jnp.broadcast_to(gone, (BLK, STAT))
        token = lax.broadcasted_iota(jnp.int32, (padded - cache_rows, STAT), 0)
        bias_ref[cache_rows:, :] = jnp.where(token < tok, 0.0, NEG)
        for copy, tail, out in zip(small, tails, outs):
            copy.wait()
            zeros = jnp.zeros((padded - cache_rows - tok, columns), F32)
            rows = jnp.concatenate([tail[...].astype(F32), zeros], axis=0)
            out[cache_rows:, :] = rows.astype(out.dtype)
        for copy in large + [rest]:
            copy.wait()

    in_hbm = pl.BlockSpec(memory_space=pltpu.HBM)
    held = (*cached, *fresh, victims, queries)
    return pl.pallas_call(
        body,
        in_specs=[in_hbm] * len(held) + [pl.BlockSpec(memory_space=pl.ANY)],
        out_specs=[pl.BlockSpec(memory_space=pltpu.VMEM)] * (n + 2),
        out_shape=[jax.ShapeDtypeStruct((padded, columns), BF16)] * n
        + [jax.ShapeDtypeStruct((padded, STAT), F32), jax.ShapeDtypeStruct(queries.shape, BF16)],
        scratch_shapes=[pltpu.VMEM(x.shape, BF16) for x in fresh]
        + [pltpu.VMEM(victims.shape, jnp.int32), pltpu.SemaphoreType.DMA((2, n + 1))],
        compiler_params=pltpu.CompilerParams(vmem_limit_bytes=24 * 1024 * 1024),
        cost_estimate=pl.CostEstimate(
            flops=0, bytes_accessed=4 * n * cache_rows * columns, transcendentals=0
        ),
        name="load",
    )(*[pltpu.with_memory_space_constraint(x, pltpu.HBM) for x in held], after)


def merged(arrays, heads, last):
    columns = heads * HD
    stats = [unpack_stats(get(slice(columns, columns + STAT))) for get in arrays]
    top = functools.reduce(jnp.maximum, [t for t, _ in stats])
    weights = [jnp.exp2(t - top) for t, _ in stats]
    mass = functools.reduce(jnp.add, [w * m for w, (_, m) in zip(weights, stats)])
    if last:
        inverse = 1.0 / jnp.where(mass > 0.0, mass, 1.0)
        weights = [w * inverse for w in weights]
    for head in range(heads):
        cols = slice(head * HD, (head + 1) * HD)
        yield cols, functools.reduce(
            jnp.add, [get(cols) * w[:, lane_of(head) : lane_of(head) + 1] for get, w in zip(arrays, weights)]
        )
    if not last:
        yield slice(columns, columns + STAT), pack_stats(top, mass)


def getter(ref, *index):
    return lambda cols: ref[(*index, slice(None), cols)].astype(F32)


def merge_rows(ins, heads, pieces, kinds):
    rows, width = ins[0].shape
    per = rows // pieces

    def body(*refs):
        outs = refs[len(ins) :]
        for cols, total in merged([getter(r) for r in refs[: len(ins)]], heads, False):
            for j, out in enumerate(outs):
                out[:, cols] = total[j * per : (j + 1) * per].astype(out.dtype)

    return call_merge(body, ins, [jax.ShapeDtypeStruct((per, width), kind) for kind in kinds])


def finish(ins, heads):
    rows = ins[0].shape[0]
    runs = next(n for n in (4, 2, 1) if heads % n == 0)
    wide = heads // runs * HD

    def body(*refs):
        out, buffer, sems = refs[len(ins) :]
        copies = []
        parts = merged([getter(r) for r in refs[: len(ins)]], heads, True)
        for head, (cols, total) in enumerate(parts):
            buffer[:, cols] = total.astype(buffer.dtype)
            if (head + 1) % (heads // runs) == 0:
                run = pl.ds(len(copies) * wide, wide)
                copy = pltpu.make_async_copy(
                    buffer.at[:, run], out.at[:, run], sems.at[len(copies)]
                )
                copy.start()
                copies.append(copy)
        for copy in copies:
            copy.wait()

    return pl.pallas_call(
        body,
        in_specs=[pl.BlockSpec(memory_space=pltpu.VMEM)] * len(ins),
        out_specs=pl.BlockSpec(memory_space=pltpu.HBM),
        out_shape=jax.ShapeDtypeStruct((rows, heads * HD), BF16),
        scratch_shapes=[
            pltpu.VMEM((rows, heads * HD), BF16), pltpu.SemaphoreType.DMA((runs,))
        ],
        compiler_params=pltpu.CompilerParams(vmem_limit_bytes=48 * 1024 * 1024),
        name="finish",
    )(*ins)


def join(pieces, after=()):
    rows = sum(p.shape[0] for p in pieces)

    def body(*refs):
        out = refs[-1]
        ins = [r[...].astype(F32) for r in refs[: len(pieces)]]
        out[...] = jnp.concatenate(ins, axis=0).astype(out.dtype)

    shape = jax.ShapeDtypeStruct((rows, pieces[0].shape[1]), pieces[0].dtype)
    return call_merge(body, pieces, [shape], after)[0]


def call_merge(body, ins, shapes, after=()):
    size = sum(math.prod(x.shape) for x in ins)
    return pl.pallas_call(
        body,
        in_specs=[pl.BlockSpec(memory_space=pltpu.VMEM)] * len(ins)
        + [pl.BlockSpec(memory_space=pl.ANY)] * len(after),
        out_specs=[pl.BlockSpec(memory_space=pltpu.VMEM)] * len(shapes),
        out_shape=shapes,
        compiler_params=pltpu.CompilerParams(vmem_limit_bytes=48 * 1024 * 1024),
        cost_estimate=pl.CostEstimate(flops=4 * size, bytes_accessed=4 * size, transcendentals=0),
        name="merge",
    )(*ins, *after)


def per_device(queries, new_keys, new_values, cache_keys, cache_values, victims):
    members = lax.axis_size("seq")
    shape = factors(members)
    a_n, b_n, c_n = shape
    heads = queries.shape[1] // HD
    tok = queries.shape[0]

    def fetch(x, *by):
        return lax.ppermute(x, "seq", partner_perm(shape, by, False))

    def give(x, *by):
        return lax.ppermute(x, "seq", partner_perm(shape, by, True))

    far_first = [0, *range(a_n - 1, 0, -1)]
    line = [queries] + [fetch(queries, a, 0, 0) for a in far_first[1:]]
    lines = [line] + [[fetch(x, 0, b, 0) for x in line] for b in range(1, b_n)]
    keys, values, bias, line[0] = load(
        (cache_keys, cache_values), (new_keys, new_values), victims[None], queries, line[-1]
    )
    plane = join([x for pieces in lines for x in pieces])
    planes = [plane] + [fetch(plane, 0, 0, c) for c in range(1, c_n)]
    sums = []
    for c, rows in enumerate(planes):
        sums += attend(rows, b_n, BF16 if c else F32, keys, values, bias, sums[:1])

    def over_cores(b, kind):
        got = [give(sums[c * b_n + b], 0, 0, c) for c in range(1, c_n)]
        return merge_rows([sums[b]] + got, heads, a_n, [kind] * a_n)

    got = [[give(x, 0, b, 0) for x in over_cores(b, BF16)] for b in range(1, b_n)]
    own = over_cores(0, F32)
    total = [[own[s]] + [pieces[s] for pieces in got] for s in range(a_n)]
    last = [
        give(merge_rows(total[s], heads, 1, [BF16])[0], far_first[s], 0, 0) for s in range(1, a_n)
    ]
    return finish([*merge_rows(total[0], heads, 1, [F32]), *last], heads)


def solution(mesh):
    rows = P(("groups", "seq"), None)
    return jax.shard_map(
        per_device,
        mesh=mesh,
        in_specs=(rows, rows, rows, rows, rows, P("groups")),
        out_specs=rows,
        check_vma=False,
    )
```

```python
import functools
import itertools
import math

import jax
import jax.numpy as jnp
from jax import lax
from jax.experimental import pallas as pl
from jax.experimental.pallas import tpu as pltpu
from jax.sharding import PartitionSpec as P

HD = 128
BLK = 128
STAT = 128
LANE = STAT // 3
PACK = 2
NEG = -1e30
F32 = jnp.float32
BF16 = jnp.bfloat16


def factors(members):
    cores = 2 if members % 2 == 0 else 1
    chips = members // cores
    far = next(a for a in range(1, chips + 1) if chips % a == 0 and a * a >= chips)
    return far, chips // far, cores


def partner(at, by, size):
    return at ^ by if size & (size - 1) == 0 else (at + by) % size


def partner_perm(shape, by, back):
    def flat(place):
        return functools.reduce(lambda at, kn: at * kn[1] + kn[0], zip(place, shape), 0)

    places = itertools.product(*map(range, shape))
    pairs = [(flat([partner(*x) for x in zip(at, by, shape)]), flat(at)) for at in places]
    return [pair[::-1] for pair in pairs] if back else pairs


def lanes(rows):
    return lax.broadcasted_iota(jnp.int32, (rows, STAT), 1)


def pack_stats(top, mass):
    high = mass.astype(BF16).astype(F32)
    return top + pltpu.roll(high, LANE, 1) + pltpu.roll(mass - high, 2 * LANE, 1)


def unpack_stats(packed):
    used = lanes(packed.shape[0]) < LANE
    mass = pltpu.roll(packed, STAT - LANE, 1) + pltpu.roll(packed, STAT - 2 * LANE, 1)
    return jnp.where(used, packed, 0.0), jnp.where(used, mass, 0.0)


def lane_of(head):
    return head % PACK * (LANE // PACK) + head // PACK


def attend_kernel(sizes, scale, bias_ref, q_ref, k_ref, v_ref, outs, top_acc, mass_acc):
    tile, steps, group = sizes
    lines = len(outs)
    rows = tile * lines
    line_rows = outs[0].shape[0]
    wide = PACK * HD
    contract_last = (((1,), (1,)), ((), ()))
    contract_first = (((0,), (0,)), ((), ()))
    mine = [lax.broadcasted_iota(jnp.int32, (rows, wide), 1) // HD == k for k in range(PACK)]

    def row_tile(r, carry):
        at = pl.ds(pl.multiple_of(r * tile, tile), tile)
        in_plane = [pl.ds(pl.multiple_of(b * line_rows + r * tile, tile), tile) for b in range(lines)]
        top_acc[...] = jnp.zeros_like(top_acc)
        mass_acc[...] = jnp.zeros_like(mass_acc)

        def heads_of(step, carry):
            def columns(i):
                return pl.ds(pl.multiple_of((step * group + i) * wide, HD), wide)

            def scores(i):
                cols = columns(i)
                q = jnp.concatenate([q_ref[rs, cols] for rs in in_plane], axis=0)
                q = jnp.concatenate([jnp.where(m, q, jnp.zeros_like(q)) for m in mine], axis=0)
                return lax.dot_general(k_ref[:, cols], q, contract_last, preferred_element_type=F32)

            def masked(score):
                bias = jnp.concatenate([bias_ref[...]] * (PACK * rows // STAT), axis=1)
                score = score * scale + bias
                top = jnp.max(score, axis=0, keepdims=True).astype(BF16).astype(F32)
                return score, top

            def weigh(i, score, top):
                score = jnp.exp2(score - top)
                top_acc[pl.ds(step * group + i, 1), :] = top
                mass_acc[pl.ds(step * group + i, 1), :] = jnp.sum(score, axis=0, keepdims=True)
                return score.astype(BF16)

            def gather_values(i, weights):
                both = lax.dot_general(
                    weights, v_ref[:, columns(i)], contract_first, preferred_element_type=F32
                )
                for k in range(PACK):
                    at_head = ((step * group + i) * PACK + k) * HD
                    cols = pl.ds(pl.multiple_of(at_head, HD), HD)
                    for b, o_ref in enumerate(outs):
                        start = k * rows + b * tile
                        one = both[start : start + tile, k * HD : (k + 1) * HD]
                        o_ref[at, cols] = one.astype(o_ref.dtype)

            score, top, weights = {}, {}, {}
            for t in range(-6, group + 3):
                if 0 <= t + 6 < group:
                    score[t + 6] = scores(t + 6)
                if 0 <= t + 2 < group:
                    score[t + 2], top[t + 2] = masked(score[t + 2])
                if 0 <= t < group:
                    weights[t] = weigh(t, score.pop(t), top.pop(t))
                if 0 <= t - 3:
                    gather_values(t - 3, weights.pop(t - 3))
            return carry

        lax.fori_loop(0, steps, heads_of, 0)
        tops, masses = top_acc[...].T, mass_acc[...].T
        packed = 0.0
        for k in range(PACK):
            part = slice(k * rows, (k + 1) * rows)
            stats = pack_stats(tops[part], masses[part])
            packed += pltpu.roll(stats, k * (LANE // PACK), 1) if k else stats
        for b, o_ref in enumerate(outs):
            width = o_ref.shape[1]
            o_ref[at, width - STAT :] = packed[b * tile : (b + 1) * tile].astype(o_ref.dtype)
        return carry

    lax.fori_loop(0, line_rows // tile, row_tile, 0)


def attend(plane, lines, kind, keys, values, bias, after=()):
    rows, columns = plane.shape[0] // lines, plane.shape[1]
    heads = columns // HD
    pairs = heads // PACK
    group = next(g for g in (10, 5, 4, 3, 2, 1) if pairs % g == 0)
    tile = next(t for t in (32, 16, rows) if rows % t == 0)
    width = columns + STAT
    scale = math.log2(math.e) / math.sqrt(HD)

    def body(*refs):
        work = refs[4 + len(after) :]
        attend_kernel(
            (tile, pairs // group, group), scale, *refs[:4], work[:lines], *work[lines:]
        )

    return pl.pallas_call(
        body,
        in_specs=[pl.BlockSpec(memory_space=pltpu.VMEM)] * 4
        + [pl.BlockSpec(memory_space=pl.ANY)] * len(after),
        out_specs=[pl.BlockSpec(memory_space=pltpu.VMEM)] * lines,
        out_shape=[jax.ShapeDtypeStruct((rows, width), kind)] * lines,
        scratch_shapes=[pltpu.VMEM((STAT, PACK * tile * lines), F32)] * 2,
        compiler_params=pltpu.CompilerParams(vmem_limit_bytes=40 * 1024 * 1024),
        cost_estimate=pl.CostEstimate(
            flops=4 * lines * rows * keys.shape[0] * columns,
            bytes_accessed=4 * keys.shape[0] * columns,
            transcendentals=lines * rows * keys.shape[0] * heads,
        ),
        name="attend",
    )(bias, plane, keys, values, *after)


def load(cached, fresh, victims, queries, after):
    cache_rows, columns = cached[0].shape
    tok = fresh[0].shape[0]
    padded = cache_rows + -(-tok // 16) * 16
    n = len(cached)

    def body(*refs):
        cached_refs, fresh_refs, victims_ref, queries_ref = refs[:n], refs[n : 2 * n], *refs[2 * n : 2 * n + 2]
        refs = refs[2 * n + 3 :]
        outs, bias_ref, q_ref, tails, ids_ref, sems = (
            refs[:n], refs[n], refs[n + 1], refs[n + 2 : 2 * n + 2], *refs[2 * n + 2 :]
        )
        ids = pltpu.make_async_copy(victims_ref, ids_ref, sems.at[1, n])
        rest = pltpu.make_async_copy(queries_ref, q_ref, sems.at[0, n])
        small = [
            pltpu.make_async_copy(src, dst, sems.at[1, i])
            for i, (src, dst) in enumerate(zip(fresh_refs, tails))
        ]
        large = [
            pltpu.make_async_copy(src, dst.at[pl.ds(0, cache_rows), :], sems.at[0, i])
            for i, (src, dst) in enumerate(zip(cached_refs, outs))
        ]
        for copy in [ids] + small + large + [rest]:
            copy.start()
        ids.wait()
        blocks = cache_rows // BLK
        first = lax.axis_index("seq") * blocks
        for block in range(blocks):
            hits = jnp.where(ids_ref[...] == first + block, 1.0, 0.0)
            hit = jnp.max(hits, axis=1, keepdims=True)
            gone = jnp.where(hit > 0.0, NEG, 0.0)
            bias_ref[block * BLK : (block + 1) * BLK, :] = jnp.broadcast_to(gone, (BLK, STAT))
        token = lax.broadcasted_iota(jnp.int32, (padded - cache_rows, STAT), 0)
        bias_ref[cache_rows:, :] = jnp.where(token < tok, 0.0, NEG)
        for copy, tail, out in zip(small, tails, outs):
            copy.wait()
            zeros = jnp.zeros((padded - cache_rows - tok, columns), F32)
            rows = jnp.concatenate([tail[...].astype(F32), zeros], axis=0)
            out[cache_rows:, :] = rows.astype(out.dtype)
        for copy in large + [rest]:
            copy.wait()

    in_hbm = pl.BlockSpec(memory_space=pltpu.HBM)
    held = (*cached, *fresh, victims, queries)
    return pl.pallas_call(
        body,
        in_specs=[in_hbm] * len(held) + [pl.BlockSpec(memory_space=pl.ANY)],
        out_specs=[pl.BlockSpec(memory_space=pltpu.VMEM)] * (n + 2),
        out_shape=[jax.ShapeDtypeStruct((padded, columns), BF16)] * n
        + [jax.ShapeDtypeStruct((padded, STAT), F32), jax.ShapeDtypeStruct(queries.shape, BF16)],
        scratch_shapes=[pltpu.VMEM(x.shape, BF16) for x in fresh]
        + [pltpu.VMEM(victims.shape, jnp.int32), pltpu.SemaphoreType.DMA((2, n + 1))],
        compiler_params=pltpu.CompilerParams(vmem_limit_bytes=24 * 1024 * 1024),
        cost_estimate=pl.CostEstimate(
            flops=0, bytes_accessed=4 * n * cache_rows * columns, transcendentals=0
        ),
        name="load",
    )(*[pltpu.with_memory_space_constraint(x, pltpu.HBM) for x in held], after)


def merged(arrays, heads, last):
    columns = heads * HD
    stats = [unpack_stats(get(slice(columns, columns + STAT))) for get in arrays]
    top = functools.reduce(jnp.maximum, [t for t, _ in stats])
    weights = [jnp.exp2(t - top) for t, _ in stats]
    mass = functools.reduce(jnp.add, [w * m for w, (_, m) in zip(weights, stats)])
    if last:
        inverse = 1.0 / jnp.where(mass > 0.0, mass, 1.0)
        weights = [w * inverse for w in weights]
    for head in range(heads):
        cols = slice(head * HD, (head + 1) * HD)
        yield cols, functools.reduce(
            jnp.add, [get(cols) * w[:, lane_of(head) : lane_of(head) + 1] for get, w in zip(arrays, weights)]
        )
    if not last:
        yield slice(columns, columns + STAT), pack_stats(top, mass)


def getter(ref, *index):
    return lambda cols: ref[(*index, slice(None), cols)].astype(F32)


def merge_rows(ins, heads, pieces, kinds):
    rows, width = ins[0].shape
    per = rows // pieces

    def body(*refs):
        outs = refs[len(ins) :]
        for cols, total in merged([getter(r) for r in refs[: len(ins)]], heads, False):
            for j, out in enumerate(outs):
                out[:, cols] = total[j * per : (j + 1) * per].astype(out.dtype)

    return call_merge(body, ins, [jax.ShapeDtypeStruct((per, width), kind) for kind in kinds])


def finish(ins, heads):
    rows = ins[0].shape[0]

    def body(*refs):
        out = refs[len(ins)]
        for cols, total in merged([getter(r) for r in refs[: len(ins)]], heads, True):
            out[:, cols] = total.astype(out.dtype)

    return call_merge(body, ins, [jax.ShapeDtypeStruct((rows, heads * HD), BF16)])[0]


def join(pieces, after=()):
    rows = sum(p.shape[0] for p in pieces)

    def body(*refs):
        out = refs[-1]
        ins = [r[...].astype(F32) for r in refs[: len(pieces)]]
        out[...] = jnp.concatenate(ins, axis=0).astype(out.dtype)

    shape = jax.ShapeDtypeStruct((rows, pieces[0].shape[1]), pieces[0].dtype)
    return call_merge(body, pieces, [shape], after)[0]


def call_merge(body, ins, shapes, after=()):
    size = sum(math.prod(x.shape) for x in ins)
    return pl.pallas_call(
        body,
        in_specs=[pl.BlockSpec(memory_space=pltpu.VMEM)] * len(ins)
        + [pl.BlockSpec(memory_space=pl.ANY)] * len(after),
        out_specs=[pl.BlockSpec(memory_space=pltpu.VMEM)] * len(shapes),
        out_shape=shapes,
        compiler_params=pltpu.CompilerParams(vmem_limit_bytes=48 * 1024 * 1024),
        cost_estimate=pl.CostEstimate(flops=4 * size, bytes_accessed=4 * size, transcendentals=0),
        name="merge",
    )(*ins, *after)


def per_device(queries, new_keys, new_values, cache_keys, cache_values, victims):
    members = lax.axis_size("seq")
    shape = factors(members)
    a_n, b_n, c_n = shape
    heads = queries.shape[1] // HD
    tok = queries.shape[0]

    def fetch(x, *by):
        return lax.ppermute(x, "seq", partner_perm(shape, by, False))

    def give(x, *by):
        return lax.ppermute(x, "seq", partner_perm(shape, by, True))

    far_first = [0, *range(a_n - 1, 0, -1)]
    line = [queries] + [fetch(queries, a, 0, 0) for a in far_first[1:]]
    lines = [line] + [[fetch(x, 0, b, 0) for x in line] for b in range(1, b_n)]
    keys, values, bias, line[0] = load(
        (cache_keys, cache_values), (new_keys, new_values), victims[None], queries, line[-1]
    )
    plane = join([x for pieces in lines for x in pieces])
    planes = [plane] + [fetch(plane, 0, 0, c) for c in range(1, c_n)]
    sums = []
    for c, rows in enumerate(planes):
        sums += attend(rows, b_n, BF16 if c else F32, keys, values, bias, sums[:1])

    def over_cores(b, kind):
        got = [give(sums[c * b_n + b], 0, 0, c) for c in range(1, c_n)]
        return merge_rows([sums[b]] + got, heads, a_n, [kind] * a_n)

    got = [[give(x, 0, b, 0) for x in over_cores(b, BF16)] for b in range(1, b_n)]
    own = over_cores(0, F32)
    total = [[own[s]] + [pieces[s] for pieces in got] for s in range(a_n)]
    last = [
        give(merge_rows(total[s], heads, 1, [BF16])[0], far_first[s], 0, 0) for s in range(1, a_n)
    ]
    return finish([*merge_rows(total[0], heads, 1, [F32]), *last], heads)


def solution(mesh):
    rows = P(("groups", "seq"), None)
    return jax.shard_map(
        per_device,
        mesh=mesh,
        in_specs=(rows, rows, rows, rows, rows, P("groups")),
        out_specs=rows,
        check_vma=False,
    )
```

```python
import functools
import itertools
import math

import jax
import jax.numpy as jnp
from jax import lax
from jax.experimental import pallas as pl
from jax.experimental.pallas import tpu as pltpu
from jax.sharding import PartitionSpec as P

HD = 128
BLK = 128
STAT = 128
LANE = STAT // 3
PACK = 2
NEG = -1e30
F32 = jnp.float32
BF16 = jnp.bfloat16


def factors(members):
    cores = 2 if members % 2 == 0 else 1
    chips = members // cores
    far = next(a for a in range(1, chips + 1) if chips % a == 0 and a * a >= chips)
    return far, chips // far, cores


def partner(at, by, size):
    return at ^ by if size & (size - 1) == 0 else (at + by) % size


def partner_perm(shape, by, back):
    def flat(place):
        return functools.reduce(lambda at, kn: at * kn[1] + kn[0], zip(place, shape), 0)

    places = itertools.product(*map(range, shape))
    pairs = [(flat([partner(*x) for x in zip(at, by, shape)]), flat(at)) for at in places]
    return [pair[::-1] for pair in pairs] if back else pairs


def lanes(rows):
    return lax.broadcasted_iota(jnp.int32, (rows, STAT), 1)


def pack_stats(top, mass):
    high = mass.astype(BF16).astype(F32)
    return top + pltpu.roll(high, LANE, 1) + pltpu.roll(mass - high, 2 * LANE, 1)


def unpack_stats(packed):
    used = lanes(packed.shape[0]) < LANE
    mass = pltpu.roll(packed, STAT - LANE, 1) + pltpu.roll(packed, STAT - 2 * LANE, 1)
    return jnp.where(used, packed, 0.0), jnp.where(used, mass, 0.0)


def lane_of(head):
    return head % PACK * (LANE // PACK) + head // PACK


def attend_kernel(sizes, scale, bias_ref, q_ref, k_ref, v_ref, outs, top_acc, mass_acc):
    tile, steps, group = sizes
    lines = len(outs)
    rows = tile * lines
    line_rows = outs[0].shape[0]
    wide = PACK * HD
    contract_last = (((1,), (1,)), ((), ()))
    contract_first = (((0,), (0,)), ((), ()))
    mine = [lax.broadcasted_iota(jnp.int32, (rows, wide), 1) // HD == k for k in range(PACK)]

    def row_tile(r, carry):
        at = pl.ds(pl.multiple_of(r * tile, tile), tile)
        in_plane = [pl.ds(pl.multiple_of(b * line_rows + r * tile, tile), tile) for b in range(lines)]
        top_acc[...] = jnp.zeros_like(top_acc)
        mass_acc[...] = jnp.zeros_like(mass_acc)

        def heads_of(step, carry):
            def columns(i):
                return pl.ds(pl.multiple_of((step * group + i) * wide, HD), wide)

            def scores(i):
                cols = columns(i)
                q = jnp.concatenate([q_ref[rs, cols] for rs in in_plane], axis=0)
                q = jnp.concatenate([jnp.where(m, q, jnp.zeros_like(q)) for m in mine], axis=0)
                return lax.dot_general(k_ref[:, cols], q, contract_last, preferred_element_type=F32)

            def masked(score):
                bias = jnp.concatenate([bias_ref[...]] * (PACK * rows // STAT), axis=1)
                score = score * scale + bias
                top = jnp.max(score, axis=0, keepdims=True).astype(BF16).astype(F32)
                return score, top

            def weigh(i, score, top):
                score = jnp.exp2(score - top)
                top_acc[pl.ds(step * group + i, 1), :] = top
                mass_acc[pl.ds(step * group + i, 1), :] = jnp.sum(score, axis=0, keepdims=True)
                return score.astype(BF16)

            def gather_values(i, weights):
                both = lax.dot_general(
                    weights, v_ref[:, columns(i)], contract_first, preferred_element_type=F32
                )
                for k in range(PACK):
                    at_head = ((step * group + i) * PACK + k) * HD
                    cols = pl.ds(pl.multiple_of(at_head, HD), HD)
                    for b, o_ref in enumerate(outs):
                        start = k * rows + b * tile
                        one = both[start : start + tile, k * HD : (k + 1) * HD]
                        o_ref[at, cols] = one.astype(o_ref.dtype)

            score, top, weights = {}, {}, {}
            for t in range(-6, group + 3):
                if 0 <= t + 6 < group:
                    score[t + 6] = scores(t + 6)
                if 0 <= t + 2 < group:
                    score[t + 2], top[t + 2] = masked(score[t + 2])
                if 0 <= t < group:
                    weights[t] = weigh(t, score.pop(t), top.pop(t))
                if 0 <= t - 3:
                    gather_values(t - 3, weights.pop(t - 3))
            return carry

        lax.fori_loop(0, steps, heads_of, 0)
        tops, masses = top_acc[...].T, mass_acc[...].T
        packed = 0.0
        for k in range(PACK):
            part = slice(k * rows, (k + 1) * rows)
            stats = pack_stats(tops[part], masses[part])
            packed += pltpu.roll(stats, k * (LANE // PACK), 1) if k else stats
        for b, o_ref in enumerate(outs):
            width = o_ref.shape[1]
            o_ref[at, width - STAT :] = packed[b * tile : (b + 1) * tile].astype(o_ref.dtype)
        return carry

    lax.fori_loop(0, line_rows // tile, row_tile, 0)


def attend(plane, lines, kind, keys, values, bias, after=()):
    rows, columns = plane.shape[0] // lines, plane.shape[1]
    heads = columns // HD
    pairs = heads // PACK
    group = next(g for g in (10, 5, 4, 3, 2, 1) if pairs % g == 0)
    tile = next(t for t in (32, 16, rows) if rows % t == 0)
    width = columns + STAT
    scale = math.log2(math.e) / math.sqrt(HD)

    def body(*refs):
        work = refs[4 + len(after) :]
        attend_kernel(
            (tile, pairs // group, group), scale, *refs[:4], work[:lines], *work[lines:]
        )

    return pl.pallas_call(
        body,
        in_specs=[pl.BlockSpec(memory_space=pltpu.VMEM)] * 4
        + [pl.BlockSpec(memory_space=pl.ANY)] * len(after),
        out_specs=[pl.BlockSpec(memory_space=pltpu.VMEM)] * lines,
        out_shape=[jax.ShapeDtypeStruct((rows, width), kind)] * lines,
        scratch_shapes=[pltpu.VMEM((STAT, PACK * tile * lines), F32)] * 2,
        compiler_params=pltpu.CompilerParams(
            vmem_limit_bytes=40 * 1024 * 1024, fuse_transposed_lhs_in_matmul=True
        ),
        cost_estimate=pl.CostEstimate(
            flops=4 * lines * rows * keys.shape[0] * columns,
            bytes_accessed=4 * keys.shape[0] * columns,
            transcendentals=lines * rows * keys.shape[0] * heads,
        ),
        name="attend",
    )(bias, plane, keys, values, *after)


def load(cached, fresh, victims, queries, after):
    cache_rows, columns = cached[0].shape
    tok = fresh[0].shape[0]
    padded = cache_rows + -(-tok // 16) * 16
    n = len(cached)

    def body(*refs):
        cached_refs, fresh_refs, victims_ref, queries_ref = refs[:n], refs[n : 2 * n], *refs[2 * n : 2 * n + 2]
        refs = refs[2 * n + 3 :]
        outs, bias_ref, q_ref, tails, ids_ref, sems = (
            refs[:n], refs[n], refs[n + 1], refs[n + 2 : 2 * n + 2], *refs[2 * n + 2 :]
        )
        ids = pltpu.make_async_copy(victims_ref, ids_ref, sems.at[1, n])
        rest = pltpu.make_async_copy(queries_ref, q_ref, sems.at[0, n])
        small = [
            pltpu.make_async_copy(src, dst, sems.at[1, i])
            for i, (src, dst) in enumerate(zip(fresh_refs, tails))
        ]
        large = [
            pltpu.make_async_copy(src, dst.at[pl.ds(0, cache_rows), :], sems.at[0, i])
            for i, (src, dst) in enumerate(zip(cached_refs, outs))
        ]
        for copy in [ids] + small + large + [rest]:
            copy.start()
        ids.wait()
        blocks = cache_rows // BLK
        first = lax.axis_index("seq") * blocks
        for block in range(blocks):
            hits = jnp.where(ids_ref[...] == first + block, 1.0, 0.0)
            hit = jnp.max(hits, axis=1, keepdims=True)
            gone = jnp.where(hit > 0.0, NEG, 0.0)
            bias_ref[block * BLK : (block + 1) * BLK, :] = jnp.broadcast_to(gone, (BLK, STAT))
        token = lax.broadcasted_iota(jnp.int32, (padded - cache_rows, STAT), 0)
        bias_ref[cache_rows:, :] = jnp.where(token < tok, 0.0, NEG)
        for copy, tail, out in zip(small, tails, outs):
            copy.wait()
            zeros = jnp.zeros((padded - cache_rows - tok, columns), F32)
            rows = jnp.concatenate([tail[...].astype(F32), zeros], axis=0)
            out[cache_rows:, :] = rows.astype(out.dtype)
        for copy in large + [rest]:
            copy.wait()

    in_hbm = pl.BlockSpec(memory_space=pltpu.HBM)
    held = (*cached, *fresh, victims, queries)
    return pl.pallas_call(
        body,
        in_specs=[in_hbm] * len(held) + [pl.BlockSpec(memory_space=pl.ANY)],
        out_specs=[pl.BlockSpec(memory_space=pltpu.VMEM)] * (n + 2),
        out_shape=[jax.ShapeDtypeStruct((padded, columns), BF16)] * n
        + [jax.ShapeDtypeStruct((padded, STAT), F32), jax.ShapeDtypeStruct(queries.shape, BF16)],
        scratch_shapes=[pltpu.VMEM(x.shape, BF16) for x in fresh]
        + [pltpu.VMEM(victims.shape, jnp.int32), pltpu.SemaphoreType.DMA((2, n + 1))],
        compiler_params=pltpu.CompilerParams(vmem_limit_bytes=24 * 1024 * 1024),
        cost_estimate=pl.CostEstimate(
            flops=0, bytes_accessed=4 * n * cache_rows * columns, transcendentals=0
        ),
        name="load",
    )(*[pltpu.with_memory_space_constraint(x, pltpu.HBM) for x in held], after)


def merged(arrays, heads, last):
    columns = heads * HD
    stats = [unpack_stats(get(slice(columns, columns + STAT))) for get in arrays]
    top = functools.reduce(jnp.maximum, [t for t, _ in stats])
    weights = [jnp.exp2(t - top) for t, _ in stats]
    mass = functools.reduce(jnp.add, [w * m for w, (_, m) in zip(weights, stats)])
    if last:
        inverse = 1.0 / jnp.where(mass > 0.0, mass, 1.0)
        weights = [w * inverse for w in weights]
    for head in range(heads):
        cols = slice(head * HD, (head + 1) * HD)
        yield cols, functools.reduce(
            jnp.add, [get(cols) * w[:, lane_of(head) : lane_of(head) + 1] for get, w in zip(arrays, weights)]
        )
    if not last:
        yield slice(columns, columns + STAT), pack_stats(top, mass)


def getter(ref, *index):
    return lambda cols: ref[(*index, slice(None), cols)].astype(F32)


def merge_rows(ins, heads, pieces, kinds):
    rows, width = ins[0].shape
    per = rows // pieces

    def body(*refs):
        outs = refs[len(ins) :]
        for cols, total in merged([getter(r) for r in refs[: len(ins)]], heads, False):
            for j, out in enumerate(outs):
                out[:, cols] = total[j * per : (j + 1) * per].astype(out.dtype)

    return call_merge(body, ins, [jax.ShapeDtypeStruct((per, width), kind) for kind in kinds])


def finish(ins, heads):
    rows = ins[0].shape[0]

    def body(*refs):
        out = refs[len(ins)]
        for cols, total in merged([getter(r) for r in refs[: len(ins)]], heads, True):
            out[:, cols] = total.astype(out.dtype)

    return call_merge(body, ins, [jax.ShapeDtypeStruct((rows, heads * HD), BF16)])[0]


def join(pieces, after=()):
    rows = sum(p.shape[0] for p in pieces)

    def body(*refs):
        out = refs[-1]
        ins = [r[...].astype(F32) for r in refs[: len(pieces)]]
        out[...] = jnp.concatenate(ins, axis=0).astype(out.dtype)

    shape = jax.ShapeDtypeStruct((rows, pieces[0].shape[1]), pieces[0].dtype)
    return call_merge(body, pieces, [shape], after)[0]


def call_merge(body, ins, shapes, after=()):
    size = sum(math.prod(x.shape) for x in ins)
    return pl.pallas_call(
        body,
        in_specs=[pl.BlockSpec(memory_space=pltpu.VMEM)] * len(ins)
        + [pl.BlockSpec(memory_space=pl.ANY)] * len(after),
        out_specs=[pl.BlockSpec(memory_space=pltpu.VMEM)] * len(shapes),
        out_shape=shapes,
        compiler_params=pltpu.CompilerParams(vmem_limit_bytes=48 * 1024 * 1024),
        cost_estimate=pl.CostEstimate(flops=4 * size, bytes_accessed=4 * size, transcendentals=0),
        name="merge",
    )(*ins, *after)


def per_device(queries, new_keys, new_values, cache_keys, cache_values, victims):
    members = lax.axis_size("seq")
    shape = factors(members)
    a_n, b_n, c_n = shape
    heads = queries.shape[1] // HD
    tok = queries.shape[0]

    def fetch(x, *by):
        return lax.ppermute(x, "seq", partner_perm(shape, by, False))

    def give(x, *by):
        return lax.ppermute(x, "seq", partner_perm(shape, by, True))

    far_first = [0, *range(a_n - 1, 0, -1)]
    line = [queries] + [fetch(queries, a, 0, 0) for a in far_first[1:]]
    lines = [line] + [[fetch(x, 0, b, 0) for x in line] for b in range(1, b_n)]
    keys, values, bias, line[0] = load(
        (cache_keys, cache_values), (new_keys, new_values), victims[None], queries, line[-1]
    )
    plane = join([x for pieces in lines for x in pieces])
    planes = [plane] + [fetch(plane, 0, 0, c) for c in range(1, c_n)]
    sums = []
    for c, rows in enumerate(planes):
        sums += attend(rows, b_n, BF16 if c else F32, keys, values, bias, sums[:1])

    def over_cores(b, kind):
        got = [give(sums[c * b_n + b], 0, 0, c) for c in range(1, c_n)]
        return merge_rows([sums[b]] + got, heads, a_n, [kind] * a_n)

    got = [[give(x, 0, b, 0) for x in over_cores(b, BF16)] for b in range(1, b_n)]
    own = over_cores(0, F32)
    total = [[own[s]] + [pieces[s] for pieces in got] for s in range(a_n)]
    last = [
        give(merge_rows(total[s], heads, 1, [BF16])[0], far_first[s], 0, 0) for s in range(1, a_n)
    ]
    return finish([*merge_rows(total[0], heads, 1, [F32]), *last], heads)


def solution(mesh):
    rows = P(("groups", "seq"), None)
    return jax.shard_map(
        per_device,
        mesh=mesh,
        in_specs=(rows, rows, rows, rows, rows, P("groups")),
        out_specs=rows,
        check_vma=False,
    )
```

```python
import functools
import itertools
import math

import jax
import jax.numpy as jnp
from jax import lax
from jax.experimental import pallas as pl
from jax.experimental.pallas import tpu as pltpu
from jax.sharding import PartitionSpec as P

HD = 128
BLK = 128
STAT = 128
LANE = STAT // 3
PACK = 2
NEG = -1e30
F32 = jnp.float32
BF16 = jnp.bfloat16


def factors(members):
    cores = 2 if members % 2 == 0 else 1
    chips = members // cores
    far = next(a for a in range(1, chips + 1) if chips % a == 0 and a * a >= chips)
    return far, chips // far, cores


def partner(at, by, size):
    return at ^ by if size & (size - 1) == 0 else (at + by) % size


def partner_perm(shape, by, back):
    def flat(place):
        return functools.reduce(lambda at, kn: at * kn[1] + kn[0], zip(place, shape), 0)

    places = itertools.product(*map(range, shape))
    pairs = [(flat([partner(*x) for x in zip(at, by, shape)]), flat(at)) for at in places]
    return [pair[::-1] for pair in pairs] if back else pairs


def lanes(rows):
    return lax.broadcasted_iota(jnp.int32, (rows, STAT), 1)


def pack_stats(top, mass):
    high = mass.astype(BF16).astype(F32)
    return top + pltpu.roll(high, LANE, 1) + pltpu.roll(mass - high, 2 * LANE, 1)


def unpack_stats(packed):
    used = lanes(packed.shape[0]) < LANE
    mass = pltpu.roll(packed, STAT - LANE, 1) + pltpu.roll(packed, STAT - 2 * LANE, 1)
    return jnp.where(used, packed, 0.0), jnp.where(used, mass, 0.0)


def lane_of(head):
    return head % PACK * (LANE // PACK) + head // PACK


def attend_kernel(sizes, scale, bias_ref, q_ref, k_ref, v_ref, outs, top_acc, mass_acc):
    tile, steps, group = sizes
    lines = len(outs)
    rows = tile * lines
    line_rows = outs[0].shape[0]
    wide = PACK * HD
    contract_last = (((1,), (1,)), ((), ()))
    contract_first = (((0,), (0,)), ((), ()))
    mine = [lax.broadcasted_iota(jnp.int32, (rows, wide), 1) // HD == k for k in range(PACK)]

    def row_tile(r, carry):
        at = pl.ds(pl.multiple_of(r * tile, tile), tile)
        in_plane = [pl.ds(pl.multiple_of(b * line_rows + r * tile, tile), tile) for b in range(lines)]
        top_acc[...] = jnp.zeros_like(top_acc)
        mass_acc[...] = jnp.zeros_like(mass_acc)

        def heads_of(step, carry):
            def columns(i):
                return pl.ds(pl.multiple_of((step * group + i) * wide, HD), wide)

            def scores(i):
                cols = columns(i)
                q = jnp.concatenate([q_ref[rs, cols] for rs in in_plane], axis=0)
                q = jnp.concatenate([jnp.where(m, q, jnp.zeros_like(q)) for m in mine], axis=0)
                return lax.dot_general(k_ref[:, cols], q, contract_last, preferred_element_type=F32)

            def masked(score):
                bias = jnp.concatenate([bias_ref[...]] * (PACK * rows // STAT), axis=1)
                score = score * scale + bias
                top = jnp.max(score, axis=0, keepdims=True).astype(BF16).astype(F32)
                return score, top

            def weigh(i, score, top):
                score = jnp.exp2(score - top)
                top_acc[pl.ds(step * group + i, 1), :] = top
                mass_acc[pl.ds(step * group + i, 1), :] = jnp.sum(score, axis=0, keepdims=True)
                return score.astype(BF16)

            def gather_values(i, weights):
                both = lax.dot_general(
                    weights, v_ref[:, columns(i)], contract_first, preferred_element_type=F32
                )
                for k in range(PACK):
                    at_head = ((step * group + i) * PACK + k) * HD
                    cols = pl.ds(pl.multiple_of(at_head, HD), HD)
                    for b, o_ref in enumerate(outs):
                        start = k * rows + b * tile
                        one = both[start : start + tile, k * HD : (k + 1) * HD]
                        o_ref[at, cols] = one.astype(o_ref.dtype)

            score, top, weights = {}, {}, {}
            for t in range(-6, group + 3):
                if 0 <= t + 6 < group:
                    score[t + 6] = scores(t + 6)
                if 0 <= t + 2 < group:
                    score[t + 2], top[t + 2] = masked(score[t + 2])
                if 0 <= t < group:
                    weights[t] = weigh(t, score.pop(t), top.pop(t))
                if 0 <= t - 3:
                    gather_values(t - 3, weights.pop(t - 3))
            return carry

        lax.fori_loop(0, steps, heads_of, 0)
        tops, masses = top_acc[...].T, mass_acc[...].T
        packed = 0.0
        for k in range(PACK):
            part = slice(k * rows, (k + 1) * rows)
            stats = pack_stats(tops[part], masses[part])
            packed += pltpu.roll(stats, k * (LANE // PACK), 1) if k else stats
        for b, o_ref in enumerate(outs):
            width = o_ref.shape[1]
            o_ref[at, width - STAT :] = packed[b * tile : (b + 1) * tile].astype(o_ref.dtype)
        return carry

    lax.fori_loop(0, line_rows // tile, row_tile, 0)


def attend(plane, lines, kind, keys, values, bias, after=()):
    rows, columns = plane.shape[0] // lines, plane.shape[1]
    heads = columns // HD
    pairs = heads // PACK
    group = next(g for g in (10, 5, 4, 3, 2, 1) if pairs % g == 0)
    tile = next(t for t in (32, 16, rows) if rows % t == 0)
    width = columns + STAT
    scale = math.log2(math.e) / math.sqrt(HD)

    def body(*refs):
        work = refs[4 + len(after) :]
        attend_kernel(
            (tile, pairs // group, group), scale, *refs[:4], work[:lines], *work[lines:]
        )

    return pl.pallas_call(
        body,
        in_specs=[pl.BlockSpec(memory_space=pltpu.VMEM)] * 4
        + [pl.BlockSpec(memory_space=pl.ANY)] * len(after),
        out_specs=[pl.BlockSpec(memory_space=pltpu.VMEM)] * lines,
        out_shape=[jax.ShapeDtypeStruct((rows, width), kind)] * lines,
        scratch_shapes=[pltpu.VMEM((STAT, PACK * tile * lines), F32)] * 2,
        compiler_params=pltpu.CompilerParams(vmem_limit_bytes=40 * 1024 * 1024),
        cost_estimate=pl.CostEstimate(
            flops=4 * lines * rows * keys.shape[0] * columns,
            bytes_accessed=4 * keys.shape[0] * columns,
            transcendentals=lines * rows * keys.shape[0] * heads,
        ),
        name="attend",
    )(bias, plane, keys, values, *after)


def load(cached, fresh, victims, queries, after):
    cache_rows, columns = cached[0].shape
    tok = fresh[0].shape[0]
    padded = cache_rows + -(-tok // 16) * 16
    n = len(cached)

    def body(*refs):
        cached_refs, fresh_refs, victims_ref, queries_ref = refs[:n], refs[n : 2 * n], *refs[2 * n : 2 * n + 2]
        refs = refs[2 * n + 3 :]
        outs, bias_ref, q_ref, tails, ids_ref, sems = (
            refs[:n], refs[n], refs[n + 1], refs[n + 2 : 2 * n + 2], *refs[2 * n + 2 :]
        )
        ids = pltpu.make_async_copy(victims_ref, ids_ref, sems.at[1, n])
        rest = pltpu.make_async_copy(queries_ref, q_ref, sems.at[0, n])
        small = [
            pltpu.make_async_copy(src, dst, sems.at[1, i])
            for i, (src, dst) in enumerate(zip(fresh_refs, tails))
        ]
        large = [
            pltpu.make_async_copy(src, dst.at[pl.ds(0, cache_rows), :], sems.at[0, i])
            for i, (src, dst) in enumerate(zip(cached_refs, outs))
        ]
        for copy in [ids] + small + large + [rest]:
            copy.start()
        ids.wait()
        blocks = cache_rows // BLK
        first = lax.axis_index("seq") * blocks
        for block in range(blocks):
            hits = jnp.where(ids_ref[...] == first + block, 1.0, 0.0)
            hit = jnp.max(hits, axis=1, keepdims=True)
            gone = jnp.where(hit > 0.0, NEG, 0.0)
            bias_ref[block * BLK : (block + 1) * BLK, :] = jnp.broadcast_to(gone, (BLK, STAT))
        token = lax.broadcasted_iota(jnp.int32, (padded - cache_rows, STAT), 0)
        bias_ref[cache_rows:, :] = jnp.where(token < tok, 0.0, NEG)
        for copy, tail, out in zip(small, tails, outs):
            copy.wait()
            zeros = jnp.zeros((padded - cache_rows - tok, columns), F32)
            rows = jnp.concatenate([tail[...].astype(F32), zeros], axis=0)
            out[cache_rows:, :] = rows.astype(out.dtype)
        for copy in large + [rest]:
            copy.wait()

    in_hbm = pl.BlockSpec(memory_space=pltpu.HBM)
    held = (*cached, *fresh, victims, queries)
    return pl.pallas_call(
        body,
        in_specs=[in_hbm] * len(held) + [pl.BlockSpec(memory_space=pl.ANY)],
        out_specs=[pl.BlockSpec(memory_space=pltpu.VMEM)] * (n + 2),
        out_shape=[jax.ShapeDtypeStruct((padded, columns), BF16)] * n
        + [jax.ShapeDtypeStruct((padded, STAT), F32), jax.ShapeDtypeStruct(queries.shape, BF16)],
        scratch_shapes=[pltpu.VMEM(x.shape, BF16) for x in fresh]
        + [pltpu.VMEM(victims.shape, jnp.int32), pltpu.SemaphoreType.DMA((2, n + 1))],
        compiler_params=pltpu.CompilerParams(vmem_limit_bytes=24 * 1024 * 1024),
        cost_estimate=pl.CostEstimate(
            flops=0, bytes_accessed=4 * n * cache_rows * columns, transcendentals=0
        ),
        name="load",
    )(*[pltpu.with_memory_space_constraint(x, pltpu.HBM) for x in held], after)


def merged(arrays, heads, last):
    columns = heads * HD
    stats = [unpack_stats(get(slice(columns, columns + STAT))) for get in arrays]
    top = functools.reduce(jnp.maximum, [t for t, _ in stats])
    weights = [jnp.exp2(t - top) for t, _ in stats]
    mass = functools.reduce(jnp.add, [w * m for w, (_, m) in zip(weights, stats)])
    if last:
        inverse = 1.0 / jnp.where(mass > 0.0, mass, 1.0)
        weights = [w * inverse for w in weights]
    for head in range(heads):
        cols = slice(head * HD, (head + 1) * HD)
        yield cols, functools.reduce(
            jnp.add, [get(cols) * w[:, lane_of(head) : lane_of(head) + 1] for get, w in zip(arrays, weights)]
        )
    if not last:
        yield slice(columns, columns + STAT), pack_stats(top, mass)


def getter(ref, *index):
    return lambda cols: ref[(*index, slice(None), cols)].astype(F32)


def merge_rows(ins, heads, pieces, kinds):
    rows, width = ins[0].shape
    per = rows // pieces

    def body(*refs):
        outs = refs[len(ins) :]
        for cols, total in merged([getter(r) for r in refs[: len(ins)]], heads, False):
            for j, out in enumerate(outs):
                out[:, cols] = total[j * per : (j + 1) * per].astype(out.dtype)

    return call_merge(body, ins, [jax.ShapeDtypeStruct((per, width), kind) for kind in kinds])


def merge_half(ins, heads, start, pieces, tok):
    width = ins[0].shape[1]
    rows = pieces * tok

    def body(*refs):
        parts = [lambda cols, r=r: r[start : start + rows, cols].astype(F32) for r in refs[: len(ins)]]
        for cols, total in merged(parts, heads, False):
            for j, out in enumerate(refs[len(ins) :]):
                out[:, cols] = total[j * tok : (j + 1) * tok].astype(out.dtype)

    return call_merge(body, ins, [jax.ShapeDtypeStruct((tok, width), BF16)] * pieces)


def finish(ins, heads):
    rows = ins[0].shape[0]

    def body(*refs):
        out = refs[len(ins)]
        for cols, total in merged([getter(r) for r in refs[: len(ins)]], heads, True):
            out[:, cols] = total.astype(out.dtype)

    return call_merge(body, ins, [jax.ShapeDtypeStruct((rows, heads * HD), BF16)])[0]


def join(pieces, after=()):
    rows = sum(p.shape[0] for p in pieces)

    def body(*refs):
        out = refs[-1]
        ins = [r[...].astype(F32) for r in refs[: len(pieces)]]
        out[...] = jnp.concatenate(ins, axis=0).astype(out.dtype)

    shape = jax.ShapeDtypeStruct((rows, pieces[0].shape[1]), pieces[0].dtype)
    return call_merge(body, pieces, [shape], after)[0]


def call_merge(body, ins, shapes, after=()):
    size = sum(math.prod(x.shape) for x in ins)
    return pl.pallas_call(
        body,
        in_specs=[pl.BlockSpec(memory_space=pltpu.VMEM)] * len(ins)
        + [pl.BlockSpec(memory_space=pl.ANY)] * len(after),
        out_specs=[pl.BlockSpec(memory_space=pltpu.VMEM)] * len(shapes),
        out_shape=shapes,
        compiler_params=pltpu.CompilerParams(vmem_limit_bytes=48 * 1024 * 1024),
        cost_estimate=pl.CostEstimate(flops=4 * size, bytes_accessed=4 * size, transcendentals=0),
        name="merge",
    )(*ins, *after)


def per_device(queries, new_keys, new_values, cache_keys, cache_values, victims):
    members = lax.axis_size("seq")
    shape = factors(members)
    a_n, b_n, c_n = shape
    heads = queries.shape[1] // HD
    tok = queries.shape[0]

    def fetch(x, *by):
        return lax.ppermute(x, "seq", partner_perm(shape, by, False))

    def give(x, *by):
        return lax.ppermute(x, "seq", partner_perm(shape, by, True))

    far_first = [0, *range(a_n - 1, 0, -1)]
    line = [queries] + [fetch(queries, a, 0, 0) for a in far_first[1:]]
    lines = [line] + [[fetch(x, 0, b, 0) for x in line] for b in range(1, b_n)]
    keys, values, bias, line[0] = load(
        (cache_keys, cache_values), (new_keys, new_values), victims[None], queries, line[-1]
    )
    plane = join([x for pieces in lines for x in pieces])
    planes = [plane] + [fetch(plane, 0, 0, c) for c in range(1, c_n)]
    sums = []
    for c, rows in enumerate(planes):
        sums += attend(rows, b_n, BF16 if c else F32, keys, values, bias, sums[:1])

    def over_cores(b, kind):
        got = [give(sums[c * b_n + b], 0, 0, c) for c in range(1, c_n)]
        if b and a_n % 2 == 0 and a_n * tok % 32 == 0:
            halves = [(h * a_n * tok // 2, a_n // 2) for h in range(2)]
            return [x for at, n in halves for x in merge_half([sums[b]] + got, heads, at, n, tok)]
        return merge_rows([sums[b]] + got, heads, a_n, [kind] * a_n)

    got = [[give(x, 0, b, 0) for x in over_cores(b, BF16)] for b in range(1, b_n)]
    own = over_cores(0, F32)
    total = [[own[s]] + [pieces[s] for pieces in got] for s in range(a_n)]
    last = [
        give(merge_rows(total[s], heads, 1, [BF16])[0], far_first[s], 0, 0) for s in range(1, a_n)
    ]
    return finish([*merge_rows(total[0], heads, 1, [F32]), *last], heads)


def solution(mesh):
    rows = P(("groups", "seq"), None)
    return jax.shard_map(
        per_device,
        mesh=mesh,
        in_specs=(rows, rows, rows, rows, rows, P("groups")),
        out_specs=rows,
        check_vma=False,
    )
```
